32 devices in a mesh: dp: 16 (over z, y, core), narrow: 2 (over x).
Axes of the slice: x: 2, y: 2, z: 4, core: 2. Of those that a mesh axis runs over, the one named last changes fastest.
Arguments:
- tokens: bfloat16 [60928, 384], P(('dp', 'narrow')), may hold values from -6 to 6
- attn_weights: bfloat16 [1536, 192], P(('dp', 'narrow')), may hold values from -4 to 4
- norm_params: float32 [3, 2, 192], replicated, may hold values from -1 to 2
- w_in: bfloat16 [2, 192, 2, 256], P(None, None, None, 'narrow'), may hold values from -0.4375 to 0.4375
- w_out: bfloat16 [2, 256, 192], P(None, 'narrow'), may hold values from -0.375 to 0.375
- cotangent: bfloat16 [60928, 384], P(('dp', 'narrow')), may hold values from -6 to 6
Outputs:
- result: bfloat16 [60928, 384], P(('dp', 'narrow'))
- input_grad: float32 [60928, 384], P(('dp', 'narrow'))
- attn_grad: float32 [1536, 192], P(('dp', 'narrow'))
- norm_grad: float32 [3, 2, 192], replicated
- w_in_grad: float32 [2, 192, 2, 256], P(None, None, None, 'narrow')
- w_out_grad: float32 [2, 256, 192], P(None, 'narrow')
The draws below stay inside these ranges and needn't reach their ends.
All inputs are finite; a program needn't handle non-finite values.
Results may differ from the reference program's by a relative error of at most 0.024.
Values may be sent and summed in bfloat16 or wider, within the bound.
No kernel may reach another device: no remote copies, remote signals or barrier semaphores. Data moves between devices by JAX's collectives and lax.ppermute only.
A program may use at most 256 MiB of HBM per device.

```python
import math
import jax
import jax.numpy as jnp
from jax import lax

HEADS = 8
HEAD = 24
D = 192
FF = 256
LAYERS = 2
SEQ = 476
SAMPLES = 256
TOKENS = 121856


def draw_attn_weights(key, part):
    key = jax.random.fold_in(key, 11)
    model_width = HEADS * HEAD
    sample_raw = jax.random.truncated_normal(key, -2.5, 2.5, (4 * LAYERS * model_width, model_width), jnp.float32)
    row_ids = jnp.arange(4 * LAYERS * model_width)
    block_ids = row_ids // model_width % 4
    factor = jnp.where(block_ids == 3, 8.0, jnp.where(block_ids < 2, 1.3, 1.0))
    return (sample_raw * factor[:, None] * model_width ** (-0.5)).astype(jnp.bfloat16)


def draw_norm_params(key, part):
    key = jax.random.fold_in(key, 23)
    raw_draw = jax.random.truncated_normal(key, -3.0, 3.0, (2 * LAYERS - 1, 2, HEADS * HEAD), jnp.float32)
    member_ids = jnp.arange(2).reshape(1, 2, 1)
    return jnp.where(member_ids == 0, 1.0 + 0.15 * raw_draw, 0.2 * raw_draw)


def steps_of(own_key, extent, pieces, least, top_value):
    gain = 1.0
    for dim, blocks in pieces:
        steps = jax.random.uniform(jax.random.fold_in(jax.random.fold_in(own_key, 6), dim), (blocks,), jnp.float32, least / len(pieces), top_value / len(pieces))
        gain = gain * jnp.repeat(jnp.exp(steps), extent[dim] // blocks).reshape((-1,) + (1,) * (len(extent) - 1 - dim))
    return gain


def gaussian(rng, dims, deviation, bound, shards=(), held_as=jnp.bfloat16):
    values = jax.random.normal(rng, dims, jnp.float32) * deviation
    if len(shards) > 0:
        values = steps_of(rng, dims, shards, -0.22, 0.18) * values
    return jnp.clip(values, min=-bound, max=bound).astype(held_as)


def setup_inputs(seed: int = 0) -> dict:
    key_of = jax.random.split(jax.random.key(seed), 7)
    return {
        "tokens": gaussian(key_of[0], (TOKENS // 2, 2 * D), 1.0, 6.0, ((0, 32),)),
        "attn_weights": draw_attn_weights(jax.random.fold_in(key_of[6], 71), 0),
        "norm_params": draw_norm_params(jax.random.fold_in(key_of[6], 71), 0),
        "w_in": gaussian(key_of[3], (LAYERS, D, 2, FF), D ** -0.5, 0.4375, ((3, 2),)),
        "w_out": gaussian(key_of[4], (LAYERS, FF, D), FF ** -0.5, 0.375, ((1, 2),)),
        "cotangent": gaussian(key_of[5], (TOKENS // 2, 2 * D), 1.0, 6.0, ((0, 32),)),
    }


HIGHEST = lax.Precision.HIGHEST

@jax.custom_vjp
def low(v):
    return lax.optimization_barrier(v.astype(jnp.bfloat16)).astype(jnp.float32)

@jax.custom_vjp
def low_back(v):
    return v

def low_keep(v):
    return (low(v), None)

def low_pass(kept, grad):
    return (grad,)

def back_keep(v):
    return (v, None)

def back_low(kept, grad):
    return (low(grad),)
low.defvjp(low_keep, low_pass)
low_back.defvjp(back_keep, back_low)

def layer_norm(stream, norm_gain, norm_shift):
    center = stream - lax.optimization_barrier(jnp.mean(stream, axis=-1, keepdims=True))
    spread = lax.optimization_barrier(jnp.mean(center * center, axis=-1, keepdims=True))
    return center * lax.rsqrt(spread + 1e-05) * norm_gain + norm_shift

def matmul(left, right):
    return jnp.dot(left, right, precision=HIGHEST)

def attend_one(triple):
    queries, key_rows, value_rows = triple
    shaped_q = queries.reshape(SEQ, HEADS, HEAD)
    shaped_k = key_rows.reshape(SEQ, HEADS, HEAD)
    shaped_v = value_rows.reshape(SEQ, HEADS, HEAD)
    scores = jnp.einsum('qhd,khd->hqk', shaped_q, shaped_k, precision=HIGHEST) * HEAD ** (-0.5)
    scores = low_back(scores)
    probs_b = low(jax.nn.softmax(scores, axis=-1))
    context = jnp.einsum('hqk,khd->qhd', probs_b, shaped_v, precision=HIGHEST)
    return context.reshape(SEQ, HEADS * HEAD)

def attention_branch(normed, weights):
    model_width = HEADS * HEAD
    joined = jnp.concatenate([weights[0], weights[1], weights[2]], axis=1)
    projected = low_back(low(matmul(normed, joined)))
    samples = normed.shape[0] // SEQ
    queries = projected[:, :model_width].reshape(samples, SEQ, model_width)
    key_rows = projected[:, model_width:2 * model_width].reshape(samples, SEQ, model_width)
    value_rows = projected[:, 2 * model_width:].reshape(samples, SEQ, model_width)
    context = lax.map(jax.checkpoint(attend_one), (queries, key_rows, value_rows))
    context = low_back(low(context.reshape(samples * SEQ, model_width)))
    return low_back(matmul(context, weights[3]))

def feed_forward(normed, weight_in, weight_out):
    mixed_pre = low_back(jnp.einsum('td,dgf->tgf', normed, weight_in, precision=HIGHEST))
    hidden = low(mixed_pre[:, 0] * jax.nn.silu(mixed_pre[:, 1]))
    return low_back(matmul(hidden, weight_out))

def forward(stream_in, attn_flat, norm_table, weight_in, weight_out):
    model_width = HEADS * HEAD
    attn_all = attn_flat.reshape(LAYERS, 4, model_width, model_width)
    stream = stream_in
    for layer_no in range(LAYERS):
        if layer_no == 0:
            normed = stream
        else:
            normed = low(layer_norm(stream, norm_table[2 * layer_no - 1, 0], norm_table[2 * layer_no - 1, 1]))
        stream = stream + attention_branch(normed, attn_all[layer_no])
        normed = low(layer_norm(stream, norm_table[2 * layer_no, 0], norm_table[2 * layer_no, 1]))
        stream = stream + feed_forward(normed, weight_in[layer_no], weight_out[layer_no])
    return stream

def reference(tokens, attn_weights, norm_params, w_in, w_out, cotangent):
    model_width = HEADS * HEAD
    per_group = math.gcd(SAMPLES, max(1, 4096 // SEQ))
    group_count = SAMPLES // per_group
    stream_all = tokens.astype(jnp.float32).reshape(group_count, per_group * SEQ, model_width)
    cotan_all = cotangent.astype(jnp.float32).reshape(group_count, per_group * SEQ, model_width)
    params = (attn_weights.astype(jnp.float32), norm_params.astype(jnp.float32), w_in.astype(jnp.float32), w_out.astype(jnp.float32))

    def one_group(totals, inputs):
        stream_in, cotan_rows = inputs
        outputs, pullback = jax.vjp(forward, stream_in, params[0], params[1], params[2], params[3])
        gradients = pullback(cotan_rows)
        totals = jax.tree.map(lambda left, right: left + right, totals, tuple(gradients[1:]))
        return (totals, (outputs.astype(jnp.bfloat16), gradients[0]))
    zero_sums = jax.tree.map(jnp.zeros_like, params)
    totals, (results, input_grads) = lax.scan(one_group, zero_sums, (stream_all, cotan_all))
    return (results.reshape(TOKENS // 2, 2 * model_width), input_grads.reshape(TOKENS // 2, 2 * model_width), totals[0], totals[1], totals[2], totals[3])
```

```python
import functools
import math

import jax
import jax.numpy as jnp
from jax import lax
from jax.experimental import pallas as pl
from jax.experimental.pallas import tpu as pltpu
from jax.sharding import PartitionSpec as P

HEADS = 8
HEAD = 24
SLOT = 32
WIDE = HEADS * SLOT
D = HEADS * HEAD
FF = 256
LAYERS = 2
SEQ = 476
PAIRS = SEQ // 2
KEYS = 240
HALF = 256
LANES = 2 * HALF
EPS = 1e-05
SCALE = HEAD ** (-0.5)
LOG2E = math.log2(math.e)

bf16 = jnp.bfloat16
f32 = jnp.float32


def mm(left, right):
    return jnp.dot(left, right, preferred_element_type=f32)


def mm_nt(left, right):
    return lax.dot_general(left, right, (((1,), (1,)), ((), ())), preferred_element_type=f32)


def fold_lanes(value):
    return value[:, 0:128] + value[:, 128:256] + value[:, 256:384] + value[:, 384:512]


def norm_forward(stream, gain, shift):
    center = stream - jnp.sum(stream, axis=0, keepdims=True) * (1.0 / D)
    inverse = lax.rsqrt(jnp.sum(center * center, axis=0, keepdims=True) * (1.0 / D) + EPS)
    unit = center * inverse
    return (unit * gain + shift, unit, inverse)


def norm_backward(grad, unit, inverse, gain):
    scaled = grad * gain
    mean = jnp.sum(scaled, axis=0, keepdims=True) * (1.0 / D)
    slope = jnp.sum(scaled * unit, axis=0, keepdims=True) * (1.0 / D)
    return inverse * (scaled - mean - unit * slope)


def kernel(
    x_ref, g_ref, wqkv_t, wqkv, wo_t, wo, win_t, win, wout_t, wout, norm_t,
    res_ref, ig_ref, d_wqkv, d_wo, d_win, d_wout, d_norm,
    e_ref, kh_ref, vh_ref, q_ref, k_ref, v_ref, do_ref, ctx_ref, ctxb_ref, rinv_ref, dp_ref, mixed_ref,
):
    @pl.when(pl.program_id(0) == 0)
    def _():
        d_wqkv[...] = jnp.zeros_like(d_wqkv)
        d_wo[...] = jnp.zeros_like(d_wo)
        d_win[...] = jnp.zeros_like(d_win)
        d_wout[...] = jnp.zeros_like(d_wout)
        d_norm[...] = jnp.zeros_like(d_norm)
        dp_ref[...] = jnp.zeros_like(dp_ref)

    lane = lax.broadcasted_iota(jnp.int32, (WIDE, LANES), 1)
    row = lax.broadcasted_iota(jnp.int32, (WIDE, LANES), 0)
    real = (lane & (HALF - 1)) < PAIRS
    slot_row = row & (SLOT - 1)
    ones_rows = jnp.logical_or(slot_row == HEAD, slot_row == HEAD + 1).astype(f32)
    head_row = lax.broadcasted_iota(jnp.int32, (SLOT, LANES), 0)

    def rows_of(h):
        return pl.ds(pl.multiple_of(h * SLOT, SLOT), SLOT)

    def attention_forward(layer, normed_b):
        qkv = mm(wqkv_t[layer], normed_b)
        q_ref[layer] = (qkv[:WIDE] * (SCALE * LOG2E)).astype(bf16)
        keys = qkv[WIDE : 2 * WIDE].astype(bf16)
        k_ref[layer] = keys
        values = jnp.where(real, qkv[2 * WIDE :] + ones_rows, 0.0).astype(bf16)
        v_ref[...] = values
        for tall, ref in ((keys.T, kh_ref), (values.T, vh_ref)):
            for h in range(HEADS):
                ref[layer, h, 0:KEYS] = tall[0:KEYS, SLOT * h : SLOT * (h + 1)]
                ref[layer, h, KEYS:] = tall[HALF : HALF + KEYS, SLOT * h : SLOT * (h + 1)]

        def one_head(h, _):
            rows = rows_of(h)
            scores = mm(kh_ref[layer, h], q_ref[layer, rows, :])
            top = jnp.max(scores, axis=0, keepdims=True)
            weights = jnp.exp2(scores - top).astype(bf16)
            e_ref[layer, h] = weights
            out = mm(v_ref[rows, 0:KEYS], weights[0:KEYS]) + mm(
                v_ref[rows, HALF : HALF + KEYS], weights[KEYS:]
            )
            inverse = 1.0 / out[HEAD : HEAD + 1]
            rinv_ref[layer, h] = inverse
            context = out * inverse
            ctx_ref[layer, rows, :] = context
            ctxb_ref[layer, rows, :] = context.astype(bf16)
            return 0

        lax.fori_loop(0, HEADS, one_head, 0)
        return mm(wo_t[layer], ctxb_ref[layer])

    def attention_backward(layer, grad_b, normed_b):
        d_wo[layer] += mm_nt(ctxb_ref[layer], grad_b)
        do_ref[...] = mm(wo[layer], grad_b)

        def one_head(h, _):
            rows = rows_of(h)
            grad = (do_ref[rows, :] * rinv_ref[layer, h]).astype(bf16).astype(f32)
            dot = -jnp.sum(grad[:HEAD] * ctx_ref[layer, rows, :][:HEAD], axis=0, keepdims=True)
            dot_high = dot.astype(bf16).astype(f32)
            grad = jnp.where(head_row == HEAD, dot_high, grad)
            grad = jnp.where(head_row == HEAD + 1, dot - dot_high, grad).astype(bf16)
            weights = e_ref[layer, h]
            d_scores = (weights.astype(f32) * mm(vh_ref[layer, h], grad)).astype(bf16)
            keys = k_ref[layer, rows, :]
            queries = q_ref[layer, rows, :]
            dq = mm(keys[:, 0:KEYS], d_scores[0:KEYS]) + mm(
                keys[:, HALF : HALF + KEYS], d_scores[KEYS:]
            )
            dp_ref[rows, :] = (dq * SCALE).astype(bf16)
            krows = pl.ds(pl.multiple_of(WIDE + h * SLOT, SLOT), SLOT)
            vrows = pl.ds(pl.multiple_of(2 * WIDE + h * SLOT, SLOT), SLOT)
            for half in range(2):
                here = slice(half * KEYS, (half + 1) * KEYS)
                lanes = slice(half * HALF, half * HALF + KEYS)
                dk = mm_nt(queries, d_scores[here]) * (1.0 / LOG2E)
                dp_ref[krows, lanes] = dk.astype(bf16)
                dv = mm_nt(grad, weights[here])
                key_lane = lax.broadcasted_iota(jnp.int32, (SLOT, KEYS), 1)
                dp_ref[vrows, lanes] = jnp.where(key_lane < PAIRS, dv, 0.0).astype(bf16)
            return 0

        lax.fori_loop(0, HEADS, one_head, 0)
        d_wqkv[layer] += mm_nt(dp_ref[...], normed_b)
        return mm(wqkv[layer], dp_ref[...])

    def add_norm(index, grad, unit):
        d_norm[2 * index] += fold_lanes(grad * unit)
        d_norm[2 * index + 1] += fold_lanes(grad)

    def gain_of(index):
        return norm_t[:, 2 * index : 2 * index + 1]

    def shift_of(index):
        return norm_t[:, 2 * index + 1 : 2 * index + 2]

    kept = []
    normed_b = x_ref[0]
    stream = normed_b.astype(f32)
    unit_a = inv_a = None
    for layer in range(LAYERS):
        if layer > 0:
            normed, unit_a, inv_a = norm_forward(
                stream, gain_of(2 * layer - 1), shift_of(2 * layer - 1)
            )
            normed_b = normed.astype(bf16)
        stream = stream + attention_forward(layer, normed_b)
        normed, unit_f, inv_f = norm_forward(stream, gain_of(2 * layer), shift_of(2 * layer))
        ffn_b = normed.astype(bf16)
        mixed = mm(win_t[layer], ffn_b)
        mixed_ref[layer] = mixed
        gate = mixed[FF:]
        hidden = (mixed[:FF] * (gate * jax.nn.sigmoid(gate))).astype(bf16)
        stream = stream + mm(wout_t[layer], hidden)
        kept.append((normed_b, unit_a, inv_a, ffn_b, unit_f, inv_f, hidden))
    res_ref[0] = stream.astype(bf16)

    grad = g_ref[0].astype(f32)
    for layer in reversed(range(LAYERS)):
        normed_b, unit_a, inv_a, ffn_b, unit_f, inv_f, hidden = kept[layer]
        grad_b = grad.astype(bf16)
        d_wout[layer] += mm_nt(hidden, grad_b)
        d_hidden = mm(wout[layer], grad_b)
        value = mixed_ref[layer, 0:FF]
        gate = mixed_ref[layer, FF:]
        sig = jax.nn.sigmoid(gate)
        d_value = (d_hidden * (gate * sig)).astype(bf16)
        d_gate = (d_hidden * value * sig * (1.0 + gate * (1.0 - sig))).astype(bf16)
        d_mixed = jnp.concatenate([d_value, d_gate], axis=0)
        d_win[layer] += mm_nt(ffn_b, d_mixed)
        d_normed = mm(win[layer], d_mixed)
        add_norm(2 * layer, d_normed, unit_f)
        grad = grad + norm_backward(d_normed, unit_f, inv_f, gain_of(2 * layer))
        d_att = attention_backward(layer, grad.astype(bf16), normed_b)
        if layer > 0:
            add_norm(2 * layer - 1, d_att, unit_a)
            grad = grad + norm_backward(d_att, unit_a, inv_a, gain_of(2 * layer - 1))
        else:
            grad = grad + d_att
    ig_ref[0] = grad


def whole(shape):
    return pl.BlockSpec(shape, lambda i: (0,) * len(shape))


def per_sample(shape):
    return pl.BlockSpec((1,) + shape, lambda i: (i, 0, 0))


def run_layers(x_t, g_t, weights, norm_t):
    samples = x_t.shape[0]
    grad_shapes = [
        (LAYERS, 3 * WIDE, D),
        (LAYERS, WIDE, D),
        (LAYERS, D, 2 * FF),
        (LAYERS, FF, D),
        (2 * (2 * LAYERS - 1), D, 128),
    ]
    return pl.pallas_call(
        kernel,
        grid=(samples,),
        in_specs=[per_sample((D, LANES))] * 2 + [whole(w.shape) for w in weights] + [whole(norm_t.shape)],
        out_specs=[per_sample((D, LANES))] * 2 + [whole(s) for s in grad_shapes],
        out_shape=[
            jax.ShapeDtypeStruct((samples, D, LANES), bf16),
            jax.ShapeDtypeStruct((samples, D, LANES), f32),
        ]
        + [jax.ShapeDtypeStruct(s, f32) for s in grad_shapes],
        scratch_shapes=[
            pltpu.VMEM((LAYERS, HEADS, 2 * KEYS, LANES), bf16),
            pltpu.VMEM((LAYERS, HEADS, 2 * KEYS, SLOT), bf16),
            pltpu.VMEM((LAYERS, HEADS, 2 * KEYS, SLOT), bf16),
            pltpu.VMEM((LAYERS, WIDE, LANES), bf16),
            pltpu.VMEM((LAYERS, WIDE, LANES), bf16),
            pltpu.VMEM((WIDE, LANES), bf16),
            pltpu.VMEM((WIDE, LANES), f32),
            pltpu.VMEM((LAYERS, WIDE, LANES), f32),
            pltpu.VMEM((LAYERS, WIDE, LANES), bf16),
            pltpu.VMEM((LAYERS, HEADS, 1, LANES), f32),
            pltpu.VMEM((3 * WIDE, LANES), bf16),
            pltpu.VMEM((LAYERS, 2 * FF, LANES), f32),
        ],
        compiler_params=pltpu.CompilerParams(
            dimension_semantics=("arbitrary",), vmem_limit_bytes=60 * 1024 * 1024
        ),
        cost_estimate=pl.CostEstimate(
            flops=samples * 40_000_000_000 // 8, bytes_accessed=20_000_000, transcendentals=0
        ),
    )(x_t, g_t, *weights, norm_t)


def to_lanes(paired, edge):
    rows = paired.shape[0]
    cube = paired.reshape(rows // PAIRS, PAIRS, 2, D).transpose(0, 3, 2, 1)
    if edge:
        fill = jnp.broadcast_to(cube[..., :1], cube.shape[:-1] + (HALF - PAIRS,))
    else:
        fill = jnp.zeros(cube.shape[:-1] + (HALF - PAIRS,), cube.dtype)
    return jnp.concatenate([cube, fill], axis=-1).reshape(rows // PAIRS, D, LANES)


def from_lanes(cube):
    samples = cube.shape[0]
    cube = cube.reshape(samples, D, 2, HALF)[..., :PAIRS].transpose(0, 3, 2, 1)
    return cube.reshape(samples * PAIRS, 2 * D)


def pad_heads(matrix, axis):
    shape = list(matrix.shape)
    split = shape[:axis] + [HEADS, HEAD] + shape[axis + 1 :]
    pads = [(0, 0)] * len(split)
    pads[axis + 1] = (0, SLOT - HEAD)
    shape[axis] = WIDE
    return jnp.pad(matrix.reshape(split), pads).reshape(shape)


def on_device(tokens, attn_weights, norm_params, w_in, w_out, cotangent):
    x_t = to_lanes(tokens, True)
    g_t = to_lanes(cotangent, False)
    attn_all = lax.all_gather(attn_weights, ("dp", "narrow"), axis=0, tiled=True)
    attn_all = attn_all.reshape(LAYERS, 4, D, D)
    win_all = lax.all_gather(w_in, "narrow", axis=3, tiled=True).reshape(LAYERS, D, 2 * FF)
    wout_all = lax.all_gather(w_out, "narrow", axis=1, tiled=True)
    wqkv = pad_heads(attn_all[:, :3].transpose(0, 2, 1, 3), 3).reshape(LAYERS, D, 3 * WIDE)
    wo = pad_heads(attn_all[:, 3], 1)
    flip = lambda w: w.transpose(0, 2, 1)
    weights = (flip(wqkv), wqkv, flip(wo), wo, flip(win_all), win_all, flip(wout_all), wout_all)
    norm_t = jnp.pad(norm_params.reshape(-1, D).T, ((0, 0), (0, 2)))
    res, ig, d_wqkv, d_wo, d_win, d_wout, d_norm = run_layers(x_t, g_t, weights, norm_t)
    d_wqkv = d_wqkv.reshape(LAYERS, 3, HEADS, SLOT, D)[:, :, :, :HEAD].reshape(LAYERS, 3, D, D)
    d_wo = d_wo.reshape(LAYERS, 1, HEADS, SLOT, D)[:, :, :, :HEAD].reshape(LAYERS, 1, D, D)
    d_attn = jnp.concatenate([d_wqkv.transpose(0, 1, 3, 2), d_wo], axis=1)
    attn_share = lax.psum_scatter(
        d_attn.reshape(LAYERS * 4 * D, D), ("dp", "narrow"), scatter_dimension=0, tiled=True
    )
    norm_total = lax.psum(jnp.sum(d_norm, axis=-1).reshape(norm_params.shape), ("dp", "narrow"))
    win_sum = lax.psum_scatter(
        d_win.reshape(LAYERS, D, 2, FF), "narrow", scatter_dimension=3, tiled=True
    )
    wout_sum = lax.psum_scatter(d_wout, "narrow", scatter_dimension=1, tiled=True)
    win_sum, wout_sum = lax.psum((win_sum, wout_sum), "dp")
    return (from_lanes(res), from_lanes(ig), attn_share, norm_total, win_sum, wout_sum)


def solution(mesh):
    rows = P(("dp", "narrow"), None)
    hidden_in = P(None, None, None, "narrow")
    hidden_out = P(None, "narrow", None)
    return jax.shard_map(
        on_device,
        mesh=mesh,
        in_specs=(rows, rows, P(), hidden_in, hidden_out, rows),
        out_specs=(rows, rows, rows, P(), hidden_in, hidden_out),
        check_vma=False,
    )
```

```python
import math

import jax
import jax.numpy as jnp
from jax import lax
from jax.experimental import pallas as pl
from jax.experimental.pallas import tpu as pltpu
from jax.sharding import PartitionSpec as P

HEADS = 8
HEAD = 24
SLOT = 32
WIDE = HEADS * SLOT
D = HEADS * HEAD
FF = 256
FFH = FF // 2
LAYERS = 2
NORMS = 2 * LAYERS - 1
SEQ = 476
PAIRS = SEQ // 2
KEYS = 240
HALF = 256
LANES = 2 * HALF
EPS = 1e-05
SCALE = HEAD ** (-0.5)
LOG2E = math.log2(math.e)
ATTN_ROWS = LAYERS * 4 * D

GROUP = 8
WIN_PART = LAYERS * D // 4
WOUT_PART = LAYERS * FFH // 4
ATTN_PART = ATTN_ROWS // GROUP
OFF_WOUT = ATTN_PART
OFF_NORM = OFF_WOUT + WOUT_PART
OFF_WIN = OFF_NORM + 16
PAY_ROWS = OFF_WIN + WIN_PART

bf16 = jnp.bfloat16
f32 = jnp.float32
AXES = ("dp", "narrow")


def mm(left, right):
    return jnp.dot(left, right, preferred_element_type=f32)


def mm_nt(left, right):
    return lax.dot_general(left, right, (((1,), (1,)), ((), ())), preferred_element_type=f32)


def fold_lanes(value):
    return value[:, 0:128] + value[:, 128:256] + value[:, 256:384] + value[:, 384:512]


def norm_forward(stream, gain, shift):
    center = stream - jnp.sum(stream, axis=0, keepdims=True) * (1.0 / D)
    inverse = lax.rsqrt(jnp.sum(center * center, axis=0, keepdims=True) * (1.0 / D) + EPS)
    unit = center * inverse
    return (unit * gain + shift, unit, inverse)


def norm_backward(grad, unit, inverse, gain):
    scaled = grad * gain
    mean = jnp.sum(scaled, axis=0, keepdims=True) * (1.0 / D)
    slope = jnp.sum(scaled * unit, axis=0, keepdims=True) * (1.0 / D)
    return inverse * (scaled - mean - unit * slope)


def tree_sum(parts):
    while len(parts) > 1:
        parts = [parts[i] + parts[i + 1] for i in range(0, len(parts), 2)]
    return parts[0]


def ds(start, size, step):
    return pl.ds(pl.multiple_of(start, step), size)


def layers_kernel(parts, *refs):
    refs = list(refs)

    def take(count):
        taken = refs[:count]
        del refs[:count]
        return taken

    me_ref, x_ref, g_ref, norm_ref, win_own, win_other, wout_own, wout_other = take(8)
    attn_refs = take(GROUP if parts else 1)
    res_ref, ig_ref = take(2)
    out_refs = take(GROUP if parts else 4)
    wqkv_t, wqkv, wo_t, wo, win_t, win, wout_t, wout, norm_t, attn_ref = take(10)
    d_wqkv, d_wo, d_win, d_wout, d_norm, d_attn = take(6)
    e_ref, kh_ref, vh_ref, q_ref, k_ref, v_ref, do_ref, ctx_ref, ctxb_ref, rinv_ref, dp_ref, mixed_ref = refs
    step = pl.program_id(0)
    rows_total = x_ref.shape[0]

    @pl.when(step == 0)
    def _():
        for ref in (d_wqkv, d_wo, d_win, d_wout, d_norm, dp_ref):
            ref[...] = jnp.zeros_like(ref)
        if parts:
            me = me_ref[0]
            upper = parts // GROUP
            each = ATTN_ROWS // parts
            for k in range(GROUP):
                for u in range(upper):
                    owner = ((me // GROUP) ^ u) * GROUP + ((me % GROUP) ^ k)
                    attn_ref[ds(owner * each, each, each), :] = attn_refs[k][u]
        else:
            attn_ref[...] = attn_refs[0][...]
        norm_t[...] = jnp.concatenate([norm_ref[...], jnp.zeros((8 - 2 * NORMS, D), f32)], axis=0).T
        gap = jnp.zeros((SLOT - HEAD, D), f32)

        def pad_heads(matrix):
            slots = []
            for h in range(HEADS):
                slots += [matrix[HEAD * h : HEAD * (h + 1)], gap]
            return jnp.concatenate(slots, axis=0)

        for layer in range(LAYERS):
            for j in range(4):
                base = (4 * layer + j) * D
                matrix = attn_ref[base : base + D, :].astype(f32)
                if j < 3:
                    tall = pad_heads(matrix.T)
                    wqkv_t[layer, j * WIDE : (j + 1) * WIDE, :] = tall.astype(bf16)
                    wqkv[layer, :, j * WIDE : (j + 1) * WIDE] = tall.T.astype(bf16)
                else:
                    tall = pad_heads(matrix)
                    wo[layer] = tall.astype(bf16)
                    wo_t[layer] = tall.T.astype(bf16)
            for p, (w1, w2) in enumerate(((win_own, wout_own), (win_other, wout_other))):
                win[layer, :, p * FF : (p + 1) * FF] = w1[layer]
                win_t[layer, p * FF : (p + 1) * FF, :] = w1[layer].astype(f32).T.astype(bf16)
                wout[layer, p * FFH : (p + 1) * FFH, :] = w2[layer]
                wout_t[layer, :, p * FFH : (p + 1) * FFH] = w2[layer].astype(f32).T.astype(bf16)

    base = step * PAIRS
    start = jnp.minimum(base // 16 * 16, rows_total - HALF)
    shift = base - start
    window = ds(start, HALF, 16)
    pair_row = lax.broadcasted_iota(jnp.int32, (HALF, 2 * D), 0)

    def load(ref, fill_first):
        rows = pltpu.roll(ref[window, :].astype(f32), lax.rem(HALF - shift, HALF), 0)
        fill = rows[0:1] if fill_first else 0.0
        cols = jnp.where(pair_row < PAIRS, rows, fill).T
        return jnp.concatenate([cols[:D], cols[D:]], axis=1)

    def store(ref, value):
        cols = jnp.concatenate([value[:, :HALF], value[:, HALF:]], axis=0)
        rows = pltpu.roll(cols.T, shift, 0)
        here = jnp.logical_and(pair_row >= shift, pair_row < shift + PAIRS)
        ref[window, :] = jnp.where(here, rows, ref[window, :].astype(f32)).astype(ref.dtype)

    lane = lax.broadcasted_iota(jnp.int32, (WIDE, LANES), 1)
    row = lax.broadcasted_iota(jnp.int32, (WIDE, LANES), 0)
    real = (lane & (HALF - 1)) < PAIRS
    slot_row = row & (SLOT - 1)
    ones_rows = jnp.logical_or(slot_row == HEAD, slot_row == HEAD + 1).astype(f32)
    head_row = lax.broadcasted_iota(jnp.int32, (SLOT, LANES), 0)

    def attention_forward(layer, normed_b):
        qkv = mm(wqkv_t[layer], normed_b)
        q_ref[layer] = (qkv[:WIDE] * (SCALE * LOG2E)).astype(bf16)
        keys = qkv[WIDE : 2 * WIDE].astype(bf16)
        k_ref[layer] = keys
        values = jnp.where(real, qkv[2 * WIDE :] + ones_rows, 0.0).astype(bf16)
        v_ref[...] = values
        for tall, ref in ((keys.T, kh_ref), (values.T, vh_ref)):
            for h in range(HEADS):
                ref[layer, h, 0:KEYS] = tall[0:KEYS, SLOT * h : SLOT * (h + 1)]
                ref[layer, h, KEYS:] = tall[HALF : HALF + KEYS, SLOT * h : SLOT * (h + 1)]

        def one_head(h, _):
            rows = ds(h * SLOT, SLOT, SLOT)
            scores = mm(kh_ref[layer, h], q_ref[layer, rows, :])
            top = jnp.max(scores, axis=0, keepdims=True)
            weights = jnp.exp2(scores - top).astype(bf16)
            e_ref[layer, h] = weights
            out = mm(v_ref[rows, 0:KEYS], weights[0:KEYS]) + mm(
                v_ref[rows, HALF : HALF + KEYS], weights[KEYS:]
            )
            inverse = 1.0 / out[HEAD : HEAD + 1]
            rinv_ref[layer, h] = inverse
            context = out * inverse
            ctx_ref[layer, rows, :] = context
            ctxb_ref[layer, rows, :] = context.astype(bf16)
            return 0

        lax.fori_loop(0, HEADS, one_head, 0)
        return mm(wo_t[layer], ctxb_ref[layer])

    def attention_backward(layer, grad_b, normed_b):
        d_wo[layer] += mm_nt(ctxb_ref[layer], grad_b)
        do_ref[...] = mm(wo[layer], grad_b)

        def one_head(h, _):
            rows = ds(h * SLOT, SLOT, SLOT)
            grad = (do_ref[rows, :] * rinv_ref[layer, h]).astype(bf16).astype(f32)
            dot = -jnp.sum(grad[:HEAD] * ctx_ref[layer, rows, :][:HEAD], axis=0, keepdims=True)
            dot_high = dot.astype(bf16).astype(f32)
            grad = jnp.where(head_row == HEAD, dot_high, grad)
            grad = jnp.where(head_row == HEAD + 1, dot - dot_high, grad).astype(bf16)
            weights = e_ref[layer, h]
            d_scores = (weights.astype(f32) * mm(vh_ref[layer, h], grad)).astype(bf16)
            keys = k_ref[layer, rows, :]
            queries = q_ref[layer, rows, :]
            dq = mm(keys[:, 0:KEYS], d_scores[0:KEYS]) + mm(
                keys[:, HALF : HALF + KEYS], d_scores[KEYS:]
            )
            dp_ref[rows, :] = (dq * SCALE).astype(bf16)
            krows = ds(WIDE + h * SLOT, SLOT, SLOT)
            vrows = ds(2 * WIDE + h * SLOT, SLOT, SLOT)
            for half in range(2):
                here = slice(half * KEYS, (half + 1) * KEYS)
                lanes = slice(half * HALF, half * HALF + KEYS)
                dk = mm_nt(queries, d_scores[here]) * (1.0 / LOG2E)
                dp_ref[krows, lanes] = dk.astype(bf16)
                dv = mm_nt(grad, weights[here])
                key_lane = lax.broadcasted_iota(jnp.int32, (SLOT, KEYS), 1)
                dp_ref[vrows, lanes] = jnp.where(key_lane < PAIRS, dv, 0.0).astype(bf16)
            return 0

        lax.fori_loop(0, HEADS, one_head, 0)
        d_wqkv[layer] += mm_nt(dp_ref[...], normed_b)
        return mm(wqkv[layer], dp_ref[...])

    def add_norm(index, grad, unit):
        d_norm[2 * index] += fold_lanes(grad * unit)
        d_norm[2 * index + 1] += fold_lanes(grad)

    def gain_of(index):
        return norm_t[:, 2 * index : 2 * index + 1]

    def shift_of(index):
        return norm_t[:, 2 * index + 1 : 2 * index + 2]

    kept = []
    stream = load(x_ref, True)
    normed_b = stream.astype(bf16)
    unit_a = inv_a = None
    for layer in range(LAYERS):
        if layer > 0:
            normed, unit_a, inv_a = norm_forward(stream, gain_of(2 * layer - 1), shift_of(2 * layer - 1))
            normed_b = normed.astype(bf16)
        stream = stream + attention_forward(layer, normed_b)
        normed, unit_f, inv_f = norm_forward(stream, gain_of(2 * layer), shift_of(2 * layer))
        ffn_b = normed.astype(bf16)
        mixed = mm(win_t[layer], ffn_b)
        mixed_ref[layer] = mixed
        hidden = []
        for p in range(2):
            value = mixed[FF * p : FF * p + FFH]
            gate = mixed[FF * p + FFH : FF * (p + 1)]
            hidden.append((value * (gate * jax.nn.sigmoid(gate))).astype(bf16))
        hidden = jnp.concatenate(hidden, axis=0)
        stream = stream + mm(wout_t[layer], hidden)
        kept.append((normed_b, unit_a, inv_a, ffn_b, unit_f, inv_f, hidden))
    store(res_ref, stream)

    grad = load(g_ref, False)
    for layer in reversed(range(LAYERS)):
        normed_b, unit_a, inv_a, ffn_b, unit_f, inv_f, hidden = kept[layer]
        grad_b = grad.astype(bf16)
        d_wout[FF * layer : FF * (layer + 1), :] += mm_nt(hidden, grad_b)
        d_hidden = mm(wout[layer], grad_b)
        d_mixed = []
        for p in range(2):
            value = mixed_ref[layer, FF * p : FF * p + FFH]
            gate = mixed_ref[layer, FF * p + FFH : FF * (p + 1)]
            part = d_hidden[FFH * p : FFH * (p + 1)]
            sig = jax.nn.sigmoid(gate)
            d_mixed.append((part * (gate * sig)).astype(bf16))
            d_mixed.append((part * value * sig * (1.0 + gate * (1.0 - sig))).astype(bf16))
        d_mixed = jnp.concatenate(d_mixed, axis=0)
        d_win[D * layer : D * (layer + 1), :] += mm_nt(ffn_b, d_mixed)
        d_normed = mm(win[layer], d_mixed)
        add_norm(2 * layer, d_normed, unit_f)
        grad = grad + norm_backward(d_normed, unit_f, inv_f, gain_of(2 * layer))
        d_att = attention_backward(layer, grad.astype(bf16), normed_b)
        if layer > 0:
            add_norm(2 * layer - 1, d_att, unit_a)
            grad = grad + norm_backward(d_att, unit_a, inv_a, gain_of(2 * layer - 1))
        else:
            grad = grad + d_att
    store(ig_ref, grad)

    @pl.when(step == pl.num_programs(0) - 1)
    def _():
        for layer in range(LAYERS):
            for j in range(4):
                source = d_wqkv[layer, j * WIDE : (j + 1) * WIDE] if j < 3 else d_wo[layer]
                slim = jnp.concatenate([source[SLOT * h : SLOT * h + HEAD] for h in range(HEADS)], axis=0)
                base = (4 * layer + j) * D
                d_attn[base : base + D, :] = slim.T if j < 3 else slim
        sums = [jnp.sum(d_norm[j].T, axis=0, keepdims=True) for j in range(2 * NORMS)]
        sums = jnp.concatenate(sums + [jnp.zeros((8 - 2 * NORMS, D), f32)], axis=0)
        if not parts:
            out_refs[0][...] = d_attn[...]
            out_refs[1][...] = d_win[...]
            out_refs[2][...] = d_wout[...]
            out_refs[3][...] = sums
            return
        me = me_ref[0]
        upper = parts // GROUP
        each = ATTN_ROWS // parts
        sums_high = sums.astype(bf16).astype(f32)
        sums = jnp.concatenate([sums_high, sums - sums_high], axis=0).astype(bf16)
        for k in range(GROUP):
            out = out_refs[k]
            kind = out.dtype
            low = (me % GROUP) ^ k
            quarter = low // 2
            half = k % 2
            for u in range(upper):
                rows = d_attn[ds((u * GROUP + low) * each, each, each), :]
                out[u * each : (u + 1) * each, 0:D] = rows.astype(kind)
            first = (quarter // 2) * FF + half * FFH + (quarter % 2) * WOUT_PART
            out[OFF_WOUT:OFF_NORM, 0:D] = d_wout[ds(first, WOUT_PART, WOUT_PART), :].astype(kind)
            out[OFF_NORM:OFF_WIN, 0:D] = sums.astype(kind)
            rows = d_win[ds(quarter * WIN_PART, WIN_PART, WIN_PART), half * FF : (half + 1) * FF]
            out[OFF_WIN:PAY_ROWS, :] = rows.astype(kind)


def run_layers(me, tokens, cotangent, norms, ffn, attn_parts, parts):
    rows = tokens.shape[0]
    samples = rows // PAIRS
    if parts:
        grad_shapes = [((PAY_ROWS, 2 * FFH), f32)] + [((PAY_ROWS, 2 * FFH), bf16)] * (GROUP - 1)
    else:
        grad_shapes = [
            ((ATTN_ROWS, D), f32),
            ((LAYERS * D, 2 * FF), f32),
            ((LAYERS * FF, D), f32),
            ((8, D), f32),
        ]
    out_shape = [((rows, 2 * D), bf16), ((rows, 2 * D), f32)] + grad_shapes
    vmem = pl.BlockSpec(memory_space=pltpu.VMEM)
    inputs = (tokens, cotangent, norms, *ffn, *attn_parts)
    scratch = [
        ((LAYERS, 3 * WIDE, D), bf16),
        ((LAYERS, D, 3 * WIDE), bf16),
        ((LAYERS, D, WIDE), bf16),
        ((LAYERS, WIDE, D), bf16),
        ((LAYERS, 2 * FF, D), bf16),
        ((LAYERS, D, 2 * FF), bf16),
        ((LAYERS, D, FF), bf16),
        ((LAYERS, FF, D), bf16),
        ((D, 8), f32),
        ((ATTN_ROWS, D), bf16),
        ((LAYERS, 3 * WIDE, D), f32),
        ((LAYERS, WIDE, D), f32),
        ((LAYERS * D, 2 * FF), f32),
        ((LAYERS * FF, D), f32),
        ((2 * NORMS, D, 128), f32),
        ((ATTN_ROWS, D), f32),
        ((LAYERS, HEADS, 2 * KEYS, LANES), bf16),
        ((LAYERS, HEADS, 2 * KEYS, SLOT), bf16),
        ((LAYERS, HEADS, 2 * KEYS, SLOT), bf16),
        ((LAYERS, WIDE, LANES), bf16),
        ((LAYERS, WIDE, LANES), bf16),
        ((WIDE, LANES), bf16),
        ((WIDE, LANES), f32),
        ((LAYERS, WIDE, LANES), f32),
        ((LAYERS, WIDE, LANES), bf16),
        ((LAYERS, HEADS, 1, LANES), f32),
        ((3 * WIDE, LANES), bf16),
        ((LAYERS, 2 * FF, LANES), f32),
    ]

    def body(*refs):
        layers_kernel(parts, *refs)

    return pl.pallas_call(
        body,
        grid=(samples,),
        in_specs=[pl.BlockSpec(memory_space=pltpu.SMEM)] + [vmem] * len(inputs),
        out_specs=[vmem] * len(out_shape),
        out_shape=[jax.ShapeDtypeStruct(*s) for s in out_shape],
        scratch_shapes=[pltpu.VMEM(*s) for s in scratch],
        compiler_params=pltpu.CompilerParams(
            dimension_semantics=("arbitrary",), vmem_limit_bytes=60 * 1024 * 1024
        ),
        cost_estimate=pl.CostEstimate(
            flops=samples * 5_000_000_000, bytes_accessed=20_000_000, transcendentals=0
        ),
    )(me, *inputs)


def small_kernel(body, out_shape, *inputs):
    vmem = pl.BlockSpec(memory_space=pltpu.VMEM)
    return pl.pallas_call(
        body,
        in_specs=[pl.BlockSpec(memory_space=pltpu.SMEM)] + [vmem] * (len(inputs) - 1),
        out_specs=[vmem] * len(out_shape),
        out_shape=[jax.ShapeDtypeStruct(*s) for s in out_shape],
        compiler_params=pltpu.CompilerParams(vmem_limit_bytes=32 * 1024 * 1024),
    )(*inputs)


def sum_gradients(me, payloads, parts):
    upper = parts // GROUP
    each = ATTN_ROWS // parts
    win_rows = WIN_PART // upper
    wout_rows = WOUT_PART // upper
    at_norm = each + wout_rows
    at_win = at_norm + 16
    rows = at_win + win_rows

    def swap(value, k):
        return lax.ppermute(value, AXES, [(i, i ^ k) for i in range(parts)])

    landed = [payloads[0]] + [swap(payloads[k], k) for k in range(1, GROUP)]

    def join_group(me_ref, *refs):
        ins, outs, total = refs[:GROUP], refs[GROUP:-1], refs[-1]
        total[...] = tree_sum([r[...].astype(f32) for r in ins])
        sums = total[OFF_NORM : OFF_NORM + 8, :] + total[OFF_NORM + 8 : OFF_WIN, :]
        high = sums.astype(bf16).astype(f32)
        norm = jnp.concatenate([high, sums - high], axis=0).astype(bf16)
        mine = me_ref[0] // GROUP
        for u in range(upper):
            out = outs[u]
            there = mine ^ u
            out[0:each, :] = total[ds(there * each, each, 8), :].astype(out.dtype)
            wout = total[ds(OFF_WOUT + there * wout_rows, wout_rows, 8), :]
            out[each:at_norm, :] = wout.astype(out.dtype)
            out[at_norm:at_win, :] = norm.astype(out.dtype)
            win = total[ds(OFF_WIN + there * win_rows, win_rows, 8), :]
            out[at_win:rows, :] = win.astype(out.dtype)

    width = 2 * FFH
    vmem = pl.BlockSpec(memory_space=pltpu.VMEM)
    sent = pl.pallas_call(
        join_group,
        in_specs=[pl.BlockSpec(memory_space=pltpu.SMEM)] + [vmem] * GROUP,
        out_specs=[vmem] * upper,
        out_shape=[jax.ShapeDtypeStruct((rows, width), f32 if u == 0 else bf16) for u in range(upper)],
        scratch_shapes=[pltpu.VMEM((PAY_ROWS, width), f32)],
        compiler_params=pltpu.CompilerParams(vmem_limit_bytes=32 * 1024 * 1024),
    )(me, *landed)
    landed = [sent[0]] + [swap(sent[u], u * GROUP) for u in range(1, upper)]
    ffn_rows = wout_rows + win_rows

    def join_rest(me_ref, *refs):
        ins, (attn, norm, ffn) = refs[:upper], refs[upper:]
        total = tree_sum([r[...].astype(f32) for r in ins])
        attn[...] = total[0:each, 0:D]
        norm[...] = total[at_norm : at_norm + 8, 0:D] + total[at_norm + 8 : at_win, 0:D]
        ffn[0:wout_rows, :] = total[each:at_norm, :].astype(bf16)
        ffn[wout_rows:, :] = total[at_win:, :].astype(bf16)

    attn, norm, ffn = small_kernel(
        join_rest, [((each, D), f32), ((8, D), f32), ((ffn_rows, width), bf16)], me, *landed
    )
    column = jnp.stack([ffn] + [swap(ffn, u * GROUP) for u in range(1, upper)])
    block = [column] + [swap(column, 2 * q) for q in range(1, 4)]

    def spread(me_ref, *refs):
        ins, (win, wout) = refs[:4], refs[4:]
        mine = me_ref[0] // GROUP
        quarter = (me_ref[0] % GROUP) // 2
        for q in range(4):
            for u in range(upper):
                piece = (quarter ^ q) * upper + (mine ^ u)
                part = ins[q][u].astype(f32)
                wout[ds(piece * wout_rows, wout_rows, 8), :] = part[:wout_rows, 0:D]
                win[ds(piece * win_rows, win_rows, 8), :] = part[wout_rows:, :]

    win, wout = small_kernel(
        spread, [((LAYERS * D, width), f32), ((LAYERS * FFH, D), f32)], me, *block
    )
    return attn, norm, win, wout


def on_device(devices, tokens, attn_weights, norm_params, w_in, w_out, cotangent):
    each = attn_weights.shape[0]
    me = (lax.axis_index("dp") * 2 + lax.axis_index("narrow")).astype(jnp.int32).reshape(1)
    staged = devices % GROUP == 0 and each % 16 == 0
    swap_halves = [(0, 1), (1, 0)]
    w_in = w_in.reshape(LAYERS, D, 2 * FFH)
    ffn = (
        w_in,
        lax.ppermute(w_in, "narrow", swap_halves),
        w_out,
        lax.ppermute(w_out, "narrow", swap_halves),
    )
    norms = norm_params.reshape(2 * NORMS, D)
    if not staged:
        attn_all = lax.all_gather(attn_weights, AXES, axis=0, tiled=True)
        res, ig, d_attn, d_win, d_wout, sums = run_layers(
            me, tokens, cotangent, norms, ffn, (attn_all,), 0
        )
        attn = lax.psum_scatter(d_attn, AXES, scatter_dimension=0, tiled=True)
        norm = lax.psum(sums, AXES)
        d_wout = d_wout.reshape(LAYERS, FF, D)
        own_in, other_in = d_win[:, :FF], d_win[:, FF:]
        own_out, other_out = d_wout[:, :FFH], d_wout[:, FFH:]
        win = lax.psum(own_in + lax.ppermute(other_in, "narrow", swap_halves), "dp")
        wout = lax.psum(own_out + lax.ppermute(other_out, "narrow", swap_halves), "dp")
    else:
        upper = devices // GROUP

        def swap(value, k):
            return lax.ppermute(value, AXES, [(i, i ^ k) for i in range(devices)])

        column = jnp.stack(
            [attn_weights] + [swap(attn_weights, u * GROUP) for u in range(1, upper)]
        )
        attn_parts = [column] + [swap(column, k) for k in range(1, GROUP)]
        res, ig, *payloads = run_layers(me, tokens, cotangent, norms, ffn, attn_parts, devices)
        attn, norm, win, wout = sum_gradients(me, payloads, devices)
    return (
        res,
        ig,
        attn,
        norm[: 2 * NORMS].reshape(norm_params.shape),
        win.reshape(LAYERS, D, 2, FFH),
        wout.reshape(LAYERS, FFH, D),
    )


def solution(mesh):
    rows = P(("dp", "narrow"), None)
    hidden_in = P(None, None, None, "narrow")
    hidden_out = P(None, "narrow", None)
    devices = mesh.shape["dp"] * mesh.shape["narrow"]

    def per_device(*args):
        return on_device(devices, *args)

    return jax.shard_map(
        per_device,
        mesh=mesh,
        in_specs=(rows, rows, P(), hidden_in, hidden_out, rows),
        out_specs=(rows, rows, rows, P(), hidden_in, hidden_out),
        check_vma=False,
    )
```

```python
import math

import jax
import jax.numpy as jnp
from jax import lax
from jax.experimental import pallas as pl
from jax.experimental.pallas import tpu as pltpu
from jax.sharding import PartitionSpec as P

HEADS = 8
HEAD = 24
SLOT = 32
WIDE = HEADS * SLOT
D = HEADS * HEAD
FF = 256
FFH = FF // 2
LAYERS = 2
NORMS = 2 * LAYERS - 1
SEQ = 476
PAIRS = SEQ // 2
KEYS = 240
HALF = 256
LANES = 2 * HALF
EPS = 1e-05
SCALE = HEAD ** (-0.5)
LOG2E = math.log2(math.e)
ATTN_ROWS = LAYERS * 4 * D

GROUP = 8
WIN_PART = LAYERS * D // 4
WOUT_PART = LAYERS * FFH // 4
ATTN_PART = ATTN_ROWS // GROUP
OFF_WOUT = ATTN_PART
OFF_NORM = OFF_WOUT + WOUT_PART
OFF_WIN = OFF_NORM + 16
PAY_ROWS = OFF_WIN + WIN_PART

bf16 = jnp.bfloat16
f32 = jnp.float32
AXES = ("dp", "narrow")


def mm(left, right):
    return jnp.dot(left, right, preferred_element_type=f32)


def mm_nt(left, right):
    return lax.dot_general(left, right, (((1,), (1,)), ((), ())), preferred_element_type=f32)


def sigmoid(value):
    return 0.5 + 0.5 * jnp.tanh(0.5 * value)


def fold_lanes(value):
    return value[:, 0:128] + value[:, 128:256] + value[:, 256:384] + value[:, 384:512]


def norm_forward(stream, gain, shift):
    center = stream - jnp.sum(stream, axis=0, keepdims=True) * (1.0 / D)
    inverse = lax.rsqrt(jnp.sum(center * center, axis=0, keepdims=True) * (1.0 / D) + EPS)
    unit = center * inverse
    return (unit * gain + shift, unit, inverse)


def norm_backward(grad, unit, inverse, gain):
    scaled = grad * gain
    mean = jnp.sum(scaled, axis=0, keepdims=True) * (1.0 / D)
    slope = jnp.sum(scaled * unit, axis=0, keepdims=True) * (1.0 / D)
    return inverse * (scaled - mean - unit * slope)


def tree_sum(parts):
    while len(parts) > 1:
        parts = [parts[i] + parts[i + 1] for i in range(0, len(parts), 2)]
    return parts[0]


def ds(start, size, step):
    return pl.ds(pl.multiple_of(start, step), size)


def layers_kernel(parts, *refs):
    refs = list(refs)

    def take(count):
        taken = refs[:count]
        del refs[:count]
        return taken

    me_ref, x_ref, g_ref, norm_ref, win_own, win_other, wout_own, wout_other = take(8)
    attn_refs = take(GROUP if parts else 1)
    res_ref, ig_ref = take(2)
    out_refs = take(GROUP if parts else 4)
    wqkv_t, wqkv, wo_t, wo, win_t, win, wout_t, wout, norm_t, attn_ref = take(10)
    d_wq, d_wkv, d_wo, d_win, d_wout, d_norm, d_attn = take(7)
    e_ref, ds_ref, kh_ref, vh_ref, q_ref, k_ref, v_ref, do_ref, do_all, q_all = take(10)
    ctx_ref, ctxb_ref, rinv_ref, dq_ref, dkv_ref, mixed_ref = refs
    step = pl.program_id(0)
    rows_total = x_ref.shape[0]

    @pl.when(step == 0)
    def _():
        for ref in (d_wq, d_wkv, d_wo, d_win, d_wout, d_norm, dkv_ref):
            ref[...] = jnp.zeros_like(ref)
        if parts:
            me = me_ref[0]
            upper = parts // GROUP
            each = ATTN_ROWS // parts
            for k in range(GROUP):
                for u in range(upper):
                    owner = ((me // GROUP) ^ u) * GROUP + ((me % GROUP) ^ k)
                    attn_ref[ds(owner * each, each, each), :] = attn_refs[k][u]
        else:
            attn_ref[...] = attn_refs[0][...]
        norm_t[...] = jnp.concatenate([norm_ref[...], jnp.zeros((8 - 2 * NORMS, D), f32)], axis=0).T
        gap = jnp.zeros((SLOT - HEAD, D), f32)

        def pad_heads(matrix):
            slots = []
            for h in range(HEADS):
                slots += [matrix[HEAD * h : HEAD * (h + 1)], gap]
            return jnp.concatenate(slots, axis=0)

        for layer in range(LAYERS):
            for j in range(4):
                base = (4 * layer + j) * D
                matrix = attn_ref[base : base + D, :].astype(f32)
                if j < 3:
                    tall = pad_heads(matrix.T)
                    wqkv_t[layer, j * WIDE : (j + 1) * WIDE, :] = tall.astype(bf16)
                    wqkv[layer, :, j * WIDE : (j + 1) * WIDE] = tall.T.astype(bf16)
                else:
                    tall = pad_heads(matrix)
                    wo[layer] = tall.astype(bf16)
                    wo_t[layer] = tall.T.astype(bf16)
            for p, (w1, w2) in enumerate(((win_own, wout_own), (win_other, wout_other))):
                win[layer, :, p * FF : (p + 1) * FF] = w1[layer]
                win_t[layer, p * FF : (p + 1) * FF, :] = w1[layer].astype(f32).T.astype(bf16)
                wout[layer, p * FFH : (p + 1) * FFH, :] = w2[layer]
                wout_t[layer, :, p * FFH : (p + 1) * FFH] = w2[layer].astype(f32).T.astype(bf16)

    base = step * PAIRS
    start = jnp.minimum(base // 16 * 16, rows_total - HALF)
    shift = base - start
    window = ds(start, HALF, 16)
    pair_row = lax.broadcasted_iota(jnp.int32, (HALF, 2 * D), 0)

    def load(ref, fill_first):
        rows = pltpu.roll(ref[window, :].astype(f32), lax.rem(HALF - shift, HALF), 0)
        fill = rows[0:1] if fill_first else 0.0
        cols = jnp.where(pair_row < PAIRS, rows, fill).T
        return jnp.concatenate([cols[:D], cols[D:]], axis=1)

    def store(ref, value):
        cols = jnp.concatenate([value[:, :HALF], value[:, HALF:]], axis=0)
        rows = pltpu.roll(cols.T, shift, 0)
        here = jnp.logical_and(pair_row >= shift, pair_row < shift + PAIRS)
        ref[window, :] = jnp.where(here, rows, ref[window, :].astype(f32)).astype(ref.dtype)

    lane = lax.broadcasted_iota(jnp.int32, (WIDE, LANES), 1)
    row = lax.broadcasted_iota(jnp.int32, (WIDE, LANES), 0)
    real = (lane & (HALF - 1)) < PAIRS
    slot_row = row & (SLOT - 1)
    ones_rows = jnp.logical_or(slot_row == HEAD, slot_row == HEAD + 1).astype(f32)
    head_row = lax.broadcasted_iota(jnp.int32, (SLOT, LANES), 0)
    lane_head = lax.broadcasted_iota(jnp.int32, (LANES, WIDE), 1) // SLOT
    key_row = lax.broadcasted_iota(jnp.int32, (2 * KEYS, WIDE), 0)
    real_key = jnp.where(key_row < KEYS, key_row, key_row - KEYS) < PAIRS

    def attention_forward(layer, normed_b):
        qkv = mm(wqkv_t[layer], normed_b)
        queries = (qkv[:WIDE] * (SCALE * LOG2E)).astype(bf16)
        q_ref[layer] = queries
        keys = qkv[WIDE : 2 * WIDE].astype(bf16)
        k_ref[layer] = keys
        values = jnp.where(real, qkv[2 * WIDE :] + ones_rows, 0.0).astype(bf16)
        v_ref[...] = values
        for tall, ref in ((keys.T, kh_ref), (values.T, vh_ref)):
            for h in range(HEADS):
                ref[layer, h, 0:KEYS] = tall[0:KEYS, SLOT * h : SLOT * (h + 1)]
                ref[layer, h, KEYS:] = tall[HALF : HALF + KEYS, SLOT * h : SLOT * (h + 1)]

        def scores_of(h):
            return mm(kh_ref[layer, h], q_ref[layer, SLOT * h : SLOT * (h + 1), :])

        scores = scores_of(0)
        for h in range(HEADS):
            rows = slice(SLOT * h, SLOT * (h + 1))
            ahead = scores_of(h + 1) if h + 1 < HEADS else None
            top = jnp.max(scores, axis=0, keepdims=True)
            weights = jnp.exp2(scores - top).astype(bf16)
            e_ref[layer, :, LANES * h : LANES * (h + 1)] = weights
            out = mm(v_ref[rows, 0:KEYS], weights[0:KEYS]) + mm(
                v_ref[rows, HALF : HALF + KEYS], weights[KEYS:]
            )
            inverse = 1.0 / out[HEAD : HEAD + 1]
            context = out * inverse
            rinv_ref[layer, rows, :] = jnp.broadcast_to(inverse, (SLOT, LANES))
            ctx_ref[layer, rows, :] = context
            ctxb_ref[layer, rows, :] = context.astype(bf16)
            scores = ahead
        return mm(wo_t[layer], ctxb_ref[layer])

    def spread_heads(ref, tall):
        for h in range(HEADS):
            ref[LANES * h : LANES * (h + 1), :] = jnp.where(lane_head == h, tall, jnp.zeros_like(tall))

    def attention_backward(layer, grad_b, normed_b):
        d_wo[layer] += mm_nt(ctxb_ref[layer], grad_b)
        grads = (mm(wo[layer], grad_b) * rinv_ref[layer]).astype(bf16)
        product = grads.astype(f32) * ctx_ref[layer]
        for h in range(HEADS):
            rows = slice(SLOT * h, SLOT * (h + 1))
            dot = -jnp.sum(product[rows][:HEAD], axis=0, keepdims=True)
            dot_high = dot.astype(bf16).astype(f32)
            grad = jnp.where(head_row == HEAD, dot_high, grads[rows].astype(f32))
            grad = jnp.where(head_row == HEAD + 1, dot - dot_high, grad)
            do_ref[rows, :] = grad.astype(bf16)
        spread_heads(do_all, do_ref[...].T)
        spread_heads(q_all, q_ref[layer].T)

        def grad_probs_of(h):
            return mm(vh_ref[layer, h], do_ref[SLOT * h : SLOT * (h + 1), :])

        grad_probs = grad_probs_of(0)
        for h in range(HEADS):
            rows = slice(SLOT * h, SLOT * (h + 1))
            ahead = grad_probs_of(h + 1) if h + 1 < HEADS else None
            d_scores = e_ref[layer, :, LANES * h : LANES * (h + 1)] * grad_probs.astype(bf16)
            ds_ref[:, LANES * h : LANES * (h + 1)] = d_scores
            dq = mm(k_ref[layer, rows, 0:KEYS], d_scores[0:KEYS]) + mm(
                k_ref[layer, rows, HALF : HALF + KEYS], d_scores[KEYS:]
            )
            dq_ref[rows, :] = (dq * SCALE).astype(bf16)
            grad_probs = ahead
        dk = (mm(ds_ref[...], q_all[...]) * (1.0 / LOG2E)).astype(bf16)
        dv = jnp.where(real_key, mm(e_ref[layer], do_all[...]), 0.0).astype(bf16)
        for half in range(2):
            here = slice(half * KEYS, (half + 1) * KEYS)
            there = slice(half * HALF, half * HALF + KEYS)
            dkv_ref[there, 0:WIDE] = dk[here]
            dkv_ref[there, WIDE:] = dv[here]
        d_wq[layer] += mm_nt(dq_ref[...], normed_b)
        d_wkv[layer] += mm(normed_b, dkv_ref[...])
        return mm(wqkv[layer, :, 0:WIDE], dq_ref[...]) + mm_nt(wqkv[layer, :, WIDE:], dkv_ref[...])

    def add_norm(index, grad, unit):
        d_norm[2 * index] += fold_lanes(grad * unit)
        d_norm[2 * index + 1] += fold_lanes(grad)

    def gain_of(index):
        return norm_t[:, 2 * index : 2 * index + 1]

    def shift_of(index):
        return norm_t[:, 2 * index + 1 : 2 * index + 2]

    kept = []
    stream = load(x_ref, True)
    normed_b = stream.astype(bf16)
    unit_a = inv_a = None
    for layer in range(LAYERS):
        if layer > 0:
            normed, unit_a, inv_a = norm_forward(stream, gain_of(2 * layer - 1), shift_of(2 * layer - 1))
            normed_b = normed.astype(bf16)
        stream = stream + attention_forward(layer, normed_b)
        normed, unit_f, inv_f = norm_forward(stream, gain_of(2 * layer), shift_of(2 * layer))
        ffn_b = normed.astype(bf16)
        mixed = mm(win_t[layer], ffn_b)
        mixed_ref[layer] = mixed
        hidden = []
        for p in range(2):
            value = mixed[FF * p : FF * p + FFH]
            gate = mixed[FF * p + FFH : FF * (p + 1)]
            hidden.append((value * (gate * sigmoid(gate))).astype(bf16))
        hidden = jnp.concatenate(hidden, axis=0)
        stream = stream + mm(wout_t[layer], hidden)
        kept.append((normed_b, unit_a, inv_a, ffn_b, unit_f, inv_f, hidden))
    store(res_ref, stream)

    grad = load(g_ref, False)
    for layer in reversed(range(LAYERS)):
        normed_b, unit_a, inv_a, ffn_b, unit_f, inv_f, hidden = kept[layer]
        grad_b = grad.astype(bf16)
        d_wout[FF * layer : FF * (layer + 1), :] += mm_nt(hidden, grad_b)
        d_hidden = mm(wout[layer], grad_b)
        d_mixed = []
        for p in range(2):
            value = mixed_ref[layer, FF * p : FF * p + FFH]
            gate = mixed_ref[layer, FF * p + FFH : FF * (p + 1)]
            part = d_hidden[FFH * p : FFH * (p + 1)]
            sig = sigmoid(gate)
            d_mixed.append((part * (gate * sig)).astype(bf16))
            d_mixed.append((part * value * sig * (1.0 + gate * (1.0 - sig))).astype(bf16))
        d_mixed = jnp.concatenate(d_mixed, axis=0)
        d_win[D * layer : D * (layer + 1), :] += mm_nt(ffn_b, d_mixed)
        d_normed = mm(win[layer], d_mixed)
        add_norm(2 * layer, d_normed, unit_f)
        grad = grad + norm_backward(d_normed, unit_f, inv_f, gain_of(2 * layer))
        d_att = attention_backward(layer, grad.astype(bf16), normed_b)
        if layer > 0:
            add_norm(2 * layer - 1, d_att, unit_a)
            grad = grad + norm_backward(d_att, unit_a, inv_a, gain_of(2 * layer - 1))
        else:
            grad = grad + d_att
    store(ig_ref, grad)

    @pl.when(step == pl.num_programs(0) - 1)
    def _():
        for layer in range(LAYERS):
            tall = d_wkv[layer].T
            sources = (d_wq[layer], tall[:WIDE], tall[WIDE:], d_wo[layer])
            for j, source in enumerate(sources):
                slim = jnp.concatenate([source[SLOT * h : SLOT * h + HEAD] for h in range(HEADS)], axis=0)
                base = (4 * layer + j) * D
                d_attn[base : base + D, :] = slim.T if j < 3 else slim
        sums = [jnp.sum(d_norm[j].T, axis=0, keepdims=True) for j in range(2 * NORMS)]
        sums = jnp.concatenate(sums + [jnp.zeros((8 - 2 * NORMS, D), f32)], axis=0)
        if not parts:
            out_refs[0][...] = d_attn[...]
            out_refs[1][...] = d_win[...]
            out_refs[2][...] = d_wout[...]
            out_refs[3][...] = sums
            return
        me = me_ref[0]
        upper = parts // GROUP
        each = ATTN_ROWS // parts
        sums_high = sums.astype(bf16).astype(f32)
        sums = jnp.concatenate([sums_high, sums - sums_high], axis=0).astype(bf16)
        for k in range(GROUP):
            out = out_refs[k]
            kind = out.dtype
            low = (me % GROUP) ^ k
            quarter = low // 2
            half = k % 2
            for u in range(upper):
                rows = d_attn[ds((u * GROUP + low) * each, each, each), :]
                out[u * each : (u + 1) * each, 0:D] = rows.astype(kind)
            first = (quarter // 2) * FF + half * FFH + (quarter % 2) * WOUT_PART
            out[OFF_WOUT:OFF_NORM, 0:D] = d_wout[ds(first, WOUT_PART, WOUT_PART), :].astype(kind)
            out[OFF_NORM:OFF_WIN, 0:D] = sums.astype(kind)
            rows = d_win[ds(quarter * WIN_PART, WIN_PART, WIN_PART), half * FF : (half + 1) * FF]
            out[OFF_WIN:PAY_ROWS, :] = rows.astype(kind)


def run_layers(me, tokens, cotangent, norms, ffn, attn_parts, parts):
    rows = tokens.shape[0]
    samples = rows // PAIRS
    if parts:
        grad_shapes = [((PAY_ROWS, 2 * FFH), f32)] + [((PAY_ROWS, 2 * FFH), bf16)] * (GROUP - 1)
    else:
        grad_shapes = [
            ((ATTN_ROWS, D), f32),
            ((LAYERS * D, 2 * FF), f32),
            ((LAYERS * FF, D), f32),
            ((8, D), f32),
        ]
    out_shape = [((rows, 2 * D), bf16), ((rows, 2 * D), f32)] + grad_shapes
    vmem = pl.BlockSpec(memory_space=pltpu.VMEM)
    inputs = (tokens, cotangent, norms, *ffn, *attn_parts)
    scratch = [
        ((LAYERS, 3 * WIDE, D), bf16),
        ((LAYERS, D, 3 * WIDE), bf16),
        ((LAYERS, D, WIDE), bf16),
        ((LAYERS, WIDE, D), bf16),
        ((LAYERS, 2 * FF, D), bf16),
        ((LAYERS, D, 2 * FF), bf16),
        ((LAYERS, D, FF), bf16),
        ((LAYERS, FF, D), bf16),
        ((D, 8), f32),
        ((ATTN_ROWS, D), bf16),
        ((LAYERS, WIDE, D), f32),
        ((LAYERS, D, 2 * WIDE), f32),
        ((LAYERS, WIDE, D), f32),
        ((LAYERS * D, 2 * FF), f32),
        ((LAYERS * FF, D), f32),
        ((2 * NORMS, D, 128), f32),
        ((ATTN_ROWS, D), f32),
        ((LAYERS, 2 * KEYS, HEADS * LANES), bf16),
        ((2 * KEYS, HEADS * LANES), bf16),
        ((LAYERS, HEADS, 2 * KEYS, SLOT), bf16),
        ((LAYERS, HEADS, 2 * KEYS, SLOT), bf16),
        ((LAYERS, WIDE, LANES), bf16),
        ((LAYERS, WIDE, LANES), bf16),
        ((WIDE, LANES), bf16),
        ((WIDE, LANES), bf16),
        ((HEADS * LANES, WIDE), bf16),
        ((HEADS * LANES, WIDE), bf16),
        ((LAYERS, WIDE, LANES), f32),
        ((LAYERS, WIDE, LANES), bf16),
        ((LAYERS, WIDE, LANES), f32),
        ((WIDE, LANES), bf16),
        ((LANES, 2 * WIDE), bf16),
        ((LAYERS, 2 * FF, LANES), f32),
    ]

    def body(*refs):
        layers_kernel(parts, *refs)

    return pl.pallas_call(
        body,
        grid=(samples,),
        in_specs=[pl.BlockSpec(memory_space=pltpu.SMEM)] + [vmem] * len(inputs),
        out_specs=[vmem] * len(out_shape),
        out_shape=[jax.ShapeDtypeStruct(*s) for s in out_shape],
        scratch_shapes=[pltpu.VMEM(*s) for s in scratch],
        compiler_params=pltpu.CompilerParams(
            dimension_semantics=("arbitrary",), vmem_limit_bytes=60 * 1024 * 1024
        ),
        cost_estimate=pl.CostEstimate(
            flops=samples * 5_000_000_000, bytes_accessed=20_000_000, transcendentals=0
        ),
    )(me, *inputs)


def small_kernel(body, out_shape, *inputs):
    vmem = pl.BlockSpec(memory_space=pltpu.VMEM)
    return pl.pallas_call(
        body,
        in_specs=[pl.BlockSpec(memory_space=pltpu.SMEM)] + [vmem] * (len(inputs) - 1),
        out_specs=[vmem] * len(out_shape),
        out_shape=[jax.ShapeDtypeStruct(*s) for s in out_shape],
        compiler_params=pltpu.CompilerParams(vmem_limit_bytes=32 * 1024 * 1024),
    )(*inputs)


def sum_gradients(me, payloads, parts):
    upper = parts // GROUP
    each = ATTN_ROWS // parts
    win_rows = WIN_PART // upper
    wout_rows = WOUT_PART // upper
    at_norm = each + wout_rows
    at_win = at_norm + 16
    rows = at_win + win_rows

    def swap(value, k):
        return lax.ppermute(value, AXES, [(i, i ^ k) for i in range(parts)])

    landed = [payloads[0]] + [swap(payloads[k], k) for k in range(1, GROUP)]

    def join_group(me_ref, *refs):
        ins, outs, total = refs[:GROUP], refs[GROUP:-1], refs[-1]
        total[...] = tree_sum([r[...].astype(f32) for r in ins])
        sums = total[OFF_NORM : OFF_NORM + 8, :] + total[OFF_NORM + 8 : OFF_WIN, :]
        high = sums.astype(bf16).astype(f32)
        norm = jnp.concatenate([high, sums - high], axis=0).astype(bf16)
        mine = me_ref[0] // GROUP
        for u in range(upper):
            out = outs[u]
            there = mine ^ u
            out[0:each, :] = total[ds(there * each, each, 8), :].astype(out.dtype)
            wout = total[ds(OFF_WOUT + there * wout_rows, wout_rows, 8), :]
            out[each:at_norm, :] = wout.astype(out.dtype)
            out[at_norm:at_win, :] = norm.astype(out.dtype)
            win = total[ds(OFF_WIN + there * win_rows, win_rows, 8), :]
            out[at_win:rows, :] = win.astype(out.dtype)

    width = 2 * FFH
    vmem = pl.BlockSpec(memory_space=pltpu.VMEM)
    sent = pl.pallas_call(
        join_group,
        in_specs=[pl.BlockSpec(memory_space=pltpu.SMEM)] + [vmem] * GROUP,
        out_specs=[vmem] * upper,
        out_shape=[jax.ShapeDtypeStruct((rows, width), f32 if u == 0 else bf16) for u in range(upper)],
        scratch_shapes=[pltpu.VMEM((PAY_ROWS, width), f32)],
        compiler_params=pltpu.CompilerParams(vmem_limit_bytes=32 * 1024 * 1024),
    )(me, *landed)
    landed = [sent[0]] + [swap(sent[u], u * GROUP) for u in range(1, upper)]
    ffn_rows = wout_rows + win_rows

    def join_rest(me_ref, *refs):
        ins, (attn, norm, ffn) = refs[:upper], refs[upper:]
        total = tree_sum([r[...].astype(f32) for r in ins])
        attn[...] = total[0:each, 0:D]
        norm[...] = total[at_norm : at_norm + 8, 0:D] + total[at_norm + 8 : at_win, 0:D]
        ffn[0:wout_rows, :] = total[each:at_norm, :].astype(bf16)
        ffn[wout_rows:, :] = total[at_win:, :].astype(bf16)

    attn, norm, ffn = small_kernel(
        join_rest, [((each, D), f32), ((8, D), f32), ((ffn_rows, width), bf16)], me, *landed
    )
    column = jnp.stack([ffn] + [swap(ffn, u * GROUP) for u in range(1, upper)])
    block = [column] + [swap(column, 2 * q) for q in range(1, 4)]

    def spread(me_ref, *refs):
        ins, (win, wout) = refs[:4], refs[4:]
        mine = me_ref[0] // GROUP
        quarter = (me_ref[0] % GROUP) // 2
        for q in range(4):
            for u in range(upper):
                piece = (quarter ^ q) * upper + (mine ^ u)
                part = ins[q][u].astype(f32)
                wout[ds(piece * wout_rows, wout_rows, 8), :] = part[:wout_rows, 0:D]
                win[ds(piece * win_rows, win_rows, 8), :] = part[wout_rows:, :]

    win, wout = small_kernel(
        spread, [((LAYERS * D, width), f32), ((LAYERS * FFH, D), f32)], me, *block
    )
    return attn, norm, win, wout


def on_device(devices, tokens, attn_weights, norm_params, w_in, w_out, cotangent):
    each = attn_weights.shape[0]
    me = (lax.axis_index("dp") * 2 + lax.axis_index("narrow")).astype(jnp.int32).reshape(1)
    staged = devices % GROUP == 0 and each % 16 == 0
    swap_halves = [(0, 1), (1, 0)]
    w_in = w_in.reshape(LAYERS, D, 2 * FFH)
    ffn = (
        w_in,
        lax.ppermute(w_in, "narrow", swap_halves),
        w_out,
        lax.ppermute(w_out, "narrow", swap_halves),
    )
    norms = norm_params.reshape(2 * NORMS, D)
    if not staged:
        attn_all = lax.all_gather(attn_weights, AXES, axis=0, tiled=True)
        res, ig, d_attn, d_win, d_wout, sums = run_layers(
            me, tokens, cotangent, norms, ffn, (attn_all,), 0
        )
        attn = lax.psum_scatter(d_attn, AXES, scatter_dimension=0, tiled=True)
        norm = lax.psum(sums, AXES)
        d_wout = d_wout.reshape(LAYERS, FF, D)
        own_in, other_in = d_win[:, :FF], d_win[:, FF:]
        own_out, other_out = d_wout[:, :FFH], d_wout[:, FFH:]
        win = lax.psum(own_in + lax.ppermute(other_in, "narrow", swap_halves), "dp")
        wout = lax.psum(own_out + lax.ppermute(other_out, "narrow", swap_halves), "dp")
    else:
        upper = devices // GROUP

        def swap(value, k):
            return lax.ppermute(value, AXES, [(i, i ^ k) for i in range(devices)])

        column = jnp.stack(
            [attn_weights] + [swap(attn_weights, u * GROUP) for u in range(1, upper)]
        )
        attn_parts = [column] + [swap(column, k) for k in range(1, GROUP)]
        res, ig, *payloads = run_layers(me, tokens, cotangent, norms, ffn, attn_parts, devices)
        attn, norm, win, wout = sum_gradients(me, payloads, devices)
    return (
        res,
        ig,
        attn,
        norm[: 2 * NORMS].reshape(norm_params.shape),
        win.reshape(LAYERS, D, 2, FFH),
        wout.reshape(LAYERS, FFH, D),
    )


def solution(mesh):
    rows = P(("dp", "narrow"), None)
    hidden_in = P(None, None, None, "narrow")
    hidden_out = P(None, "narrow", None)
    devices = mesh.shape["dp"] * mesh.shape["narrow"]

    def per_device(*args):
        return on_device(devices, *args)

    return jax.shard_map(
        per_device,
        mesh=mesh,
        in_specs=(rows, rows, P(), hidden_in, hidden_out, rows),
        out_specs=(rows, rows, rows, P(), hidden_in, hidden_out),
        check_vma=False,
    )
```

```python
import math

import jax
import jax.numpy as jnp
from jax import lax
from jax.experimental import pallas as pl
from jax.experimental.pallas import tpu as pltpu
from jax.sharding import PartitionSpec as P

HEADS = 8
HEAD = 24
SLOT = 32
WIDE = HEADS * SLOT
D = HEADS * HEAD
FF = 256
FFH = FF // 2
LAYERS = 2
NORMS = 2 * LAYERS - 1
SEQ = 476
PAIRS = SEQ // 2
KEYS = 240
HALF = 256
LANES = 2 * HALF
EPS = 1e-05
SCALE = HEAD ** (-0.5)
LOG2E = math.log2(math.e)
ATTN_ROWS = LAYERS * 4 * D

GROUP = 8
WIN_PART = LAYERS * D // 4
WOUT_PART = LAYERS * FFH // 4
ATTN_PART = ATTN_ROWS // GROUP
OFF_WOUT = ATTN_PART
OFF_NORM = OFF_WOUT + WOUT_PART
OFF_WIN = OFF_NORM + 16
PAY_ROWS = OFF_WIN + WIN_PART

bf16 = jnp.bfloat16
f32 = jnp.float32
AXES = ("dp", "narrow")


def mm(left, right):
    return jnp.dot(left, right, preferred_element_type=f32)


def mm_nt(left, right):
    return lax.dot_general(left, right, (((1,), (1,)), ((), ())), preferred_element_type=f32)


def sigmoid(value):
    return 0.5 + 0.5 * jnp.tanh(0.5 * value)


def fold_lanes(value):
    return value[:, 0:128] + value[:, 128:256] + value[:, 256:384] + value[:, 384:512]


def norm_forward(stream, gain, shift):
    center = stream - jnp.sum(stream, axis=0, keepdims=True) * (1.0 / D)
    inverse = lax.rsqrt(jnp.sum(center * center, axis=0, keepdims=True) * (1.0 / D) + EPS)
    unit = center * inverse
    return (unit * gain + shift, unit, inverse)


def norm_backward(grad, unit, inverse, gain):
    scaled = grad * gain
    mean = jnp.sum(scaled, axis=0, keepdims=True) * (1.0 / D)
    slope = jnp.sum(scaled * unit, axis=0, keepdims=True) * (1.0 / D)
    return inverse * (scaled - mean - unit * slope)


def tree_sum(parts):
    while len(parts) > 1:
        parts = [parts[i] + parts[i + 1] for i in range(0, len(parts), 2)]
    return parts[0]


def ds(start, size, step):
    return pl.ds(pl.multiple_of(start, step), size)


def layers_kernel(parts, *refs):
    refs = list(refs)

    def take(count):
        taken = refs[:count]
        del refs[:count]
        return taken

    x_ref, g_ref, norm_ref, win_first, win_second, wout_first, wout_second = take(7)
    (attn_in,) = take(1)
    res_ref, ig_ref = take(2)
    out_refs = take(1 if parts else 4)
    wqkv_t, wqkv, wo_t, wo, win_t, win, wout_t, wout, norm_t, attn_ref = take(10)
    d_wq, d_wkv, d_wo, d_win, d_wout, d_norm, d_attn = take(7)
    e_ref, ds_ref, kh_ref, vh_ref, q_ref, k_ref, v_ref, do_ref, do_all, q_all = take(10)
    ctx_ref, ctxb_ref, rinv_ref, dq_ref, dkv_ref, mixed_ref = refs
    step = pl.program_id(0)
    rows_total = x_ref.shape[0]

    @pl.when(step == 0)
    def _():
        for ref in (d_wq, d_wkv, d_wo, d_win, d_wout, d_norm, dkv_ref):
            ref[...] = jnp.zeros_like(ref)
        if parts:
            each = ATTN_ROWS // parts
            for k in range(GROUP):
                for u in range(parts // GROUP):
                    owner = u * GROUP + k
                    attn_ref[owner * each : (owner + 1) * each, :] = attn_in[k, u]
        else:
            attn_ref[...] = attn_in[...]
        norm_t[...] = jnp.concatenate([norm_ref[...], jnp.zeros((8 - 2 * NORMS, D), f32)], axis=0).T
        gap = jnp.zeros((SLOT - HEAD, D), f32)

        def pad_heads(matrix):
            slots = []
            for h in range(HEADS):
                slots += [matrix[HEAD * h : HEAD * (h + 1)], gap]
            return jnp.concatenate(slots, axis=0)

        for layer in range(LAYERS):
            for j in range(4):
                base = (4 * layer + j) * D
                matrix = attn_ref[base : base + D, :].astype(f32)
                if j < 3:
                    tall = pad_heads(matrix.T)
                    wqkv_t[layer, j * WIDE : (j + 1) * WIDE, :] = tall.astype(bf16)
                    wqkv[layer, :, j * WIDE : (j + 1) * WIDE] = tall.T.astype(bf16)
                else:
                    tall = pad_heads(matrix)
                    wo[layer] = tall.astype(bf16)
                    wo_t[layer] = tall.T.astype(bf16)
            for p, (w1, w2) in enumerate(((win_first, wout_first), (win_second, wout_second))):
                win[layer, :, p * FF : (p + 1) * FF] = w1[layer]
                win_t[layer, p * FF : (p + 1) * FF, :] = w1[layer].astype(f32).T.astype(bf16)
                wout[layer, p * FFH : (p + 1) * FFH, :] = w2[layer]
                wout_t[layer, :, p * FFH : (p + 1) * FFH] = w2[layer].astype(f32).T.astype(bf16)

    base = step * PAIRS
    start = jnp.minimum(base // 16 * 16, rows_total - HALF)
    shift = base - start
    window = ds(start, HALF, 16)
    pair_row = lax.broadcasted_iota(jnp.int32, (HALF, 2 * D), 0)

    def load(ref, fill_first):
        rows = pltpu.roll(ref[window, :].astype(f32), lax.rem(HALF - shift, HALF), 0)
        fill = rows[0:1] if fill_first else 0.0
        cols = jnp.where(pair_row < PAIRS, rows, fill).T
        return jnp.concatenate([cols[:D], cols[D:]], axis=1)

    def store(ref, value):
        cols = jnp.concatenate([value[:, :HALF], value[:, HALF:]], axis=0)
        rows = pltpu.roll(cols.T, shift, 0)
        here = jnp.logical_and(pair_row >= shift, pair_row < shift + PAIRS)
        ref[window, :] = jnp.where(here, rows, ref[window, :].astype(f32)).astype(ref.dtype)

    lane = lax.broadcasted_iota(jnp.int32, (WIDE, LANES), 1)
    row = lax.broadcasted_iota(jnp.int32, (WIDE, LANES), 0)
    real = (lane & (HALF - 1)) < PAIRS
    slot_row = row & (SLOT - 1)
    ones_rows = jnp.logical_or(slot_row == HEAD, slot_row == HEAD + 1).astype(f32)
    head_row = lax.broadcasted_iota(jnp.int32, (SLOT, LANES), 0)
    lane_head = lax.broadcasted_iota(jnp.int32, (LANES, WIDE), 1) // SLOT
    key_row = lax.broadcasted_iota(jnp.int32, (2 * KEYS, WIDE), 0)
    real_key = jnp.where(key_row < KEYS, key_row, key_row - KEYS) < PAIRS

    def attention_forward(layer, normed_b):
        qkv = mm(wqkv_t[layer], normed_b)
        queries = (qkv[:WIDE] * (SCALE * LOG2E)).astype(bf16)
        q_ref[layer] = queries
        keys = qkv[WIDE : 2 * WIDE].astype(bf16)
        k_ref[layer] = keys
        values = jnp.where(real, qkv[2 * WIDE :] + ones_rows, 0.0).astype(bf16)
        v_ref[...] = values
        for tall, ref in ((keys.T, kh_ref), (values.T, vh_ref)):
            for h in range(HEADS):
                ref[layer, h, 0:KEYS] = tall[0:KEYS, SLOT * h : SLOT * (h + 1)]
                ref[layer, h, KEYS:] = tall[HALF : HALF + KEYS, SLOT * h : SLOT * (h + 1)]

        def scores_of(h):
            return mm(kh_ref[layer, h], q_ref[layer, SLOT * h : SLOT * (h + 1), :])

        scores = scores_of(0)
        for h in range(HEADS):
            rows = slice(SLOT * h, SLOT * (h + 1))
            ahead = scores_of(h + 1) if h + 1 < HEADS else None
            top = jnp.max(scores, axis=0, keepdims=True)
            weights = jnp.exp2(scores - top).astype(bf16)
            e_ref[layer, :, LANES * h : LANES * (h + 1)] = weights
            out = mm(v_ref[rows, 0:KEYS], weights[0:KEYS]) + mm(
                v_ref[rows, HALF : HALF + KEYS], weights[KEYS:]
            )
            inverse = 1.0 / out[HEAD : HEAD + 1]
            context = out * inverse
            rinv_ref[layer, rows, :] = jnp.broadcast_to(inverse, (SLOT, LANES))
            ctx_ref[layer, rows, :] = context
            ctxb_ref[layer, rows, :] = context.astype(bf16)
            scores = ahead
        return mm(wo_t[layer], ctxb_ref[layer])

    def spread_heads(ref, tall):
        for h in range(HEADS):
            ref[LANES * h : LANES * (h + 1), :] = jnp.where(lane_head == h, tall, jnp.zeros_like(tall))

    def attention_backward(layer, grad_b, normed_b):
        d_wo[layer] += mm_nt(ctxb_ref[layer], grad_b)
        grads = (mm(wo[layer], grad_b) * rinv_ref[layer]).astype(bf16)
        product = grads.astype(f32) * ctx_ref[layer]
        for h in range(HEADS):
            rows = slice(SLOT * h, SLOT * (h + 1))
            dot = -jnp.sum(product[rows][:HEAD], axis=0, keepdims=True)
            dot_high = dot.astype(bf16).astype(f32)
            grad = jnp.where(head_row == HEAD, dot_high, grads[rows].astype(f32))
            grad = jnp.where(head_row == HEAD + 1, dot - dot_high, grad)
            do_ref[rows, :] = grad.astype(bf16)
        spread_heads(do_all, do_ref[...].T)
        spread_heads(q_all, q_ref[layer].T)

        def grad_probs_of(h):
            return mm(vh_ref[layer, h], do_ref[SLOT * h : SLOT * (h + 1), :])

        grad_probs = grad_probs_of(0)
        for h in range(HEADS):
            rows = slice(SLOT * h, SLOT * (h + 1))
            ahead = grad_probs_of(h + 1) if h + 1 < HEADS else None
            d_scores = e_ref[layer, :, LANES * h : LANES * (h + 1)] * grad_probs.astype(bf16)
            ds_ref[:, LANES * h : LANES * (h + 1)] = d_scores
            dq = mm(k_ref[layer, rows, 0:KEYS], d_scores[0:KEYS]) + mm(
                k_ref[layer, rows, HALF : HALF + KEYS], d_scores[KEYS:]
            )
            dq_ref[rows, :] = (dq * SCALE).astype(bf16)
            grad_probs = ahead
        dk = (mm(ds_ref[...], q_all[...]) * (1.0 / LOG2E)).astype(bf16)
        dv = jnp.where(real_key, mm(e_ref[layer], do_all[...]), 0.0).astype(bf16)
        for half in range(2):
            here = slice(half * KEYS, (half + 1) * KEYS)
            there = slice(half * HALF, half * HALF + KEYS)
            dkv_ref[there, 0:WIDE] = dk[here]
            dkv_ref[there, WIDE:] = dv[here]
        d_wq[layer] += mm_nt(dq_ref[...], normed_b)
        d_wkv[layer] += mm(normed_b, dkv_ref[...])
        return mm(wqkv[layer, :, 0:WIDE], dq_ref[...]) + mm_nt(wqkv[layer, :, WIDE:], dkv_ref[...])

    def add_norm(index, grad, unit):
        d_norm[2 * index] += fold_lanes(grad * unit)
        d_norm[2 * index + 1] += fold_lanes(grad)

    def gain_of(index):
        return norm_t[:, 2 * index : 2 * index + 1]

    def shift_of(index):
        return norm_t[:, 2 * index + 1 : 2 * index + 2]

    kept = []
    stream = load(x_ref, True)
    normed_b = stream.astype(bf16)
    unit_a = inv_a = None
    for layer in range(LAYERS):
        if layer > 0:
            normed, unit_a, inv_a = norm_forward(stream, gain_of(2 * layer - 1), shift_of(2 * layer - 1))
            normed_b = normed.astype(bf16)
        stream = stream + attention_forward(layer, normed_b)
        normed, unit_f, inv_f = norm_forward(stream, gain_of(2 * layer), shift_of(2 * layer))
        ffn_b = normed.astype(bf16)
        mixed = mm(win_t[layer], ffn_b)
        mixed_ref[layer] = mixed
        hidden = []
        for p in range(2):
            value = mixed[FF * p : FF * p + FFH]
            gate = mixed[FF * p + FFH : FF * (p + 1)]
            hidden.append((value * (gate * sigmoid(gate))).astype(bf16))
        hidden = jnp.concatenate(hidden, axis=0)
        stream = stream + mm(wout_t[layer], hidden)
        kept.append((normed_b, unit_a, inv_a, ffn_b, unit_f, inv_f, hidden))
    store(res_ref, stream)

    grad = load(g_ref, False)
    for layer in reversed(range(LAYERS)):
        normed_b, unit_a, inv_a, ffn_b, unit_f, inv_f, hidden = kept[layer]
        grad_b = grad.astype(bf16)
        d_wout[FF * layer : FF * (layer + 1), :] += mm_nt(hidden, grad_b)
        d_hidden = mm(wout[layer], grad_b)
        d_mixed = []
        for p in range(2):
            value = mixed_ref[layer, FF * p : FF * p + FFH]
            gate = mixed_ref[layer, FF * p + FFH : FF * (p + 1)]
            part = d_hidden[FFH * p : FFH * (p + 1)]
            sig = sigmoid(gate)
            d_mixed.append((part * (gate * sig)).astype(bf16))
            d_mixed.append((part * value * sig * (1.0 + gate * (1.0 - sig))).astype(bf16))
        d_mixed = jnp.concatenate(d_mixed, axis=0)
        d_win[D * layer : D * (layer + 1), :] += mm_nt(ffn_b, d_mixed)
        d_normed = mm(win[layer], d_mixed)
        add_norm(2 * layer, d_normed, unit_f)
        grad = grad + norm_backward(d_normed, unit_f, inv_f, gain_of(2 * layer))
        d_att = attention_backward(layer, grad.astype(bf16), normed_b)
        if layer > 0:
            add_norm(2 * layer - 1, d_att, unit_a)
            grad = grad + norm_backward(d_att, unit_a, inv_a, gain_of(2 * layer - 1))
        else:
            grad = grad + d_att
    store(ig_ref, grad)

    @pl.when(step == pl.num_programs(0) - 1)
    def _():
        for layer in range(LAYERS):
            tall = d_wkv[layer].T
            sources = (d_wq[layer], tall[:WIDE], tall[WIDE:], d_wo[layer])
            for j, source in enumerate(sources):
                slim = jnp.concatenate([source[SLOT * h : SLOT * h + HEAD] for h in range(HEADS)], axis=0)
                base = (4 * layer + j) * D
                d_attn[base : base + D, :] = slim.T if j < 3 else slim
        sums = [jnp.sum(d_norm[j].T, axis=0, keepdims=True) for j in range(2 * NORMS)]
        sums = jnp.concatenate(sums + [jnp.zeros((8 - 2 * NORMS, D), f32)], axis=0)
        if not parts:
            out_refs[0][...] = d_attn[...]
            out_refs[1][...] = d_win[...]
            out_refs[2][...] = d_wout[...]
            out_refs[3][...] = sums
            return
        upper = parts // GROUP
        each = ATTN_ROWS // parts
        sums_high = sums.astype(bf16).astype(f32)
        sums = jnp.concatenate([sums_high, sums - sums_high], axis=0).astype(bf16)
        (out,) = out_refs
        for k in range(GROUP):
            quarter = k // 2
            half = k % 2
            for u in range(upper):
                base = (u * GROUP + k) * each
                out[k, u * each : (u + 1) * each, 0:D] = d_attn[base : base + each, :].astype(bf16)
            base = (quarter // 2) * FF + half * FFH + (quarter % 2) * WOUT_PART
            out[k, OFF_WOUT:OFF_NORM, 0:D] = d_wout[base : base + WOUT_PART, :].astype(bf16)
            out[k, OFF_NORM:OFF_WIN, 0:D] = sums
            rows = d_win[quarter * WIN_PART : (quarter + 1) * WIN_PART, half * FF : (half + 1) * FF]
            out[k, OFF_WIN:PAY_ROWS, :] = rows.astype(bf16)


def run_layers(tokens, cotangent, norms, ffn, attn, parts):
    rows = tokens.shape[0]
    samples = rows // PAIRS
    if parts:
        grad_shapes = [((GROUP, PAY_ROWS, 2 * FFH), bf16)]
    else:
        grad_shapes = [
            ((ATTN_ROWS, D), f32),
            ((LAYERS * D, 2 * FF), f32),
            ((LAYERS * FF, D), f32),
            ((8, D), f32),
        ]
    out_shape = [((rows, 2 * D), bf16), ((rows, 2 * D), f32)] + grad_shapes
    vmem = pl.BlockSpec(memory_space=pltpu.VMEM)
    inputs = (tokens, cotangent, norms, *ffn, attn)
    scratch = [
        ((LAYERS, 3 * WIDE, D), bf16),
        ((LAYERS, D, 3 * WIDE), bf16),
        ((LAYERS, D, WIDE), bf16),
        ((LAYERS, WIDE, D), bf16),
        ((LAYERS, 2 * FF, D), bf16),
        ((LAYERS, D, 2 * FF), bf16),
        ((LAYERS, D, FF), bf16),
        ((LAYERS, FF, D), bf16),
        ((D, 8), f32),
        ((ATTN_ROWS, D), bf16),
        ((LAYERS, WIDE, D), f32),
        ((LAYERS, D, 2 * WIDE), f32),
        ((LAYERS, WIDE, D), f32),
        ((LAYERS * D, 2 * FF), f32),
        ((LAYERS * FF, D), f32),
        ((2 * NORMS, D, 128), f32),
        ((ATTN_ROWS, D), f32),
        ((LAYERS, 2 * KEYS, HEADS * LANES), bf16),
        ((2 * KEYS, HEADS * LANES), bf16),
        ((LAYERS, HEADS, 2 * KEYS, SLOT), bf16),
        ((LAYERS, HEADS, 2 * KEYS, SLOT), bf16),
        ((LAYERS, WIDE, LANES), bf16),
        ((LAYERS, WIDE, LANES), bf16),
        ((WIDE, LANES), bf16),
        ((WIDE, LANES), bf16),
        ((HEADS * LANES, WIDE), bf16),
        ((HEADS * LANES, WIDE), bf16),
        ((LAYERS, WIDE, LANES), f32),
        ((LAYERS, WIDE, LANES), bf16),
        ((LAYERS, WIDE, LANES), f32),
        ((WIDE, LANES), bf16),
        ((LANES, 2 * WIDE), bf16),
        ((LAYERS, 2 * FF, LANES), f32),
    ]

    def body(*refs):
        layers_kernel(parts, *refs)

    return pl.pallas_call(
        body,
        grid=(samples,),
        in_specs=[vmem] * len(inputs),
        out_specs=[vmem] * len(out_shape),
        out_shape=[jax.ShapeDtypeStruct(*s) for s in out_shape],
        scratch_shapes=[pltpu.VMEM(*s) for s in scratch],
        compiler_params=pltpu.CompilerParams(
            dimension_semantics=("arbitrary",), vmem_limit_bytes=60 * 1024 * 1024
        ),
        cost_estimate=pl.CostEstimate(
            flops=samples * 5_000_000_000, bytes_accessed=20_000_000, transcendentals=0
        ),
    )(*inputs)


def small_kernel(body, out_shape, *inputs, scratch=()):
    vmem = pl.BlockSpec(memory_space=pltpu.VMEM)
    return pl.pallas_call(
        body,
        in_specs=[vmem] * len(inputs),
        out_specs=[vmem] * len(out_shape),
        out_shape=[jax.ShapeDtypeStruct(*s) for s in out_shape],
        scratch_shapes=[pltpu.VMEM(*s) for s in scratch],
        compiler_params=pltpu.CompilerParams(vmem_limit_bytes=32 * 1024 * 1024),
    )(*inputs)


def swap_blocks(blocks, groups):
    return lax.all_to_all(blocks, AXES, 0, 0, axis_index_groups=groups, tiled=True)


def groups_of(parts):
    upper = parts // GROUP
    near = [[u * GROUP + k for k in range(GROUP)] for u in range(upper)]
    far = [[u * GROUP + k for u in range(upper)] for k in range(GROUP)]
    same_half = [[u * GROUP + 2 * q + p for q in range(4)] for u in range(upper) for p in range(2)]
    return near, far, same_half


def sum_gradients(payload, parts):
    near, far, same_half = groups_of(parts)
    upper = parts // GROUP
    each = ATTN_ROWS // parts
    win_rows = WIN_PART // upper
    wout_rows = WOUT_PART // upper
    at_norm = each + wout_rows
    at_win = at_norm + 16
    rows = at_win + win_rows
    ffn_rows = wout_rows + win_rows
    width = 2 * FFH

    def join_group(landed, out, total):
        total[...] = tree_sum([landed[k].astype(f32) for k in range(GROUP)])
        sums = total[OFF_NORM : OFF_NORM + 8, :] + total[OFF_NORM + 8 : OFF_WIN, :]
        high = sums.astype(bf16).astype(f32)
        norm = jnp.concatenate([high, sums - high], axis=0).astype(bf16)
        for u in range(upper):
            out[u, 0:each, :] = total[u * each : (u + 1) * each, :].astype(bf16)
            base = OFF_WOUT + u * wout_rows
            out[u, each:at_norm, :] = total[base : base + wout_rows, :].astype(bf16)
            out[u, at_norm:at_win, :] = norm
            base = OFF_WIN + u * win_rows
            out[u, at_win:rows, :] = total[base : base + win_rows, :].astype(bf16)

    (sent,) = small_kernel(
        join_group,
        [((upper, rows, width), bf16)],
        swap_blocks(payload, near),
        scratch=[((PAY_ROWS, width), f32)],
    )

    def join_rest(landed, attn, norm, ffn):
        total = tree_sum([landed[u].astype(f32) for u in range(upper)])
        attn[...] = total[0:each, 0:D]
        norm[...] = total[at_norm : at_norm + 8, 0:D] + total[at_norm + 8 : at_win, 0:D]
        for u in range(upper):
            ffn[u, 0:wout_rows, :] = total[each:at_norm, :].astype(bf16)
            ffn[u, wout_rows:, :] = total[at_win:, :].astype(bf16)

    attn, norm, ffn = small_kernel(
        join_rest,
        [((each, D), f32), ((8, D), f32), ((upper, ffn_rows, width), bf16)],
        swap_blocks(sent, far),
    )
    column = swap_blocks(ffn, far)
    block = swap_blocks(jnp.broadcast_to(column, (4,) + column.shape), same_half)

    def spread(landed, win, wout):
        for q in range(4):
            for u in range(upper):
                piece = q * upper + u
                part = landed[q, u].astype(f32)
                wout[piece * wout_rows : (piece + 1) * wout_rows, :] = part[:wout_rows, 0:D]
                win[piece * win_rows : (piece + 1) * win_rows, :] = part[wout_rows:, :]

    win, wout = small_kernel(spread, [((LAYERS * D, width), f32), ((LAYERS * FFH, D), f32)], block)
    return attn, norm, win, wout


def on_device(devices, tokens, attn_weights, norm_params, w_in, w_out, cotangent):
    each = attn_weights.shape[0]
    staged = devices % GROUP == 0 and each % 16 == 0
    swap_halves = [(0, 1), (1, 0)]
    w_in = w_in.reshape(LAYERS, D, 2 * FFH)
    w_in_other = lax.ppermute(w_in, "narrow", swap_halves)
    w_out_other = lax.ppermute(w_out, "narrow", swap_halves)
    first = lax.axis_index("narrow") == 0
    ffn = (
        jnp.where(first, w_in, w_in_other),
        jnp.where(first, w_in_other, w_in),
        jnp.where(first, w_out, w_out_other),
        jnp.where(first, w_out_other, w_out),
    )
    norms = norm_params.reshape(2 * NORMS, D)
    if not staged:
        attn_all = lax.all_gather(attn_weights, AXES, axis=0, tiled=True)
        res, ig, d_attn, d_win, d_wout, sums = run_layers(tokens, cotangent, norms, ffn, attn_all, 0)
        attn = lax.psum_scatter(d_attn, AXES, scatter_dimension=0, tiled=True)
        norm = lax.psum(sums, AXES)
        d_win = jnp.stack([d_win[:, :FF], d_win[:, FF:]])
        d_wout = d_wout.reshape(LAYERS, 2, FFH, D).transpose(1, 0, 2, 3)
        win = lax.psum_scatter(d_win, "narrow", scatter_dimension=0, tiled=False)
        wout = lax.psum_scatter(d_wout, "narrow", scatter_dimension=0, tiled=False)
        win, wout = lax.psum((win, wout), "dp")
    else:
        near, far, _ = groups_of(devices)
        upper = devices // GROUP
        column = swap_blocks(jnp.broadcast_to(attn_weights, (upper, each, D)), far)
        attn_all = swap_blocks(jnp.broadcast_to(column, (GROUP, upper, each, D)), near)
        res, ig, payload = run_layers(tokens, cotangent, norms, ffn, attn_all, devices)
        attn, norm, win, wout = sum_gradients(payload, devices)
    return (
        res,
        ig,
        attn,
        norm[: 2 * NORMS].reshape(norm_params.shape),
        win.reshape(LAYERS, D, 2, FFH),
        wout.reshape(LAYERS, FFH, D),
    )


def solution(mesh):
    rows = P(("dp", "narrow"), None)
    hidden_in = P(None, None, None, "narrow")
    hidden_out = P(None, "narrow", None)
    devices = mesh.shape["dp"] * mesh.shape["narrow"]

    def per_device(*args):
        return on_device(devices, *args)

    return jax.shard_map(
        per_device,
        mesh=mesh,
        in_specs=(rows, rows, P(), hidden_in, hidden_out, rows),
        out_specs=(rows, rows, rows, P(), hidden_in, hidden_out),
        check_vma=False,
    )
```

```python
import math

import jax
import jax.numpy as jnp
from jax import lax
from jax.experimental import pallas as pl
from jax.experimental.pallas import tpu as pltpu
from jax.sharding import PartitionSpec as P

HEADS = 8
HEAD = 24
SLOT = 32
WIDE = HEADS * SLOT
D = HEADS * HEAD
FF = 256
FFH = FF // 2
LAYERS = 2
NORMS = 2 * LAYERS - 1
SEQ = 476
PAIRS = SEQ // 2
KEYS = 240
HALF = 256
LANES = 2 * HALF
EPS = 1e-05
SCALE = HEAD ** (-0.5)
LOG2E = math.log2(math.e)
ATTN_ROWS = LAYERS * 4 * D

GROUP = 8
NEAR = (0, 1, 4, 5)
TWIN = 2
WIN_PART = LAYERS * D // 4
WOUT_PART = LAYERS * FFH // 4
ATTN_PART = ATTN_ROWS // GROUP
OFF_WOUT = ATTN_PART
OFF_NORM = OFF_WOUT + WOUT_PART
OFF_WIN = OFF_NORM + 16
PAY_ROWS = OFF_WIN + WIN_PART

bf16 = jnp.bfloat16
f32 = jnp.float32
AXES = ("dp", "narrow")


def mm(left, right):
    return jnp.dot(left, right, preferred_element_type=f32)


def mm_nt(left, right):
    return lax.dot_general(left, right, (((1,), (1,)), ((), ())), preferred_element_type=f32)


def sigmoid(value):
    return 0.5 + 0.5 * jnp.tanh(0.5 * value)


def fold_lanes(value):
    return value[:, 0:128] + value[:, 128:256] + value[:, 256:384] + value[:, 384:512]


def norm_forward(stream, gain, shift):
    center = stream - jnp.sum(stream, axis=0, keepdims=True) * (1.0 / D)
    inverse = lax.rsqrt(jnp.sum(center * center, axis=0, keepdims=True) * (1.0 / D) + EPS)
    unit = center * inverse
    return (unit * gain + shift, unit, inverse)


def norm_backward(grad, unit, inverse, gain):
    scaled = grad * gain
    mean = jnp.sum(scaled, axis=0, keepdims=True) * (1.0 / D)
    slope = jnp.sum(scaled * unit, axis=0, keepdims=True) * (1.0 / D)
    return inverse * (scaled - mean - unit * slope)


def tree_sum(parts):
    while len(parts) > 1:
        parts = [parts[i] + parts[i + 1] for i in range(0, len(parts), 2)]
    return parts[0]


def ds(start, size, step):
    return pl.ds(pl.multiple_of(start, step), size)


def layers_kernel(parts, *refs):
    refs = list(refs)

    def take(count):
        taken = refs[:count]
        del refs[:count]
        return taken

    me_ref, x_ref, g_ref, norm_ref, win_own, win_other, wout_own, wout_other = take(8)
    attn_refs = take(2 if parts else 1)
    res_ref, ig_ref = take(2)
    out_refs = take(2 if parts else 4)
    wqkv_t, wqkv, wo_t, wo, win_t, win, wout_t, wout, norm_t, attn_ref = take(10)
    d_wq, d_wkv, d_wo, d_win, d_wout, d_norm, d_attn = take(7)
    e_ref, ds_ref, kh_ref, vh_ref, q_ref, k_ref, v_ref, do_ref, do_all, q_all = take(10)
    ctx_ref, ctxb_ref, rinv_ref, dq_ref, dkv_ref, mixed_ref = refs
    step = pl.program_id(0)
    rows_total = x_ref.shape[0]

    @pl.when(step == 0)
    def _():
        for ref in (d_wq, d_wkv, d_wo, d_win, d_wout, d_norm, dkv_ref):
            ref[...] = jnp.zeros_like(ref)
        if parts:
            me = me_ref[0]
            upper = parts // GROUP
            each = ATTN_ROWS // parts
            for t, ref in enumerate(attn_refs):
                for j, k in enumerate(NEAR):
                    for u in range(upper):
                        owner = ((me // GROUP) ^ u) * GROUP + ((me % GROUP) ^ k ^ (TWIN * t))
                        attn_ref[ds(owner * each, each, each), :] = ref[j, u]
        else:
            attn_ref[...] = attn_refs[0][...]
        norm_t[...] = jnp.concatenate([norm_ref[...], jnp.zeros((8 - 2 * NORMS, D), f32)], axis=0).T
        gap = jnp.zeros((SLOT - HEAD, D), f32)

        def pad_heads(matrix):
            slots = []
            for h in range(HEADS):
                slots += [matrix[HEAD * h : HEAD * (h + 1)], gap]
            return jnp.concatenate(slots, axis=0)

        for layer in range(LAYERS):
            for j in range(4):
                base = (4 * layer + j) * D
                matrix = attn_ref[base : base + D, :].astype(f32)
                if j < 3:
                    tall = pad_heads(matrix.T)
                    wqkv_t[layer, j * WIDE : (j + 1) * WIDE, :] = tall.astype(bf16)
                    wqkv[layer, :, j * WIDE : (j + 1) * WIDE] = tall.T.astype(bf16)
                else:
                    tall = pad_heads(matrix)
                    wo[layer] = tall.astype(bf16)
                    wo_t[layer] = tall.T.astype(bf16)
            for p, (w1, w2) in enumerate(((win_own, wout_own), (win_other, wout_other))):
                win[layer, :, p * FF : (p + 1) * FF] = w1[layer]
                win_t[layer, p * FF : (p + 1) * FF, :] = w1[layer].astype(f32).T.astype(bf16)
                wout[layer, p * FFH : (p + 1) * FFH, :] = w2[layer]
                wout_t[layer, :, p * FFH : (p + 1) * FFH] = w2[layer].astype(f32).T.astype(bf16)

    base = step * PAIRS
    start = jnp.minimum(base // 16 * 16, rows_total - HALF)
    shift = base - start
    window = ds(start, HALF, 16)
    pair_row = lax.broadcasted_iota(jnp.int32, (HALF, 2 * D), 0)

    def load(ref, fill_first):
        rows = pltpu.roll(ref[window, :].astype(f32), lax.rem(HALF - shift, HALF), 0)
        fill = rows[0:1] if fill_first else 0.0
        cols = jnp.where(pair_row < PAIRS, rows, fill).T
        return jnp.concatenate([cols[:D], cols[D:]], axis=1)

    def store(ref, value):
        cols = jnp.concatenate([value[:, :HALF], value[:, HALF:]], axis=0)
        rows = pltpu.roll(cols.T, shift, 0)
        here = jnp.logical_and(pair_row >= shift, pair_row < shift + PAIRS)
        ref[window, :] = jnp.where(here, rows, ref[window, :].astype(f32)).astype(ref.dtype)

    lane = lax.broadcasted_iota(jnp.int32, (WIDE, LANES), 1)
    row = lax.broadcasted_iota(jnp.int32, (WIDE, LANES), 0)
    real = (lane & (HALF - 1)) < PAIRS
    slot_row = row & (SLOT - 1)
    ones_rows = jnp.logical_or(slot_row == HEAD, slot_row == HEAD + 1).astype(f32)
    head_row = lax.broadcasted_iota(jnp.int32, (SLOT, LANES), 0)
    lane_head = lax.broadcasted_iota(jnp.int32, (LANES, WIDE), 1) // SLOT
    key_row = lax.broadcasted_iota(jnp.int32, (2 * KEYS, WIDE), 0)
    real_key = jnp.where(key_row < KEYS, key_row, key_row - KEYS) < PAIRS

    def attention_forward(layer, normed_b):
        qkv = mm(wqkv_t[layer], normed_b)
        queries = (qkv[:WIDE] * (SCALE * LOG2E)).astype(bf16)
        q_ref[layer] = queries
        keys = qkv[WIDE : 2 * WIDE].astype(bf16)
        k_ref[layer] = keys
        values = jnp.where(real, qkv[2 * WIDE :] + ones_rows, 0.0).astype(bf16)
        v_ref[...] = values
        for tall, ref in ((keys.T, kh_ref), (values.T, vh_ref)):
            for h in range(HEADS):
                ref[layer, h, 0:KEYS] = tall[0:KEYS, SLOT * h : SLOT * (h + 1)]
                ref[layer, h, KEYS:] = tall[HALF : HALF + KEYS, SLOT * h : SLOT * (h + 1)]

        def scores_of(h):
            return mm(kh_ref[layer, h], q_ref[layer, SLOT * h : SLOT * (h + 1), :])

        scores = scores_of(0)
        for h in range(HEADS):
            rows = slice(SLOT * h, SLOT * (h + 1))
            ahead = scores_of(h + 1) if h + 1 < HEADS else None
            top = jnp.max(scores, axis=0, keepdims=True)
            weights = jnp.exp2(scores - top).astype(bf16)
            e_ref[layer, :, LANES * h : LANES * (h + 1)] = weights
            out = mm(v_ref[rows, 0:KEYS], weights[0:KEYS]) + mm(
                v_ref[rows, HALF : HALF + KEYS], weights[KEYS:]
            )
            inverse = 1.0 / out[HEAD : HEAD + 1]
            context = out * inverse
            rinv_ref[layer, rows, :] = jnp.broadcast_to(inverse, (SLOT, LANES))
            ctx_ref[layer, rows, :] = context
            ctxb_ref[layer, rows, :] = context.astype(bf16)
            scores = ahead
        return mm(wo_t[layer], ctxb_ref[layer])

    def spread_heads(ref, tall):
        for h in range(HEADS):
            ref[LANES * h : LANES * (h + 1), :] = jnp.where(lane_head == h, tall, jnp.zeros_like(tall))

    def attention_backward(layer, grad_b, normed_b):
        d_wo[layer] += mm_nt(ctxb_ref[layer], grad_b)
        grads = (mm(wo[layer], grad_b) * rinv_ref[layer]).astype(bf16)
        product = grads.astype(f32) * ctx_ref[layer]
        for h in range(HEADS):
            rows = slice(SLOT * h, SLOT * (h + 1))
            dot = -jnp.sum(product[rows][:HEAD], axis=0, keepdims=True)
            dot_high = dot.astype(bf16).astype(f32)
            grad = jnp.where(head_row == HEAD, dot_high, grads[rows].astype(f32))
            grad = jnp.where(head_row == HEAD + 1, dot - dot_high, grad)
            do_ref[rows, :] = grad.astype(bf16)
        spread_heads(do_all, do_ref[...].T)
        spread_heads(q_all, q_ref[layer].T)

        def grad_probs_of(h):
            return mm(vh_ref[layer, h], do_ref[SLOT * h : SLOT * (h + 1), :])

        grad_probs = grad_probs_of(0)
        for h in range(HEADS):
            rows = slice(SLOT * h, SLOT * (h + 1))
            ahead = grad_probs_of(h + 1) if h + 1 < HEADS else None
            d_scores = e_ref[layer, :, LANES * h : LANES * (h + 1)] * grad_probs.astype(bf16)
            ds_ref[:, LANES * h : LANES * (h + 1)] = d_scores
            dq = mm(k_ref[layer, rows, 0:KEYS], d_scores[0:KEYS]) + mm(
                k_ref[layer, rows, HALF : HALF + KEYS], d_scores[KEYS:]
            )
            dq_ref[rows, :] = (dq * SCALE).astype(bf16)
            grad_probs = ahead
        dk = (mm(ds_ref[...], q_all[...]) * (1.0 / LOG2E)).astype(bf16)
        dv = jnp.where(real_key, mm(e_ref[layer], do_all[...]), 0.0).astype(bf16)
        for half in range(2):
            here = slice(half * KEYS, (half + 1) * KEYS)
            there = slice(half * HALF, half * HALF + KEYS)
            dkv_ref[there, 0:WIDE] = dk[here]
            dkv_ref[there, WIDE:] = dv[here]
        d_wq[layer] += mm_nt(dq_ref[...], normed_b)
        d_wkv[layer] += mm(normed_b, dkv_ref[...])
        return mm(wqkv[layer, :, 0:WIDE], dq_ref[...]) + mm_nt(wqkv[layer, :, WIDE:], dkv_ref[...])

    def add_norm(index, grad, unit):
        d_norm[2 * index] += fold_lanes(grad * unit)
        d_norm[2 * index + 1] += fold_lanes(grad)

    def gain_of(index):
        return norm_t[:, 2 * index : 2 * index + 1]

    def shift_of(index):
        return norm_t[:, 2 * index + 1 : 2 * index + 2]

    kept = []
    stream = load(x_ref, True)
    normed_b = stream.astype(bf16)
    unit_a = inv_a = None
    for layer in range(LAYERS):
        if layer > 0:
            normed, unit_a, inv_a = norm_forward(stream, gain_of(2 * layer - 1), shift_of(2 * layer - 1))
            normed_b = normed.astype(bf16)
        stream = stream + attention_forward(layer, normed_b)
        normed, unit_f, inv_f = norm_forward(stream, gain_of(2 * layer), shift_of(2 * layer))
        ffn_b = normed.astype(bf16)
        mixed = mm(win_t[layer], ffn_b)
        mixed_ref[layer] = mixed
        hidden = []
        for p in range(2):
            value = mixed[FF * p : FF * p + FFH]
            gate = mixed[FF * p + FFH : FF * (p + 1)]
            hidden.append((value * (gate * sigmoid(gate))).astype(bf16))
        hidden = jnp.concatenate(hidden, axis=0)
        stream = stream + mm(wout_t[layer], hidden)
        kept.append((normed_b, unit_a, inv_a, ffn_b, unit_f, inv_f, hidden))
    store(res_ref, stream)

    grad = load(g_ref, False)
    for layer in reversed(range(LAYERS)):
        normed_b, unit_a, inv_a, ffn_b, unit_f, inv_f, hidden = kept[layer]
        grad_b = grad.astype(bf16)
        d_wout[FF * layer : FF * (layer + 1), :] += mm_nt(hidden, grad_b)
        d_hidden = mm(wout[layer], grad_b)
        d_mixed = []
        for p in range(2):
            value = mixed_ref[layer, FF * p : FF * p + FFH]
            gate = mixed_ref[layer, FF * p + FFH : FF * (p + 1)]
            part = d_hidden[FFH * p : FFH * (p + 1)]
            sig = sigmoid(gate)
            d_mixed.append((part * (gate * sig)).astype(bf16))
            d_mixed.append((part * value * sig * (1.0 + gate * (1.0 - sig))).astype(bf16))
        d_mixed = jnp.concatenate(d_mixed, axis=0)
        d_win[D * layer : D * (layer + 1), :] += mm_nt(ffn_b, d_mixed)
        d_normed = mm(win[layer], d_mixed)
        add_norm(2 * layer, d_normed, unit_f)
        grad = grad + norm_backward(d_normed, unit_f, inv_f, gain_of(2 * layer))
        d_att = attention_backward(layer, grad.astype(bf16), normed_b)
        if layer > 0:
            add_norm(2 * layer - 1, d_att, unit_a)
            grad = grad + norm_backward(d_att, unit_a, inv_a, gain_of(2 * layer - 1))
        else:
            grad = grad + d_att
    store(ig_ref, grad)

    @pl.when(step == pl.num_programs(0) - 1)
    def _():
        for layer in range(LAYERS):
            tall = d_wkv[layer].T
            sources = (d_wq[layer], tall[:WIDE], tall[WIDE:], d_wo[layer])
            for j, source in enumerate(sources):
                slim = jnp.concatenate([source[SLOT * h : SLOT * h + HEAD] for h in range(HEADS)], axis=0)
                base = (4 * layer + j) * D
                d_attn[base : base + D, :] = slim.T if j < 3 else slim
        sums = [jnp.sum(d_norm[j].T, axis=0, keepdims=True) for j in range(2 * NORMS)]
        sums = jnp.concatenate(sums + [jnp.zeros((8 - 2 * NORMS, D), f32)], axis=0)
        if not parts:
            out_refs[0][...] = d_attn[...]
            out_refs[1][...] = d_win[...]
            out_refs[2][...] = d_wout[...]
            out_refs[3][...] = sums
            return
        me = me_ref[0]
        upper = parts // GROUP
        each = ATTN_ROWS // parts
        sums_high = sums.astype(bf16).astype(f32)
        sums = jnp.concatenate([sums_high, sums - sums_high], axis=0).astype(bf16)
        for t, out in enumerate(out_refs):
            for j, k in enumerate(NEAR):
                kind = out.dtype
                low = (me % GROUP) ^ k ^ (TWIN * t)
                quarter = low // 2
                half = k % 2
                for u in range(upper):
                    rows = d_attn[ds((u * GROUP + low) * each, each, each), :]
                    out[j, u * each : (u + 1) * each, 0:D] = rows.astype(kind)
                first = (quarter // 2) * FF + half * FFH + (quarter % 2) * WOUT_PART
                out[j, OFF_WOUT:OFF_NORM, 0:D] = d_wout[ds(first, WOUT_PART, WOUT_PART), :].astype(kind)
                out[j, OFF_NORM:OFF_WIN, 0:D] = sums.astype(kind)
                rows = d_win[ds(quarter * WIN_PART, WIN_PART, WIN_PART), half * FF : (half + 1) * FF]
                out[j, OFF_WIN:PAY_ROWS, :] = rows.astype(kind)


def run_layers(me, tokens, cotangent, norms, ffn, attn_parts, parts):
    rows = tokens.shape[0]
    samples = rows // PAIRS
    if parts:
        grad_shapes = [((len(NEAR), PAY_ROWS, 2 * FFH), kind) for kind in (f32, bf16)]
    else:
        grad_shapes = [
            ((ATTN_ROWS, D), f32),
            ((LAYERS * D, 2 * FF), f32),
            ((LAYERS * FF, D), f32),
            ((8, D), f32),
        ]
    out_shape = [((rows, 2 * D), bf16), ((rows, 2 * D), f32)] + grad_shapes
    vmem = pl.BlockSpec(memory_space=pltpu.VMEM)
    inputs = (tokens, cotangent, norms, *ffn, *attn_parts)
    scratch = [
        ((LAYERS, 3 * WIDE, D), bf16),
        ((LAYERS, D, 3 * WIDE), bf16),
        ((LAYERS, D, WIDE), bf16),
        ((LAYERS, WIDE, D), bf16),
        ((LAYERS, 2 * FF, D), bf16),
        ((LAYERS, D, 2 * FF), bf16),
        ((LAYERS, D, FF), bf16),
        ((LAYERS, FF, D), bf16),
        ((D, 8), f32),
        ((ATTN_ROWS, D), bf16),
        ((LAYERS, WIDE, D), f32),
        ((LAYERS, D, 2 * WIDE), f32),
        ((LAYERS, WIDE, D), f32),
        ((LAYERS * D, 2 * FF), f32),
        ((LAYERS * FF, D), f32),
        ((2 * NORMS, D, 128), f32),
        ((ATTN_ROWS, D), f32),
        ((LAYERS, 2 * KEYS, HEADS * LANES), bf16),
        ((2 * KEYS, HEADS * LANES), bf16),
        ((LAYERS, HEADS, 2 * KEYS, SLOT), bf16),
        ((LAYERS, HEADS, 2 * KEYS, SLOT), bf16),
        ((LAYERS, WIDE, LANES), bf16),
        ((LAYERS, WIDE, LANES), bf16),
        ((WIDE, LANES), bf16),
        ((WIDE, LANES), bf16),
        ((HEADS * LANES, WIDE), bf16),
        ((HEADS * LANES, WIDE), bf16),
        ((LAYERS, WIDE, LANES), f32),
        ((LAYERS, WIDE, LANES), bf16),
        ((LAYERS, WIDE, LANES), f32),
        ((WIDE, LANES), bf16),
        ((LANES, 2 * WIDE), bf16),
        ((LAYERS, 2 * FF, LANES), f32),
    ]

    def body(*refs):
        layers_kernel(parts, *refs)

    return pl.pallas_call(
        body,
        grid=(samples,),
        in_specs=[pl.BlockSpec(memory_space=pltpu.SMEM)] + [vmem] * len(inputs),
        out_specs=[vmem] * len(out_shape),
        out_shape=[jax.ShapeDtypeStruct(*s) for s in out_shape],
        scratch_shapes=[pltpu.VMEM(*s) for s in scratch],
        compiler_params=pltpu.CompilerParams(
            dimension_semantics=("arbitrary",), vmem_limit_bytes=60 * 1024 * 1024
        ),
        cost_estimate=pl.CostEstimate(
            flops=samples * 5_000_000_000, bytes_accessed=20_000_000, transcendentals=0
        ),
    )(me, *inputs)


def small_kernel(body, out_shape, *inputs, scratch=()):
    vmem = pl.BlockSpec(memory_space=pltpu.VMEM)
    return pl.pallas_call(
        body,
        in_specs=[pl.BlockSpec(memory_space=pltpu.SMEM)] + [vmem] * (len(inputs) - 1),
        out_specs=[vmem] * len(out_shape),
        out_shape=[jax.ShapeDtypeStruct(*s) for s in out_shape],
        scratch_shapes=[pltpu.VMEM(*s) for s in scratch],
        compiler_params=pltpu.CompilerParams(vmem_limit_bytes=32 * 1024 * 1024),
    )(*inputs)


def sum_gradients(me, payloads, parts):
    upper = parts // GROUP
    each = ATTN_ROWS // parts
    win_rows = WIN_PART // upper
    wout_rows = WOUT_PART // upper
    at_norm = each + wout_rows
    at_win = at_norm + 16
    rows = at_win + win_rows

    def swap(value, k):
        return lax.ppermute(value, AXES, [(i, i ^ k) for i in range(parts)])

    def join_twins(me_ref, mine, theirs, keep, *sends):
        for j, out in enumerate((keep, *sends)):
            total = mine[j] + theirs[j].astype(f32)
            out[0:OFF_NORM] = total[0:OFF_NORM].astype(out.dtype)
            sums = total[OFF_NORM : OFF_NORM + 8] + total[OFF_NORM + 8 : OFF_WIN]
            high = sums.astype(bf16).astype(f32)
            norm = jnp.concatenate([high, sums - high], axis=0).astype(bf16)
            out[OFF_NORM:OFF_WIN] = norm.astype(out.dtype)
            out[OFF_WIN:] = total[OFF_WIN:].astype(out.dtype)

    width = 2 * FFH
    keep, *sends = small_kernel(
        join_twins,
        [((PAY_ROWS, width), f32)] + [((PAY_ROWS, width), bf16)] * (len(NEAR) - 1),
        me,
        payloads[0],
        swap(payloads[1], TWIN),
    )
    landed = [keep] + [swap(sent, k) for sent, k in zip(sends, NEAR[1:], strict=True)]

    def join_group(me_ref, *refs):
        ins, outs, total = refs[: len(NEAR)], refs[len(NEAR) : -1], refs[-1]
        total[...] = tree_sum([r[...].astype(f32) for r in ins])
        sums = total[OFF_NORM : OFF_NORM + 8, :] + total[OFF_NORM + 8 : OFF_WIN, :]
        high = sums.astype(bf16).astype(f32)
        norm = jnp.concatenate([high, sums - high], axis=0).astype(bf16)
        mine = me_ref[0] // GROUP
        for u in range(upper):
            out = outs[u]
            there = mine ^ u
            out[0:each, :] = total[ds(there * each, each, 8), :].astype(out.dtype)
            wout = total[ds(OFF_WOUT + there * wout_rows, wout_rows, 8), :]
            out[each:at_norm, :] = wout.astype(out.dtype)
            out[at_norm:at_win, :] = norm.astype(out.dtype)
            win = total[ds(OFF_WIN + there * win_rows, win_rows, 8), :]
            out[at_win:rows, :] = win.astype(out.dtype)

    sent = small_kernel(
        join_group,
        [((rows, width), f32 if u == 0 else bf16) for u in range(upper)],
        me,
        *landed,
        scratch=[((PAY_ROWS, width), f32)],
    )
    landed = [sent[0]] + [swap(sent[u], u * GROUP) for u in range(1, upper)]
    ffn_rows = wout_rows + win_rows

    def join_rest(me_ref, *refs):
        ins, (attn, norm, ffn) = refs[:upper], refs[upper:]
        total = tree_sum([r[...].astype(f32) for r in ins])
        attn[...] = total[0:each, 0:D]
        norm[...] = total[at_norm : at_norm + 8, 0:D] + total[at_norm + 8 : at_win, 0:D]
        ffn[0:wout_rows, :] = total[each:at_norm, :].astype(bf16)
        ffn[wout_rows:, :] = total[at_win:, :].astype(bf16)

    attn, norm, ffn = small_kernel(
        join_rest, [((each, D), f32), ((8, D), f32), ((ffn_rows, width), bf16)], me, *landed
    )
    column = jnp.stack([ffn] + [swap(ffn, u * GROUP) for u in range(1, upper)])
    block = [column] + [swap(column, 2 * q) for q in range(1, 4)]

    def spread(me_ref, *refs):
        ins, (win, wout) = refs[:4], refs[4:]
        mine = me_ref[0] // GROUP
        quarter = (me_ref[0] % GROUP) // 2
        for q in range(4):
            for u in range(upper):
                piece = (quarter ^ q) * upper + (mine ^ u)
                part = ins[q][u].astype(f32)
                wout[ds(piece * wout_rows, wout_rows, 8), :] = part[:wout_rows, 0:D]
                win[ds(piece * win_rows, win_rows, 8), :] = part[wout_rows:, :]

    win, wout = small_kernel(
        spread, [((LAYERS * D, width), f32), ((LAYERS * FFH, D), f32)], me, *block
    )
    return attn, norm, win, wout


def on_device(devices, tokens, attn_weights, norm_params, w_in, w_out, cotangent):
    each = attn_weights.shape[0]
    me = (lax.axis_index("dp") * 2 + lax.axis_index("narrow")).astype(jnp.int32).reshape(1)
    staged = devices % GROUP == 0 and each % 16 == 0
    swap_halves = [(0, 1), (1, 0)]
    w_in = w_in.reshape(LAYERS, D, 2 * FFH)
    ffn = (
        w_in,
        lax.ppermute(w_in, "narrow", swap_halves),
        w_out,
        lax.ppermute(w_out, "narrow", swap_halves),
    )
    norms = norm_params.reshape(2 * NORMS, D)
    if not staged:
        attn_all = lax.all_gather(attn_weights, AXES, axis=0, tiled=True)
        res, ig, d_attn, d_win, d_wout, sums = run_layers(
            me, tokens, cotangent, norms, ffn, (attn_all,), 0
        )
        attn = lax.psum_scatter(d_attn, AXES, scatter_dimension=0, tiled=True)
        norm = lax.psum(sums, AXES)
        d_wout = d_wout.reshape(LAYERS, FF, D)
        own_in, other_in = d_win[:, :FF], d_win[:, FF:]
        own_out, other_out = d_wout[:, :FFH], d_wout[:, FFH:]
        win = lax.psum(own_in + lax.ppermute(other_in, "narrow", swap_halves), "dp")
        wout = lax.psum(own_out + lax.ppermute(other_out, "narrow", swap_halves), "dp")
    else:
        upper = devices // GROUP

        def swap(value, k):
            return lax.ppermute(value, AXES, [(i, i ^ k) for i in range(devices)])

        column = jnp.stack(
            [attn_weights] + [swap(attn_weights, u * GROUP) for u in range(1, upper)]
        )
        plane = jnp.stack([column] + [swap(column, k) for k in NEAR[1:]])
        attn_parts = [plane, swap(plane, TWIN)]
        res, ig, *payloads = run_layers(me, tokens, cotangent, norms, ffn, attn_parts, devices)
        attn, norm, win, wout = sum_gradients(me, payloads, devices)
    return (
        res,
        ig,
        attn,
        norm[: 2 * NORMS].reshape(norm_params.shape),
        win.reshape(LAYERS, D, 2, FFH),
        wout.reshape(LAYERS, FFH, D),
    )


def solution(mesh):
    rows = P(("dp", "narrow"), None)
    hidden_in = P(None, None, None, "narrow")
    hidden_out = P(None, "narrow", None)
    devices = mesh.shape["dp"] * mesh.shape["narrow"]

    def per_device(*args):
        return on_device(devices, *args)

    return jax.shard_map(
        per_device,
        mesh=mesh,
        in_specs=(rows, rows, P(), hidden_in, hidden_out, rows),
        out_specs=(rows, rows, rows, P(), hidden_in, hidden_out),
        check_vma=False,
    )
```

```python
import math

import jax
import jax.numpy as jnp
from jax import lax
from jax.experimental import pallas as pl
from jax.experimental.pallas import tpu as pltpu
from jax.sharding import PartitionSpec as P

HEADS = 8
HEAD = 24
SLOT = 32
WIDE = HEADS * SLOT
D = HEADS * HEAD
FF = 256
FFH = FF // 2
LAYERS = 2
NORMS = 2 * LAYERS - 1
SEQ = 476
PAIRS = SEQ // 2
KEYS = 240
HALF = 256
LANES = 2 * HALF
EPS = 1e-05
SCALE = HEAD ** (-0.5)
LOG2E = math.log2(math.e)
ATTN_ROWS = LAYERS * 4 * D

GROUP = 8
NEAR = (0, 1, 4, 5)
TWIN = 2
WIN_PART = LAYERS * D // 4
WOUT_PART = LAYERS * FFH // 4
ATTN_PART = ATTN_ROWS // GROUP // LAYERS
OFF_WOUT = ATTN_PART
OFF_NORM = OFF_WOUT + WOUT_PART
OFF_WIN = OFF_NORM + 16
PAY_ROWS = OFF_WIN + WIN_PART

bf16 = jnp.bfloat16
f32 = jnp.float32
AXES = ("dp", "narrow")


def mm(left, right):
    return jnp.dot(left, right, preferred_element_type=f32)


def mm_nt(left, right):
    return lax.dot_general(left, right, (((1,), (1,)), ((), ())), preferred_element_type=f32)


def sigmoid(value):
    return 0.5 + 0.5 * jnp.tanh(0.5 * value)


def fold_lanes(value):
    return value[:, 0:128] + value[:, 128:256] + value[:, 256:384] + value[:, 384:512]


def norm_forward(stream, gain, shift):
    center = stream - jnp.sum(stream, axis=0, keepdims=True) * (1.0 / D)
    inverse = lax.rsqrt(jnp.sum(center * center, axis=0, keepdims=True) * (1.0 / D) + EPS)
    unit = center * inverse
    return (unit * gain + shift, unit, inverse)


def norm_backward(grad, unit, inverse, gain):
    scaled = grad * gain
    mean = jnp.sum(scaled, axis=0, keepdims=True) * (1.0 / D)
    slope = jnp.sum(scaled * unit, axis=0, keepdims=True) * (1.0 / D)
    return inverse * (scaled - mean - unit * slope)


def tree_sum(parts):
    while len(parts) > 1:
        parts = [parts[i] + parts[i + 1] for i in range(0, len(parts), 2)]
    return parts[0]


def ds(start, size, step):
    return pl.ds(pl.multiple_of(start, step), size)


def take(refs, count):
    taken = refs[:count]
    del refs[:count]
    return taken


def pad_heads(matrix):
    gap = jnp.zeros((SLOT - HEAD, D), f32)
    slots = []
    for h in range(HEADS):
        slots += [matrix[HEAD * h : HEAD * (h + 1)], gap]
    return jnp.concatenate(slots, axis=0)


def slim_heads(matrix):
    return jnp.concatenate([matrix[SLOT * h : SLOT * h + HEAD] for h in range(HEADS)], axis=0)


def head_rows(h):
    return slice(SLOT * h, SLOT * (h + 1))


def sample_window(step, rows_total, align):
    base = step * PAIRS
    start = jnp.minimum(base // align * align, rows_total - HALF)
    return ds(start, HALF, align), base - start


def load_sample(ref, step, fill_first):
    window, shift = sample_window(step, ref.shape[0], 16)
    rows = pltpu.roll(ref[window, :].astype(f32), lax.rem(HALF - shift, HALF), 0)
    pair_row = lax.broadcasted_iota(jnp.int32, (HALF, 2 * D), 0)
    cols = jnp.where(pair_row < PAIRS, rows, rows[0:1] if fill_first else 0.0).T
    return jnp.concatenate([cols[:D], cols[D:]], axis=1)


def store_sample(ref, step, value):
    window, shift = sample_window(step, ref.shape[0], 16 if ref.dtype == bf16 else 8)
    cols = jnp.concatenate([value[:, :HALF], value[:, HALF:]], axis=0)
    rows = pltpu.roll(cols.T, shift, 0)
    pair_row = lax.broadcasted_iota(jnp.int32, (HALF, 2 * D), 0)
    here = jnp.logical_and(pair_row >= shift, pair_row < shift + PAIRS)
    ref[window, :] = jnp.where(here, rows, ref[window, :].astype(f32)).astype(ref.dtype)


def attention_forward(normed_b, wqkv_t, wo_t, state, kh_ref, v_ref):
    e_ref, vh_ref, q_ref, k_ref, ctx_ref, rinv_ref = state
    lane = lax.broadcasted_iota(jnp.int32, (WIDE, LANES), 1)
    slot_row = lax.broadcasted_iota(jnp.int32, (WIDE, LANES), 0) & (SLOT - 1)
    real = (lane & (HALF - 1)) < PAIRS
    ones_rows = jnp.logical_or(slot_row == HEAD, slot_row == HEAD + 1).astype(f32)
    qkv = mm(wqkv_t, normed_b)
    q_ref[0] = (qkv[:WIDE] * (SCALE * LOG2E)).astype(bf16)
    keys = qkv[WIDE : 2 * WIDE].astype(bf16)
    k_ref[0] = keys
    values = jnp.where(real, qkv[2 * WIDE :] + ones_rows, 0.0).astype(bf16)
    v_ref[...] = values
    for tall, ref in ((keys.T, kh_ref), (values.T, vh_ref)):
        for h in range(HEADS):
            ref[0, h, 0:KEYS] = tall[0:KEYS, head_rows(h)]
            ref[0, h, KEYS:] = tall[HALF : HALF + KEYS, head_rows(h)]

    def scores_of(h):
        return mm(kh_ref[0, h], q_ref[0, head_rows(h), :])

    scores = scores_of(0)
    for h in range(HEADS):
        rows = head_rows(h)
        ahead = scores_of(h + 1) if h + 1 < HEADS else None
        top = jnp.max(scores, axis=0, keepdims=True)
        weights = jnp.exp2(scores - top).astype(bf16)
        e_ref[0, :, LANES * h : LANES * (h + 1)] = weights
        out = mm(v_ref[rows, 0:KEYS], weights[0:KEYS]) + mm(
            v_ref[rows, HALF : HALF + KEYS], weights[KEYS:]
        )
        inverse = 1.0 / out[HEAD : HEAD + 1]
        rinv_ref[0, h : h + 1, :] = inverse
        ctx_ref[0, rows, :] = out * inverse
        scores = ahead
    return mm(wo_t, ctx_ref[0].astype(bf16))


def attention_backward(grad_b, normed_b, wo, wqkv, state, work, sums):
    e_ref, vh_ref, q_ref, k_ref, ctx_ref, rinv_ref = state
    ds_ref, do_ref, do_all, q_all, dq_ref, dkv_ref = work
    d_wq, d_wkv, d_wo = sums
    head_row = lax.broadcasted_iota(jnp.int32, (SLOT, LANES), 0)
    lane_head = lax.broadcasted_iota(jnp.int32, (LANES, WIDE), 1) // SLOT
    key_row = lax.broadcasted_iota(jnp.int32, (2 * KEYS, WIDE), 0)
    real_key = jnp.where(key_row < KEYS, key_row, key_row - KEYS) < PAIRS

    def spread_heads(ref, tall):
        for h in range(HEADS):
            ref[LANES * h : LANES * (h + 1), :] = jnp.where(lane_head == h, tall, jnp.zeros_like(tall))

    context = ctx_ref[0]
    d_wo[...] += mm_nt(context.astype(bf16), grad_b)
    d_context = mm(wo, grad_b)
    for h in range(HEADS):
        rows = head_rows(h)
        grad = (d_context[rows] * rinv_ref[0, h : h + 1, :]).astype(bf16).astype(f32)
        dot = -jnp.sum(grad[:HEAD] * context[rows][:HEAD], axis=0, keepdims=True)
        dot_high = dot.astype(bf16).astype(f32)
        grad = jnp.where(head_row == HEAD, dot_high, grad)
        grad = jnp.where(head_row == HEAD + 1, dot - dot_high, grad)
        do_ref[rows, :] = grad.astype(bf16)
    spread_heads(do_all, do_ref[...].T)
    spread_heads(q_all, q_ref[0].T)

    def grad_probs_of(h):
        return mm(vh_ref[0, h], do_ref[head_rows(h), :])

    grad_probs = grad_probs_of(0)
    for h in range(HEADS):
        rows = head_rows(h)
        ahead = grad_probs_of(h + 1) if h + 1 < HEADS else None
        d_scores = e_ref[0, :, LANES * h : LANES * (h + 1)] * grad_probs.astype(bf16)
        ds_ref[:, LANES * h : LANES * (h + 1)] = d_scores
        dq = mm(k_ref[0, rows, 0:KEYS], d_scores[0:KEYS]) + mm(
            k_ref[0, rows, HALF : HALF + KEYS], d_scores[KEYS:]
        )
        dq_ref[rows, :] = (dq * SCALE).astype(bf16)
        grad_probs = ahead
    dk = (mm(ds_ref[...], q_all[...]) * (1.0 / LOG2E)).astype(bf16)
    dv = jnp.where(real_key, mm(e_ref[0], do_all[...]), 0.0).astype(bf16)
    for half in range(2):
        here = slice(half * KEYS, (half + 1) * KEYS)
        there = slice(half * HALF, half * HALF + KEYS)
        dkv_ref[there, 0:WIDE] = dk[here]
        dkv_ref[there, WIDE:] = dv[here]
    d_wq[...] += mm_nt(dq_ref[...], normed_b)
    d_wkv[...] += mm(normed_b, dkv_ref[...])
    return mm(wqkv[:, 0:WIDE], dq_ref[...]) + mm_nt(wqkv[:, WIDE:], dkv_ref[...])


def finish_attention(d_attn, sums):
    d_wq, d_wkv, d_wo = sums
    tall = d_wkv[...].T
    for j, source in enumerate((d_wq[...], tall[:WIDE], tall[WIDE:], d_wo[...])):
        slim = slim_heads(source)
        d_attn[j * D : (j + 1) * D, :] = slim.T if j < 3 else slim


def pack_attention(out, j, low, d_attn, parts):
    each = ATTN_ROWS // parts
    for u in range(parts // GROUP // LAYERS):
        rows = d_attn[ds((u * GROUP + low) * each, each, each), :]
        out[j, u * each : (u + 1) * each, 0:D] = rows.astype(out.dtype)


STATE = [
    ((2 * KEYS, HEADS * LANES), bf16),
    ((HEADS, 2 * KEYS, SLOT), bf16),
    ((WIDE, LANES), bf16),
    ((WIDE, LANES), bf16),
    ((WIDE, LANES), f32),
    ((HEADS, LANES), f32),
]
WORK = [
    ((2 * KEYS, HEADS * LANES), bf16),
    ((WIDE, LANES), bf16),
    ((HEADS * LANES, WIDE), bf16),
    ((HEADS * LANES, WIDE), bf16),
    ((WIDE, LANES), bf16),
    ((LANES, 2 * WIDE), bf16),
]
SUMS = [((WIDE, D), f32), ((D, 2 * WIDE), f32), ((WIDE, D), f32)]


def main_kernel(parts, *refs):
    refs = list(refs)
    me_ref, x_ref, g_ref, norm_ref, win_own, win_other, wout_own, wout_other = take(refs, 8)
    attn_refs = take(refs, 2 if parts else 1)
    (res_ref,) = take(refs, 1)
    state_low = take(refs, len(STATE))
    normed_out, grad_out, wqkv_out, wo_out = take(refs, 4)
    out_refs = take(refs, 2 if parts else 4)
    wqkv_t, wqkv, wo_t, wo, win_t, win, wout_t, wout, norm_t, attn_ref = take(refs, 10)
    state_high = take(refs, len(STATE))
    work = take(refs, len(WORK))
    sums = take(refs, len(SUMS))
    d_win, d_wout, d_norm, d_attn, kh_ref, v_ref, mixed_ref = refs
    dkv_ref = work[-1]
    step = pl.program_id(0)

    @pl.when(step == 0)
    def _():
        for ref in (*sums, d_win, d_wout, d_norm, dkv_ref):
            ref[...] = jnp.zeros_like(ref)
        if parts:
            me = me_ref[0]
            each = ATTN_ROWS // parts
            for t, ref in enumerate(attn_refs):
                for j, k in enumerate(NEAR):
                    for u in range(parts // GROUP):
                        owner = ((me // GROUP) ^ u) * GROUP + ((me % GROUP) ^ k ^ (TWIN * t))
                        attn_ref[ds(owner * each, each, each), :] = ref[j, u]
        else:
            attn_ref[...] = attn_refs[0][...]
        norm_t[...] = jnp.concatenate([norm_ref[...], jnp.zeros((8 - 2 * NORMS, D), f32)], axis=0).T
        for layer in range(LAYERS):
            for j in range(4):
                base = (4 * layer + j) * D
                matrix = attn_ref[base : base + D, :].astype(f32)
                if j < 3:
                    tall = pad_heads(matrix.T)
                    wqkv_t[layer, j * WIDE : (j + 1) * WIDE, :] = tall.astype(bf16)
                    ref = wqkv if layer else wqkv_out
                    ref[:, j * WIDE : (j + 1) * WIDE] = tall.T.astype(bf16)
                else:
                    tall = pad_heads(matrix)
                    ref = wo if layer else wo_out
                    ref[...] = tall.astype(bf16)
                    wo_t[layer] = tall.T.astype(bf16)
            for p, (w1, w2) in enumerate(((win_own, wout_own), (win_other, wout_other))):
                win[layer, :, p * FF : (p + 1) * FF] = w1[layer]
                win_t[layer, p * FF : (p + 1) * FF, :] = w1[layer].astype(f32).T.astype(bf16)
                wout[layer, p * FFH : (p + 1) * FFH, :] = w2[layer]
                wout_t[layer, :, p * FFH : (p + 1) * FFH] = w2[layer].astype(f32).T.astype(bf16)

    def add_norm(index, grad, unit):
        d_norm[2 * index] += fold_lanes(grad * unit)
        d_norm[2 * index + 1] += fold_lanes(grad)

    def gain_of(index):
        return norm_t[:, 2 * index : 2 * index + 1]

    def shift_of(index):
        return norm_t[:, 2 * index + 1 : 2 * index + 2]

    kept = []
    stream = load_sample(x_ref, step, True)
    normed_b = stream.astype(bf16)
    normed_out[0] = normed_b
    unit_a = inv_a = None
    for layer, state in enumerate((state_low, state_high)):
        if layer > 0:
            normed, unit_a, inv_a = norm_forward(stream, gain_of(2 * layer - 1), shift_of(2 * layer - 1))
            normed_b = normed.astype(bf16)
        stream = stream + attention_forward(normed_b, wqkv_t[layer], wo_t[layer], state, kh_ref, v_ref)
        normed, unit_f, inv_f = norm_forward(stream, gain_of(2 * layer), shift_of(2 * layer))
        ffn_b = normed.astype(bf16)
        mixed = mm(win_t[layer], ffn_b)
        mixed_ref[layer] = mixed
        hidden = []
        for p in range(2):
            value = mixed[FF * p : FF * p + FFH]
            gate = mixed[FF * p + FFH : FF * (p + 1)]
            hidden.append((value * (gate * sigmoid(gate))).astype(bf16))
        hidden = jnp.concatenate(hidden, axis=0)
        stream = stream + mm(wout_t[layer], hidden)
        kept.append((normed_b, unit_a, inv_a, ffn_b, unit_f, inv_f, hidden))
    store_sample(res_ref, step, stream)

    grad = load_sample(g_ref, step, False)
    for layer in reversed(range(LAYERS)):
        normed_b, unit_a, inv_a, ffn_b, unit_f, inv_f, hidden = kept[layer]
        grad_b = grad.astype(bf16)
        d_wout[FF * layer : FF * (layer + 1), :] += mm_nt(hidden, grad_b)
        d_hidden = mm(wout[layer], grad_b)
        d_mixed = []
        for p in range(2):
            value = mixed_ref[layer, FF * p : FF * p + FFH]
            gate = mixed_ref[layer, FF * p + FFH : FF * (p + 1)]
            part = d_hidden[FFH * p : FFH * (p + 1)]
            sig = sigmoid(gate)
            d_mixed.append((part * (gate * sig)).astype(bf16))
            d_mixed.append((part * value * sig * (1.0 + gate * (1.0 - sig))).astype(bf16))
        d_mixed = jnp.concatenate(d_mixed, axis=0)
        d_win[D * layer : D * (layer + 1), :] += mm_nt(ffn_b, d_mixed)
        d_normed = mm(win[layer], d_mixed)
        add_norm(2 * layer, d_normed, unit_f)
        grad = grad + norm_backward(d_normed, unit_f, inv_f, gain_of(2 * layer))
        if layer > 0:
            d_att = attention_backward(grad.astype(bf16), normed_b, wo[...], wqkv[...], state_high, work, sums)
            add_norm(2 * layer - 1, d_att, unit_a)
            grad = grad + norm_backward(d_att, unit_a, inv_a, gain_of(2 * layer - 1))
    grad_out[0] = grad

    @pl.when(step == pl.num_programs(0) - 1)
    def _():
        finish_attention(d_attn, sums)
        folded = [jnp.sum(d_norm[j].T, axis=0, keepdims=True) for j in range(2 * NORMS)]
        folded = jnp.concatenate(folded + [jnp.zeros((8 - 2 * NORMS, D), f32)], axis=0)
        if not parts:
            out_refs[0][...] = d_attn[...]
            out_refs[1][...] = d_win[...]
            out_refs[2][...] = d_wout[...]
            out_refs[3][...] = folded
            return
        me = me_ref[0]
        high = folded.astype(bf16).astype(f32)
        folded = jnp.concatenate([high, folded - high], axis=0).astype(bf16)
        for t, out in enumerate(out_refs):
            for j, k in enumerate(NEAR):
                kind = out.dtype
                low = (me % GROUP) ^ k ^ (TWIN * t)
                quarter = low // 2
                half = k % 2
                pack_attention(out, j, low, d_attn, parts)
                first = (quarter // 2) * FF + half * FFH + (quarter % 2) * WOUT_PART
                out[j, OFF_WOUT:OFF_NORM, 0:D] = d_wout[ds(first, WOUT_PART, WOUT_PART), :].astype(kind)
                out[j, OFF_NORM:OFF_WIN, 0:D] = folded.astype(kind)
                rows = d_win[ds(quarter * WIN_PART, WIN_PART, WIN_PART), half * FF : (half + 1) * FF]
                out[j, OFF_WIN:PAY_ROWS, :] = rows.astype(kind)


def low_kernel(parts, first, last, *refs):
    refs = list(refs)
    (me_ref,) = take(refs, 1)
    state = take(refs, len(STATE))
    normed_ref, grad_ref, wqkv_ref, wo_ref = take(refs, 4)
    before = [] if first else take(refs, 1 + len(SUMS))[1:]
    (ig_ref,) = take(refs, 1)
    after = take(refs, (2 if parts else 1) if last else len(SUMS))
    work = take(refs, len(WORK))
    sums = take(refs, len(SUMS))
    (d_attn,) = refs
    step = pl.program_id(0)

    @pl.when(step == 0)
    def _():
        for i, ref in enumerate(sums):
            ref[...] = jnp.zeros_like(ref) if first else before[i][...]
        work[-1][...] = jnp.zeros_like(work[-1])

    grad = grad_ref[0]
    d_att = attention_backward(grad.astype(bf16), normed_ref[0], wo_ref[...], wqkv_ref[...], state, work, sums)
    store_sample(ig_ref, step, grad + d_att)

    @pl.when(step == pl.num_programs(0) - 1)
    def _():
        if not last:
            for ref, total in zip(after, sums, strict=True):
                ref[...] = total[...]
            return
        finish_attention(d_attn, sums)
        if not parts:
            after[0][...] = d_attn[...]
            return
        for t, out in enumerate(after):
            for j, k in enumerate(NEAR):
                pack_attention(out, j, (me_ref[0] % GROUP) ^ k ^ (TWIN * t), d_attn, parts)


VMEM = pl.BlockSpec(memory_space=pltpu.VMEM)
SMEM = pl.BlockSpec(memory_space=pltpu.SMEM)


def shapes_of(pairs):
    return [jax.ShapeDtypeStruct(*pair) for pair in pairs]


def vmem_of(pairs):
    return [pltpu.VMEM(*pair) for pair in pairs]


def per_sample(pairs, first=0):
    def spec(shape):
        return pl.BlockSpec((1, *shape), lambda i: (i + first,) + (0,) * len(shape))

    return [spec(shape) for shape, _ in pairs]


def kernel_params(samples, flops):
    return {
        "compiler_params": pltpu.CompilerParams(
            dimension_semantics=("arbitrary",), vmem_limit_bytes=60 * 1024 * 1024
        ),
        "cost_estimate": pl.CostEstimate(
            flops=samples * flops, bytes_accessed=samples * 8_000_000, transcendentals=0
        ),
    }


CARRIED = STATE + [((D, LANES), bf16), ((D, LANES), f32)]


def run_main(me, tokens, cotangent, norms, ffn, attn_parts, parts):
    rows = tokens.shape[0]
    samples = rows // PAIRS
    if parts:
        grad_shapes = [((len(NEAR), PAY_ROWS, 2 * FFH), kind) for kind in (f32, bf16)]
    else:
        grad_shapes = [
            ((4 * D, D), f32),
            ((LAYERS * D, 2 * FF), f32),
            ((LAYERS * FF, D), f32),
            ((8, D), f32),
        ]
    carried = [((samples, *shape), kind) for shape, kind in CARRIED]
    plain = [((D, 3 * WIDE), bf16), ((WIDE, D), bf16)]
    inputs = (tokens, cotangent, norms, *ffn, *attn_parts)
    scratch = [
        ((LAYERS, 3 * WIDE, D), bf16),
        ((D, 3 * WIDE), bf16),
        ((LAYERS, D, WIDE), bf16),
        ((WIDE, D), bf16),
        ((LAYERS, 2 * FF, D), bf16),
        ((LAYERS, D, 2 * FF), bf16),
        ((LAYERS, D, FF), bf16),
        ((LAYERS, FF, D), bf16),
        ((D, 8), f32),
        ((ATTN_ROWS, D), bf16),
        *[((1, *shape), kind) for shape, kind in STATE],
        *WORK,
        *SUMS,
        ((LAYERS * D, 2 * FF), f32),
        ((LAYERS * FF, D), f32),
        ((2 * NORMS, D, 128), f32),
        ((4 * D, D), f32),
        ((1, HEADS, 2 * KEYS, SLOT), bf16),
        ((WIDE, LANES), bf16),
        ((LAYERS, 2 * FF, LANES), f32),
    ]

    def body(*refs):
        main_kernel(parts, *refs)

    res, *rest = pl.pallas_call(
        body,
        grid=(samples,),
        in_specs=[SMEM] + [VMEM] * len(inputs),
        out_specs=[VMEM, *per_sample(CARRIED), *[VMEM] * (len(plain) + len(grad_shapes))],
        out_shape=shapes_of([((rows, 2 * D), bf16), *carried, *plain, *grad_shapes]),
        scratch_shapes=vmem_of(scratch),
        **kernel_params(samples, 4_000_000_000),
    )(me, *inputs)
    kept = len(CARRIED) + len(plain)
    return res, rest[:kept], rest[kept:]


def run_low(me, carried, before, rows, parts, call, calls):
    samples = rows // PAIRS // calls
    last = call == calls - 1
    grad_shapes = [((len(NEAR), ATTN_PART, D), kind) for kind in (f32, bf16)] if parts else [((4 * D, D), f32)]
    if not last:
        grad_shapes = SUMS
    before_specs = [pl.BlockSpec(memory_space=pl.ANY)] + [VMEM] * len(SUMS) if before else []

    def body(*refs):
        low_kernel(parts, not before, last, *refs)

    ig, *rest = pl.pallas_call(
        body,
        grid=(samples,),
        in_specs=[SMEM, *per_sample(CARRIED, call * samples), VMEM, VMEM, *before_specs],
        out_specs=[pl.BlockSpec((rows // calls, 2 * D), lambda i: (call, 0)), *[VMEM] * len(grad_shapes)],
        out_shape=shapes_of([((rows, 2 * D), f32), *grad_shapes]),
        scratch_shapes=vmem_of([*WORK, *SUMS, ((4 * D, D), f32)]),
        input_output_aliases={1 + len(carried): 0} if before else {},
        **kernel_params(samples, 1_400_000_000),
    )(me, *carried, *before)
    return ig, rest


def small_kernel(body, out_shape, *inputs, scratch=()):
    return pl.pallas_call(
        body,
        in_specs=[SMEM] + [VMEM] * (len(inputs) - 1),
        out_specs=[VMEM] * len(out_shape),
        out_shape=shapes_of(out_shape),
        scratch_shapes=vmem_of(scratch),
        compiler_params=pltpu.CompilerParams(vmem_limit_bytes=32 * 1024 * 1024),
    )(*inputs)


def resplit(sums):
    high = sums.astype(bf16).astype(f32)
    return jnp.concatenate([high, sums - high], axis=0).astype(bf16)


class Exchange:
    def __init__(self, me, parts):
        self.me = me
        self.parts = parts
        self.upper = parts // GROUP
        self.each = ATTN_ROWS // parts
        self.win_rows = WIN_PART // self.upper
        self.wout_rows = WOUT_PART // self.upper
        self.at_norm = self.each + self.wout_rows
        self.at_win = self.at_norm + 16
        self.rows = self.at_win + self.win_rows

    def swap(self, value, k):
        return lax.ppermute(value, AXES, [(i, i ^ k) for i in range(self.parts)])

    def twins(self, mine, theirs):
        rows, width = mine.shape[1:]
        mixed = rows == PAY_ROWS

        def body(me_ref, mine, theirs, *outs):
            for j, out in enumerate(outs):
                total = mine[j] + theirs[j].astype(f32)
                if mixed:
                    out[0:OFF_NORM] = total[0:OFF_NORM].astype(out.dtype)
                    sums = total[OFF_NORM : OFF_NORM + 8] + total[OFF_NORM + 8 : OFF_WIN]
                    out[OFF_NORM:OFF_WIN] = resplit(sums).astype(out.dtype)
                    out[OFF_WIN:] = total[OFF_WIN:].astype(out.dtype)
                else:
                    out[...] = total.astype(out.dtype)

        return small_kernel(
            body,
            [((rows, width), f32)] + [((rows, width), bf16)] * (len(NEAR) - 1),
            self.me,
            mine,
            theirs,
        )

    def across_plane(self, parts):
        return [parts[0]] + [self.swap(part, k) for part, k in zip(parts[1:], NEAR[1:], strict=True)]

    def across_rest(self, parts):
        return [parts[0]] + [self.swap(parts[u], u * GROUP) for u in range(1, self.upper)]

    def plane_low(self, landed):
        each, upper = self.each, self.upper

        def body(me_ref, *refs):
            ins, outs, total = refs[: len(NEAR)], refs[len(NEAR) : -1], refs[-1]
            total[...] = tree_sum([r[...].astype(f32) for r in ins])
            for u, out in enumerate(outs):
                there = jnp.minimum((me_ref[0] // GROUP) ^ u, upper // LAYERS - 1)
                out[...] = total[ds(there * each, each, 8), :].astype(out.dtype)

        shapes = [((each, D), f32 if u == 0 else bf16) for u in range(upper)]
        return small_kernel(body, shapes, self.me, *landed, scratch=[((ATTN_PART, D), f32)])

    def plane_main(self, landed):
        each, upper, wout_rows, win_rows = self.each, self.upper, self.wout_rows, self.win_rows
        at_norm, at_win, rows = self.at_norm, self.at_win, self.rows

        def body(me_ref, *refs):
            ins, outs, total = refs[: len(NEAR)], refs[len(NEAR) : -1], refs[-1]
            total[...] = tree_sum([r[...].astype(f32) for r in ins])
            norm = resplit(total[OFF_NORM : OFF_NORM + 8, :] + total[OFF_NORM + 8 : OFF_WIN, :])
            for u, out in enumerate(outs):
                there = (me_ref[0] // GROUP) ^ u
                attn = jnp.maximum(there - upper // LAYERS, 0)
                out[0:each, :] = total[ds(attn * each, each, 8), :].astype(out.dtype)
                wout = total[ds(OFF_WOUT + there * wout_rows, wout_rows, 8), :]
                out[each:at_norm, :] = wout.astype(out.dtype)
                out[at_norm:at_win, :] = norm.astype(out.dtype)
                win = total[ds(OFF_WIN + there * win_rows, win_rows, 8), :]
                out[at_win:rows, :] = win.astype(out.dtype)

        shapes = [((rows, 2 * FFH), f32 if u == 0 else bf16) for u in range(upper)]
        return small_kernel(body, shapes, self.me, *landed, scratch=[((PAY_ROWS, 2 * FFH), f32)])

    def rest_main(self, landed):
        each, upper, wout_rows, win_rows = self.each, self.upper, self.wout_rows, self.win_rows
        at_norm, at_win = self.at_norm, self.at_win
        ffn_rows = wout_rows + win_rows

        def body(me_ref, *refs):
            ins, (attn, norm, ffn) = refs[:upper], refs[upper:]
            total = tree_sum([r[...].astype(f32) for r in ins])
            attn[...] = total[0:each, 0:D]
            norm[...] = total[at_norm : at_norm + 8, 0:D] + total[at_norm + 8 : at_win, 0:D]
            ffn[0:wout_rows, :] = total[each:at_norm, :].astype(bf16)
            ffn[wout_rows:, :] = total[at_win:, :].astype(bf16)

        shapes = [((each, D), f32), ((8, D), f32), ((ffn_rows, 2 * FFH), bf16)]
        return small_kernel(body, shapes, self.me, *landed)

    def rest_low(self, landed, high):
        upper = self.upper

        def body(me_ref, *refs):
            ins, high, out = refs[:upper], refs[upper], refs[upper + 1]
            total = tree_sum([r[...].astype(f32) for r in ins])
            out[...] = jnp.where(me_ref[0] // GROUP < upper // LAYERS, total, high[...])

        return small_kernel(body, [((self.each, D), f32)], self.me, *landed, high)[0]

    def spread(self, ffn):
        upper, wout_rows, win_rows = self.upper, self.wout_rows, self.win_rows
        column = jnp.stack([ffn] + [self.swap(ffn, u * GROUP) for u in range(1, upper)])
        block = [column] + [self.swap(column, 2 * q) for q in range(1, 4)]

        def body(me_ref, *refs):
            ins, (win, wout) = refs[:4], refs[4:]
            mine = me_ref[0] // GROUP
            quarter = (me_ref[0] % GROUP) // 2
            for q in range(4):
                for u in range(upper):
                    piece = (quarter ^ q) * upper + (mine ^ u)
                    part = ins[q][u].astype(f32)
                    wout[ds(piece * wout_rows, wout_rows, 8), :] = part[:wout_rows, 0:D]
                    win[ds(piece * win_rows, win_rows, 8), :] = part[wout_rows:, :]

        shapes = [((LAYERS * D, 2 * FFH), f32), ((LAYERS * FFH, D), f32)]
        return small_kernel(body, shapes, self.me, *block)


CALLS = 2


def on_device(devices, tokens, attn_weights, norm_params, w_in, w_out, cotangent):
    each = attn_weights.shape[0]
    rows = tokens.shape[0]
    me = (lax.axis_index("dp") * 2 + lax.axis_index("narrow")).astype(jnp.int32).reshape(1)
    staged = devices % (GROUP * LAYERS) == 0 and each % 16 == 0
    swap_halves = [(0, 1), (1, 0)]
    w_in = w_in.reshape(LAYERS, D, 2 * FFH)
    w_in_other = lax.ppermute(w_in, "narrow", swap_halves)
    w_out_other = lax.ppermute(w_out, "narrow", swap_halves)
    norms = norm_params.reshape(2 * NORMS, D)
    if not staged:
        attn_all = lax.all_gather(attn_weights, AXES, axis=0, tiled=True)
        ffn = (w_in, w_in_other, w_out, w_out_other)
        res, carried, (d_high, d_win, d_wout, sums) = run_main(
            me, tokens, cotangent, norms, ffn, (attn_all,), 0
        )
        before = []
        for call in range(CALLS):
            ig, rest = run_low(me, carried, before, rows, 0, call, CALLS)
            before = [ig, *rest]
        d_attn = jnp.concatenate([rest[0], d_high], axis=0)
        attn = lax.psum_scatter(d_attn, AXES, scatter_dimension=0, tiled=True)
        norm = lax.psum(sums, AXES)
        d_wout = d_wout.reshape(LAYERS, FF, D)
        own_in, other_in = d_win[:, :FF], d_win[:, FF:]
        own_out, other_out = d_wout[:, :FFH], d_wout[:, FFH:]
        win = lax.psum(own_in + lax.ppermute(other_in, "narrow", swap_halves), "dp")
        wout = lax.psum(own_out + lax.ppermute(other_out, "narrow", swap_halves), "dp")
    else:
        ex = Exchange(me, devices)
        column = jnp.stack(ex.across_rest([attn_weights] * ex.upper))
        column, w_in_other, w_out_other = lax.optimization_barrier((column, w_in_other, w_out_other))
        ffn = (w_in, w_in_other, w_out, w_out_other)
        plane = jnp.stack(ex.across_plane([column] * len(NEAR)))
        attn_parts = [plane, ex.swap(plane, TWIN)]
        res, carried, (keep, send) = run_main(me, tokens, cotangent, norms, ffn, attn_parts, devices)
        send = ex.swap(send, TWIN)
        ig, rest = run_low(me, carried, [], rows, devices, 0, CALLS)
        pieces = ex.twins(keep, send)
        before = [ig, *rest]
        before, pieces = lax.optimization_barrier((before, pieces))
        landed = ex.across_plane(pieces)
        ig, (keep_low, send_low) = run_low(me, carried, before, rows, devices, 1, CALLS)
        pieces_low = ex.twins(keep_low, ex.swap(send_low, TWIN))
        landed = ex.across_rest(ex.plane_main(landed))
        landed_low = ex.across_rest(ex.plane_low(ex.across_plane(pieces_low)))
        high, norm, ffn_sums = ex.rest_main(landed)
        win, wout = ex.spread(ffn_sums)
        attn = ex.rest_low(landed_low, high)
    return (
        res,
        ig,
        attn,
        norm[: 2 * NORMS].reshape(norm_params.shape),
        win.reshape(LAYERS, D, 2, FFH),
        wout.reshape(LAYERS, FFH, D),
    )


def solution(mesh):
    rows = P(("dp", "narrow"), None)
    hidden_in = P(None, None, None, "narrow")
    hidden_out = P(None, "narrow", None)
    devices = mesh.shape["dp"] * mesh.shape["narrow"]

    def per_device(*args):
        return on_device(devices, *args)

    return jax.shard_map(
        per_device,
        mesh=mesh,
        in_specs=(rows, rows, P(), hidden_in, hidden_out, rows),
        out_specs=(rows, rows, rows, P(), hidden_in, hidden_out),
        check_vma=False,
    )
```

```python
import math

import jax
import jax.numpy as jnp
from jax import lax
from jax.experimental import pallas as pl
from jax.experimental.pallas import tpu as pltpu
from jax.sharding import PartitionSpec as P

HEADS = 8
HEAD = 24
SLOT = 32
WIDE = HEADS * SLOT
D = HEADS * HEAD
FF = 256
FFH = FF // 2
LAYERS = 2
NORMS = 2 * LAYERS - 1
SEQ = 476
PAIRS = SEQ // 2
KEYS = 240
HALF = 256
LANES = 2 * HALF
EPS = 1e-05
SCALE = HEAD ** (-0.5)
LOG2E = math.log2(math.e)
ATTN_ROWS = LAYERS * 4 * D

GROUP = 8
NEAR = (0, 1, 4, 5)
TWIN = 2
WIN_PART = LAYERS * D // 4
WOUT_PART = LAYERS * FFH // 4
ATTN_PART = ATTN_ROWS // GROUP
OFF_WOUT = ATTN_PART
OFF_NORM = OFF_WOUT + WOUT_PART
OFF_WIN = OFF_NORM + 16
PAY_ROWS = OFF_WIN + WIN_PART

bf16 = jnp.bfloat16
f32 = jnp.float32
AXES = ("dp", "narrow")

TOGETHER = 2
LAG = 40
VMEM_BYTES = 60 * 1024 * 1024


def mm(left, right):
    return jnp.dot(left, right, preferred_element_type=f32)


def mm_nt(left, right):
    return lax.dot_general(left, right, (((1,), (1,)), ((), ())), preferred_element_type=f32)


def sigmoid(value):
    return 0.5 + 0.5 * jnp.tanh(0.5 * value)


def fold_lanes(value):
    return value[:, 0:128] + value[:, 128:256] + value[:, 256:384] + value[:, 384:512]


def norm_forward(stream, gain, shift):
    center = stream - jnp.sum(stream, axis=0, keepdims=True) * (1.0 / D)
    inverse = lax.rsqrt(jnp.sum(center * center, axis=0, keepdims=True) * (1.0 / D) + EPS)
    unit = center * inverse
    return (unit * gain + shift, unit, inverse)


def norm_backward(grad, unit, inverse, gain):
    scaled = grad * gain
    mean = jnp.sum(scaled, axis=0, keepdims=True) * (1.0 / D)
    slope = jnp.sum(scaled * unit, axis=0, keepdims=True) * (1.0 / D)
    return inverse * (scaled - mean - unit * slope)


def tree_sum(parts):
    while len(parts) > 1:
        parts = [parts[i] + parts[i + 1] for i in range(0, len(parts), 2)]
    return parts[0]


def ds(start, size, step):
    return pl.ds(pl.multiple_of(start, step), size)


def take(refs, count):
    taken = refs[:count]
    del refs[:count]
    return taken


def pad_heads(matrix):
    gap = jnp.zeros((SLOT - HEAD, D), f32)
    slots = []
    for h in range(HEADS):
        slots += [matrix[HEAD * h : HEAD * (h + 1)], gap]
    return jnp.concatenate(slots, axis=0)


def slim_heads(matrix):
    return jnp.concatenate([matrix[SLOT * h : SLOT * h + HEAD] for h in range(HEADS)], axis=0)


def head_rows(h):
    return slice(SLOT * h, SLOT * (h + 1))


def sample_window(step, rows_total, align):
    base = step * PAIRS
    start = jnp.minimum(base // align * align, rows_total - HALF)
    return ds(start, HALF, align), base - start


def load_sample(ref, step, fill_first):
    window, shift = sample_window(step, ref.shape[0], 16)
    rows = pltpu.roll(ref[window, :].astype(f32), lax.rem(HALF - shift, HALF), 0)
    pair_row = lax.broadcasted_iota(jnp.int32, (HALF, 2 * D), 0)
    cols = jnp.where(pair_row < PAIRS, rows, rows[0:1] if fill_first else 0.0).T
    return jnp.concatenate([cols[:D], cols[D:]], axis=1)


def store_sample(ref, step, value):
    window, shift = sample_window(step, ref.shape[0], 16 if ref.dtype == bf16 else 8)
    cols = jnp.concatenate([value[:, :HALF], value[:, HALF:]], axis=0)
    rows = pltpu.roll(cols.T, shift, 0)
    pair_row = lax.broadcasted_iota(jnp.int32, (HALF, 2 * D), 0)
    here = jnp.logical_and(pair_row >= shift, pair_row < shift + PAIRS)
    ref[window, :] = jnp.where(here, rows, ref[window, :].astype(f32)).astype(ref.dtype)


def attention_forward(normed_b, wqkv_t, wo_t, state, kt_ref, v_ref):
    e_ref, vt_ref, q_ref, k_ref, ctx_ref, rinv_ref = state
    lane = lax.broadcasted_iota(jnp.int32, (WIDE, LANES), 1)
    slot_row = lax.broadcasted_iota(jnp.int32, (WIDE, LANES), 0) & (SLOT - 1)
    real = (lane & (HALF - 1)) < PAIRS
    ones_rows = jnp.logical_or(slot_row == HEAD, slot_row == HEAD + 1).astype(f32)
    keys = mm(wqkv_t[WIDE : 2 * WIDE], normed_b).astype(bf16)
    k_ref[...] = keys
    q_ref[...] = (mm(wqkv_t[:WIDE], normed_b) * (SCALE * LOG2E)).astype(bf16)
    yield None
    values = jnp.where(real, mm(wqkv_t[2 * WIDE :], normed_b) + ones_rows, 0.0).astype(bf16)
    v_ref[...] = values
    for cols, ref in ((keys, kt_ref), (values, vt_ref)):
        tall = cols.T
        ref[0:KEYS] = tall[0:KEYS]
        ref[KEYS:] = tall[HALF : HALF + KEYS]

    def scores_of(h):
        return mm(kt_ref[:, head_rows(h)], q_ref[head_rows(h), :])

    scores = scores_of(0)
    yield None
    for h in range(HEADS):
        rows = head_rows(h)
        ahead = scores_of(h + 1) if h + 1 < HEADS else None
        top = jnp.max(scores, axis=0, keepdims=True)
        weights = jnp.exp2(scores - top).astype(bf16)
        e_ref[:, LANES * h : LANES * (h + 1)] = weights
        out = mm(v_ref[rows, 0:KEYS], weights[0:KEYS]) + mm(
            v_ref[rows, HALF : HALF + KEYS], weights[KEYS:]
        )
        inverse = 1.0 / out[HEAD : HEAD + 1]
        rinv_ref[h : h + 1, :] = inverse
        ctx_ref[rows, :] = out * inverse
        scores = ahead
        yield None
    yield mm(wo_t, ctx_ref[...].astype(bf16))


def attention_backward(grad_b, normed_b, wo, wqkv, state, work, sums):
    e_ref, vt_ref, q_ref, k_ref, ctx_ref, rinv_ref = state
    do_ref, block_ref, dq_ref, dkv_ref = work
    d_wq, d_wkv, d_wo = sums
    head_row = lax.broadcasted_iota(jnp.int32, (SLOT, LANES), 0)
    lane_head = lax.broadcasted_iota(jnp.int32, (LANES, WIDE), 1) // SLOT
    key_row = lax.broadcasted_iota(jnp.int32, (2 * KEYS, WIDE), 0)
    real_key = jnp.where(key_row < KEYS, key_row, key_row - KEYS) < PAIRS

    def spread_heads(tall):
        for h in range(HEADS):
            part = jnp.where(lane_head == h, tall, jnp.zeros_like(tall))
            block_ref[LANES * h : LANES * (h + 1), :] = part

    def keep(value, lanes):
        for half in range(2):
            here = slice(half * KEYS, (half + 1) * KEYS)
            dkv_ref[half * HALF : half * HALF + KEYS, lanes] = value[here]

    d_context = mm(wo, grad_b)
    for h in range(HEADS):
        rows = head_rows(h)
        grad = (d_context[rows] * rinv_ref[h : h + 1, :]).astype(bf16).astype(f32)
        dot = -jnp.sum(grad[:HEAD] * ctx_ref[rows, :][:HEAD], axis=0, keepdims=True)
        dot_high = dot.astype(bf16).astype(f32)
        grad = jnp.where(head_row == HEAD, dot_high, grad)
        grad = jnp.where(head_row == HEAD + 1, dot - dot_high, grad)
        do_ref[rows, :] = grad.astype(bf16)
    yield None
    d_wo[...] += mm_nt(ctx_ref[...].astype(bf16), grad_b)
    spread_heads(do_ref[...].T)
    yield None
    dv = mm(e_ref[...], block_ref[...])
    keep(jnp.where(real_key, dv, 0.0).astype(bf16), slice(WIDE, 2 * WIDE))

    def grad_probs_of(h):
        return mm(vt_ref[:, head_rows(h)], do_ref[head_rows(h), :])

    grad_probs = grad_probs_of(0)
    yield None
    for h in range(HEADS):
        rows = head_rows(h)
        ahead = grad_probs_of(h + 1) if h + 1 < HEADS else None
        d_scores = e_ref[:, LANES * h : LANES * (h + 1)] * grad_probs.astype(bf16)
        e_ref[:, LANES * h : LANES * (h + 1)] = d_scores
        dq = mm(k_ref[rows, 0:KEYS], d_scores[0:KEYS]) + mm(
            k_ref[rows, HALF : HALF + KEYS], d_scores[KEYS:]
        )
        dq_ref[rows, :] = (dq * SCALE).astype(bf16)
        grad_probs = ahead
        yield None
    spread_heads(q_ref[...].T)
    yield None
    dk = mm(e_ref[...], block_ref[...])
    keep((dk * (1.0 / LOG2E)).astype(bf16), slice(0, WIDE))
    d_wq[...] += mm_nt(dq_ref[...], normed_b)
    yield None
    d_wkv[...] += mm(normed_b, dkv_ref[...])
    yield mm(wqkv[:, 0:WIDE], dq_ref[...]) + mm_nt(wqkv[:, WIDE:], dkv_ref[...])


STATE = [
    ((2 * KEYS, HEADS * LANES), bf16),
    ((2 * KEYS, WIDE), bf16),
    ((WIDE, LANES), bf16),
    ((WIDE, LANES), bf16),
    ((WIDE, LANES), f32),
    ((HEADS, LANES), f32),
]
WORK = [
    ((WIDE, LANES), bf16),
    ((HEADS * LANES, WIDE), bf16),
    ((WIDE, LANES), bf16),
    ((LANES, 2 * WIDE), bf16),
]
BUNDLE = [
    *STATE,
    *STATE,
    *WORK,
    ((2 * KEYS, WIDE), bf16),
    ((WIDE, LANES), bf16),
    ((LAYERS, 2 * FF, LANES), bf16),
]
SUMS = [((WIDE, D), f32), ((D, 2 * WIDE), f32), ((WIDE, D), f32)]
GRADS = [
    *SUMS,
    *SUMS,
    ((LAYERS * D, 2 * FF), f32),
    ((LAYERS * FF, D), f32),
    ((2 * NORMS, D, 128), f32),
]


def main_kernel(attn_diffs, *refs):
    refs = list(refs)
    me_ref, x_ref, g_ref, norm_ref, win_own, win_other, wout_own, wout_other = take(refs, 8)
    attn_refs = take(refs, len(attn_diffs) if attn_diffs else 1)
    res_ref, ig_ref = take(refs, 2)
    sums = (take(refs, 3), take(refs, 3))
    d_win, d_wout, d_norm = take(refs, 3)
    wqkv_t, wqkv, wo_t, wo, win_t, win, wout_t, wout, norm_t, attn_ref = take(refs, 10)
    step = pl.program_id(0)
    bundles = [take(refs, len(BUNDLE)) for _ in range(TOGETHER)]

    @pl.when(step == 0)
    def _():
        for ref in (*sums[0], *sums[1], d_win, d_wout, d_norm):
            ref[...] = jnp.zeros_like(ref)
        for bundle in bundles:
            dkv_ref = bundle[2 * len(STATE) + len(WORK) - 1]
            dkv_ref[...] = jnp.zeros_like(dkv_ref)
        if attn_diffs:
            me = me_ref[0]
            for ref, diffs in zip(attn_refs, attn_diffs, strict=True):
                each = ref.shape[1]
                for i, diff in enumerate(diffs):
                    attn_ref[ds((me ^ diff) * each, each, each), :] = ref[i]
        else:
            attn_ref[...] = attn_refs[0][...]
        norm_t[...] = jnp.concatenate([norm_ref[...], jnp.zeros((8 - 2 * NORMS, D), f32)], axis=0).T
        for layer in range(LAYERS):
            for j in range(4):
                base = (4 * layer + j) * D
                matrix = attn_ref[base : base + D, :].astype(f32)
                if j < 3:
                    tall = pad_heads(matrix.T)
                    wqkv_t[layer, j * WIDE : (j + 1) * WIDE, :] = tall.astype(bf16)
                    wqkv[layer, :, j * WIDE : (j + 1) * WIDE] = tall.T.astype(bf16)
                else:
                    tall = pad_heads(matrix)
                    wo[layer] = tall.astype(bf16)
                    wo_t[layer] = tall.T.astype(bf16)
            for p, (w1, w2) in enumerate(((win_own, wout_own), (win_other, wout_other))):
                win[layer, :, p * FF : (p + 1) * FF] = w1[layer]
                win_t[layer, p * FF : (p + 1) * FF, :] = w1[layer].astype(f32).T.astype(bf16)
                wout[layer, p * FFH : (p + 1) * FFH, :] = w2[layer]
                wout_t[layer, :, p * FFH : (p + 1) * FFH] = w2[layer].astype(f32).T.astype(bf16)

    def add_norm(index, grad, unit):
        d_norm[2 * index] += fold_lanes(grad * unit)
        d_norm[2 * index + 1] += fold_lanes(grad)

    def gain_of(index):
        return norm_t[:, 2 * index : 2 * index + 1]

    def shift_of(index):
        return norm_t[:, 2 * index + 1 : 2 * index + 2]

    def one_sample(sample, bundle):
        bundle = list(bundle)
        states = (take(bundle, len(STATE)), take(bundle, len(STATE)))
        work = take(bundle, len(WORK))
        kt_ref, v_ref, mixed_ref = bundle
        kept = []
        stream = load_sample(x_ref, sample, True)
        normed_b = stream.astype(bf16)
        unit_a = inv_a = None
        yield
        for layer in range(LAYERS):
            if layer > 0:
                normed, unit_a, inv_a = norm_forward(stream, gain_of(2 * layer - 1), shift_of(2 * layer - 1))
                normed_b = normed.astype(bf16)
            for branch in attention_forward(normed_b, wqkv_t[layer], wo_t[layer], states[layer], kt_ref, v_ref):
                yield
            stream = stream + branch
            normed, unit_f, inv_f = norm_forward(stream, gain_of(2 * layer), shift_of(2 * layer))
            ffn_b = normed.astype(bf16)
            yield
            hidden = []
            for p in range(2):
                mixed = mm(win_t[layer, FF * p : FF * (p + 1)], ffn_b)
                mixed_ref[layer, FF * p : FF * (p + 1)] = mixed.astype(bf16)
                gate = mixed[FFH:]
                hidden.append((mixed[:FFH] * (gate * sigmoid(gate))).astype(bf16))
                yield
            hidden = jnp.concatenate(hidden, axis=0)
            stream = stream + mm(wout_t[layer], hidden)
            kept.append((normed_b, unit_a, inv_a, ffn_b, unit_f, inv_f, hidden))
            yield
        store_sample(res_ref, sample, stream)
        yield
        grad = load_sample(g_ref, sample, False)
        yield
        for layer in reversed(range(LAYERS)):
            normed_b, unit_a, inv_a, ffn_b, unit_f, inv_f, hidden = kept[layer]
            grad_b = grad.astype(bf16)
            d_hidden = mm(wout[layer], grad_b)
            d_mixed = []
            for p in range(2):
                value = mixed_ref[layer, FF * p : FF * p + FFH].astype(f32)
                gate = mixed_ref[layer, FF * p + FFH : FF * (p + 1)].astype(f32)
                part = d_hidden[FFH * p : FFH * (p + 1)]
                sig = sigmoid(gate)
                d_mixed.append((part * (gate * sig)).astype(bf16))
                d_mixed.append((part * value * sig * (1.0 + gate * (1.0 - sig))).astype(bf16))
                yield
            d_mixed = jnp.concatenate(d_mixed, axis=0)
            d_normed = mm(win[layer], d_mixed)
            d_wout[FF * layer : FF * (layer + 1), :] += mm_nt(hidden, grad_b)
            yield
            d_win[D * layer : D * (layer + 1), :] += mm_nt(ffn_b, d_mixed)
            add_norm(2 * layer, d_normed, unit_f)
            grad = grad + norm_backward(d_normed, unit_f, inv_f, gain_of(2 * layer))
            yield
            for d_att in attention_backward(
                grad.astype(bf16), normed_b, wo[layer], wqkv[layer], states[layer], work, sums[layer]
            ):
                yield
            if layer > 0:
                add_norm(2 * layer - 1, d_att, unit_a)
                grad = grad + norm_backward(d_att, unit_a, inv_a, gain_of(2 * layer - 1))
            else:
                grad = grad + d_att
            yield
        store_sample(ig_ref, sample, grad)
        yield

    running = [one_sample(step * TOGETHER + i, bundles[i]) for i in range(TOGETHER)]
    turn = 0
    while running:
        for i, program in enumerate(list(running)):
            if turn >= LAG * i and next(program, running) is running:
                running.remove(program)
        turn += 1


VMEM = pl.BlockSpec(memory_space=pltpu.VMEM)
SMEM = pl.BlockSpec(memory_space=pltpu.SMEM)


def shapes_of(pairs):
    return [jax.ShapeDtypeStruct(*pair) for pair in pairs]


def vmem_of(pairs):
    return [pltpu.VMEM(*pair) for pair in pairs]


def run_main(me, tokens, cotangent, norms, ffn, attn_parts, attn_diffs):
    rows = tokens.shape[0]
    samples = rows // PAIRS
    inputs = (tokens, cotangent, norms, *ffn, *attn_parts)
    scratch = [
        ((LAYERS, 3 * WIDE, D), bf16),
        ((LAYERS, D, 3 * WIDE), bf16),
        ((LAYERS, D, WIDE), bf16),
        ((LAYERS, WIDE, D), bf16),
        ((LAYERS, 2 * FF, D), bf16),
        ((LAYERS, D, 2 * FF), bf16),
        ((LAYERS, D, FF), bf16),
        ((LAYERS, FF, D), bf16),
        ((D, 8), f32),
        ((ATTN_ROWS, D), bf16),
        *BUNDLE * TOGETHER,
    ]

    def body(*refs):
        main_kernel(attn_diffs, *refs)

    out_shape = [((rows, 2 * D), bf16), ((rows, 2 * D), f32), *GRADS]
    res, ig, *grads = pl.pallas_call(
        body,
        grid=(samples // TOGETHER,),
        in_specs=[SMEM] + [VMEM] * len(inputs),
        out_specs=[VMEM] * len(out_shape),
        out_shape=shapes_of(out_shape),
        scratch_shapes=vmem_of(scratch),
        compiler_params=pltpu.CompilerParams(
            dimension_semantics=("arbitrary",), vmem_limit_bytes=VMEM_BYTES
        ),
        cost_estimate=pl.CostEstimate(
            flops=samples * 5_000_000_000, bytes_accessed=20_000_000, transcendentals=0
        ),
    )(me, *inputs)
    return res, ig, grads


def small_kernel(body, out_shape, *inputs, scratch=()):
    return pl.pallas_call(
        body,
        in_specs=[SMEM] + [VMEM] * (len(inputs) - 1),
        out_specs=[VMEM] * len(out_shape),
        out_shape=shapes_of(out_shape),
        scratch_shapes=vmem_of(scratch),
        compiler_params=pltpu.CompilerParams(vmem_limit_bytes=32 * 1024 * 1024),
    )(*inputs)


def resplit(sums):
    high = sums.astype(bf16).astype(f32)
    return jnp.concatenate([high, sums - high], axis=0).astype(bf16)


def finish_attention(d_attn, grads):
    for layer in range(LAYERS):
        d_wq, d_wkv, d_wo = grads[3 * layer : 3 * layer + 3]
        tall = d_wkv[...].T
        for j, source in enumerate((d_wq[...], tall[:WIDE], tall[WIDE:], d_wo[...])):
            slim = slim_heads(source)
            base = (4 * layer + j) * D
            d_attn[base : base + D, :] = slim.T if j < 3 else slim


def finish_norms(d_norm):
    sums = [jnp.sum(d_norm[j].T, axis=0, keepdims=True) for j in range(2 * NORMS)]
    return jnp.concatenate(sums + [jnp.zeros((8 - 2 * NORMS, D), f32)], axis=0)


def plain_gradients(me, grads):
    def body(me_ref, *refs):
        ins, (attn, win, wout, norm) = refs[: len(GRADS)], refs[len(GRADS) :]
        finish_attention(attn, ins)
        win[...] = ins[6][...]
        wout[...] = ins[7][...]
        norm[...] = finish_norms(ins[8])

    shapes = [((ATTN_ROWS, D), f32), GRADS[6], GRADS[7], ((8, D), f32)]
    return small_kernel(body, shapes, me, *grads)


class Exchange:
    def __init__(self, me, parts):
        self.me = me
        self.parts = parts
        self.upper = parts // GROUP
        self.each = ATTN_ROWS // parts
        self.bits = [1 << i for i in range(self.upper.bit_length() - 1)]

    def swap(self, value, k):
        return lax.ppermute(value, AXES, [(i, i ^ k) for i in range(self.parts)])

    def both(self, mine, theirs):
        def body(me_ref, mine, theirs, out):
            out[0 : mine.shape[0]] = mine[...]
            out[mine.shape[0] :] = theirs[...]

        shape = (2 * mine.shape[0], *mine.shape[1:])
        return small_kernel(body, [(shape, mine.dtype)], self.me, mine, theirs)[0]

    def gather(self, rows):
        block, diffs = rows[None], [0]
        for bit in [GROUP * b for b in reversed(self.bits)] + [4, 1]:
            block = self.both(block, self.swap(block, bit))
            diffs = diffs + [d ^ bit for d in diffs]
        return [block, self.swap(block, TWIN)], [diffs, [d ^ TWIN for d in diffs]]

    def pack(self, grads):
        each, upper = self.each, self.upper

        def body(me_ref, *refs):
            ins, outs, d_attn = refs[: len(GRADS)], refs[len(GRADS) : -1], refs[-1]
            finish_attention(d_attn, ins)
            d_win, d_wout, d_norm = ins[6:]
            norm = resplit(finish_norms(d_norm))
            for t, out in enumerate(outs):
                for j, k in enumerate(NEAR):
                    kind = out.dtype
                    low = (me_ref[0] % GROUP) ^ k ^ (TWIN * t)
                    quarter = low // 2
                    half = k % 2
                    for u in range(upper):
                        rows = d_attn[ds((u * GROUP + low) * each, each, each), :]
                        out[j, u * each : (u + 1) * each, 0:D] = rows.astype(kind)
                    first = (quarter // 2) * FF + half * FFH + (quarter % 2) * WOUT_PART
                    out[j, OFF_WOUT:OFF_NORM, 0:D] = d_wout[ds(first, WOUT_PART, WOUT_PART), :].astype(kind)
                    out[j, OFF_NORM:OFF_WIN, 0:D] = norm.astype(kind)
                    rows = d_win[ds(quarter * WIN_PART, WIN_PART, WIN_PART), half * FF : (half + 1) * FF]
                    out[j, OFF_WIN:PAY_ROWS, :] = rows.astype(kind)

        shapes = [((len(NEAR), PAY_ROWS, 2 * FFH), kind) for kind in (f32, bf16)]
        return small_kernel(body, shapes, self.me, *grads, scratch=[((ATTN_ROWS, D), f32)])

    def twins(self, mine, theirs):
        def body(me_ref, mine, theirs, *outs):
            for j, out in enumerate(outs):
                total = mine[j] + theirs[j].astype(f32)
                out[0:OFF_NORM] = total[0:OFF_NORM].astype(out.dtype)
                sums = total[OFF_NORM : OFF_NORM + 8] + total[OFF_NORM + 8 : OFF_WIN]
                out[OFF_NORM:OFF_WIN] = resplit(sums).astype(out.dtype)
                out[OFF_WIN:] = total[OFF_WIN:].astype(out.dtype)

        shape = (PAY_ROWS, 2 * FFH)
        shapes = [(shape, f32)] + [(shape, bf16)] * (len(NEAR) - 1)
        return small_kernel(body, shapes, self.me, mine, theirs)

    def across_plane(self, pieces):
        return [pieces[0]] + [self.swap(piece, k) for piece, k in zip(pieces[1:], NEAR[1:], strict=True)]

    def emit(self, total, blocks, at, keep, send):
        half = len(blocks) // 2
        each = self.each
        for out, rows in ((keep, blocks[:half]), (send, blocks[half:])):
            for i, row in enumerate(rows):
                out[i * each : (i + 1) * each, :] = total[ds(row, each, 8), :].astype(out.dtype)
        first = half * each
        last = at + OFF_NORM - OFF_WOUT
        norm = resplit(total[last : last + 8, :] + total[last + 8 : last + 16, :])
        rest = [
            total[at:last, :].astype(bf16),
            norm,
            total[last + 16 : at + PAY_ROWS - OFF_WOUT, :].astype(bf16),
        ]
        for out in (keep, send):
            row = first
            for part in rest:
                out[row : row + part.shape[0], :] = part.astype(out.dtype)
                row += part.shape[0]

    def stage_shapes(self, blocks):
        shape = (blocks * self.each + PAY_ROWS - OFF_WOUT, 2 * FFH)
        return [(shape, f32), (shape, bf16)]

    def after_plane(self, landed):
        def body(me_ref, *refs):
            ins, (keep, send, total) = refs[: len(NEAR)], refs[len(NEAR) :]
            total[...] = tree_sum([r[...].astype(f32) for r in ins])
            mine = me_ref[0] // GROUP
            order = [r for r in range(self.upper) if not r & 1] + [r for r in range(self.upper) if r & 1]
            self.emit(total, [(mine ^ r) * self.each for r in order], OFF_WOUT, keep, send)

        scratch = [((PAY_ROWS, 2 * FFH), f32)]
        return small_kernel(body, self.stage_shapes(self.upper // 2), self.me, *landed, scratch=scratch)

    def after_bit(self, mine, theirs, blocks):
        def body(me_ref, mine, theirs, keep, send, total):
            total[...] = mine[...] + theirs[...].astype(f32)
            self.emit(total, [i * self.each for i in range(blocks)], blocks * self.each, keep, send)

        (shape, _), _ = self.stage_shapes(blocks)
        return small_kernel(
            body, self.stage_shapes(blocks // 2), self.me, mine, theirs, scratch=[(shape, f32)]
        )

    def after_rest(self, mine, theirs):
        each = self.each
        at_norm = each + WOUT_PART
        ffn_rows = WOUT_PART + WIN_PART

        def body(me_ref, mine, theirs, attn, norm, ffn):
            total = mine[...] + theirs[...].astype(f32)
            attn[...] = total[0:each, 0:D]
            norm[...] = total[at_norm : at_norm + 8, 0:D] + total[at_norm + 8 : at_norm + 16, 0:D]
            ffn[0, 0:WOUT_PART, :] = total[each:at_norm, :].astype(bf16)
            ffn[0, WOUT_PART:, :] = total[at_norm + 16 :, :].astype(bf16)

        shapes = [((each, D), f32), ((8, D), f32), ((1, ffn_rows, 2 * FFH), bf16)]
        return small_kernel(body, shapes, self.me, mine, theirs)

    def spread(self, ffn):
        block = self.both(ffn, self.swap(ffn, 4))
        theirs = self.swap(block, TWIN)

        def body(me_ref, mine, theirs, win, wout):
            for t, ref in enumerate((mine, theirs)):
                for i in range(2):
                    quarter = ((me_ref[0] % GROUP) ^ (4 * i) ^ (TWIN * t)) // 2
                    part = ref[i].astype(f32)
                    wout[ds(quarter * WOUT_PART, WOUT_PART, WOUT_PART), :] = part[:WOUT_PART, 0:D]
                    win[ds(quarter * WIN_PART, WIN_PART, WIN_PART), :] = part[WOUT_PART:, :]

        shapes = [((LAYERS * D, 2 * FFH), f32), ((LAYERS * FFH, D), f32)]
        return small_kernel(body, shapes, self.me, block, theirs)

    def sum_all(self, grads):
        keep, send = self.pack(grads)
        keep, send = self.after_plane(self.across_plane(self.twins(keep, self.swap(send, TWIN))))
        blocks = self.upper // 2
        for bit in self.bits[:-1]:
            keep, send = self.after_bit(keep, self.swap(send, GROUP * bit), blocks)
            blocks //= 2
        attn, norm, ffn = self.after_rest(keep, self.swap(send, GROUP * self.bits[-1]))
        return attn, norm, *self.spread(ffn)


def on_device(devices, tokens, attn_weights, norm_params, w_in, w_out, cotangent):
    each = attn_weights.shape[0]
    me = (lax.axis_index("dp") * 2 + lax.axis_index("narrow")).astype(jnp.int32).reshape(1)
    staged = devices % (2 * GROUP) == 0 and each % 16 == 0
    swap_halves = [(0, 1), (1, 0)]
    w_in = w_in.reshape(LAYERS, D, 2 * FFH)
    w_in_other = lax.ppermute(w_in, "narrow", swap_halves)
    w_out_other = lax.ppermute(w_out, "narrow", swap_halves)
    ffn = (w_in, w_in_other, w_out, w_out_other)
    norms = norm_params.reshape(2 * NORMS, D)
    if not staged:
        attn_all = lax.all_gather(attn_weights, AXES, axis=0, tiled=True)
        res, ig, grads = run_main(me, tokens, cotangent, norms, ffn, (attn_all,), None)
        d_attn, d_win, d_wout, sums = plain_gradients(me, grads)
        attn = lax.psum_scatter(d_attn, AXES, scatter_dimension=0, tiled=True)
        norm = lax.psum(sums, AXES)
        d_wout = d_wout.reshape(LAYERS, FF, D)
        own_in, other_in = d_win[:, :FF], d_win[:, FF:]
        own_out, other_out = d_wout[:, :FFH], d_wout[:, FFH:]
        win = lax.psum(own_in + lax.ppermute(other_in, "narrow", swap_halves), "dp")
        wout = lax.psum(own_out + lax.ppermute(other_out, "narrow", swap_halves), "dp")
    else:
        ex = Exchange(me, devices)
        attn_parts, attn_diffs = ex.gather(attn_weights)
        res, ig, grads = run_main(me, tokens, cotangent, norms, ffn, attn_parts, attn_diffs)
        attn, norm, win, wout = ex.sum_all(grads)
    return (
        res,
        ig,
        attn,
        norm[: 2 * NORMS].reshape(norm_params.shape),
        win.reshape(LAYERS, D, 2, FFH),
        wout.reshape(LAYERS, FFH, D),
    )


def solution(mesh):
    rows = P(("dp", "narrow"), None)
    hidden_in = P(None, None, None, "narrow")
    hidden_out = P(None, "narrow", None)
    devices = mesh.shape["dp"] * mesh.shape["narrow"]

    def per_device(*args):
        return on_device(devices, *args)

    return jax.shard_map(
        per_device,
        mesh=mesh,
        in_specs=(rows, rows, P(), hidden_in, hidden_out, rows),
        out_specs=(rows, rows, rows, P(), hidden_in, hidden_out),
        check_vma=False,
    )
```

```python
import math

import jax
import jax.numpy as jnp
from jax import lax
from jax.experimental import pallas as pl
from jax.experimental.pallas import tpu as pltpu
from jax.sharding import PartitionSpec as P

HEADS = 8
HEAD = 24
SLOT = 32
WIDE = HEADS * SLOT
D = HEADS * HEAD
FF = 256
FFH = FF // 2
LAYERS = 2
NORMS = 2 * LAYERS - 1
SEQ = 476
PAIRS = SEQ // 2
KEYS = 240
HALF = 256
LANES = 2 * HALF
EPS = 1e-05
SCALE = HEAD ** (-0.5)
LOG2E = math.log2(math.e)
ATTN_ROWS = LAYERS * 4 * D

GROUP = 8
NEAR = (0, 1, 4, 5)
TWIN = 2
WIN_PART = LAYERS * D // 4
WOUT_PART = LAYERS * FFH // 4
ATTN_PART = ATTN_ROWS // GROUP
OFF_WOUT = ATTN_PART
OFF_NORM = OFF_WOUT + WOUT_PART
OFF_WIN = OFF_NORM + 16
PAY_ROWS = OFF_WIN + WIN_PART

bf16 = jnp.bfloat16
f32 = jnp.float32
AXES = ("dp", "narrow")

TOGETHER = 1
LAG = 0
SAFE = 72.0
VMEM_BYTES = 60 * 1024 * 1024


def mm(left, right):
    return jnp.dot(left, right, preferred_element_type=f32)


def mm_nt(left, right):
    return lax.dot_general(left, right, (((1,), (1,)), ((), ())), preferred_element_type=f32)


def sigmoid(value):
    return 0.5 + 0.5 * jnp.tanh(0.5 * value)


def fold_lanes(value):
    return value[:, 0:128] + value[:, 128:256] + value[:, 256:384] + value[:, 384:512]


def norm_forward(stream, gain, shift):
    center = stream - jnp.sum(stream, axis=0, keepdims=True) * (1.0 / D)
    inverse = lax.rsqrt(jnp.sum(center * center, axis=0, keepdims=True) * (1.0 / D) + EPS)
    unit = center * inverse
    return (unit * gain + shift, unit, inverse)


def norm_backward(grad, unit, inverse, gain):
    scaled = grad * gain
    mean = jnp.sum(scaled, axis=0, keepdims=True) * (1.0 / D)
    slope = jnp.sum(scaled * unit, axis=0, keepdims=True) * (1.0 / D)
    return inverse * (scaled - mean - unit * slope)


def tree_sum(parts):
    while len(parts) > 1:
        parts = [parts[i] + parts[i + 1] for i in range(0, len(parts), 2)]
    return parts[0]


def ds(start, size, step):
    return pl.ds(pl.multiple_of(start, step), size)


def take(refs, count):
    taken = refs[:count]
    del refs[:count]
    return taken


def pad_heads(matrix):
    gap = jnp.zeros((SLOT - HEAD, D), f32)
    slots = []
    for h in range(HEADS):
        slots += [matrix[HEAD * h : HEAD * (h + 1)], gap]
    return jnp.concatenate(slots, axis=0)


def slim_heads(matrix):
    return jnp.concatenate([matrix[SLOT * h : SLOT * h + HEAD] for h in range(HEADS)], axis=0)


def head_rows(h):
    return slice(SLOT * h, SLOT * (h + 1))


def sample_window(step, rows_total, align):
    base = step * PAIRS
    start = jnp.minimum(base // align * align, rows_total - HALF)
    return ds(start, HALF, align), base - start


def load_sample(ref, step, fill_first):
    window, shift = sample_window(step, ref.shape[0], 16)
    rows = pltpu.roll(ref[window, :].astype(f32), lax.rem(HALF - shift, HALF), 0)
    pair_row = lax.broadcasted_iota(jnp.int32, (HALF, 2 * D), 0)
    cols = jnp.where(pair_row < PAIRS, rows, rows[0:1] if fill_first else 0.0).T
    return jnp.concatenate([cols[:D], cols[D:]], axis=1)


def store_sample(ref, step, value):
    window, shift = sample_window(step, ref.shape[0], 16 if ref.dtype == bf16 else 8)
    cols = jnp.concatenate([value[:, :HALF], value[:, HALF:]], axis=0)
    rows = pltpu.roll(cols.T, shift, 0)
    pair_row = lax.broadcasted_iota(jnp.int32, (HALF, 2 * D), 0)
    here = jnp.logical_and(pair_row >= shift, pair_row < shift + PAIRS)
    ref[window, :] = jnp.where(here, rows, ref[window, :].astype(f32)).astype(ref.dtype)


def attention_forward(normed_b, wqkv_t, wo_t, state, kt_ref, v_ref):
    e_ref, vt_ref, q_ref, k_ref, ctx_ref, rinv_ref = state
    lane = lax.broadcasted_iota(jnp.int32, (WIDE, LANES), 1)
    slot_row = lax.broadcasted_iota(jnp.int32, (WIDE, LANES), 0) & (SLOT - 1)
    real = (lane & (HALF - 1)) < PAIRS
    ones_rows = jnp.logical_or(slot_row == HEAD, slot_row == HEAD + 1).astype(f32)
    keys = mm(wqkv_t[WIDE : 2 * WIDE], normed_b).astype(bf16)
    k_ref[...] = keys
    q_ref[...] = (mm(wqkv_t[:WIDE], normed_b) * (SCALE * LOG2E)).astype(bf16)
    yield None
    values = jnp.where(real, mm(wqkv_t[2 * WIDE :], normed_b) + ones_rows, 0.0).astype(bf16)
    v_ref[...] = values
    for cols, ref in ((keys, kt_ref), (values, vt_ref)):
        tall = cols.T
        ref[0:KEYS] = tall[0:KEYS]
        ref[KEYS:] = tall[HALF : HALF + KEYS]

    def norms(ref):
        squares = ref[...].astype(f32)
        squares = (squares * squares).reshape(HEADS, SLOT, LANES)
        return jnp.max(jnp.sum(squares, axis=1), axis=1, keepdims=True)

    safe = jnp.max(norms(q_ref) * norms(k_ref)) <= SAFE * SAFE
    yield None

    def finish(h, rows, weights):
        out = mm(v_ref[rows, 0:KEYS], weights[0:KEYS]) + mm(
            v_ref[rows, HALF : HALF + KEYS], weights[KEYS:]
        )
        inverse = 1.0 / out[HEAD : HEAD + 1]
        rinv_ref[pl.ds(h, 1), :] = inverse
        ctx_ref[rows, :] = out * inverse

    @pl.when(safe)
    def _():
        for h in range(HEADS + 1):
            if h < HEADS:
                scores = mm(kt_ref[:, head_rows(h)], q_ref[head_rows(h), :])
                e_ref[:, LANES * h : LANES * (h + 1)] = jnp.exp2(scores).astype(bf16)
            if h > 0:
                finish(h - 1, head_rows(h - 1), e_ref[:, LANES * (h - 1) : LANES * h])

    @pl.when(jnp.logical_not(safe))
    def _():
        def one_head(h, _):
            queries = q_ref[...]
            mine = lax.broadcasted_iota(jnp.int32, (WIDE, LANES), 0) // SLOT == h
            scores = mm(kt_ref[...], jnp.where(mine, queries, jnp.zeros_like(queries)))
            top = jnp.max(scores, axis=0, keepdims=True)
            weights = jnp.exp2(scores - top).astype(bf16)
            e_ref[:, ds(h * LANES, LANES, LANES)] = weights
            finish(h, ds(h * SLOT, SLOT, SLOT), weights)
            return 0

        lax.fori_loop(0, HEADS, one_head, 0)

    yield mm(wo_t, ctx_ref[...].astype(bf16))


def attention_backward(grad_b, normed_b, wo, wqkv, state, work, sums):
    e_ref, vt_ref, q_ref, k_ref, ctx_ref, rinv_ref = state
    do_ref, block_ref, dq_ref, dkv_ref = work
    d_wq, d_wkv, d_wo = sums
    head_row = lax.broadcasted_iota(jnp.int32, (SLOT, LANES), 0)
    lane_head = lax.broadcasted_iota(jnp.int32, (LANES, WIDE), 1) // SLOT
    key_row = lax.broadcasted_iota(jnp.int32, (2 * KEYS, WIDE), 0)
    real_key = jnp.where(key_row < KEYS, key_row, key_row - KEYS) < PAIRS

    def spread_heads(tall):
        for h in range(HEADS):
            part = jnp.where(lane_head == h, tall, jnp.zeros_like(tall))
            block_ref[LANES * h : LANES * (h + 1), :] = part

    def keep(value, lanes):
        for half in range(2):
            here = slice(half * KEYS, (half + 1) * KEYS)
            dkv_ref[half * HALF : half * HALF + KEYS, lanes] = value[here]

    d_context = mm(wo, grad_b)
    for h in range(HEADS):
        rows = head_rows(h)
        grad = (d_context[rows] * rinv_ref[h : h + 1, :]).astype(bf16).astype(f32)
        dot = -jnp.sum(grad[:HEAD] * ctx_ref[rows, :][:HEAD], axis=0, keepdims=True)
        dot_high = dot.astype(bf16).astype(f32)
        grad = jnp.where(head_row == HEAD, dot_high, grad)
        grad = jnp.where(head_row == HEAD + 1, dot - dot_high, grad)
        do_ref[rows, :] = grad.astype(bf16)
    yield None
    d_wo[...] += mm_nt(ctx_ref[...].astype(bf16), grad_b)
    spread_heads(do_ref[...].T)
    yield None
    dv = mm(e_ref[...], block_ref[...])
    keep(jnp.where(real_key, dv, 0.0).astype(bf16), slice(WIDE, 2 * WIDE))

    yield None
    for h in range(HEADS + 1):
        if h < HEADS:
            lanes = slice(LANES * h, LANES * (h + 1))
            grad_probs = mm(vt_ref[:, head_rows(h)], do_ref[head_rows(h), :])
            e_ref[:, lanes] = e_ref[:, lanes] * grad_probs.astype(bf16)
        if h > 0:
            rows = head_rows(h - 1)
            lanes = slice(LANES * (h - 1), LANES * h)
            dq = mm(k_ref[rows, 0:KEYS], e_ref[0:KEYS, lanes]) + mm(
                k_ref[rows, HALF : HALF + KEYS], e_ref[KEYS:, lanes]
            )
            dq_ref[rows, :] = (dq * SCALE).astype(bf16)
        yield None
    spread_heads(q_ref[...].T)
    yield None
    dk = mm(e_ref[...], block_ref[...])
    keep((dk * (1.0 / LOG2E)).astype(bf16), slice(0, WIDE))
    d_wq[...] += mm_nt(dq_ref[...], normed_b)
    yield None
    d_wkv[...] += mm(normed_b, dkv_ref[...])
    yield mm(wqkv[:, 0:WIDE], dq_ref[...]) + mm_nt(wqkv[:, WIDE:], dkv_ref[...])


STATE = [
    ((2 * KEYS, HEADS * LANES), bf16),
    ((2 * KEYS, WIDE), bf16),
    ((WIDE, LANES), bf16),
    ((WIDE, LANES), bf16),
    ((WIDE, LANES), f32),
    ((HEADS, LANES), f32),
]
WORK = [
    ((WIDE, LANES), bf16),
    ((HEADS * LANES, WIDE), bf16),
    ((WIDE, LANES), bf16),
    ((LANES, 2 * WIDE), bf16),
]
BUNDLE = [
    *STATE,
    *STATE,
    *WORK,
    ((2 * KEYS, WIDE), bf16),
    ((WIDE, LANES), bf16),
    ((LAYERS, 2 * FF, LANES), f32),
]
SUMS = [((WIDE, D), f32), ((D, 2 * WIDE), f32), ((WIDE, D), f32)]
GRADS = [
    *SUMS,
    *SUMS,
    ((LAYERS * D, 2 * FF), f32),
    ((LAYERS * FF, D), f32),
    ((2 * NORMS, D, 128), f32),
]


def main_kernel(attn_diffs, *refs):
    refs = list(refs)
    me_ref, x_ref, g_ref, norm_ref, win_own, win_other, wout_own, wout_other = take(refs, 8)
    attn_refs = take(refs, len(attn_diffs) if attn_diffs else 1)
    res_ref, ig_ref = take(refs, 2)
    sums = (take(refs, 3), take(refs, 3))
    d_win, d_wout, d_norm = take(refs, 3)
    wqkv_t, wqkv, wo_t, wo, win_t, win, wout_t, wout, norm_t, attn_ref = take(refs, 10)
    step = pl.program_id(0)
    bundles = [take(refs, len(BUNDLE)) for _ in range(TOGETHER)]

    @pl.when(step == 0)
    def _():
        for ref in (*sums[0], *sums[1], d_win, d_wout, d_norm):
            ref[...] = jnp.zeros_like(ref)
        for bundle in bundles:
            dkv_ref = bundle[2 * len(STATE) + len(WORK) - 1]
            dkv_ref[...] = jnp.zeros_like(dkv_ref)
        if attn_diffs:
            me = me_ref[0]
            for ref, diffs in zip(attn_refs, attn_diffs, strict=True):
                each = ref.shape[1]
                for i, diff in enumerate(diffs):
                    attn_ref[ds((me ^ diff) * each, each, each), :] = ref[i]
        else:
            attn_ref[...] = attn_refs[0][...]
        norm_t[...] = jnp.concatenate([norm_ref[...], jnp.zeros((8 - 2 * NORMS, D), f32)], axis=0).T
        for layer in range(LAYERS):
            for j in range(4):
                base = (4 * layer + j) * D
                matrix = attn_ref[base : base + D, :].astype(f32)
                if j < 3:
                    tall = pad_heads(matrix.T)
                    wqkv_t[layer, j * WIDE : (j + 1) * WIDE, :] = tall.astype(bf16)
                    wqkv[layer, :, j * WIDE : (j + 1) * WIDE] = tall.T.astype(bf16)
                else:
                    tall = pad_heads(matrix)
                    wo[layer] = tall.astype(bf16)
                    wo_t[layer] = tall.T.astype(bf16)
            for p, (w1, w2) in enumerate(((win_own, wout_own), (win_other, wout_other))):
                win[layer, :, p * FF : (p + 1) * FF] = w1[layer]
                win_t[layer, p * FF : (p + 1) * FF, :] = w1[layer].astype(f32).T.astype(bf16)
                wout[layer, p * FFH : (p + 1) * FFH, :] = w2[layer]
                wout_t[layer, :, p * FFH : (p + 1) * FFH] = w2[layer].astype(f32).T.astype(bf16)

    def add_norm(index, grad, unit):
        d_norm[2 * index] += fold_lanes(grad * unit)
        d_norm[2 * index + 1] += fold_lanes(grad)

    def gain_of(index):
        return norm_t[:, 2 * index : 2 * index + 1]

    def shift_of(index):
        return norm_t[:, 2 * index + 1 : 2 * index + 2]

    def one_sample(sample, bundle):
        bundle = list(bundle)
        states = (take(bundle, len(STATE)), take(bundle, len(STATE)))
        work = take(bundle, len(WORK))
        kt_ref, v_ref, mixed_ref = bundle
        kept = []
        stream = load_sample(x_ref, sample, True)
        normed_b = stream.astype(bf16)
        unit_a = inv_a = None
        yield
        for layer in range(LAYERS):
            if layer > 0:
                normed, unit_a, inv_a = norm_forward(stream, gain_of(2 * layer - 1), shift_of(2 * layer - 1))
                normed_b = normed.astype(bf16)
            for branch in attention_forward(normed_b, wqkv_t[layer], wo_t[layer], states[layer], kt_ref, v_ref):
                yield
            stream = stream + branch
            normed, unit_f, inv_f = norm_forward(stream, gain_of(2 * layer), shift_of(2 * layer))
            ffn_b = normed.astype(bf16)
            yield
            hidden = []
            for p in range(2):
                mixed = mm(win_t[layer, FF * p : FF * (p + 1)], ffn_b)
                mixed_ref[layer, FF * p : FF * (p + 1)] = mixed
                gate = mixed[FFH:]
                hidden.append((mixed[:FFH] * (gate * sigmoid(gate))).astype(bf16))
                yield
            hidden = jnp.concatenate(hidden, axis=0)
            stream = stream + mm(wout_t[layer], hidden)
            kept.append((normed_b, unit_a, inv_a, ffn_b, unit_f, inv_f, hidden))
            yield
        store_sample(res_ref, sample, stream)
        yield
        grad = load_sample(g_ref, sample, False)
        yield
        for layer in reversed(range(LAYERS)):
            normed_b, unit_a, inv_a, ffn_b, unit_f, inv_f, hidden = kept[layer]
            grad_b = grad.astype(bf16)
            d_hidden = mm(wout[layer], grad_b)
            d_mixed = []
            for p in range(2):
                value = mixed_ref[layer, FF * p : FF * p + FFH]
                gate = mixed_ref[layer, FF * p + FFH : FF * (p + 1)]
                part = d_hidden[FFH * p : FFH * (p + 1)]
                sig = sigmoid(gate)
                d_mixed.append((part * (gate * sig)).astype(bf16))
                d_mixed.append((part * value * sig * (1.0 + gate * (1.0 - sig))).astype(bf16))
                yield
            d_mixed = jnp.concatenate(d_mixed, axis=0)
            d_normed = mm(win[layer], d_mixed)
            d_wout[FF * layer : FF * (layer + 1), :] += mm_nt(hidden, grad_b)
            yield
            d_win[D * layer : D * (layer + 1), :] += mm_nt(ffn_b, d_mixed)
            add_norm(2 * layer, d_normed, unit_f)
            grad = grad + norm_backward(d_normed, unit_f, inv_f, gain_of(2 * layer))
            yield
            for d_att in attention_backward(
                grad.astype(bf16), normed_b, wo[layer], wqkv[layer], states[layer], work, sums[layer]
            ):
                yield
            if layer > 0:
                add_norm(2 * layer - 1, d_att, unit_a)
                grad = grad + norm_backward(d_att, unit_a, inv_a, gain_of(2 * layer - 1))
            else:
                grad = grad + d_att
            yield
        store_sample(ig_ref, sample, grad)
        yield

    running = [one_sample(step * TOGETHER + i, bundles[i]) for i in range(TOGETHER)]
    turn = 0
    while running:
        for i, program in enumerate(list(running)):
            if turn >= LAG * i and next(program, running) is running:
                running.remove(program)
        turn += 1


VMEM = pl.BlockSpec(memory_space=pltpu.VMEM)
SMEM = pl.BlockSpec(memory_space=pltpu.SMEM)


def shapes_of(pairs):
    return [jax.ShapeDtypeStruct(*pair) for pair in pairs]


def vmem_of(pairs):
    return [pltpu.VMEM(*pair) for pair in pairs]


def run_main(me, tokens, cotangent, norms, ffn, attn_parts, attn_diffs):
    rows = tokens.shape[0]
    samples = rows // PAIRS
    inputs = (tokens, cotangent, norms, *ffn, *attn_parts)
    scratch = [
        ((LAYERS, 3 * WIDE, D), bf16),
        ((LAYERS, D, 3 * WIDE), bf16),
        ((LAYERS, D, WIDE), bf16),
        ((LAYERS, WIDE, D), bf16),
        ((LAYERS, 2 * FF, D), bf16),
        ((LAYERS, D, 2 * FF), bf16),
        ((LAYERS, D, FF), bf16),
        ((LAYERS, FF, D), bf16),
        ((D, 8), f32),
        ((ATTN_ROWS, D), bf16),
        *BUNDLE * TOGETHER,
    ]

    def body(*refs):
        main_kernel(attn_diffs, *refs)

    out_shape = [((rows, 2 * D), bf16), ((rows, 2 * D), f32), *GRADS]
    res, ig, *grads = pl.pallas_call(
        body,
        grid=(samples // TOGETHER,),
        in_specs=[SMEM] + [VMEM] * len(inputs),
        out_specs=[VMEM] * len(out_shape),
        out_shape=shapes_of(out_shape),
        scratch_shapes=vmem_of(scratch),
        compiler_params=pltpu.CompilerParams(
            dimension_semantics=("arbitrary",), vmem_limit_bytes=VMEM_BYTES
        ),
        cost_estimate=pl.CostEstimate(
            flops=samples * 5_000_000_000, bytes_accessed=20_000_000, transcendentals=0
        ),
    )(me, *inputs)
    return res, ig, grads


def small_kernel(body, out_shape, *inputs, scratch=()):
    return pl.pallas_call(
        body,
        in_specs=[SMEM] + [VMEM] * (len(inputs) - 1),
        out_specs=[VMEM] * len(out_shape),
        out_shape=shapes_of(out_shape),
        scratch_shapes=vmem_of(scratch),
        compiler_params=pltpu.CompilerParams(vmem_limit_bytes=32 * 1024 * 1024),
    )(*inputs)


def resplit(sums):
    high = sums.astype(bf16).astype(f32)
    return jnp.concatenate([high, sums - high], axis=0).astype(bf16)


def finish_attention(d_attn, grads):
    for layer in range(LAYERS):
        d_wq, d_wkv, d_wo = grads[3 * layer : 3 * layer + 3]
        tall = d_wkv[...].T
        for j, source in enumerate((d_wq[...], tall[:WIDE], tall[WIDE:], d_wo[...])):
            slim = slim_heads(source)
            base = (4 * layer + j) * D
            d_attn[base : base + D, :] = slim.T if j < 3 else slim


def finish_norms(d_norm):
    sums = [jnp.sum(d_norm[j].T, axis=0, keepdims=True) for j in range(2 * NORMS)]
    return jnp.concatenate(sums + [jnp.zeros((8 - 2 * NORMS, D), f32)], axis=0)


def plain_gradients(me, grads):
    def body(me_ref, *refs):
        ins, (attn, win, wout, norm) = refs[: len(GRADS)], refs[len(GRADS) :]
        finish_attention(attn, ins)
        win[...] = ins[6][...]
        wout[...] = ins[7][...]
        norm[...] = finish_norms(ins[8])

    shapes = [((ATTN_ROWS, D), f32), GRADS[6], GRADS[7], ((8, D), f32)]
    return small_kernel(body, shapes, me, *grads)


class Exchange:
    def __init__(self, me, parts):
        self.me = me
        self.parts = parts
        self.upper = parts // GROUP
        self.each = ATTN_ROWS // parts
        self.bits = [1 << i for i in range(self.upper.bit_length() - 1)]

    def swap(self, value, k):
        return lax.ppermute(value, AXES, [(i, i ^ k) for i in range(self.parts)])

    def stack(self, blocks):
        size, kind = blocks[0].shape, blocks[0].dtype
        count = math.prod(size[:-2])

        def body(me_ref, *refs):
            ins, out = refs[:-1], refs[-1]
            for i, ref in enumerate(ins):
                if len(size) == 2:
                    out[i] = ref[...]
                else:
                    out[i * count : (i + 1) * count] = ref[...]

        shape = (len(blocks) * count, *size[-2:])
        return small_kernel(body, [(shape, kind)], self.me, *blocks)[0]

    def gather(self, rows, beside):
        far = [GROUP * u for u in range(self.upper)]
        column = self.stack([rows] + [self.swap(rows, k) for k in far[1:]])
        column, beside = lax.optimization_barrier((column, beside))
        plane = self.stack([column] + [self.swap(column, k) for k in NEAR[1:]])
        diffs = [k ^ u for k in NEAR for u in far]
        return [plane, self.swap(plane, TWIN)], [diffs, [d ^ TWIN for d in diffs]], beside

    def pack(self, grads):
        each, upper = self.each, self.upper

        def body(me_ref, *refs):
            ins, outs, d_attn = refs[: len(GRADS)], refs[len(GRADS) : -1], refs[-1]
            finish_attention(d_attn, ins)
            d_win, d_wout, d_norm = ins[6:]
            norm = resplit(finish_norms(d_norm))
            for t, out in enumerate(outs):
                for j, k in enumerate(NEAR):
                    kind = out.dtype
                    low = (me_ref[0] % GROUP) ^ k ^ (TWIN * t)
                    quarter = low // 2
                    half = k % 2
                    for u in range(upper):
                        rows = d_attn[ds((u * GROUP + low) * each, each, each), :]
                        out[j, u * each : (u + 1) * each, 0:D] = rows.astype(kind)
                    first = (quarter // 2) * FF + half * FFH + (quarter % 2) * WOUT_PART
                    out[j, OFF_WOUT:OFF_NORM, 0:D] = d_wout[ds(first, WOUT_PART, WOUT_PART), :].astype(kind)
                    out[j, OFF_NORM:OFF_WIN, 0:D] = norm.astype(kind)
                    rows = d_win[ds(quarter * WIN_PART, WIN_PART, WIN_PART), half * FF : (half + 1) * FF]
                    out[j, OFF_WIN:PAY_ROWS, :] = rows.astype(kind)

        shapes = [((len(NEAR), PAY_ROWS, 2 * FFH), kind) for kind in (f32, bf16)]
        return small_kernel(body, shapes, self.me, *grads, scratch=[((ATTN_ROWS, D), f32)])

    def twins(self, mine, theirs):
        def body(me_ref, mine, theirs, *outs):
            for j, out in enumerate(outs):
                total = mine[j] + theirs[j].astype(f32)
                out[0:OFF_NORM] = total[0:OFF_NORM].astype(out.dtype)
                sums = total[OFF_NORM : OFF_NORM + 8] + total[OFF_NORM + 8 : OFF_WIN]
                out[OFF_NORM:OFF_WIN] = resplit(sums).astype(out.dtype)
                out[OFF_WIN:] = total[OFF_WIN:].astype(out.dtype)

        shape = (PAY_ROWS, 2 * FFH)
        shapes = [(shape, f32)] + [(shape, bf16)] * (len(NEAR) - 1)
        return small_kernel(body, shapes, self.me, mine, theirs)

    def across_plane(self, pieces):
        return [pieces[0]] + [self.swap(piece, k) for piece, k in zip(pieces[1:], NEAR[1:], strict=True)]

    def emit(self, total, blocks, at, keep, send):
        half = len(blocks) // 2
        each = self.each
        for out, rows in ((keep, blocks[:half]), (send, blocks[half:])):
            for i, row in enumerate(rows):
                out[i * each : (i + 1) * each, :] = total[ds(row, each, 8), :].astype(out.dtype)
        first = half * each
        last = at + OFF_NORM - OFF_WOUT
        norm = resplit(total[last : last + 8, :] + total[last + 8 : last + 16, :])
        rest = [
            total[at:last, :].astype(bf16),
            norm,
            total[last + 16 : at + PAY_ROWS - OFF_WOUT, :].astype(bf16),
        ]
        for out in (keep, send):
            row = first
            for part in rest:
                out[row : row + part.shape[0], :] = part.astype(out.dtype)
                row += part.shape[0]

    def stage_shapes(self, blocks):
        shape = (blocks * self.each + PAY_ROWS - OFF_WOUT, 2 * FFH)
        return [(shape, f32), (shape, bf16)]

    def after_plane(self, landed):
        def body(me_ref, *refs):
            ins, (keep, send, total) = refs[: len(NEAR)], refs[len(NEAR) :]
            total[...] = tree_sum([r[...].astype(f32) for r in ins])
            mine = me_ref[0] // GROUP
            order = [r for r in range(self.upper) if not r & 1] + [r for r in range(self.upper) if r & 1]
            self.emit(total, [(mine ^ r) * self.each for r in order], OFF_WOUT, keep, send)

        scratch = [((PAY_ROWS, 2 * FFH), f32)]
        return small_kernel(body, self.stage_shapes(self.upper // 2), self.me, *landed, scratch=scratch)

    def after_bit(self, mine, theirs, blocks):
        def body(me_ref, mine, theirs, keep, send, total):
            total[...] = mine[...] + theirs[...].astype(f32)
            self.emit(total, [i * self.each for i in range(blocks)], blocks * self.each, keep, send)

        (shape, _), _ = self.stage_shapes(blocks)
        return small_kernel(
            body, self.stage_shapes(blocks // 2), self.me, mine, theirs, scratch=[(shape, f32)]
        )

    def after_rest(self, mine, theirs):
        each = self.each
        at_norm = each + WOUT_PART
        ffn_rows = WOUT_PART + WIN_PART

        def body(me_ref, mine, theirs, attn, norm, ffn):
            total = mine[...] + theirs[...].astype(f32)
            attn[...] = total[0:each, 0:D]
            norm[...] = total[at_norm : at_norm + 8, 0:D] + total[at_norm + 8 : at_norm + 16, 0:D]
            ffn[0, 0:WOUT_PART, :] = total[each:at_norm, :].astype(bf16)
            ffn[0, WOUT_PART:, :] = total[at_norm + 16 :, :].astype(bf16)

        shapes = [((each, D), f32), ((8, D), f32), ((1, ffn_rows, 2 * FFH), bf16)]
        return small_kernel(body, shapes, self.me, mine, theirs)

    def spread(self, ffn):
        block = self.stack([ffn, self.swap(ffn, 4)])
        theirs = self.swap(block, TWIN)

        def body(me_ref, mine, theirs, win, wout):
            for t, ref in enumerate((mine, theirs)):
                for i in range(2):
                    quarter = ((me_ref[0] % GROUP) ^ (4 * i) ^ (TWIN * t)) // 2
                    part = ref[i].astype(f32)
                    wout[ds(quarter * WOUT_PART, WOUT_PART, WOUT_PART), :] = part[:WOUT_PART, 0:D]
                    win[ds(quarter * WIN_PART, WIN_PART, WIN_PART), :] = part[WOUT_PART:, :]

        shapes = [((LAYERS * D, 2 * FFH), f32), ((LAYERS * FFH, D), f32)]
        return small_kernel(body, shapes, self.me, block, theirs)

    def sum_all(self, grads):
        keep, send = self.pack(grads)
        keep, send = self.after_plane(self.across_plane(self.twins(keep, self.swap(send, TWIN))))
        blocks = self.upper // 2
        for bit in self.bits[:-1]:
            keep, send = self.after_bit(keep, self.swap(send, GROUP * bit), blocks)
            blocks //= 2
        attn, norm, ffn = self.after_rest(keep, self.swap(send, GROUP * self.bits[-1]))
        return attn, norm, *self.spread(ffn)


def on_device(devices, tokens, attn_weights, norm_params, w_in, w_out, cotangent):
    each = attn_weights.shape[0]
    me = (lax.axis_index("dp") * 2 + lax.axis_index("narrow")).astype(jnp.int32).reshape(1)
    staged = devices % (2 * GROUP) == 0 and each % 16 == 0
    swap_halves = [(0, 1), (1, 0)]
    w_in = w_in.reshape(LAYERS, D, 2 * FFH)
    w_in_other = lax.ppermute(w_in, "narrow", swap_halves)
    w_out_other = lax.ppermute(w_out, "narrow", swap_halves)
    ffn = (w_in, w_in_other, w_out, w_out_other)
    norms = norm_params.reshape(2 * NORMS, D)
    if not staged:
        attn_all = lax.all_gather(attn_weights, AXES, axis=0, tiled=True)
        res, ig, grads = run_main(me, tokens, cotangent, norms, ffn, (attn_all,), None)
        d_attn, d_win, d_wout, sums = plain_gradients(me, grads)
        attn = lax.psum_scatter(d_attn, AXES, scatter_dimension=0, tiled=True)
        norm = lax.psum(sums, AXES)
        d_wout = d_wout.reshape(LAYERS, FF, D)
        own_in, other_in = d_win[:, :FF], d_win[:, FF:]
        own_out, other_out = d_wout[:, :FFH], d_wout[:, FFH:]
        win = lax.psum(own_in + lax.ppermute(other_in, "narrow", swap_halves), "dp")
        wout = lax.psum(own_out + lax.ppermute(other_out, "narrow", swap_halves), "dp")
    else:
        ex = Exchange(me, devices)
        attn_parts, attn_diffs, others = ex.gather(attn_weights, (w_in_other, w_out_other))
        ffn = (w_in, others[0], w_out, others[1])
        res, ig, grads = run_main(me, tokens, cotangent, norms, ffn, attn_parts, attn_diffs)
        attn, norm, win, wout = ex.sum_all(grads)
    return (
        res,
        ig,
        attn,
        norm[: 2 * NORMS].reshape(norm_params.shape),
        win.reshape(LAYERS, D, 2, FFH),
        wout.reshape(LAYERS, FFH, D),
    )


def solution(mesh):
    rows = P(("dp", "narrow"), None)
    hidden_in = P(None, None, None, "narrow")
    hidden_out = P(None, "narrow", None)
    devices = mesh.shape["dp"] * mesh.shape["narrow"]

    def per_device(*args):
        return on_device(devices, *args)

    return jax.shard_map(
        per_device,
        mesh=mesh,
        in_specs=(rows, rows, P(), hidden_in, hidden_out, rows),
        out_specs=(rows, rows, rows, P(), hidden_in, hidden_out),
        check_vma=False,
    )
```

```python
import math

import jax
import jax.numpy as jnp
from jax import lax
from jax.experimental import pallas as pl
from jax.experimental.pallas import tpu as pltpu
from jax.sharding import PartitionSpec as P

HEADS = 8
HEAD = 24
SLOT = 32
WIDE = HEADS * SLOT
D = HEADS * HEAD
FF = 256
FFH = FF // 2
LAYERS = 2
NORMS = 2 * LAYERS - 1
SEQ = 476
PAIRS = SEQ // 2
KEYS = 240
HALF = 256
LANES = 2 * HALF
EPS = 1e-05
SCALE = HEAD ** (-0.5)
LOG2E = math.log2(math.e)
ATTN_ROWS = LAYERS * 4 * D

GROUP = 8
NEAR = (0, 1, 4, 5)
TWIN = 2
WIN_PART = LAYERS * D // 4
WOUT_PART = LAYERS * FFH // 4
ATTN_PART = ATTN_ROWS // GROUP
OFF_WOUT = ATTN_PART
OFF_NORM = OFF_WOUT + WOUT_PART
OFF_WIN = OFF_NORM + 16
PAY_ROWS = OFF_WIN + WIN_PART

bf16 = jnp.bfloat16
f32 = jnp.float32
AXES = ("dp", "narrow")

SAFE = 72.0
VMEM_BYTES = 60 * 1024 * 1024


def mm(left, right):
    return jnp.dot(left, right, preferred_element_type=f32)


def mm_nt(left, right):
    return lax.dot_general(left, right, (((1,), (1,)), ((), ())), preferred_element_type=f32)


def sigmoid(value):
    return 0.5 + 0.5 * jnp.tanh(0.5 * value)


def fold_lanes(value):
    return value[:, 0:128] + value[:, 128:256] + value[:, 256:384] + value[:, 384:512]


def norm_forward(stream, gain, shift):
    center = stream - jnp.sum(stream, axis=0, keepdims=True) * (1.0 / D)
    inverse = lax.rsqrt(jnp.sum(center * center, axis=0, keepdims=True) * (1.0 / D) + EPS)
    unit = center * inverse
    return (unit * gain + shift, unit, inverse)


def norm_backward(grad, unit, inverse, gain):
    scaled = grad * gain
    mean = jnp.sum(scaled, axis=0, keepdims=True) * (1.0 / D)
    slope = jnp.sum(scaled * unit, axis=0, keepdims=True) * (1.0 / D)
    return inverse * (scaled - mean - unit * slope)


def tree_sum(parts):
    while len(parts) > 1:
        parts = [parts[i] + parts[i + 1] for i in range(0, len(parts), 2)]
    return parts[0]


def ds(start, size, step):
    return pl.ds(pl.multiple_of(start, step), size)


def take(refs, count):
    taken = refs[:count]
    del refs[:count]
    return taken


def pad_heads(matrix):
    gap = jnp.zeros((SLOT - HEAD, D), f32)
    slots = []
    for h in range(HEADS):
        slots += [matrix[HEAD * h : HEAD * (h + 1)], gap]
    return jnp.concatenate(slots, axis=0)


def slim_heads(matrix):
    return jnp.concatenate([matrix[SLOT * h : SLOT * h + HEAD] for h in range(HEADS)], axis=0)


def head_rows(h):
    return slice(SLOT * h, SLOT * (h + 1))


def sample_window(step, rows_total, align):
    base = step * PAIRS
    start = jnp.minimum(base // align * align, rows_total - HALF)
    return ds(start, HALF, align), base - start


def load_sample(ref, step, fill_first):
    window, shift = sample_window(step, ref.shape[0], 16)
    rows = pltpu.roll(ref[window, :].astype(f32), lax.rem(HALF - shift, HALF), 0)
    pair_row = lax.broadcasted_iota(jnp.int32, (HALF, 2 * D), 0)
    cols = jnp.where(pair_row < PAIRS, rows, rows[0:1] if fill_first else 0.0).T
    return jnp.concatenate([cols[:D], cols[D:]], axis=1)


def store_sample(ref, step, value):
    window, shift = sample_window(step, ref.shape[0], 16 if ref.dtype == bf16 else 8)
    cols = jnp.concatenate([value[:, :HALF], value[:, HALF:]], axis=0)
    rows = pltpu.roll(cols.T, shift, 0)
    pair_row = lax.broadcasted_iota(jnp.int32, (HALF, 2 * D), 0)
    here = jnp.logical_and(pair_row >= shift, pair_row < shift + PAIRS)
    ref[window, :] = jnp.where(here, rows, ref[window, :].astype(f32)).astype(ref.dtype)


def attention_forward(normed_b, wqkv_t, wo_t, state, kh_ref, v_ref):
    e_ref, vh_ref, q_ref, k_ref, ctx_ref, rinv_ref = state
    lane = lax.broadcasted_iota(jnp.int32, (WIDE, LANES), 1)
    slot_row = lax.broadcasted_iota(jnp.int32, (WIDE, LANES), 0) & (SLOT - 1)
    real = (lane & (HALF - 1)) < PAIRS
    ones_rows = jnp.logical_or(slot_row == HEAD, slot_row == HEAD + 1).astype(f32)
    qkv = mm(wqkv_t, normed_b)
    queries = (qkv[:WIDE] * (SCALE * LOG2E)).astype(bf16)
    q_ref[...] = queries
    keys = qkv[WIDE : 2 * WIDE].astype(bf16)
    k_ref[...] = keys
    values = jnp.where(real, qkv[2 * WIDE :] + ones_rows, 0.0).astype(bf16)
    v_ref[...] = values
    for tall, ref in ((keys.T, kh_ref), (values.T, vh_ref)):
        for h in range(HEADS):
            ref[h, 0:KEYS] = tall[0:KEYS, head_rows(h)]
            ref[h, KEYS:] = tall[HALF : HALF + KEYS, head_rows(h)]

    def norms(value):
        squares = value.astype(f32)
        squares = (squares * squares).reshape(HEADS, SLOT, LANES)
        return jnp.max(jnp.sum(squares, axis=1), axis=1, keepdims=True)

    safe = jnp.max(norms(queries) * norms(keys)) <= SAFE * SAFE

    def finish(h, rows, weights):
        out = mm(v_ref[rows, 0:KEYS], weights[0:KEYS]) + mm(
            v_ref[rows, HALF : HALF + KEYS], weights[KEYS:]
        )
        inverse = 1.0 / out[HEAD : HEAD + 1]
        rinv_ref[pl.ds(h, 1), :] = inverse
        ctx_ref[rows, :] = out * inverse

    @pl.when(safe)
    def _():
        def scores_of(h):
            return mm(kh_ref[h], q_ref[head_rows(h), :])

        scores = scores_of(0)
        for h in range(HEADS):
            ahead = scores_of(h + 1) if h + 1 < HEADS else None
            weights = jnp.exp2(scores).astype(bf16)
            e_ref[:, LANES * h : LANES * (h + 1)] = weights
            finish(h, head_rows(h), weights)
            scores = ahead

    @pl.when(jnp.logical_not(safe))
    def _():
        def one_head(h, _):
            rows = ds(h * SLOT, SLOT, SLOT)
            scores = mm(kh_ref[h], q_ref[rows, :])
            top = jnp.max(scores, axis=0, keepdims=True)
            weights = jnp.exp2(scores - top).astype(bf16)
            e_ref[:, ds(h * LANES, LANES, LANES)] = weights
            finish(h, rows, weights)
            return 0

        lax.fori_loop(0, HEADS, one_head, 0)

    return mm(wo_t, ctx_ref[...].astype(bf16))


def attention_backward(grad_b, normed_b, wo, wqkv, state, work, sums):
    e_ref, vh_ref, q_ref, k_ref, ctx_ref, rinv_ref = state
    ds_ref, do_ref, do_all, q_all, dq_ref, dkv_ref = work
    d_wq, d_wkv, d_wo = sums
    head_row = lax.broadcasted_iota(jnp.int32, (SLOT, LANES), 0)
    lane_head = lax.broadcasted_iota(jnp.int32, (LANES, WIDE), 1) // SLOT
    key_row = lax.broadcasted_iota(jnp.int32, (2 * KEYS, WIDE), 0)
    real_key = jnp.where(key_row < KEYS, key_row, key_row - KEYS) < PAIRS

    def spread_heads(ref, tall):
        for h in range(HEADS):
            part = jnp.where(lane_head == h, tall, jnp.zeros_like(tall))
            ref[LANES * h : LANES * (h + 1), :] = part

    d_wo[...] += mm_nt(ctx_ref[...].astype(bf16), grad_b)
    d_context = mm(wo, grad_b)
    for h in range(HEADS):
        rows = head_rows(h)
        grad = (d_context[rows] * rinv_ref[h : h + 1, :]).astype(bf16).astype(f32)
        dot = -jnp.sum(grad[:HEAD] * ctx_ref[rows, :][:HEAD], axis=0, keepdims=True)
        dot_high = dot.astype(bf16).astype(f32)
        grad = jnp.where(head_row == HEAD, dot_high, grad)
        grad = jnp.where(head_row == HEAD + 1, dot - dot_high, grad)
        do_ref[rows, :] = grad.astype(bf16)
    spread_heads(do_all, do_ref[...].T)
    spread_heads(q_all, q_ref[...].T)

    def grad_probs_of(h):
        return mm(vh_ref[h], do_ref[head_rows(h), :])

    grad_probs = grad_probs_of(0)
    for h in range(HEADS):
        rows = head_rows(h)
        lanes = slice(LANES * h, LANES * (h + 1))
        ahead = grad_probs_of(h + 1) if h + 1 < HEADS else None
        d_scores = e_ref[:, lanes] * grad_probs.astype(bf16)
        ds_ref[:, lanes] = d_scores
        dq = mm(k_ref[rows, 0:KEYS], d_scores[0:KEYS]) + mm(
            k_ref[rows, HALF : HALF + KEYS], d_scores[KEYS:]
        )
        dq_ref[rows, :] = (dq * SCALE).astype(bf16)
        grad_probs = ahead
    dk = (mm(ds_ref[...], q_all[...]) * (1.0 / LOG2E)).astype(bf16)
    dv = jnp.where(real_key, mm(e_ref[...], do_all[...]), 0.0).astype(bf16)
    for half in range(2):
        here = slice(half * KEYS, (half + 1) * KEYS)
        there = slice(half * HALF, half * HALF + KEYS)
        dkv_ref[there, 0:WIDE] = dk[here]
        dkv_ref[there, WIDE:] = dv[here]
    d_wq[...] += mm_nt(dq_ref[...], normed_b)
    d_wkv[...] += mm(normed_b, dkv_ref[...])
    return mm(wqkv[:, 0:WIDE], dq_ref[...]) + mm_nt(wqkv[:, WIDE:], dkv_ref[...])


def resplit(sums):
    high = sums.astype(bf16).astype(f32)
    return jnp.concatenate([high, sums - high], axis=0).astype(bf16)


def finish_attention(d_attn, sums):
    for layer in range(LAYERS):
        d_wq, d_wkv, d_wo = sums[layer]
        tall = d_wkv[...].T
        for j, source in enumerate((d_wq[...], tall[:WIDE], tall[WIDE:], d_wo[...])):
            slim = slim_heads(source)
            base = (4 * layer + j) * D
            d_attn[base : base + D, :] = slim.T if j < 3 else slim


def finish_norms(d_norm):
    sums = [jnp.sum(d_norm[j].T, axis=0, keepdims=True) for j in range(2 * NORMS)]
    return jnp.concatenate(sums + [jnp.zeros((8 - 2 * NORMS, D), f32)], axis=0)


def pack_gradients(outs, me, parts, d_attn, d_win, d_wout, norms):
    each, upper = ATTN_ROWS // parts, parts // GROUP
    norms = resplit(norms)
    for t, out in enumerate(outs):
        for j, k in enumerate(NEAR):
            kind = out.dtype
            low = (me % GROUP) ^ k ^ (TWIN * t)
            quarter = low // 2
            half = k % 2
            for u in range(upper):
                rows = d_attn[ds((u * GROUP + low) * each, each, each), :]
                out[j, u * each : (u + 1) * each, 0:D] = rows.astype(kind)
            first = (quarter // 2) * FF + half * FFH + (quarter % 2) * WOUT_PART
            out[j, OFF_WOUT:OFF_NORM, 0:D] = d_wout[ds(first, WOUT_PART, WOUT_PART), :].astype(kind)
            out[j, OFF_NORM:OFF_WIN, 0:D] = norms.astype(kind)
            rows = d_win[ds(quarter * WIN_PART, WIN_PART, WIN_PART), half * FF : (half + 1) * FF]
            out[j, OFF_WIN:PAY_ROWS, :] = rows.astype(kind)


STATE = [
    ((2 * KEYS, HEADS * LANES), bf16),
    ((HEADS, 2 * KEYS, SLOT), bf16),
    ((WIDE, LANES), bf16),
    ((WIDE, LANES), bf16),
    ((WIDE, LANES), f32),
    ((HEADS, LANES), f32),
]
WORK = [
    ((2 * KEYS, HEADS * LANES), bf16),
    ((WIDE, LANES), bf16),
    ((HEADS * LANES, WIDE), bf16),
    ((HEADS * LANES, WIDE), bf16),
    ((WIDE, LANES), bf16),
    ((LANES, 2 * WIDE), bf16),
]
SUMS = [((WIDE, D), f32), ((D, 2 * WIDE), f32), ((WIDE, D), f32)]
GRADS = [
    *SUMS,
    *SUMS,
    ((LAYERS * D, 2 * FF), f32),
    ((LAYERS * FF, D), f32),
    ((2 * NORMS, D, 128), f32),
    ((ATTN_ROWS, D), f32),
]
SCRATCH = [
    ((LAYERS, 3 * WIDE, D), bf16),
    ((LAYERS, D, 3 * WIDE), bf16),
    ((LAYERS, D, WIDE), bf16),
    ((LAYERS, WIDE, D), bf16),
    ((LAYERS, 2 * FF, D), bf16),
    ((LAYERS, D, 2 * FF), bf16),
    ((LAYERS, D, FF), bf16),
    ((LAYERS, FF, D), bf16),
    ((D, 8), f32),
    ((ATTN_ROWS, D), bf16),
    *GRADS,
    *STATE,
    *STATE,
    *WORK,
    ((HEADS, 2 * KEYS, SLOT), bf16),
    ((WIDE, LANES), bf16),
    ((LAYERS, 2 * FF, LANES), f32),
]


def main_kernel(parts, attn_diffs, *refs):
    refs = list(refs)
    me_ref, x_ref, g_ref, norm_ref, win_own, win_other, wout_own, wout_other = take(refs, 8)
    attn_refs = take(refs, len(attn_diffs) if attn_diffs else 1)
    res_ref, ig_ref = take(refs, 2)
    outs = take(refs, 2 if attn_diffs else 4)
    wqkv_t, wqkv, wo_t, wo, win_t, win, wout_t, wout, norm_t, attn_ref = take(refs, 10)
    sums = (take(refs, 3), take(refs, 3))
    d_win, d_wout, d_norm, d_attn = take(refs, 4)
    states = (take(refs, len(STATE)), take(refs, len(STATE)))
    work = take(refs, len(WORK))
    kh_ref, v_ref, mixed_ref = refs
    dkv_ref = work[-1]
    step = pl.program_id(0)

    @pl.when(step == 0)
    def _():
        for ref in (*sums[0], *sums[1], d_win, d_wout, d_norm, dkv_ref):
            ref[...] = jnp.zeros_like(ref)
        if attn_diffs:
            me = me_ref[0]
            for ref, diffs in zip(attn_refs, attn_diffs, strict=True):
                each = ref.shape[1]
                for i, diff in enumerate(diffs):
                    attn_ref[ds((me ^ diff) * each, each, each), :] = ref[i]
        else:
            attn_ref[...] = attn_refs[0][...]
        norm_t[...] = jnp.concatenate([norm_ref[...], jnp.zeros((8 - 2 * NORMS, D), f32)], axis=0).T
        for layer in range(LAYERS):
            for j in range(4):
                base = (4 * layer + j) * D
                matrix = attn_ref[base : base + D, :].astype(f32)
                if j < 3:
                    tall = pad_heads(matrix.T)
                    wqkv_t[layer, j * WIDE : (j + 1) * WIDE, :] = tall.astype(bf16)
                    wqkv[layer, :, j * WIDE : (j + 1) * WIDE] = tall.T.astype(bf16)
                else:
                    tall = pad_heads(matrix)
                    wo[layer] = tall.astype(bf16)
                    wo_t[layer] = tall.T.astype(bf16)
            for p, (w1, w2) in enumerate(((win_own, wout_own), (win_other, wout_other))):
                win[layer, :, p * FF : (p + 1) * FF] = w1[layer]
                win_t[layer, p * FF : (p + 1) * FF, :] = w1[layer].astype(f32).T.astype(bf16)
                wout[layer, p * FFH : (p + 1) * FFH, :] = w2[layer]
                wout_t[layer, :, p * FFH : (p + 1) * FFH] = w2[layer].astype(f32).T.astype(bf16)

    def add_norm(index, grad, unit):
        d_norm[2 * index] += fold_lanes(grad * unit)
        d_norm[2 * index + 1] += fold_lanes(grad)

    def gain_of(index):
        return norm_t[:, 2 * index : 2 * index + 1]

    def shift_of(index):
        return norm_t[:, 2 * index + 1 : 2 * index + 2]

    kept = []
    stream = load_sample(x_ref, step, True)
    normed_b = stream.astype(bf16)
    unit_a = inv_a = None
    for layer in range(LAYERS):
        if layer > 0:
            normed, unit_a, inv_a = norm_forward(stream, gain_of(2 * layer - 1), shift_of(2 * layer - 1))
            normed_b = normed.astype(bf16)
        stream = stream + attention_forward(
            normed_b, wqkv_t[layer], wo_t[layer], states[layer], kh_ref, v_ref
        )
        normed, unit_f, inv_f = norm_forward(stream, gain_of(2 * layer), shift_of(2 * layer))
        ffn_b = normed.astype(bf16)
        mixed = mm(win_t[layer], ffn_b)
        mixed_ref[layer] = mixed
        hidden = []
        for p in range(2):
            value = mixed[FF * p : FF * p + FFH]
            gate = mixed[FF * p + FFH : FF * (p + 1)]
            hidden.append((value * (gate * sigmoid(gate))).astype(bf16))
        hidden = jnp.concatenate(hidden, axis=0)
        stream = stream + mm(wout_t[layer], hidden)
        kept.append((normed_b, unit_a, inv_a, ffn_b, unit_f, inv_f, hidden))
    store_sample(res_ref, step, stream)

    grad = load_sample(g_ref, step, False)
    for layer in reversed(range(LAYERS)):
        normed_b, unit_a, inv_a, ffn_b, unit_f, inv_f, hidden = kept[layer]
        grad_b = grad.astype(bf16)
        d_wout[FF * layer : FF * (layer + 1), :] += mm_nt(hidden, grad_b)
        d_hidden = mm(wout[layer], grad_b)
        d_mixed = []
        for p in range(2):
            value = mixed_ref[layer, FF * p : FF * p + FFH]
            gate = mixed_ref[layer, FF * p + FFH : FF * (p + 1)]
            part = d_hidden[FFH * p : FFH * (p + 1)]
            sig = sigmoid(gate)
            d_mixed.append((part * (gate * sig)).astype(bf16))
            d_mixed.append((part * value * sig * (1.0 + gate * (1.0 - sig))).astype(bf16))
        d_mixed = jnp.concatenate(d_mixed, axis=0)
        d_win[D * layer : D * (layer + 1), :] += mm_nt(ffn_b, d_mixed)
        d_normed = mm(win[layer], d_mixed)
        add_norm(2 * layer, d_normed, unit_f)
        grad = grad + norm_backward(d_normed, unit_f, inv_f, gain_of(2 * layer))
        d_att = attention_backward(
            grad.astype(bf16), normed_b, wo[layer], wqkv[layer], states[layer], work, sums[layer]
        )
        if layer > 0:
            add_norm(2 * layer - 1, d_att, unit_a)
            grad = grad + norm_backward(d_att, unit_a, inv_a, gain_of(2 * layer - 1))
        else:
            grad = grad + d_att
    store_sample(ig_ref, step, grad)

    @pl.when(step == pl.num_programs(0) - 1)
    def _():
        finish_attention(d_attn, sums)
        norms = finish_norms(d_norm)
        if attn_diffs:
            pack_gradients(outs, me_ref[0], parts, d_attn, d_win, d_wout, norms)
        else:
            for out, value in zip(outs, (d_attn[...], d_win[...], d_wout[...], norms), strict=True):
                out[...] = value


VMEM = pl.BlockSpec(memory_space=pltpu.VMEM)
SMEM = pl.BlockSpec(memory_space=pltpu.SMEM)


def shapes_of(pairs):
    return [jax.ShapeDtypeStruct(*pair) for pair in pairs]


def vmem_of(pairs):
    return [pltpu.VMEM(*pair) for pair in pairs]


def run_main(me, tokens, cotangent, norms, ffn, attn_parts, parts, attn_diffs):
    rows = tokens.shape[0]
    samples = rows // PAIRS
    inputs = (tokens, cotangent, norms, *ffn, *attn_parts)
    if attn_diffs:
        grads = [((len(NEAR), PAY_ROWS, 2 * FFH), kind) for kind in (f32, bf16)]
    else:
        grads = [((ATTN_ROWS, D), f32), GRADS[6], GRADS[7], ((8, D), f32)]

    def body(*refs):
        main_kernel(parts, attn_diffs, *refs)

    out_shape = [((rows, 2 * D), bf16), ((rows, 2 * D), f32), *grads]
    res, ig, *grads = pl.pallas_call(
        body,
        grid=(samples,),
        in_specs=[SMEM] + [VMEM] * len(inputs),
        out_specs=[VMEM] * len(out_shape),
        out_shape=shapes_of(out_shape),
        scratch_shapes=vmem_of(SCRATCH),
        compiler_params=pltpu.CompilerParams(
            dimension_semantics=("arbitrary",), vmem_limit_bytes=VMEM_BYTES
        ),
        cost_estimate=pl.CostEstimate(
            flops=samples * 5_000_000_000, bytes_accessed=20_000_000, transcendentals=0
        ),
    )(me, *inputs)
    return res, ig, grads


def small_kernel(body, out_shape, *inputs, scratch=()):
    return pl.pallas_call(
        body,
        in_specs=[SMEM] + [VMEM] * (len(inputs) - 1),
        out_specs=[VMEM] * len(out_shape),
        out_shape=shapes_of(out_shape),
        scratch_shapes=vmem_of(scratch),
        compiler_params=pltpu.CompilerParams(vmem_limit_bytes=32 * 1024 * 1024),
    )(*inputs)


class Exchange:
    def __init__(self, me, parts):
        self.me = me
        self.parts = parts
        self.upper = parts // GROUP
        self.each = ATTN_ROWS // parts
        self.bits = [1 << i for i in range(self.upper.bit_length() - 1)]

    def swap(self, value, k):
        return lax.ppermute(value, AXES, [(i, i ^ k) for i in range(self.parts)])

    def stack(self, blocks):
        size, kind = blocks[0].shape, blocks[0].dtype
        count = math.prod(size[:-2])

        def body(me_ref, *refs):
            ins, out = refs[:-1], refs[-1]
            for i, ref in enumerate(ins):
                if len(size) == 2:
                    out[i] = ref[...]
                else:
                    out[i * count : (i + 1) * count] = ref[...]

        shape = (len(blocks) * count, *size[-2:])
        return small_kernel(body, [(shape, kind)], self.me, *blocks)[0]

    def gather(self, rows, beside):
        far = [GROUP * u for u in range(self.upper)]
        column = self.stack([rows] + [self.swap(rows, k) for k in far[1:]])
        column, beside = lax.optimization_barrier((column, beside))
        plane = self.stack([column] + [self.swap(column, k) for k in NEAR[1:]])
        diffs = [k ^ u for k in NEAR for u in far]
        return [plane, self.swap(plane, TWIN)], [diffs, [d ^ TWIN for d in diffs]], beside

    def twins(self, mine, theirs):
        def body(me_ref, mine, theirs, *outs):
            for j, out in enumerate(outs):
                total = mine[j] + theirs[j].astype(f32)
                out[0:OFF_NORM] = total[0:OFF_NORM].astype(out.dtype)
                sums = total[OFF_NORM : OFF_NORM + 8] + total[OFF_NORM + 8 : OFF_WIN]
                out[OFF_NORM:OFF_WIN] = resplit(sums).astype(out.dtype)
                out[OFF_WIN:] = total[OFF_WIN:].astype(out.dtype)

        shape = (PAY_ROWS, 2 * FFH)
        shapes = [(shape, f32)] + [(shape, bf16)] * (len(NEAR) - 1)
        return small_kernel(body, shapes, self.me, mine, theirs)

    def across_plane(self, pieces):
        return [pieces[0]] + [self.swap(piece, k) for piece, k in zip(pieces[1:], NEAR[1:], strict=True)]

    def emit(self, total, blocks, at, keep, send):
        half = len(blocks) // 2
        each = self.each
        for out, rows in ((keep, blocks[:half]), (send, blocks[half:])):
            for i, row in enumerate(rows):
                out[i * each : (i + 1) * each, :] = total[ds(row, each, 8), :].astype(out.dtype)
        first = half * each
        last = at + OFF_NORM - OFF_WOUT
        norm = resplit(total[last : last + 8, :] + total[last + 8 : last + 16, :])
        rest = [
            total[at:last, :].astype(bf16),
            norm,
            total[last + 16 : at + PAY_ROWS - OFF_WOUT, :].astype(bf16),
        ]
        for out in (keep, send):
            row = first
            for part in rest:
                out[row : row + part.shape[0], :] = part.astype(out.dtype)
                row += part.shape[0]

    def stage_shapes(self, blocks):
        shape = (blocks * self.each + PAY_ROWS - OFF_WOUT, 2 * FFH)
        return [(shape, f32), (shape, bf16)]

    def after_plane(self, landed):
        def body(me_ref, *refs):
            ins, (keep, send, total) = refs[: len(NEAR)], refs[len(NEAR) :]
            total[...] = tree_sum([r[...].astype(f32) for r in ins])
            mine = me_ref[0] // GROUP
            order = [r for r in range(self.upper) if not r & 1] + [r for r in range(self.upper) if r & 1]
            self.emit(total, [(mine ^ r) * self.each for r in order], OFF_WOUT, keep, send)

        scratch = [((PAY_ROWS, 2 * FFH), f32)]
        return small_kernel(body, self.stage_shapes(self.upper // 2), self.me, *landed, scratch=scratch)

    def after_bit(self, mine, theirs, blocks):
        def body(me_ref, mine, theirs, keep, send, total):
            total[...] = mine[...] + theirs[...].astype(f32)
            self.emit(total, [i * self.each for i in range(blocks)], blocks * self.each, keep, send)

        (shape, _), _ = self.stage_shapes(blocks)
        return small_kernel(
            body, self.stage_shapes(blocks // 2), self.me, mine, theirs, scratch=[(shape, f32)]
        )

    def after_rest(self, mine, theirs):
        each = self.each
        at_norm = each + WOUT_PART
        ffn_rows = WOUT_PART + WIN_PART

        def body(me_ref, mine, theirs, attn, norm, ffn):
            total = mine[...] + theirs[...].astype(f32)
            attn[...] = total[0:each, 0:D]
            norm[...] = total[at_norm : at_norm + 8, 0:D] + total[at_norm + 8 : at_norm + 16, 0:D]
            ffn[0, 0:WOUT_PART, :] = total[each:at_norm, :].astype(bf16)
            ffn[0, WOUT_PART:, :] = total[at_norm + 16 :, :].astype(bf16)

        shapes = [((each, D), f32), ((8, D), f32), ((1, ffn_rows, 2 * FFH), bf16)]
        return small_kernel(body, shapes, self.me, mine, theirs)

    def spread(self, ffn):
        block = self.stack([ffn, self.swap(ffn, 4)])
        theirs = self.swap(block, TWIN)

        def body(me_ref, mine, theirs, win, wout):
            for t, ref in enumerate((mine, theirs)):
                for i in range(2):
                    quarter = ((me_ref[0] % GROUP) ^ (4 * i) ^ (TWIN * t)) // 2
                    part = ref[i].astype(f32)
                    wout[ds(quarter * WOUT_PART, WOUT_PART, WOUT_PART), :] = part[:WOUT_PART, 0:D]
                    win[ds(quarter * WIN_PART, WIN_PART, WIN_PART), :] = part[WOUT_PART:, :]

        shapes = [((LAYERS * D, 2 * FFH), f32), ((LAYERS * FFH, D), f32)]
        return small_kernel(body, shapes, self.me, block, theirs)

    def sum_all(self, keep, send):
        keep, send = self.after_plane(self.across_plane(self.twins(keep, self.swap(send, TWIN))))
        blocks = self.upper // 2
        for bit in self.bits[:-1]:
            keep, send = self.after_bit(keep, self.swap(send, GROUP * bit), blocks)
            blocks //= 2
        attn, norm, ffn = self.after_rest(keep, self.swap(send, GROUP * self.bits[-1]))
        return attn, norm, *self.spread(ffn)


def on_device(devices, tokens, attn_weights, norm_params, w_in, w_out, cotangent):
    each = attn_weights.shape[0]
    me = (lax.axis_index("dp") * 2 + lax.axis_index("narrow")).astype(jnp.int32).reshape(1)
    staged = devices % (2 * GROUP) == 0 and each % 16 == 0
    swap_halves = [(0, 1), (1, 0)]
    w_in = w_in.reshape(LAYERS, D, 2 * FFH)
    w_in_other = lax.ppermute(w_in, "narrow", swap_halves)
    w_out_other = lax.ppermute(w_out, "narrow", swap_halves)
    ffn = (w_in, w_in_other, w_out, w_out_other)
    norms = norm_params.reshape(2 * NORMS, D)
    if not staged:
        attn_all = lax.all_gather(attn_weights, AXES, axis=0, tiled=True)
        res, ig, grads = run_main(me, tokens, cotangent, norms, ffn, (attn_all,), devices, None)
        d_attn, d_win, d_wout, sums = grads
        attn = lax.psum_scatter(d_attn, AXES, scatter_dimension=0, tiled=True)
        norm = lax.psum(sums, AXES)
        d_wout = d_wout.reshape(LAYERS, FF, D)
        own_in, other_in = d_win[:, :FF], d_win[:, FF:]
        own_out, other_out = d_wout[:, :FFH], d_wout[:, FFH:]
        win = lax.psum(own_in + lax.ppermute(other_in, "narrow", swap_halves), "dp")
        wout = lax.psum(own_out + lax.ppermute(other_out, "narrow", swap_halves), "dp")
    else:
        ex = Exchange(me, devices)
        attn_parts, attn_diffs, others = ex.gather(attn_weights, (w_in_other, w_out_other))
        ffn = (w_in, others[0], w_out, others[1])
        res, ig, grads = run_main(me, tokens, cotangent, norms, ffn, attn_parts, devices, attn_diffs)
        attn, norm, win, wout = ex.sum_all(*grads)
    return (
        res,
        ig,
        attn,
        norm[: 2 * NORMS].reshape(norm_params.shape),
        win.reshape(LAYERS, D, 2, FFH),
        wout.reshape(LAYERS, FFH, D),
    )


def solution(mesh):
    rows = P(("dp", "narrow"), None)
    hidden_in = P(None, None, None, "narrow")
    hidden_out = P(None, "narrow", None)
    devices = mesh.shape["dp"] * mesh.shape["narrow"]

    def per_device(*args):
        return on_device(devices, *args)

    return jax.shard_map(
        per_device,
        mesh=mesh,
        in_specs=(rows, rows, P(), hidden_in, hidden_out, rows),
        out_specs=(rows, rows, rows, P(), hidden_in, hidden_out),
        check_vma=False,
    )
```

```python
import math

import jax
import jax.numpy as jnp
from jax import lax
from jax.experimental import pallas as pl
from jax.experimental.pallas import tpu as pltpu
from jax.sharding import PartitionSpec as P

HEADS = 8
HEAD = 24
SLOT = 32
WIDE = HEADS * SLOT
D = HEADS * HEAD
FF = 256
FFH = FF // 2
LAYERS = 2
NORMS = 2 * LAYERS - 1
SEQ = 476
PAIRS = SEQ // 2
KEYS = 240
HALF = 256
LANES = 2 * HALF
EPS = 1e-05
SCALE = HEAD ** (-0.5)
LOG2E = math.log2(math.e)
ATTN_ROWS = LAYERS * 4 * D

GROUP = 8
NEAR = (0, 1, 4, 5)
TWIN = 2
WIN_PART = LAYERS * D // 4
WOUT_PART = LAYERS * FFH // 4
ATTN_PART = ATTN_ROWS // GROUP
OFF_WOUT = ATTN_PART
OFF_NORM = OFF_WOUT + WOUT_PART
OFF_WIN = OFF_NORM + 16
PAY_ROWS = OFF_WIN + WIN_PART

bf16 = jnp.bfloat16
f32 = jnp.float32
AXES = ("dp", "narrow")

VMEM_BYTES = 60 * 1024 * 1024


def mm(left, right):
    return jnp.dot(left, right, preferred_element_type=f32)


def mm_nt(left, right):
    return lax.dot_general(left, right, (((1,), (1,)), ((), ())), preferred_element_type=f32)


def sigmoid(value):
    return 0.5 + 0.5 * jnp.tanh(0.5 * value)


def fold_lanes(value):
    return value[:, 0:128] + value[:, 128:256] + value[:, 256:384] + value[:, 384:512]


def norm_forward(stream, gain, shift):
    center = stream - jnp.sum(stream, axis=0, keepdims=True) * (1.0 / D)
    inverse = lax.rsqrt(jnp.sum(center * center, axis=0, keepdims=True) * (1.0 / D) + EPS)
    unit = center * inverse
    return (unit * gain + shift, unit, inverse)


def norm_backward(grad, unit, inverse, gain):
    scaled = grad * gain
    mean = jnp.sum(scaled, axis=0, keepdims=True) * (1.0 / D)
    slope = jnp.sum(scaled * unit, axis=0, keepdims=True) * (1.0 / D)
    return inverse * (scaled - mean - unit * slope)


def tree_sum(parts):
    while len(parts) > 1:
        parts = [parts[i] + parts[i + 1] for i in range(0, len(parts), 2)]
    return parts[0]


def ds(start, size, step):
    return pl.ds(pl.multiple_of(start, step), size)


def take(refs, count):
    taken = refs[:count]
    del refs[:count]
    return taken


def pad_heads(matrix):
    gap = jnp.zeros((SLOT - HEAD, D), f32)
    slots = []
    for h in range(HEADS):
        slots += [matrix[HEAD * h : HEAD * (h + 1)], gap]
    return jnp.concatenate(slots, axis=0)


def slim_heads(matrix):
    return jnp.concatenate([matrix[SLOT * h : SLOT * h + HEAD] for h in range(HEADS)], axis=0)


def head_rows(h):
    return slice(SLOT * h, SLOT * (h + 1))


def sample_window(step, rows_total, align):
    base = step * PAIRS
    start = jnp.minimum(base // align * align, rows_total - HALF)
    return ds(start, HALF, align), base - start


def load_sample(ref, step, fill_first):
    window, shift = sample_window(step, ref.shape[0], 16)
    rows = pltpu.roll(ref[window, :].astype(f32), lax.rem(HALF - shift, HALF), 0)
    pair_row = lax.broadcasted_iota(jnp.int32, (HALF, 2 * D), 0)
    cols = jnp.where(pair_row < PAIRS, rows, rows[0:1] if fill_first else 0.0).T
    return jnp.concatenate([cols[:D], cols[D:]], axis=1)


def store_sample(ref, step, value):
    window, shift = sample_window(step, ref.shape[0], 16 if ref.dtype == bf16 else 8)
    cols = jnp.concatenate([value[:, :HALF], value[:, HALF:]], axis=0)
    rows = pltpu.roll(cols.T, shift, 0)
    pair_row = lax.broadcasted_iota(jnp.int32, (HALF, 2 * D), 0)
    here = jnp.logical_and(pair_row >= shift, pair_row < shift + PAIRS)
    ref[window, :] = jnp.where(here, rows, ref[window, :].astype(f32)).astype(ref.dtype)


def attention_forward(normed_b, wqkv_t, wo_t, state, kh_ref, v_ref):
    e_ref, vh_ref, q_ref, k_ref, ctx_ref, rinv_ref = state
    lane = lax.broadcasted_iota(jnp.int32, (WIDE, LANES), 1)
    slot_row = lax.broadcasted_iota(jnp.int32, (WIDE, LANES), 0) & (SLOT - 1)
    real = (lane & (HALF - 1)) < PAIRS
    ones_rows = jnp.logical_or(slot_row == HEAD, slot_row == HEAD + 1).astype(f32)
    qkv = mm(wqkv_t, normed_b)
    queries = (qkv[:WIDE] * (SCALE * LOG2E)).astype(bf16)
    q_ref[...] = queries
    keys = qkv[WIDE : 2 * WIDE].astype(bf16)
    k_ref[...] = keys
    values = jnp.where(real, qkv[2 * WIDE :] + ones_rows, 0.0).astype(bf16)
    v_ref[...] = values
    for tall, ref in ((keys.T, kh_ref), (values.T, vh_ref)):
        for h in range(HEADS):
            ref[h, 0:KEYS] = tall[0:KEYS, head_rows(h)]
            ref[h, KEYS:] = tall[HALF : HALF + KEYS, head_rows(h)]

    def scores_of(h):
        return mm(kh_ref[h], q_ref[head_rows(h), :])

    scores = scores_of(0)
    for h in range(HEADS):
        rows = head_rows(h)
        ahead = scores_of(h + 1) if h + 1 < HEADS else None
        top = jnp.max(scores, axis=0, keepdims=True)
        weights = jnp.exp2(scores - top).astype(bf16)
        e_ref[:, LANES * h : LANES * (h + 1)] = weights
        out = mm(v_ref[rows, 0:KEYS], weights[0:KEYS]) + mm(
            v_ref[rows, HALF : HALF + KEYS], weights[KEYS:]
        )
        inverse = 1.0 / out[HEAD : HEAD + 1]
        rinv_ref[h : h + 1, :] = inverse
        ctx_ref[rows, :] = out * inverse
        scores = ahead
    return mm(wo_t, ctx_ref[...].astype(bf16))


def attention_backward(grad_b, normed_b, wo, wqkv, state, work, sums):
    e_ref, vh_ref, q_ref, k_ref, ctx_ref, rinv_ref = state
    ds_ref, do_ref, do_all, q_all, dq_ref, dkv_ref = work
    d_wq, d_wkv, d_wo = sums
    head_row = lax.broadcasted_iota(jnp.int32, (SLOT, LANES), 0)
    lane_head = lax.broadcasted_iota(jnp.int32, (LANES, WIDE), 1) // SLOT
    key_row = lax.broadcasted_iota(jnp.int32, (2 * KEYS, WIDE), 0)
    real_key = jnp.where(key_row < KEYS, key_row, key_row - KEYS) < PAIRS

    def spread_heads(ref, tall):
        for h in range(HEADS):
            part = jnp.where(lane_head == h, tall, jnp.zeros_like(tall))
            ref[LANES * h : LANES * (h + 1), :] = part

    d_wo[...] += mm_nt(ctx_ref[...].astype(bf16), grad_b)
    d_context = mm(wo, grad_b)
    for h in range(HEADS):
        rows = head_rows(h)
        grad = (d_context[rows] * rinv_ref[h : h + 1, :]).astype(bf16).astype(f32)
        dot = -jnp.sum(grad[:HEAD] * ctx_ref[rows, :][:HEAD], axis=0, keepdims=True)
        dot_high = dot.astype(bf16).astype(f32)
        grad = jnp.where(head_row == HEAD, dot_high, grad)
        grad = jnp.where(head_row == HEAD + 1, dot - dot_high, grad)
        do_ref[rows, :] = grad.astype(bf16)
    spread_heads(do_all, do_ref[...].T)
    spread_heads(q_all, q_ref[...].T)

    for h in range(HEADS + 1):
        if h < HEADS:
            lanes = slice(LANES * h, LANES * (h + 1))
            grad_probs = mm(vh_ref[h], do_ref[head_rows(h), :])
            ds_ref[:, lanes] = e_ref[:, lanes] * grad_probs.astype(bf16)
        if h > 0:
            rows = head_rows(h - 1)
            lanes = slice(LANES * (h - 1), LANES * h)
            dq = mm(k_ref[rows, 0:KEYS], ds_ref[0:KEYS, lanes]) + mm(
                k_ref[rows, HALF : HALF + KEYS], ds_ref[KEYS:, lanes]
            )
            dq_ref[rows, :] = (dq * SCALE).astype(bf16)
    dk = (mm(ds_ref[...], q_all[...]) * (1.0 / LOG2E)).astype(bf16)
    dv = jnp.where(real_key, mm(e_ref[...], do_all[...]), 0.0).astype(bf16)
    for half in range(2):
        here = slice(half * KEYS, (half + 1) * KEYS)
        there = slice(half * HALF, half * HALF + KEYS)
        dkv_ref[there, 0:WIDE] = dk[here]
        dkv_ref[there, WIDE:] = dv[here]
    d_wq[...] += mm_nt(dq_ref[...], normed_b)
    d_wkv[...] += mm(normed_b, dkv_ref[...])
    return mm(wqkv[:, 0:WIDE], dq_ref[...]) + mm_nt(wqkv[:, WIDE:], dkv_ref[...])


def resplit(sums):
    high = sums.astype(bf16).astype(f32)
    return jnp.concatenate([high, sums - high], axis=0).astype(bf16)


def finish_attention(d_attn, sums):
    for layer in range(LAYERS):
        d_wq, d_wkv, d_wo = sums[layer]
        tall = d_wkv[...].T
        for j, source in enumerate((d_wq[...], tall[:WIDE], tall[WIDE:], d_wo[...])):
            slim = slim_heads(source)
            base = (4 * layer + j) * D
            d_attn[base : base + D, :] = slim.T if j < 3 else slim


def finish_norms(d_norm):
    sums = [jnp.sum(d_norm[j].T, axis=0, keepdims=True) for j in range(2 * NORMS)]
    return jnp.concatenate(sums + [jnp.zeros((8 - 2 * NORMS, D), f32)], axis=0)


def pack_gradients(outs, me, parts, d_attn, d_win, d_wout, norms):
    each, upper = ATTN_ROWS // parts, parts // GROUP
    norms = resplit(norms)
    for t, out in enumerate(outs):
        for j, k in enumerate(NEAR):
            kind = out.dtype
            low = (me % GROUP) ^ k ^ (TWIN * t)
            quarter = low // 2
            half = k % 2
            for u in range(upper):
                rows = d_attn[ds((u * GROUP + low) * each, each, each), :]
                out[j, u * each : (u + 1) * each, 0:D] = rows.astype(kind)
            first = (quarter // 2) * FF + half * FFH + (quarter % 2) * WOUT_PART
            out[j, OFF_WOUT:OFF_NORM, 0:D] = d_wout[ds(first, WOUT_PART, WOUT_PART), :].astype(kind)
            out[j, OFF_NORM:OFF_WIN, 0:D] = norms.astype(kind)
            rows = d_win[ds(quarter * WIN_PART, WIN_PART, WIN_PART), half * FF : (half + 1) * FF]
            out[j, OFF_WIN:PAY_ROWS, :] = rows.astype(kind)


STATE = [
    ((2 * KEYS, HEADS * LANES), bf16),
    ((HEADS, 2 * KEYS, SLOT), bf16),
    ((WIDE, LANES), bf16),
    ((WIDE, LANES), bf16),
    ((WIDE, LANES), f32),
    ((HEADS, LANES), f32),
]
WORK = [
    ((2 * KEYS, HEADS * LANES), bf16),
    ((WIDE, LANES), bf16),
    ((HEADS * LANES, WIDE), bf16),
    ((HEADS * LANES, WIDE), bf16),
    ((WIDE, LANES), bf16),
    ((LANES, 2 * WIDE), bf16),
]
SUMS = [((WIDE, D), f32), ((D, 2 * WIDE), f32), ((WIDE, D), f32)]
GRADS = [
    *SUMS,
    *SUMS,
    ((LAYERS * D, 2 * FF), f32),
    ((LAYERS * FF, D), f32),
    ((2 * NORMS, D, 128), f32),
    ((ATTN_ROWS, D), f32),
]
SCRATCH = [
    ((LAYERS, 3 * WIDE, D), bf16),
    ((LAYERS, D, 3 * WIDE), bf16),
    ((LAYERS, D, WIDE), bf16),
    ((LAYERS, WIDE, D), bf16),
    ((LAYERS, 2 * FF, D), bf16),
    ((LAYERS, D, 2 * FF), bf16),
    ((LAYERS, D, FF), bf16),
    ((LAYERS, FF, D), bf16),
    ((D, 8), f32),
    ((ATTN_ROWS, D), bf16),
    *GRADS,
    *STATE,
    *STATE,
    *WORK,
    ((HEADS, 2 * KEYS, SLOT), bf16),
    ((WIDE, LANES), bf16),
    ((LAYERS, 2 * FF, LANES), f32),
]


def main_kernel(parts, attn_diffs, *refs):
    refs = list(refs)
    me_ref, x_ref, g_ref, norm_ref, win_own, win_other, wout_own, wout_other = take(refs, 8)
    attn_refs = take(refs, len(attn_diffs) if attn_diffs else 1)
    res_ref, ig_ref = take(refs, 2)
    outs = take(refs, 2 if attn_diffs else 4)
    wqkv_t, wqkv, wo_t, wo, win_t, win, wout_t, wout, norm_t, attn_ref = take(refs, 10)
    sums = (take(refs, 3), take(refs, 3))
    d_win, d_wout, d_norm, d_attn = take(refs, 4)
    states = (take(refs, len(STATE)), take(refs, len(STATE)))
    work = take(refs, len(WORK))
    kh_ref, v_ref, mixed_ref = refs
    dkv_ref = work[-1]
    step = pl.program_id(0)

    @pl.when(step == 0)
    def _():
        for ref in (*sums[0], *sums[1], d_win, d_wout, d_norm, dkv_ref):
            ref[...] = jnp.zeros_like(ref)
        if attn_diffs:
            me = me_ref[0]
            for ref, diffs in zip(attn_refs, attn_diffs, strict=True):
                each = ref.shape[1]
                for i, diff in enumerate(diffs):
                    attn_ref[ds((me ^ diff) * each, each, each), :] = ref[i]
        else:
            attn_ref[...] = attn_refs[0][...]
        norm_t[...] = jnp.concatenate([norm_ref[...], jnp.zeros((8 - 2 * NORMS, D), f32)], axis=0).T
        for layer in range(LAYERS):
            for j in range(4):
                base = (4 * layer + j) * D
                matrix = attn_ref[base : base + D, :].astype(f32)
                if j < 3:
                    tall = pad_heads(matrix.T)
                    wqkv_t[layer, j * WIDE : (j + 1) * WIDE, :] = tall.astype(bf16)
                    wqkv[layer, :, j * WIDE : (j + 1) * WIDE] = tall.T.astype(bf16)
                else:
                    tall = pad_heads(matrix)
                    wo[layer] = tall.astype(bf16)
                    wo_t[layer] = tall.T.astype(bf16)
            for p, (w1, w2) in enumerate(((win_own, wout_own), (win_other, wout_other))):
                win[layer, :, p * FF : (p + 1) * FF] = w1[layer]
                win_t[layer, p * FF : (p + 1) * FF, :] = w1[layer].astype(f32).T.astype(bf16)
                wout[layer, p * FFH : (p + 1) * FFH, :] = w2[layer]
                wout_t[layer, :, p * FFH : (p + 1) * FFH] = w2[layer].astype(f32).T.astype(bf16)

    def add_norm(index, grad, unit):
        d_norm[2 * index] += fold_lanes(grad * unit)
        d_norm[2 * index + 1] += fold_lanes(grad)

    def gain_of(index):
        return norm_t[:, 2 * index : 2 * index + 1]

    def shift_of(index):
        return norm_t[:, 2 * index + 1 : 2 * index + 2]

    kept = []
    stream = load_sample(x_ref, step, True)
    normed_b = stream.astype(bf16)
    unit_a = inv_a = None
    for layer in range(LAYERS):
        if layer > 0:
            normed, unit_a, inv_a = norm_forward(stream, gain_of(2 * layer - 1), shift_of(2 * layer - 1))
            normed_b = normed.astype(bf16)
        stream = stream + attention_forward(
            normed_b, wqkv_t[layer], wo_t[layer], states[layer], kh_ref, v_ref
        )
        normed, unit_f, inv_f = norm_forward(stream, gain_of(2 * layer), shift_of(2 * layer))
        ffn_b = normed.astype(bf16)
        mixed = mm(win_t[layer], ffn_b)
        mixed_ref[layer] = mixed
        hidden = []
        for p in range(2):
            value = mixed[FF * p : FF * p + FFH]
            gate = mixed[FF * p + FFH : FF * (p + 1)]
            hidden.append((value * (gate * sigmoid(gate))).astype(bf16))
        hidden = jnp.concatenate(hidden, axis=0)
        stream = stream + mm(wout_t[layer], hidden)
        kept.append((normed_b, unit_a, inv_a, ffn_b, unit_f, inv_f, hidden))
    store_sample(res_ref, step, stream)

    grad = load_sample(g_ref, step, False)
    for layer in reversed(range(LAYERS)):
        normed_b, unit_a, inv_a, ffn_b, unit_f, inv_f, hidden = kept[layer]
        grad_b = grad.astype(bf16)
        d_wout[FF * layer : FF * (layer + 1), :] += mm_nt(hidden, grad_b)
        d_hidden = mm(wout[layer], grad_b)
        d_mixed = []
        for p in range(2):
            value = mixed_ref[layer, FF * p : FF * p + FFH]
            gate = mixed_ref[layer, FF * p + FFH : FF * (p + 1)]
            part = d_hidden[FFH * p : FFH * (p + 1)]
            sig = sigmoid(gate)
            d_mixed.append((part * (gate * sig)).astype(bf16))
            d_mixed.append((part * value * sig * (1.0 + gate * (1.0 - sig))).astype(bf16))
        d_mixed = jnp.concatenate(d_mixed, axis=0)
        d_win[D * layer : D * (layer + 1), :] += mm_nt(ffn_b, d_mixed)
        d_normed = mm(win[layer], d_mixed)
        add_norm(2 * layer, d_normed, unit_f)
        grad = grad + norm_backward(d_normed, unit_f, inv_f, gain_of(2 * layer))
        d_att = attention_backward(
            grad.astype(bf16), normed_b, wo[layer], wqkv[layer], states[layer], work, sums[layer]
        )
        if layer > 0:
            add_norm(2 * layer - 1, d_att, unit_a)
            grad = grad + norm_backward(d_att, unit_a, inv_a, gain_of(2 * layer - 1))
        else:
            grad = grad + d_att
    store_sample(ig_ref, step, grad)

    @pl.when(step == pl.num_programs(0) - 1)
    def _():
        finish_attention(d_attn, sums)
        norms = finish_norms(d_norm)
        if attn_diffs:
            pack_gradients(outs, me_ref[0], parts, d_attn, d_win, d_wout, norms)
        else:
            for out, value in zip(outs, (d_attn[...], d_win[...], d_wout[...], norms), strict=True):
                out[...] = value


VMEM = pl.BlockSpec(memory_space=pltpu.VMEM)
SMEM = pl.BlockSpec(memory_space=pltpu.SMEM)


def shapes_of(pairs):
    return [jax.ShapeDtypeStruct(*pair) for pair in pairs]


def vmem_of(pairs):
    return [pltpu.VMEM(*pair) for pair in pairs]


def run_main(me, tokens, cotangent, norms, ffn, attn_parts, parts, attn_diffs):
    rows = tokens.shape[0]
    samples = rows // PAIRS
    inputs = (tokens, cotangent, norms, *ffn, *attn_parts)
    if attn_diffs:
        grads = [((len(NEAR), PAY_ROWS, 2 * FFH), kind) for kind in (f32, bf16)]
    else:
        grads = [((ATTN_ROWS, D), f32), GRADS[6], GRADS[7], ((8, D), f32)]

    def body(*refs):
        main_kernel(parts, attn_diffs, *refs)

    out_shape = [((rows, 2 * D), bf16), ((rows, 2 * D), f32), *grads]
    res, ig, *grads = pl.pallas_call(
        body,
        grid=(samples,),
        in_specs=[SMEM] + [VMEM] * len(inputs),
        out_specs=[VMEM] * len(out_shape),
        out_shape=shapes_of(out_shape),
        scratch_shapes=vmem_of(SCRATCH),
        compiler_params=pltpu.CompilerParams(
            dimension_semantics=("arbitrary",), vmem_limit_bytes=VMEM_BYTES
        ),
        cost_estimate=pl.CostEstimate(
            flops=samples * 5_000_000_000, bytes_accessed=20_000_000, transcendentals=0
        ),
    )(me, *inputs)
    return res, ig, grads


def small_kernel(body, out_shape, *inputs, scratch=()):
    return pl.pallas_call(
        body,
        in_specs=[SMEM] + [VMEM] * (len(inputs) - 1),
        out_specs=[VMEM] * len(out_shape),
        out_shape=shapes_of(out_shape),
        scratch_shapes=vmem_of(scratch),
        compiler_params=pltpu.CompilerParams(vmem_limit_bytes=32 * 1024 * 1024),
    )(*inputs)


class Exchange:
    def __init__(self, me, parts):
        self.me = me
        self.parts = parts
        self.upper = parts // GROUP
        self.each = ATTN_ROWS // parts
        self.bits = [1 << i for i in range(self.upper.bit_length() - 1)]

    def swap(self, value, k):
        return lax.ppermute(value, AXES, [(i, i ^ k) for i in range(self.parts)])

    def stack(self, blocks):
        size, kind = blocks[0].shape, blocks[0].dtype
        count = math.prod(size[:-2])

        def body(me_ref, *refs):
            ins, out = refs[:-1], refs[-1]
            for i, ref in enumerate(ins):
                if len(size) == 2:
                    out[i] = ref[...]
                else:
                    out[i * count : (i + 1) * count] = ref[...]

        shape = (len(blocks) * count, *size[-2:])
        return small_kernel(body, [(shape, kind)], self.me, *blocks)[0]

    def gather(self, rows, beside):
        far = [GROUP * u for u in range(self.upper)]
        column = self.stack([rows] + [self.swap(rows, k) for k in far[1:]])
        column, beside = lax.optimization_barrier((column, beside))
        plane = self.stack([column] + [self.swap(column, k) for k in NEAR[1:]])
        diffs = [k ^ u for k in NEAR for u in far]
        return [plane, self.swap(plane, TWIN)], [diffs, [d ^ TWIN for d in diffs]], beside

    def twins(self, mine, theirs):
        def body(me_ref, mine, theirs, *outs):
            for j, out in enumerate(outs):
                total = mine[j] + theirs[j].astype(f32)
                out[0:OFF_NORM] = total[0:OFF_NORM].astype(out.dtype)
                sums = total[OFF_NORM : OFF_NORM + 8] + total[OFF_NORM + 8 : OFF_WIN]
                out[OFF_NORM:OFF_WIN] = resplit(sums).astype(out.dtype)
                out[OFF_WIN:] = total[OFF_WIN:].astype(out.dtype)

        shape = (PAY_ROWS, 2 * FFH)
        shapes = [(shape, f32)] + [(shape, bf16)] * (len(NEAR) - 1)
        return small_kernel(body, shapes, self.me, mine, theirs)

    def across_plane(self, pieces):
        return [pieces[0]] + [self.swap(piece, k) for piece, k in zip(pieces[1:], NEAR[1:], strict=True)]

    def emit(self, total, blocks, at, keep, send):
        half = len(blocks) // 2
        each = self.each
        for out, rows in ((keep, blocks[:half]), (send, blocks[half:])):
            for i, row in enumerate(rows):
                out[i * each : (i + 1) * each, :] = total[ds(row, each, 8), :].astype(out.dtype)
        first = half * each
        last = at + OFF_NORM - OFF_WOUT
        norm = resplit(total[last : last + 8, :] + total[last + 8 : last + 16, :])
        rest = [
            total[at:last, :].astype(bf16),
            norm,
            total[last + 16 : at + PAY_ROWS - OFF_WOUT, :].astype(bf16),
        ]
        for out in (keep, send):
            row = first
            for part in rest:
                out[row : row + part.shape[0], :] = part.astype(out.dtype)
                row += part.shape[0]

    def stage_shapes(self, blocks):
        shape = (blocks * self.each + PAY_ROWS - OFF_WOUT, 2 * FFH)
        return [(shape, f32), (shape, bf16)]

    def after_plane(self, landed):
        def body(me_ref, *refs):
            ins, (keep, send, total) = refs[: len(NEAR)], refs[len(NEAR) :]
            total[...] = tree_sum([r[...].astype(f32) for r in ins])
            mine = me_ref[0] // GROUP
            order = [r for r in range(self.upper) if not r & 1] + [r for r in range(self.upper) if r & 1]
            self.emit(total, [(mine ^ r) * self.each for r in order], OFF_WOUT, keep, send)

        scratch = [((PAY_ROWS, 2 * FFH), f32)]
        return small_kernel(body, self.stage_shapes(self.upper // 2), self.me, *landed, scratch=scratch)

    def after_bit(self, mine, theirs, blocks):
        def body(me_ref, mine, theirs, keep, send, total):
            total[...] = mine[...] + theirs[...].astype(f32)
            self.emit(total, [i * self.each for i in range(blocks)], blocks * self.each, keep, send)

        (shape, _), _ = self.stage_shapes(blocks)
        return small_kernel(
            body, self.stage_shapes(blocks // 2), self.me, mine, theirs, scratch=[(shape, f32)]
        )

    def after_rest(self, mine, theirs):
        each = self.each
        at_norm = each + WOUT_PART
        ffn_rows = WOUT_PART + WIN_PART

        def body(me_ref, mine, theirs, attn, norm, ffn):
            total = mine[...] + theirs[...].astype(f32)
            attn[...] = total[0:each, 0:D]
            norm[...] = total[at_norm : at_norm + 8, 0:D] + total[at_norm + 8 : at_norm + 16, 0:D]
            ffn[0, 0:WOUT_PART, :] = total[each:at_norm, :].astype(bf16)
            ffn[0, WOUT_PART:, :] = total[at_norm + 16 :, :].astype(bf16)

        shapes = [((each, D), f32), ((8, D), f32), ((1, ffn_rows, 2 * FFH), bf16)]
        return small_kernel(body, shapes, self.me, mine, theirs)

    def spread(self, ffn):
        block = self.stack([ffn, self.swap(ffn, 4)])
        theirs = self.swap(block, TWIN)

        def body(me_ref, mine, theirs, win, wout):
            for t, ref in enumerate((mine, theirs)):
                for i in range(2):
                    quarter = ((me_ref[0] % GROUP) ^ (4 * i) ^ (TWIN * t)) // 2
                    part = ref[i].astype(f32)
                    wout[ds(quarter * WOUT_PART, WOUT_PART, WOUT_PART), :] = part[:WOUT_PART, 0:D]
                    win[ds(quarter * WIN_PART, WIN_PART, WIN_PART), :] = part[WOUT_PART:, :]

        shapes = [((LAYERS * D, 2 * FFH), f32), ((LAYERS * FFH, D), f32)]
        return small_kernel(body, shapes, self.me, block, theirs)

    def sum_all(self, keep, send):
        keep, send = self.after_plane(self.across_plane(self.twins(keep, self.swap(send, TWIN))))
        blocks = self.upper // 2
        for bit in self.bits[:-1]:
            keep, send = self.after_bit(keep, self.swap(send, GROUP * bit), blocks)
            blocks //= 2
        attn, norm, ffn = self.after_rest(keep, self.swap(send, GROUP * self.bits[-1]))
        return attn, norm, *self.spread(ffn)


def on_device(devices, tokens, attn_weights, norm_params, w_in, w_out, cotangent):
    each = attn_weights.shape[0]
    me = (lax.axis_index("dp") * 2 + lax.axis_index("narrow")).astype(jnp.int32).reshape(1)
    staged = devices % (2 * GROUP) == 0 and each % 16 == 0
    swap_halves = [(0, 1), (1, 0)]
    w_in = w_in.reshape(LAYERS, D, 2 * FFH)
    w_in_other = lax.ppermute(w_in, "narrow", swap_halves)
    w_out_other = lax.ppermute(w_out, "narrow", swap_halves)
    ffn = (w_in, w_in_other, w_out, w_out_other)
    norms = norm_params.reshape(2 * NORMS, D)
    if not staged:
        attn_all = lax.all_gather(attn_weights, AXES, axis=0, tiled=True)
        res, ig, grads = run_main(me, tokens, cotangent, norms, ffn, (attn_all,), devices, None)
        d_attn, d_win, d_wout, sums = grads
        attn = lax.psum_scatter(d_attn, AXES, scatter_dimension=0, tiled=True)
        norm = lax.psum(sums, AXES)
        d_wout = d_wout.reshape(LAYERS, FF, D)
        own_in, other_in = d_win[:, :FF], d_win[:, FF:]
        own_out, other_out = d_wout[:, :FFH], d_wout[:, FFH:]
        win = lax.psum(own_in + lax.ppermute(other_in, "narrow", swap_halves), "dp")
        wout = lax.psum(own_out + lax.ppermute(other_out, "narrow", swap_halves), "dp")
    else:
        ex = Exchange(me, devices)
        attn_parts, attn_diffs, others = ex.gather(attn_weights, (w_in_other, w_out_other))
        ffn = (w_in, others[0], w_out, others[1])
        res, ig, grads = run_main(me, tokens, cotangent, norms, ffn, attn_parts, devices, attn_diffs)
        attn, norm, win, wout = ex.sum_all(*grads)
    return (
        res,
        ig,
        attn,
        norm[: 2 * NORMS].reshape(norm_params.shape),
        win.reshape(LAYERS, D, 2, FFH),
        wout.reshape(LAYERS, FFH, D),
    )


def solution(mesh):
    rows = P(("dp", "narrow"), None)
    hidden_in = P(None, None, None, "narrow")
    hidden_out = P(None, "narrow", None)
    devices = mesh.shape["dp"] * mesh.shape["narrow"]

    def per_device(*args):
        return on_device(devices, *args)

    return jax.shard_map(
        per_device,
        mesh=mesh,
        in_specs=(rows, rows, P(), hidden_in, hidden_out, rows),
        out_specs=(rows, rows, rows, P(), hidden_in, hidden_out),
        check_vma=False,
    )
```

```python
import math

import jax
import jax.numpy as jnp
from jax import lax
from jax.experimental import pallas as pl
from jax.experimental.pallas import tpu as pltpu
from jax.sharding import PartitionSpec as P

HEADS = 8
HEAD = 24
SLOT = 32
WIDE = HEADS * SLOT
QUAD = 128 // SLOT
D = HEADS * HEAD
FF = 256
FFH = FF // 2
LAYERS = 2
NORMS = 2 * LAYERS - 1
SEQ = 476
PAIRS = SEQ // 2
KEYS = 240
HALF = 256
LANES = 2 * HALF
EPS = 1e-05
SCALE = HEAD ** (-0.5)
LOG2E = math.log2(math.e)
ATTN_ROWS = LAYERS * 4 * D

GROUP = 8
NEAR = (0, 1, 4, 5)
TWIN = 2
WIN_PART = LAYERS * D // 4
WOUT_PART = LAYERS * FFH // 4
ATTN_PART = ATTN_ROWS // GROUP
OFF_WOUT = ATTN_PART
OFF_NORM = OFF_WOUT + WOUT_PART
OFF_WIN = OFF_NORM + 16
PAY_ROWS = OFF_WIN + WIN_PART

bf16 = jnp.bfloat16
f32 = jnp.float32
AXES = ("dp", "narrow")

VMEM_BYTES = 60 * 1024 * 1024


def mm(left, right):
    return jnp.dot(left, right, preferred_element_type=f32)


def mm_nt(left, right):
    return lax.dot_general(left, right, (((1,), (1,)), ((), ())), preferred_element_type=f32)


def sigmoid(value):
    return 0.5 + 0.5 * jnp.tanh(0.5 * value)


def fold_lanes(value):
    return value[:, 0:128] + value[:, 128:256] + value[:, 256:384] + value[:, 384:512]


def norm_forward(stream, gain, shift):
    center = stream - jnp.sum(stream, axis=0, keepdims=True) * (1.0 / D)
    inverse = lax.rsqrt(jnp.sum(center * center, axis=0, keepdims=True) * (1.0 / D) + EPS)
    unit = center * inverse
    return (unit * gain + shift, unit, inverse)


def norm_backward(grad, unit, inverse, gain):
    scaled = grad * gain
    mean = jnp.sum(scaled, axis=0, keepdims=True) * (1.0 / D)
    slope = jnp.sum(scaled * unit, axis=0, keepdims=True) * (1.0 / D)
    return inverse * (scaled - mean - unit * slope)


def tree_sum(parts):
    while len(parts) > 1:
        parts = [parts[i] + parts[i + 1] for i in range(0, len(parts), 2)]
    return parts[0]


def ds(start, size, step):
    return pl.ds(pl.multiple_of(start, step), size)


def take(refs, count):
    taken = refs[:count]
    del refs[:count]
    return taken


def pad_heads(matrix):
    gap = jnp.zeros((SLOT - HEAD, D), f32)
    slots = []
    for h in range(HEADS):
        slots += [matrix[HEAD * h : HEAD * (h + 1)], gap]
    return jnp.concatenate(slots, axis=0)


def slim_heads(matrix):
    return jnp.concatenate([matrix[SLOT * h : SLOT * h + HEAD] for h in range(HEADS)], axis=0)


def head_rows(h):
    return slice(SLOT * h, SLOT * (h + 1))


def sample_window(step, rows_total, align):
    base = step * PAIRS
    start = jnp.minimum(base // align * align, rows_total - HALF)
    return ds(start, HALF, align), base - start


def load_sample(ref, step, fill_first):
    window, shift = sample_window(step, ref.shape[0], 16)
    rows = pltpu.roll(ref[window, :].astype(f32), lax.rem(HALF - shift, HALF), 0)
    pair_row = lax.broadcasted_iota(jnp.int32, (HALF, 2 * D), 0)
    cols = jnp.where(pair_row < PAIRS, rows, rows[0:1] if fill_first else 0.0).T
    return jnp.concatenate([cols[:D], cols[D:]], axis=1)


def store_sample(ref, step, value):
    window, shift = sample_window(step, ref.shape[0], 16 if ref.dtype == bf16 else 8)
    cols = jnp.concatenate([value[:, :HALF], value[:, HALF:]], axis=0)
    rows = pltpu.roll(cols.T, shift, 0)
    pair_row = lax.broadcasted_iota(jnp.int32, (HALF, 2 * D), 0)
    here = jnp.logical_and(pair_row >= shift, pair_row < shift + PAIRS)
    ref[window, :] = jnp.where(here, rows, ref[window, :].astype(f32)).astype(ref.dtype)


def attention_forward(normed_b, wqkv_t, wo_t, state, kh_ref, v_ref):
    e_ref, vh_ref, q_ref, k_ref, ctx_ref, rinv_ref = state
    lane = lax.broadcasted_iota(jnp.int32, (WIDE, LANES), 1)
    slot_row = lax.broadcasted_iota(jnp.int32, (WIDE, LANES), 0) & (SLOT - 1)
    real = (lane & (HALF - 1)) < PAIRS
    ones_rows = jnp.logical_or(slot_row == HEAD, slot_row == HEAD + 1).astype(f32)
    qkv = mm(wqkv_t, normed_b)
    queries = (qkv[:WIDE] * (SCALE * LOG2E)).astype(bf16)
    q_ref[...] = queries
    keys = qkv[WIDE : 2 * WIDE].astype(bf16)
    k_ref[...] = keys
    values = jnp.where(real, qkv[2 * WIDE :] + ones_rows, 0.0).astype(bf16)
    v_ref[...] = values
    for tall, ref in ((keys.T, kh_ref), (values.T, vh_ref)):
        for h in range(HEADS):
            ref[h, 0:KEYS] = tall[0:KEYS, head_rows(h)]
            ref[h, KEYS:] = tall[HALF : HALF + KEYS, head_rows(h)]

    def scores_of(h):
        return mm(kh_ref[h], q_ref[head_rows(h), :])

    scores = scores_of(0)
    for h in range(HEADS):
        rows = head_rows(h)
        ahead = scores_of(h + 1) if h + 1 < HEADS else None
        top = jnp.max(scores, axis=0, keepdims=True)
        weights = jnp.exp2(scores - top).astype(bf16)
        e_ref[:, LANES * h : LANES * (h + 1)] = weights
        out = mm(v_ref[rows, 0:KEYS], weights[0:KEYS]) + mm(
            v_ref[rows, HALF : HALF + KEYS], weights[KEYS:]
        )
        inverse = 1.0 / out[HEAD : HEAD + 1]
        rinv_ref[h : h + 1, :] = inverse
        ctx_ref[rows, :] = out * inverse
        scores = ahead
    return mm(wo_t, ctx_ref[...].astype(bf16))


def attention_backward(grad_b, normed_b, wo, wqkv, state, work, sums):
    e_ref, vh_ref, q_ref, k_ref, ctx_ref, rinv_ref = state
    ds_ref, do_ref, do_all, q_all, dq_ref, dkv_ref = work
    d_wq, d_wkv, d_wo = sums
    head_row = lax.broadcasted_iota(jnp.int32, (SLOT, LANES), 0)
    lane_head = lax.broadcasted_iota(jnp.int32, (LANES, 128), 1) // SLOT
    key_row = lax.broadcasted_iota(jnp.int32, (2 * KEYS, 128), 0)
    real_key = jnp.where(key_row < KEYS, key_row, key_row - KEYS) < PAIRS

    def spread_heads(ref, tall):
        for h in range(HEADS):
            part = tall[:, 128 * (h // QUAD) : 128 * (h // QUAD + 1)]
            ref[LANES * h : LANES * (h + 1), :] = jnp.where(lane_head == h % QUAD, part, jnp.zeros_like(part))

    def gather_heads(left, right):
        half = QUAD * LANES
        return [mm(left[:, half * g : half * (g + 1)], right[half * g : half * (g + 1), :]) for g in range(2)]

    d_wo[...] += mm_nt(ctx_ref[...].astype(bf16), grad_b)
    d_context = mm(wo, grad_b)
    for h in range(HEADS):
        rows = head_rows(h)
        grad = (d_context[rows] * rinv_ref[h : h + 1, :]).astype(bf16).astype(f32)
        dot = -jnp.sum(grad[:HEAD] * ctx_ref[rows, :][:HEAD], axis=0, keepdims=True)
        dot_high = dot.astype(bf16).astype(f32)
        grad = jnp.where(head_row == HEAD, dot_high, grad)
        grad = jnp.where(head_row == HEAD + 1, dot - dot_high, grad)
        do_ref[rows, :] = grad.astype(bf16)
    spread_heads(do_all, do_ref[...].T)
    spread_heads(q_all, q_ref[...].T)

    for h in range(HEADS + 1):
        if h < HEADS:
            lanes = slice(LANES * h, LANES * (h + 1))
            grad_probs = mm(vh_ref[h], do_ref[head_rows(h), :])
            ds_ref[:, lanes] = e_ref[:, lanes] * grad_probs.astype(bf16)
        if h > 0:
            rows = head_rows(h - 1)
            lanes = slice(LANES * (h - 1), LANES * h)
            dq = mm(k_ref[rows, 0:KEYS], ds_ref[0:KEYS, lanes]) + mm(
                k_ref[rows, HALF : HALF + KEYS], ds_ref[KEYS:, lanes]
            )
            dq_ref[rows, :] = (dq * SCALE).astype(bf16)
    dk = [(part * (1.0 / LOG2E)).astype(bf16) for part in gather_heads(ds_ref, q_all)]
    dv = [jnp.where(real_key, part, 0.0).astype(bf16) for part in gather_heads(e_ref, do_all)]
    for i, part in enumerate(dk + dv):
        for half in range(2):
            there = slice(half * HALF, half * HALF + KEYS)
            dkv_ref[there, 128 * i : 128 * (i + 1)] = part[half * KEYS : (half + 1) * KEYS]
    d_wq[...] += mm_nt(dq_ref[...], normed_b)
    d_wkv[...] += mm(normed_b, dkv_ref[...])
    return mm(wqkv[:, 0:WIDE], dq_ref[...]) + mm_nt(wqkv[:, WIDE:], dkv_ref[...])


def resplit(sums):
    high = sums.astype(bf16).astype(f32)
    return jnp.concatenate([high, sums - high], axis=0).astype(bf16)


def finish_attention(d_attn, sums):
    for layer in range(LAYERS):
        d_wq, d_wkv, d_wo = sums[layer]
        tall = d_wkv[...].T
        for j, source in enumerate((d_wq[...], tall[:WIDE], tall[WIDE:], d_wo[...])):
            slim = slim_heads(source)
            base = (4 * layer + j) * D
            d_attn[base : base + D, :] = slim.T if j < 3 else slim


def finish_norms(d_norm):
    sums = [jnp.sum(d_norm[j].T, axis=0, keepdims=True) for j in range(2 * NORMS)]
    return jnp.concatenate(sums + [jnp.zeros((8 - 2 * NORMS, D), f32)], axis=0)


def pack_gradients(outs, me, parts, d_attn, d_win, d_wout, norms):
    each, upper = ATTN_ROWS // parts, parts // GROUP
    norms = resplit(norms)
    for t, out in enumerate(outs):
        for j, k in enumerate(NEAR):
            kind = out.dtype
            low = (me % GROUP) ^ k ^ (TWIN * t)
            quarter = low // 2
            half = k % 2
            for u in range(upper):
                rows = d_attn[ds((u * GROUP + low) * each, each, each), :]
                out[j, u * each : (u + 1) * each, 0:D] = rows.astype(kind)
            first = (quarter // 2) * FF + half * FFH + (quarter % 2) * WOUT_PART
            out[j, OFF_WOUT:OFF_NORM, 0:D] = d_wout[ds(first, WOUT_PART, WOUT_PART), :].astype(kind)
            out[j, OFF_NORM:OFF_WIN, 0:D] = norms.astype(kind)
            rows = d_win[ds(quarter * WIN_PART, WIN_PART, WIN_PART), half * FF : (half + 1) * FF]
            out[j, OFF_WIN:PAY_ROWS, :] = rows.astype(kind)


STATE = [
    ((2 * KEYS, HEADS * LANES), bf16),
    ((HEADS, 2 * KEYS, SLOT), bf16),
    ((WIDE, LANES), bf16),
    ((WIDE, LANES), bf16),
    ((WIDE, LANES), f32),
    ((HEADS, LANES), f32),
]
WORK = [
    ((2 * KEYS, HEADS * LANES), bf16),
    ((WIDE, LANES), bf16),
    ((HEADS * LANES, 128), bf16),
    ((HEADS * LANES, 128), bf16),
    ((WIDE, LANES), bf16),
    ((LANES, 2 * WIDE), bf16),
]
SUMS = [((WIDE, D), f32), ((D, 2 * WIDE), f32), ((WIDE, D), f32)]
GRADS = [
    *SUMS,
    *SUMS,
    ((LAYERS * D, 2 * FF), f32),
    ((LAYERS * FF, D), f32),
    ((2 * NORMS, D, 128), f32),
    ((ATTN_ROWS, D), f32),
]
SCRATCH = [
    ((LAYERS, 3 * WIDE, D), bf16),
    ((LAYERS, D, 3 * WIDE), bf16),
    ((LAYERS, D, WIDE), bf16),
    ((LAYERS, WIDE, D), bf16),
    ((LAYERS, 2 * FF, D), bf16),
    ((LAYERS, D, 2 * FF), bf16),
    ((LAYERS, D, FF), bf16),
    ((LAYERS, FF, D), bf16),
    ((D, 8), f32),
    ((ATTN_ROWS, D), bf16),
    *GRADS,
    *STATE,
    *STATE,
    *WORK,
    ((HEADS, 2 * KEYS, SLOT), bf16),
    ((WIDE, LANES), bf16),
    ((LAYERS, 2 * FF, LANES), f32),
    ((2 * LAYERS * D, FFH), f32),
]


def main_kernel(parts, attn_diffs, *refs):
    refs = list(refs)
    me_ref, x_ref, g_ref, norm_ref, win_own, win_other, wout_own, wout_other = take(refs, 8)
    attn_refs = take(refs, len(attn_diffs) if attn_diffs else 1)
    res_ref, ig_ref = take(refs, 2)
    outs = take(refs, 2 if attn_diffs else 4)
    wqkv_t, wqkv, wo_t, wo, win_t, win, wout_t, wout, norm_t, attn_ref = take(refs, 10)
    sums = (take(refs, 3), take(refs, 3))
    d_win, d_wout, d_norm, d_attn = take(refs, 4)
    states = (take(refs, len(STATE)), take(refs, len(STATE)))
    work = take(refs, len(WORK))
    kh_ref, v_ref, mixed_ref, win_rows = refs
    dkv_ref = work[-1]
    step = pl.program_id(0)

    @pl.when(step == 0)
    def _():
        for ref in (*sums[0], *sums[1], d_win, d_wout, d_norm, dkv_ref):
            ref[...] = jnp.zeros_like(ref)
        if attn_diffs:
            me = me_ref[0]
            for ref, diffs in zip(attn_refs, attn_diffs, strict=True):
                each = ref.shape[1]
                for i, diff in enumerate(diffs):
                    attn_ref[ds((me ^ diff) * each, each, each), :] = ref[i]
        else:
            attn_ref[...] = attn_refs[0][...]
        norms = [norm_ref[i] for i in range(NORMS)]
        norm_t[...] = jnp.concatenate(norms + [jnp.zeros((8 - 2 * NORMS, D), f32)], axis=0).T
        for layer in range(LAYERS):
            for j in range(4):
                base = (4 * layer + j) * D
                matrix = attn_ref[base : base + D, :].astype(f32)
                if j < 3:
                    tall = pad_heads(matrix.T)
                    wqkv_t[layer, j * WIDE : (j + 1) * WIDE, :] = tall.astype(bf16)
                    wqkv[layer, :, j * WIDE : (j + 1) * WIDE] = tall.T.astype(bf16)
                else:
                    tall = pad_heads(matrix)
                    wo[layer] = tall.astype(bf16)
                    wo_t[layer] = tall.T.astype(bf16)
        for p, (w1, w2) in enumerate(((win_own, wout_own), (win_other, wout_other))):
            win_rows[...] = w1[...].astype(f32)
            for layer in range(LAYERS):
                for g in range(2):
                    part = win_rows[pl.ds(2 * layer * D + g, D, stride=2), :]
                    here = slice(p * FF + g * FFH, p * FF + (g + 1) * FFH)
                    win[layer, :, here] = part.astype(bf16)
                    win_t[layer, here, :] = part.T.astype(bf16)
                wout_t[layer, :, p * FFH : (p + 1) * FFH] = w2[layer]
                wout[layer, p * FFH : (p + 1) * FFH, :] = w2[layer].astype(f32).T.astype(bf16)

    def add_norm(index, grad, unit):
        d_norm[2 * index] += fold_lanes(grad * unit)
        d_norm[2 * index + 1] += fold_lanes(grad)

    def gain_of(index):
        return norm_t[:, 2 * index : 2 * index + 1]

    def shift_of(index):
        return norm_t[:, 2 * index + 1 : 2 * index + 2]

    kept = []
    stream = load_sample(x_ref, step, True)
    normed_b = stream.astype(bf16)
    unit_a = inv_a = None
    for layer in range(LAYERS):
        if layer > 0:
            normed, unit_a, inv_a = norm_forward(stream, gain_of(2 * layer - 1), shift_of(2 * layer - 1))
            normed_b = normed.astype(bf16)
        stream = stream + attention_forward(
            normed_b, wqkv_t[layer], wo_t[layer], states[layer], kh_ref, v_ref
        )
        normed, unit_f, inv_f = norm_forward(stream, gain_of(2 * layer), shift_of(2 * layer))
        ffn_b = normed.astype(bf16)
        mixed = mm(win_t[layer], ffn_b)
        mixed_ref[layer] = mixed
        hidden = []
        for p in range(2):
            value = mixed[FF * p : FF * p + FFH]
            gate = mixed[FF * p + FFH : FF * (p + 1)]
            hidden.append((value * (gate * sigmoid(gate))).astype(bf16))
        hidden = jnp.concatenate(hidden, axis=0)
        stream = stream + mm(wout_t[layer], hidden)
        kept.append((normed_b, unit_a, inv_a, ffn_b, unit_f, inv_f, hidden))
    store_sample(res_ref, step, stream)

    grad = load_sample(g_ref, step, False)
    for layer in reversed(range(LAYERS)):
        normed_b, unit_a, inv_a, ffn_b, unit_f, inv_f, hidden = kept[layer]
        grad_b = grad.astype(bf16)
        d_wout[FF * layer : FF * (layer + 1), :] += mm_nt(hidden, grad_b)
        d_hidden = mm(wout[layer], grad_b)
        d_mixed = []
        for p in range(2):
            value = mixed_ref[layer, FF * p : FF * p + FFH]
            gate = mixed_ref[layer, FF * p + FFH : FF * (p + 1)]
            part = d_hidden[FFH * p : FFH * (p + 1)]
            sig = sigmoid(gate)
            d_mixed.append((part * (gate * sig)).astype(bf16))
            d_mixed.append((part * value * sig * (1.0 + gate * (1.0 - sig))).astype(bf16))
        d_mixed = jnp.concatenate(d_mixed, axis=0)
        d_win[D * layer : D * (layer + 1), :] += mm_nt(ffn_b, d_mixed)
        d_normed = mm(win[layer], d_mixed)
        add_norm(2 * layer, d_normed, unit_f)
        grad = grad + norm_backward(d_normed, unit_f, inv_f, gain_of(2 * layer))
        d_att = attention_backward(
            grad.astype(bf16), normed_b, wo[layer], wqkv[layer], states[layer], work, sums[layer]
        )
        if layer > 0:
            add_norm(2 * layer - 1, d_att, unit_a)
            grad = grad + norm_backward(d_att, unit_a, inv_a, gain_of(2 * layer - 1))
        else:
            grad = grad + d_att
    store_sample(ig_ref, step, grad)

    @pl.when(step == pl.num_programs(0) - 1)
    def _():
        finish_attention(d_attn, sums)
        norms = finish_norms(d_norm)
        if attn_diffs:
            pack_gradients(outs, me_ref[0], parts, d_attn, d_win, d_wout, norms)
        else:
            for out, value in zip(outs, (d_attn[...], d_win[...], d_wout[...], norms), strict=True):
                out[...] = value


VMEM = pl.BlockSpec(memory_space=pltpu.VMEM)
SMEM = pl.BlockSpec(memory_space=pltpu.SMEM)


def shapes_of(pairs):
    return [jax.ShapeDtypeStruct(*pair) for pair in pairs]


def vmem_of(pairs):
    return [pltpu.VMEM(*pair) for pair in pairs]


def run_main(me, tokens, cotangent, norm_params, ffn, attn_parts, parts, attn_diffs):
    rows = tokens.shape[0]
    samples = rows // PAIRS
    inputs = (tokens, cotangent, norm_params, *ffn, *attn_parts)
    if attn_diffs:
        grads = [((len(NEAR), PAY_ROWS, 2 * FFH), bf16)] * 2
    else:
        grads = [((ATTN_ROWS, D), f32), GRADS[6], GRADS[7], ((8, D), f32)]

    def body(*refs):
        main_kernel(parts, attn_diffs, *refs)

    out_shape = [((rows, 2 * D), bf16), ((rows, 2 * D), f32), *grads]
    res, ig, *grads = pl.pallas_call(
        body,
        grid=(samples,),
        in_specs=[SMEM] + [VMEM] * len(inputs),
        out_specs=[VMEM] * len(out_shape),
        out_shape=shapes_of(out_shape),
        scratch_shapes=vmem_of(SCRATCH),
        compiler_params=pltpu.CompilerParams(
            dimension_semantics=("arbitrary",), vmem_limit_bytes=VMEM_BYTES
        ),
        cost_estimate=pl.CostEstimate(
            flops=samples * 5_000_000_000, bytes_accessed=20_000_000, transcendentals=0
        ),
    )(me, *inputs)
    return res, ig, grads


def small_kernel(body, out_shape, *inputs, scratch=()):
    return pl.pallas_call(
        body,
        in_specs=[SMEM] + [VMEM] * (len(inputs) - 1),
        out_specs=[VMEM] * len(out_shape),
        out_shape=shapes_of(out_shape),
        scratch_shapes=vmem_of(scratch),
        compiler_params=pltpu.CompilerParams(vmem_limit_bytes=32 * 1024 * 1024),
    )(*inputs)


class Exchange:
    def __init__(self, me, parts):
        self.me = me
        self.parts = parts
        self.upper = parts // GROUP
        self.each = ATTN_ROWS // parts
        self.bits = [1 << i for i in range(self.upper.bit_length() - 1)]

    def swap(self, value, k):
        return lax.ppermute(value, AXES, [(i, i ^ k) for i in range(self.parts)])

    def stack(self, blocks):
        size, kind = blocks[0].shape, blocks[0].dtype
        count = math.prod(size[:-2])

        def body(me_ref, *refs):
            ins, out = refs[:-1], refs[-1]
            for i, ref in enumerate(ins):
                if len(size) == 2:
                    out[i] = ref[...]
                else:
                    out[i * count : (i + 1) * count] = ref[...]

        shape = (len(blocks) * count, *size[-2:])
        return small_kernel(body, [(shape, kind)], self.me, *blocks)[0]

    def gather(self, rows, beside):
        far = [GROUP * u for u in range(self.upper)]
        column = self.stack([rows] + [self.swap(rows, k) for k in far[1:]])
        column, beside = lax.optimization_barrier((column, beside))
        plane = self.stack([column] + [self.swap(column, k) for k in NEAR[1:]])
        diffs = [k ^ u for k in NEAR for u in far]
        return [plane, self.swap(plane, TWIN)], [diffs, [d ^ TWIN for d in diffs]], beside

    def twins(self, mine, theirs):
        def body(me_ref, mine, theirs, *outs):
            for j, out in enumerate(outs):
                total = mine[j].astype(f32) + theirs[j].astype(f32)
                out[0:OFF_NORM] = total[0:OFF_NORM].astype(out.dtype)
                sums = total[OFF_NORM : OFF_NORM + 8] + total[OFF_NORM + 8 : OFF_WIN]
                out[OFF_NORM:OFF_WIN] = resplit(sums).astype(out.dtype)
                out[OFF_WIN:] = total[OFF_WIN:].astype(out.dtype)

        shape = (PAY_ROWS, 2 * FFH)
        shapes = [(shape, f32)] + [(shape, bf16)] * (len(NEAR) - 1)
        return small_kernel(body, shapes, self.me, mine, theirs)

    def across_plane(self, pieces):
        return [pieces[0]] + [self.swap(piece, k) for piece, k in zip(pieces[1:], NEAR[1:], strict=True)]

    def emit(self, total, blocks, at, keep, send):
        half = len(blocks) // 2
        each = self.each
        for out, rows in ((keep, blocks[:half]), (send, blocks[half:])):
            for i, row in enumerate(rows):
                out[i * each : (i + 1) * each, :] = total[ds(row, each, 8), :].astype(out.dtype)
        first = half * each
        last = at + OFF_NORM - OFF_WOUT
        norm = resplit(total[last : last + 8, :] + total[last + 8 : last + 16, :])
        rest = [
            total[at:last, :].astype(bf16),
            norm,
            total[last + 16 : at + PAY_ROWS - OFF_WOUT, :].astype(bf16),
        ]
        for out in (keep, send):
            row = first
            for part in rest:
                out[row : row + part.shape[0], :] = part.astype(out.dtype)
                row += part.shape[0]

    def stage_shapes(self, blocks):
        shape = (blocks * self.each + PAY_ROWS - OFF_WOUT, 2 * FFH)
        return [(shape, f32), (shape, bf16)]

    def after_plane(self, landed):
        def body(me_ref, *refs):
            ins, (keep, send, total) = refs[: len(NEAR)], refs[len(NEAR) :]
            total[...] = tree_sum([r[...].astype(f32) for r in ins])
            mine = me_ref[0] // GROUP
            order = [r for r in range(self.upper) if not r & 1] + [r for r in range(self.upper) if r & 1]
            self.emit(total, [(mine ^ r) * self.each for r in order], OFF_WOUT, keep, send)

        scratch = [((PAY_ROWS, 2 * FFH), f32)]
        return small_kernel(body, self.stage_shapes(self.upper // 2), self.me, *landed, scratch=scratch)

    def after_bit(self, mine, theirs, blocks):
        def body(me_ref, mine, theirs, keep, send, total):
            total[...] = mine[...] + theirs[...].astype(f32)
            self.emit(total, [i * self.each for i in range(blocks)], blocks * self.each, keep, send)

        (shape, _), _ = self.stage_shapes(blocks)
        return small_kernel(
            body, self.stage_shapes(blocks // 2), self.me, mine, theirs, scratch=[(shape, f32)]
        )

    def after_rest(self, mine, theirs):
        each = self.each
        at_norm = each + WOUT_PART
        ffn_rows = WOUT_PART + WIN_PART

        def body(me_ref, mine, theirs, attn, norm, ffn):
            total = mine[...] + theirs[...].astype(f32)
            attn[...] = total[0:each, 0:D]
            norm[...] = total[at_norm : at_norm + 8, 0:D] + total[at_norm + 8 : at_norm + 16, 0:D]
            ffn[0, 0:WOUT_PART, :] = total[each:at_norm, :].astype(bf16)
            ffn[0, WOUT_PART:, :] = total[at_norm + 16 :, :].astype(bf16)

        shapes = [((each, D), f32), ((8, D), f32), ((1, ffn_rows, 2 * FFH), bf16)]
        return small_kernel(body, shapes, self.me, mine, theirs)

    def spread(self, ffn):
        block = self.stack([ffn, self.swap(ffn, 4)])
        theirs = self.swap(block, TWIN)

        def body(me_ref, mine, theirs, win, wout, rows):
            for t, ref in enumerate((mine, theirs)):
                for i in range(2):
                    quarter = ((me_ref[0] % GROUP) ^ (4 * i) ^ (TWIN * t)) // 2
                    part = ref[i].astype(f32)
                    rows[ds(quarter * WOUT_PART, WOUT_PART, WOUT_PART), :] = part[:WOUT_PART, 0:D]
                    for g in range(2):
                        there = pl.ds(2 * WIN_PART * quarter + g, WIN_PART, stride=2)
                        win[there, :] = part[WOUT_PART:, FFH * g : FFH * (g + 1)]
            for layer in range(LAYERS):
                wout[layer] = rows[FFH * layer : FFH * (layer + 1), :].T

        shapes = [((2 * LAYERS * D, FFH), f32), ((LAYERS, D, FFH), f32)]
        scratch = [((LAYERS * FFH, D), f32)]
        return small_kernel(body, shapes, self.me, block, theirs, scratch=scratch)

    def sum_all(self, keep, send):
        keep, send = self.after_plane(self.across_plane(self.twins(keep, self.swap(send, TWIN))))
        blocks = self.upper // 2
        for bit in self.bits[:-1]:
            keep, send = self.after_bit(keep, self.swap(send, GROUP * bit), blocks)
            blocks //= 2
        attn, norm, ffn = self.after_rest(keep, self.swap(send, GROUP * self.bits[-1]))
        return attn, norm, *self.spread(ffn)


def on_device(devices, tokens, attn_weights, norm_params, w_in, w_out, cotangent):
    each = attn_weights.shape[0]
    me = (lax.axis_index("dp") * 2 + lax.axis_index("narrow")).astype(jnp.int32).reshape(1)
    staged = devices % (2 * GROUP) == 0 and each % 16 == 0
    swap_halves = [(0, 1), (1, 0)]
    w_in = w_in.reshape(2 * LAYERS * D, FFH)
    w_out = w_out.transpose(0, 2, 1)
    w_in_other = lax.ppermute(w_in, "narrow", swap_halves)
    w_out_other = lax.ppermute(w_out, "narrow", swap_halves)
    ffn = (w_in, w_in_other, w_out, w_out_other)
    if not staged:
        attn_all = lax.all_gather(attn_weights, AXES, axis=0, tiled=True)
        res, ig, grads = run_main(me, tokens, cotangent, norm_params, ffn, (attn_all,), devices, None)
        d_attn, d_win, d_wout, sums = grads
        attn = lax.psum_scatter(d_attn, AXES, scatter_dimension=0, tiled=True)
        norm = lax.psum(sums, AXES)
        d_wout = d_wout.reshape(LAYERS, FF, D)
        own_in, other_in = d_win[:, :FF], d_win[:, FF:]
        own_out, other_out = d_wout[:, :FFH], d_wout[:, FFH:]
        win = lax.psum(own_in + lax.ppermute(other_in, "narrow", swap_halves), "dp")
        wout = lax.psum(own_out + lax.ppermute(other_out, "narrow", swap_halves), "dp")
        wout = wout.transpose(0, 2, 1)
    else:
        ex = Exchange(me, devices)
        attn_parts, attn_diffs, others = ex.gather(attn_weights, (w_in_other, w_out_other))
        ffn = (w_in, others[0], w_out, others[1])
        res, ig, grads = run_main(me, tokens, cotangent, norm_params, ffn, attn_parts, devices, attn_diffs)
        attn, norm, win, wout = ex.sum_all(*grads)
    return (
        res,
        ig,
        attn,
        norm[: 2 * NORMS].reshape(norm_params.shape),
        win.reshape(LAYERS, D, 2, FFH),
        wout.transpose(0, 2, 1),
    )


def solution(mesh):
    rows = P(("dp", "narrow"), None)
    hidden_in = P(None, None, None, "narrow")
    hidden_out = P(None, "narrow", None)
    devices = mesh.shape["dp"] * mesh.shape["narrow"]

    def per_device(*args):
        return on_device(devices, *args)

    return jax.shard_map(
        per_device,
        mesh=mesh,
        in_specs=(rows, rows, P(), hidden_in, hidden_out, rows),
        out_specs=(rows, rows, rows, P(), hidden_in, hidden_out),
        check_vma=False,
    )
```

```python
import math

import jax
import jax.numpy as jnp
from jax import lax
from jax.experimental import pallas as pl
from jax.experimental.pallas import tpu as pltpu
from jax.sharding import PartitionSpec as P

HEADS = 8
HEAD = 24
SLOT = 32
WIDE = HEADS * SLOT
D = HEADS * HEAD
FF = 256
FFH = FF // 2
LAYERS = 2
NORMS = 2 * LAYERS - 1
SEQ = 476
PAIRS = SEQ // 2
KEYS = 240
HALF = 256
LANES = 2 * HALF
EPS = 1e-05
SCALE = HEAD ** (-0.5)
LOG2E = math.log2(math.e)
ATTN_ROWS = LAYERS * 4 * D

GROUP = 8
NEAR = (0, 1, 4, 5)
TWIN = 2
WIN_PART = LAYERS * D // 4
WOUT_PART = LAYERS * FFH // 4
ATTN_PART = ATTN_ROWS // GROUP
OFF_WOUT = ATTN_PART
OFF_NORM = OFF_WOUT + WOUT_PART
OFF_WIN = OFF_NORM + 16
PAY_ROWS = OFF_WIN + WIN_PART

bf16 = jnp.bfloat16
f32 = jnp.float32
AXES = ("dp", "narrow")

VMEM_BYTES = 60 * 1024 * 1024


def mm(left, right):
    return jnp.dot(left, right, preferred_element_type=f32)


def mm_nt(left, right):
    return lax.dot_general(left, right, (((1,), (1,)), ((), ())), preferred_element_type=f32)


def sigmoid(value):
    return 0.5 + 0.5 * jnp.tanh(0.5 * value)


def fold_lanes(value):
    return value[:, 0:128] + value[:, 128:256] + value[:, 256:384] + value[:, 384:512]


def norm_forward(stream, gain, shift):
    center = stream - jnp.sum(stream, axis=0, keepdims=True) * (1.0 / D)
    inverse = lax.rsqrt(jnp.sum(center * center, axis=0, keepdims=True) * (1.0 / D) + EPS)
    unit = center * inverse
    return (unit * gain + shift, unit, inverse)


def norm_backward(grad, unit, inverse, gain):
    scaled = grad * gain
    mean = jnp.sum(scaled, axis=0, keepdims=True) * (1.0 / D)
    slope = jnp.sum(scaled * unit, axis=0, keepdims=True) * (1.0 / D)
    return inverse * (scaled - mean - unit * slope)


def tree_sum(parts):
    while len(parts) > 1:
        parts = [parts[i] + parts[i + 1] for i in range(0, len(parts), 2)]
    return parts[0]


def ds(start, size, step):
    return pl.ds(pl.multiple_of(start, step), size)


def take(refs, count):
    taken = refs[:count]
    del refs[:count]
    return taken


def pad_heads(matrix):
    gap = jnp.zeros((SLOT - HEAD, D), f32)
    slots = []
    for h in range(HEADS):
        slots += [matrix[HEAD * h : HEAD * (h + 1)], gap]
    return jnp.concatenate(slots, axis=0)


def slim_heads(matrix):
    return jnp.concatenate([matrix[SLOT * h : SLOT * h + HEAD] for h in range(HEADS)], axis=0)


def head_rows(h):
    return slice(SLOT * h, SLOT * (h + 1))


def sample_window(step, rows_total, align):
    base = step * PAIRS
    start = jnp.minimum(base // align * align, rows_total - HALF)
    return ds(start, HALF, align), base - start


def load_sample(ref, step, fill_first):
    window, shift = sample_window(step, ref.shape[0], 16)
    rows = pltpu.roll(ref[window, :].astype(f32), lax.rem(HALF - shift, HALF), 0)
    pair_row = lax.broadcasted_iota(jnp.int32, (HALF, 2 * D), 0)
    cols = jnp.where(pair_row < PAIRS, rows, rows[0:1] if fill_first else 0.0).T
    return jnp.concatenate([cols[:D], cols[D:]], axis=1)


def store_sample(ref, step, value):
    window, shift = sample_window(step, ref.shape[0], 16 if ref.dtype == bf16 else 8)
    cols = jnp.concatenate([value[:, :HALF], value[:, HALF:]], axis=0)
    rows = pltpu.roll(cols.T, shift, 0)
    pair_row = lax.broadcasted_iota(jnp.int32, (HALF, 2 * D), 0)
    here = jnp.logical_and(pair_row >= shift, pair_row < shift + PAIRS)
    ref[window, :] = jnp.where(here, rows, ref[window, :].astype(f32)).astype(ref.dtype)


def attention_forward(normed_b, wqkv_t, wo_t, state, kh_ref, v_ref):
    e_ref, vh_ref, q_ref, k_ref, ctx_ref, rinv_ref = state
    lane = lax.broadcasted_iota(jnp.int32, (WIDE, LANES), 1)
    slot_row = lax.broadcasted_iota(jnp.int32, (WIDE, LANES), 0) & (SLOT - 1)
    real = (lane & (HALF - 1)) < PAIRS
    ones_rows = jnp.logical_or(slot_row == HEAD, slot_row == HEAD + 1).astype(f32)
    qkv = mm(wqkv_t, normed_b)
    queries = (qkv[:WIDE] * (SCALE * LOG2E)).astype(bf16)
    q_ref[...] = queries
    keys = qkv[WIDE : 2 * WIDE].astype(bf16)
    k_ref[...] = keys
    values = jnp.where(real, qkv[2 * WIDE :] + ones_rows, 0.0).astype(bf16)
    v_ref[...] = values
    for tall, ref in ((keys.T, kh_ref), (values.T, vh_ref)):
        for h in range(HEADS):
            ref[h, 0:KEYS] = tall[0:KEYS, head_rows(h)]
            ref[h, KEYS:] = tall[HALF : HALF + KEYS, head_rows(h)]

    def scores_of(h):
        return mm(kh_ref[h], q_ref[head_rows(h), :])

    scores = scores_of(0)
    for h in range(HEADS):
        rows = head_rows(h)
        ahead = scores_of(h + 1) if h + 1 < HEADS else None
        top = jnp.max(scores, axis=0, keepdims=True)
        weights = jnp.exp2(scores - top).astype(bf16)
        e_ref[:, LANES * h : LANES * (h + 1)] = weights
        out = mm(v_ref[rows, 0:KEYS], weights[0:KEYS]) + mm(
            v_ref[rows, HALF : HALF + KEYS], weights[KEYS:]
        )
        inverse = 1.0 / out[HEAD : HEAD + 1]
        rinv_ref[h : h + 1, :] = inverse
        ctx_ref[rows, :] = out * inverse
        scores = ahead
    return mm(wo_t, ctx_ref[...].astype(bf16))


def attention_backward(grad_b, normed_b, wo, wqkv, state, work, sums):
    e_ref, vh_ref, q_ref, k_ref, ctx_ref, rinv_ref = state
    ds_ref, do_ref, do_all, q_all, dq_ref, dkv_ref = work
    d_wq, d_wkv, d_wo = sums
    head_row = lax.broadcasted_iota(jnp.int32, (SLOT, LANES), 0)
    lane_head = lax.broadcasted_iota(jnp.int32, (LANES, WIDE), 1) // SLOT
    key_row = lax.broadcasted_iota(jnp.int32, (2 * KEYS, WIDE), 0)
    real_key = jnp.where(key_row < KEYS, key_row, key_row - KEYS) < PAIRS

    def spread_heads(ref, tall):
        for h in range(HEADS):
            part = jnp.where(lane_head == h, tall, jnp.zeros_like(tall))
            ref[LANES * h : LANES * (h + 1), :] = part

    d_wo[...] += mm_nt(ctx_ref[...].astype(bf16), grad_b)
    d_context = mm(wo, grad_b)
    for h in range(HEADS):
        rows = head_rows(h)
        grad = (d_context[rows] * rinv_ref[h : h + 1, :]).astype(bf16).astype(f32)
        dot = -jnp.sum(grad[:HEAD] * ctx_ref[rows, :][:HEAD], axis=0, keepdims=True)
        dot_high = dot.astype(bf16).astype(f32)
        grad = jnp.where(head_row == HEAD, dot_high, grad)
        grad = jnp.where(head_row == HEAD + 1, dot - dot_high, grad)
        do_ref[rows, :] = grad.astype(bf16)
    spread_heads(do_all, do_ref[...].T)
    spread_heads(q_all, q_ref[...].T)

    for h in range(HEADS + 1):
        if h < HEADS:
            lanes = slice(LANES * h, LANES * (h + 1))
            grad_probs = mm(vh_ref[h], do_ref[head_rows(h), :])
            ds_ref[:, lanes] = e_ref[:, lanes] * grad_probs.astype(bf16)
        if h > 0:
            rows = head_rows(h - 1)
            lanes = slice(LANES * (h - 1), LANES * h)
            dq = mm(k_ref[rows, 0:KEYS], ds_ref[0:KEYS, lanes]) + mm(
                k_ref[rows, HALF : HALF + KEYS], ds_ref[KEYS:, lanes]
            )
            dq_ref[rows, :] = (dq * SCALE).astype(bf16)
    dk = (mm(ds_ref[...], q_all[...]) * (1.0 / LOG2E)).astype(bf16)
    dv = jnp.where(real_key, mm(e_ref[...], do_all[...]), 0.0).astype(bf16)
    for half in range(2):
        here = slice(half * KEYS, (half + 1) * KEYS)
        there = slice(half * HALF, half * HALF + KEYS)
        dkv_ref[there, 0:WIDE] = dk[here]
        dkv_ref[there, WIDE:] = dv[here]
    d_wq[...] += mm_nt(dq_ref[...], normed_b)
    d_wkv[...] += mm(normed_b, dkv_ref[...])
    return mm(wqkv[:, 0:WIDE], dq_ref[...]) + mm_nt(wqkv[:, WIDE:], dkv_ref[...])


def resplit(sums):
    high = sums.astype(bf16).astype(f32)
    return jnp.concatenate([high, sums - high], axis=0).astype(bf16)


def finish_attention(d_attn, sums):
    for layer in range(LAYERS):
        d_wq, d_wkv, d_wo = sums[layer]
        tall = d_wkv[...].T
        for j, source in enumerate((d_wq[...], tall[:WIDE], tall[WIDE:], d_wo[...])):
            slim = slim_heads(source)
            base = (4 * layer + j) * D
            d_attn[base : base + D, :] = slim.T if j < 3 else slim


def finish_norms(d_norm):
    sums = [jnp.sum(d_norm[j].T, axis=0, keepdims=True) for j in range(2 * NORMS)]
    return jnp.concatenate(sums + [jnp.zeros((8 - 2 * NORMS, D), f32)], axis=0)


def pack_gradients(outs, me, parts, d_attn, d_win, d_wout, norms):
    each, upper = ATTN_ROWS // parts, parts // GROUP
    norms = resplit(norms)
    for t, out in enumerate(outs):
        for j, k in enumerate(NEAR):
            kind = out.dtype
            low = (me % GROUP) ^ k ^ (TWIN * t)
            quarter = low // 2
            half = k % 2
            for u in range(upper):
                rows = d_attn[ds((u * GROUP + low) * each, each, each), :]
                out[j, u * each : (u + 1) * each, 0:D] = rows.astype(kind)
            first = (quarter // 2) * FF + half * FFH + (quarter % 2) * WOUT_PART
            out[j, OFF_WOUT:OFF_NORM, 0:D] = d_wout[ds(first, WOUT_PART, WOUT_PART), :].astype(kind)
            out[j, OFF_NORM:OFF_WIN, 0:D] = norms.astype(kind)
            rows = d_win[ds(quarter * WIN_PART, WIN_PART, WIN_PART), half * FF : (half + 1) * FF]
            out[j, OFF_WIN:PAY_ROWS, :] = rows.astype(kind)


STATE = [
    ((2 * KEYS, HEADS * LANES), bf16),
    ((HEADS, 2 * KEYS, SLOT), bf16),
    ((WIDE, LANES), bf16),
    ((WIDE, LANES), bf16),
    ((WIDE, LANES), f32),
    ((HEADS, LANES), f32),
]
WORK = [
    ((2 * KEYS, HEADS * LANES), bf16),
    ((WIDE, LANES), bf16),
    ((HEADS * LANES, WIDE), bf16),
    ((HEADS * LANES, WIDE), bf16),
    ((WIDE, LANES), bf16),
    ((LANES, 2 * WIDE), bf16),
]
SUMS = [((WIDE, D), f32), ((D, 2 * WIDE), f32), ((WIDE, D), f32)]
GRADS = [
    *SUMS,
    *SUMS,
    ((LAYERS * D, 2 * FF), f32),
    ((LAYERS * FF, D), f32),
    ((2 * NORMS, D, 128), f32),
    ((ATTN_ROWS, D), f32),
]
SCRATCH = [
    ((LAYERS, 3 * WIDE, D), bf16),
    ((LAYERS, D, 3 * WIDE), bf16),
    ((LAYERS, D, WIDE), bf16),
    ((LAYERS, WIDE, D), bf16),
    ((LAYERS, 2 * FF, D), bf16),
    ((LAYERS, D, 2 * FF), bf16),
    ((LAYERS, D, FF), bf16),
    ((LAYERS, FF, D), bf16),
    ((D, 8), f32),
    ((ATTN_ROWS, D), bf16),
    *GRADS,
    *STATE,
    *STATE,
    *WORK,
    ((HEADS, 2 * KEYS, SLOT), bf16),
    ((WIDE, LANES), bf16),
    ((LAYERS, 2 * FF, LANES), f32),
    ((2 * LAYERS * D, FFH), f32),
]


def main_kernel(parts, attn_diffs, *refs):
    refs = list(refs)
    me_ref, x_ref, g_ref, norm_ref, win_own, win_other, wout_own, wout_other = take(refs, 8)
    attn_refs = take(refs, len(attn_diffs) if attn_diffs else 1)
    res_ref, ig_ref = take(refs, 2)
    outs = take(refs, 2 if attn_diffs else 4)
    wqkv_t, wqkv, wo_t, wo, win_t, win, wout_t, wout, norm_t, attn_ref = take(refs, 10)
    sums = (take(refs, 3), take(refs, 3))
    d_win, d_wout, d_norm, d_attn = take(refs, 4)
    states = (take(refs, len(STATE)), take(refs, len(STATE)))
    work = take(refs, len(WORK))
    kh_ref, v_ref, mixed_ref, win_rows = refs
    dkv_ref = work[-1]
    step = pl.program_id(0)

    @pl.when(step == 0)
    def _():
        for ref in (*sums[0], *sums[1], d_win, d_wout, d_norm, dkv_ref):
            ref[...] = jnp.zeros_like(ref)
        if attn_diffs:
            me = me_ref[0]
            for ref, diffs in zip(attn_refs, attn_diffs, strict=True):
                each = ref.shape[1]
                for i, diff in enumerate(diffs):
                    attn_ref[ds((me ^ diff) * each, each, each), :] = ref[i]
        else:
            attn_ref[...] = attn_refs[0][...]
        norms = [norm_ref[i] for i in range(NORMS)]
        norm_t[...] = jnp.concatenate(norms + [jnp.zeros((8 - 2 * NORMS, D), f32)], axis=0).T
        for layer in range(LAYERS):
            for j in range(4):
                base = (4 * layer + j) * D
                matrix = attn_ref[base : base + D, :].astype(f32)
                if j < 3:
                    tall = pad_heads(matrix.T)
                    wqkv_t[layer, j * WIDE : (j + 1) * WIDE, :] = tall.astype(bf16)
                    wqkv[layer, :, j * WIDE : (j + 1) * WIDE] = tall.T.astype(bf16)
                else:
                    tall = pad_heads(matrix)
                    wo[layer] = tall.astype(bf16)
                    wo_t[layer] = tall.T.astype(bf16)
        for p, (w1, w2) in enumerate(((win_own, wout_own), (win_other, wout_other))):
            win_rows[...] = w1[...].astype(f32)
            for layer in range(LAYERS):
                for g in range(2):
                    part = win_rows[pl.ds(2 * layer * D + g, D, stride=2), :]
                    here = slice(p * FF + g * FFH, p * FF + (g + 1) * FFH)
                    win[layer, :, here] = part.astype(bf16)
                    win_t[layer, here, :] = part.T.astype(bf16)
                wout_t[layer, :, p * FFH : (p + 1) * FFH] = w2[layer]
                wout[layer, p * FFH : (p + 1) * FFH, :] = w2[layer].astype(f32).T.astype(bf16)

    def add_norm(index, grad, unit):
        d_norm[2 * index] += fold_lanes(grad * unit)
        d_norm[2 * index + 1] += fold_lanes(grad)

    def gain_of(index):
        return norm_t[:, 2 * index : 2 * index + 1]

    def shift_of(index):
        return norm_t[:, 2 * index + 1 : 2 * index + 2]

    kept = []
    normed_b = x_ref[0]
    stream = normed_b.astype(f32)
    unit_a = inv_a = None
    for layer in range(LAYERS):
        if layer > 0:
            normed, unit_a, inv_a = norm_forward(stream, gain_of(2 * layer - 1), shift_of(2 * layer - 1))
            normed_b = normed.astype(bf16)
        stream = stream + attention_forward(
            normed_b, wqkv_t[layer], wo_t[layer], states[layer], kh_ref, v_ref
        )
        normed, unit_f, inv_f = norm_forward(stream, gain_of(2 * layer), shift_of(2 * layer))
        ffn_b = normed.astype(bf16)
        mixed = mm(win_t[layer], ffn_b)
        mixed_ref[layer] = mixed
        hidden = []
        for p in range(2):
            value = mixed[FF * p : FF * p + FFH]
            gate = mixed[FF * p + FFH : FF * (p + 1)]
            hidden.append((value * (gate * sigmoid(gate))).astype(bf16))
        hidden = jnp.concatenate(hidden, axis=0)
        stream = stream + mm(wout_t[layer], hidden)
        kept.append((normed_b, unit_a, inv_a, ffn_b, unit_f, inv_f, hidden))
    res_ref[0] = stream.astype(bf16)

    grad = g_ref[0].astype(f32)
    for layer in reversed(range(LAYERS)):
        normed_b, unit_a, inv_a, ffn_b, unit_f, inv_f, hidden = kept[layer]
        grad_b = grad.astype(bf16)
        d_wout[FF * layer : FF * (layer + 1), :] += mm_nt(hidden, grad_b)
        d_hidden = mm(wout[layer], grad_b)
        d_mixed = []
        for p in range(2):
            value = mixed_ref[layer, FF * p : FF * p + FFH]
            gate = mixed_ref[layer, FF * p + FFH : FF * (p + 1)]
            part = d_hidden[FFH * p : FFH * (p + 1)]
            sig = sigmoid(gate)
            d_mixed.append((part * (gate * sig)).astype(bf16))
            d_mixed.append((part * value * sig * (1.0 + gate * (1.0 - sig))).astype(bf16))
        d_mixed = jnp.concatenate(d_mixed, axis=0)
        d_win[D * layer : D * (layer + 1), :] += mm_nt(ffn_b, d_mixed)
        d_normed = mm(win[layer], d_mixed)
        add_norm(2 * layer, d_normed, unit_f)
        grad = grad + norm_backward(d_normed, unit_f, inv_f, gain_of(2 * layer))
        d_att = attention_backward(
            grad.astype(bf16), normed_b, wo[layer], wqkv[layer], states[layer], work, sums[layer]
        )
        if layer > 0:
            add_norm(2 * layer - 1, d_att, unit_a)
            grad = grad + norm_backward(d_att, unit_a, inv_a, gain_of(2 * layer - 1))
        else:
            grad = grad + d_att
    ig_ref[0] = grad

    @pl.when(step == pl.num_programs(0) - 1)
    def _():
        finish_attention(d_attn, sums)
        norms = finish_norms(d_norm)
        if attn_diffs:
            pack_gradients(outs, me_ref[0], parts, d_attn, d_win, d_wout, norms)
        else:
            for out, value in zip(outs, (d_attn[...], d_win[...], d_wout[...], norms), strict=True):
                out[...] = value


VMEM = pl.BlockSpec(memory_space=pltpu.VMEM)
SMEM = pl.BlockSpec(memory_space=pltpu.SMEM)


def shapes_of(pairs):
    return [jax.ShapeDtypeStruct(*pair) for pair in pairs]


def vmem_of(pairs):
    return [pltpu.VMEM(*pair) for pair in pairs]


def per_sample():
    return pl.BlockSpec((1, D, LANES), lambda i: (i, 0, 0))


def to_columns(rows, fill_first):
    samples = rows.shape[0] // PAIRS

    def body(rows_ref, out_ref):
        out_ref[0] = load_sample(rows_ref, pl.program_id(0), fill_first).astype(bf16)

    return pl.pallas_call(
        body,
        grid=(samples,),
        in_specs=[VMEM],
        out_specs=per_sample(),
        out_shape=jax.ShapeDtypeStruct((samples, D, LANES), bf16),
        compiler_params=pltpu.CompilerParams(vmem_limit_bytes=32 * 1024 * 1024),
    )(rows)


def to_rows(columns):
    samples = columns.shape[0]

    def body(columns_ref, out_ref):
        store_sample(out_ref, pl.program_id(0), columns_ref[0].astype(f32))

    return pl.pallas_call(
        body,
        grid=(samples,),
        in_specs=[per_sample()],
        out_specs=VMEM,
        out_shape=jax.ShapeDtypeStruct((samples * PAIRS, 2 * D), columns.dtype),
        compiler_params=pltpu.CompilerParams(vmem_limit_bytes=32 * 1024 * 1024),
    )(columns)


def run_main(me, tokens, cotangent, norm_params, ffn, attn_parts, parts, attn_diffs):
    samples = tokens.shape[0]
    inputs = (norm_params, *ffn, *attn_parts)
    if attn_diffs:
        grads = [((len(NEAR), PAY_ROWS, 2 * FFH), bf16)] * 2
    else:
        grads = [((ATTN_ROWS, D), f32), GRADS[6], GRADS[7], ((8, D), f32)]

    def body(*refs):
        main_kernel(parts, attn_diffs, *refs)

    out_shape = [((samples, D, LANES), bf16), ((samples, D, LANES), f32), *grads]
    res, ig, *grads = pl.pallas_call(
        body,
        grid=(samples,),
        in_specs=[SMEM, per_sample(), per_sample()] + [VMEM] * len(inputs),
        out_specs=[per_sample(), per_sample()] + [VMEM] * len(grads),
        out_shape=shapes_of(out_shape),
        scratch_shapes=vmem_of(SCRATCH),
        compiler_params=pltpu.CompilerParams(
            dimension_semantics=("arbitrary",), vmem_limit_bytes=VMEM_BYTES
        ),
        cost_estimate=pl.CostEstimate(
            flops=samples * 5_000_000_000, bytes_accessed=20_000_000, transcendentals=0
        ),
    )(me, tokens, cotangent, *inputs)
    return res, ig, grads


def small_kernel(body, out_shape, *inputs, scratch=()):
    return pl.pallas_call(
        body,
        in_specs=[SMEM] + [VMEM] * (len(inputs) - 1),
        out_specs=[VMEM] * len(out_shape),
        out_shape=shapes_of(out_shape),
        scratch_shapes=vmem_of(scratch),
        compiler_params=pltpu.CompilerParams(vmem_limit_bytes=32 * 1024 * 1024),
    )(*inputs)


class Exchange:
    def __init__(self, me, parts):
        self.me = me
        self.parts = parts
        self.upper = parts // GROUP
        self.each = ATTN_ROWS // parts
        self.bits = [1 << i for i in range(self.upper.bit_length() - 1)]

    def swap(self, value, k):
        return lax.ppermute(value, AXES, [(i, i ^ k) for i in range(self.parts)])

    def stack(self, blocks):
        size, kind = blocks[0].shape, blocks[0].dtype
        count = math.prod(size[:-2])

        def body(me_ref, *refs):
            ins, out = refs[:-1], refs[-1]
            for i, ref in enumerate(ins):
                if len(size) == 2:
                    out[i] = ref[...]
                else:
                    out[i * count : (i + 1) * count] = ref[...]

        shape = (len(blocks) * count, *size[-2:])
        return small_kernel(body, [(shape, kind)], self.me, *blocks)[0]

    def gather(self, rows, beside_rest, beside_plane):
        far = [GROUP * u for u in range(self.upper)]
        landed = [rows] + [self.swap(rows, k) for k in far[1:]]
        landed, beside_rest = lax.optimization_barrier((landed, beside_rest))
        column = self.stack(landed)
        landed = [column] + [self.swap(column, k) for k in NEAR[1:]]
        landed, beside_plane = lax.optimization_barrier((landed, beside_plane))
        plane = self.stack(landed)
        diffs = [k ^ u for k in NEAR for u in far]
        parts, diffs = [plane, self.swap(plane, TWIN)], [diffs, [d ^ TWIN for d in diffs]]
        return parts, diffs, beside_rest, beside_plane

    def twins(self, mine, theirs):
        def body(me_ref, mine, theirs, *outs):
            for j, out in enumerate(outs):
                total = mine[j].astype(f32) + theirs[j].astype(f32)
                out[0:OFF_NORM] = total[0:OFF_NORM].astype(out.dtype)
                sums = total[OFF_NORM : OFF_NORM + 8] + total[OFF_NORM + 8 : OFF_WIN]
                out[OFF_NORM:OFF_WIN] = resplit(sums).astype(out.dtype)
                out[OFF_WIN:] = total[OFF_WIN:].astype(out.dtype)

        shape = (PAY_ROWS, 2 * FFH)
        shapes = [(shape, f32)] + [(shape, bf16)] * (len(NEAR) - 1)
        return small_kernel(body, shapes, self.me, mine, theirs)

    def across_plane(self, pieces):
        return [pieces[0]] + [self.swap(piece, k) for piece, k in zip(pieces[1:], NEAR[1:], strict=True)]

    def emit(self, total, blocks, at, keep, send):
        half = len(blocks) // 2
        each = self.each
        for out, rows in ((keep, blocks[:half]), (send, blocks[half:])):
            for i, row in enumerate(rows):
                out[i * each : (i + 1) * each, :] = total[ds(row, each, 8), :].astype(out.dtype)
        first = half * each
        last = at + OFF_NORM - OFF_WOUT
        norm = resplit(total[last : last + 8, :] + total[last + 8 : last + 16, :])
        rest = [
            total[at:last, :].astype(bf16),
            norm,
            total[last + 16 : at + PAY_ROWS - OFF_WOUT, :].astype(bf16),
        ]
        for out in (keep, send):
            row = first
            for part in rest:
                out[row : row + part.shape[0], :] = part.astype(out.dtype)
                row += part.shape[0]

    def stage_shapes(self, blocks):
        shape = (blocks * self.each + PAY_ROWS - OFF_WOUT, 2 * FFH)
        return [(shape, f32), (shape, bf16)]

    def after_plane(self, landed):
        def body(me_ref, *refs):
            ins, (keep, send, total) = refs[: len(NEAR)], refs[len(NEAR) :]
            total[...] = tree_sum([r[...].astype(f32) for r in ins])
            mine = me_ref[0] // GROUP
            order = [r for r in range(self.upper) if not r & 1] + [r for r in range(self.upper) if r & 1]
            self.emit(total, [(mine ^ r) * self.each for r in order], OFF_WOUT, keep, send)

        scratch = [((PAY_ROWS, 2 * FFH), f32)]
        return small_kernel(body, self.stage_shapes(self.upper // 2), self.me, *landed, scratch=scratch)

    def after_bit(self, mine, theirs, blocks):
        def body(me_ref, mine, theirs, keep, send, total):
            total[...] = mine[...] + theirs[...].astype(f32)
            self.emit(total, [i * self.each for i in range(blocks)], blocks * self.each, keep, send)

        (shape, _), _ = self.stage_shapes(blocks)
        return small_kernel(
            body, self.stage_shapes(blocks // 2), self.me, mine, theirs, scratch=[(shape, f32)]
        )

    def after_rest(self, mine, theirs):
        each = self.each
        at_norm = each + WOUT_PART
        ffn_rows = WOUT_PART + WIN_PART

        def body(me_ref, mine, theirs, attn, norm, ffn):
            total = mine[...] + theirs[...].astype(f32)
            attn[...] = total[0:each, 0:D]
            norm[...] = total[at_norm : at_norm + 8, 0:D] + total[at_norm + 8 : at_norm + 16, 0:D]
            ffn[0, 0:WOUT_PART, :] = total[each:at_norm, :].astype(bf16)
            ffn[0, WOUT_PART:, :] = total[at_norm + 16 :, :].astype(bf16)

        shapes = [((each, D), f32), ((8, D), f32), ((1, ffn_rows, 2 * FFH), bf16)]
        return small_kernel(body, shapes, self.me, mine, theirs)

    def spread(self, ffn):
        block = self.stack([ffn, self.swap(ffn, 4)])
        theirs = self.swap(block, TWIN)

        def body(me_ref, mine, theirs, win, wout, rows):
            for t, ref in enumerate((mine, theirs)):
                for i in range(2):
                    quarter = ((me_ref[0] % GROUP) ^ (4 * i) ^ (TWIN * t)) // 2
                    part = ref[i].astype(f32)
                    rows[ds(quarter * WOUT_PART, WOUT_PART, WOUT_PART), :] = part[:WOUT_PART, 0:D]
                    for g in range(2):
                        there = pl.ds(2 * WIN_PART * quarter + g, WIN_PART, stride=2)
                        win[there, :] = part[WOUT_PART:, FFH * g : FFH * (g + 1)]
            for layer in range(LAYERS):
                wout[layer] = rows[FFH * layer : FFH * (layer + 1), :].T

        shapes = [((2 * LAYERS * D, FFH), f32), ((LAYERS, D, FFH), f32)]
        scratch = [((LAYERS * FFH, D), f32)]
        return small_kernel(body, shapes, self.me, block, theirs, scratch=scratch)

    def sum_all(self, keep, send, res, ig):
        landed = self.across_plane(self.twins(keep, self.swap(send, TWIN)))
        landed, res = lax.optimization_barrier((landed, to_rows(res)))
        keep, send = self.after_plane(landed)
        blocks = self.upper // 2
        for bit in self.bits[:-1]:
            keep, send = self.after_bit(keep, self.swap(send, GROUP * bit), blocks)
            blocks //= 2
        theirs = self.swap(send, GROUP * self.bits[-1])
        theirs, ig = lax.optimization_barrier((theirs, to_rows(ig)))
        attn, norm, ffn = self.after_rest(keep, theirs)
        return res, ig, attn, norm, *self.spread(ffn)


def on_device(devices, tokens, attn_weights, norm_params, w_in, w_out, cotangent):
    each = attn_weights.shape[0]
    me = (lax.axis_index("dp") * 2 + lax.axis_index("narrow")).astype(jnp.int32).reshape(1)
    staged = devices % (2 * GROUP) == 0 and each % 16 == 0
    x_t = to_columns(tokens, True)
    g_t = to_columns(cotangent, False)
    swap_halves = [(0, 1), (1, 0)]
    w_in = w_in.reshape(2 * LAYERS * D, FFH)
    w_out = w_out.transpose(0, 2, 1)
    w_in_other = lax.ppermute(w_in, "narrow", swap_halves)
    w_out_other = lax.ppermute(w_out, "narrow", swap_halves)
    ffn = (w_in, w_in_other, w_out, w_out_other)
    if not staged:
        attn_all = lax.all_gather(attn_weights, AXES, axis=0, tiled=True)
        res, ig, grads = run_main(me, x_t, g_t, norm_params, ffn, (attn_all,), devices, None)
        res, ig = to_rows(res), to_rows(ig)
        d_attn, d_win, d_wout, sums = grads
        attn = lax.psum_scatter(d_attn, AXES, scatter_dimension=0, tiled=True)
        norm = lax.psum(sums, AXES)
        d_wout = d_wout.reshape(LAYERS, FF, D)
        own_in, other_in = d_win[:, :FF], d_win[:, FF:]
        own_out, other_out = d_wout[:, :FFH], d_wout[:, FFH:]
        win = lax.psum(own_in + lax.ppermute(other_in, "narrow", swap_halves), "dp")
        wout = lax.psum(own_out + lax.ppermute(other_out, "narrow", swap_halves), "dp")
        wout = wout.transpose(0, 2, 1)
    else:
        ex = Exchange(me, devices)
        attn_parts, attn_diffs, (x_t, *others), g_t = ex.gather(
            attn_weights, (x_t, w_in_other, w_out_other), g_t
        )
        ffn = (w_in, others[0], w_out, others[1])
        res, ig, grads = run_main(me, x_t, g_t, norm_params, ffn, attn_parts, devices, attn_diffs)
        res, ig, attn, norm, win, wout = ex.sum_all(*grads, res, ig)
    return (
        res,
        ig,
        attn,
        norm[: 2 * NORMS].reshape(norm_params.shape),
        win.reshape(LAYERS, D, 2, FFH),
        wout.transpose(0, 2, 1),
    )


def solution(mesh):
    rows = P(("dp", "narrow"), None)
    hidden_in = P(None, None, None, "narrow")
    hidden_out = P(None, "narrow", None)
    devices = mesh.shape["dp"] * mesh.shape["narrow"]

    def per_device(*args):
        return on_device(devices, *args)

    return jax.shard_map(
        per_device,
        mesh=mesh,
        in_specs=(rows, rows, P(), hidden_in, hidden_out, rows),
        out_specs=(rows, rows, rows, P(), hidden_in, hidden_out),
        check_vma=False,
    )
```

```python
import math

import jax
import jax.numpy as jnp
from jax import lax
from jax.experimental import pallas as pl
from jax.experimental.pallas import tpu as pltpu
from jax.sharding import PartitionSpec as P

HEADS = 8
HEAD = 24
SLOT = 32
WIDE = HEADS * SLOT
D = HEADS * HEAD
FF = 256
FFH = FF // 2
LAYERS = 2
NORMS = 2 * LAYERS - 1
SEQ = 476
PAIRS = SEQ // 2
KEYS = 240
HALF = 256
LANES = 2 * HALF
EPS = 1e-05
SCALE = HEAD ** (-0.5)
LOG2E = math.log2(math.e)
ATTN_ROWS = LAYERS * 4 * D

GROUP = 8
NEAR = (0, 1, 4, 5)
TWIN = 2
WIN_PART = LAYERS * D // 4
WOUT_PART = LAYERS * FFH // 4
ATTN_PART = ATTN_ROWS // GROUP
OFF_WOUT = ATTN_PART
OFF_NORM = OFF_WOUT + WOUT_PART
OFF_WIN = OFF_NORM + 16
PAY_ROWS = OFF_WIN + WIN_PART

bf16 = jnp.bfloat16
f32 = jnp.float32
AXES = ("dp", "narrow")

VMEM_BYTES = 60 * 1024 * 1024


def mm(left, right):
    return jnp.dot(left, right, preferred_element_type=f32)


def mm_nt(left, right):
    return lax.dot_general(left, right, (((1,), (1,)), ((), ())), preferred_element_type=f32)


def sigmoid(value):
    return 0.5 + 0.5 * jnp.tanh(0.5 * value)


def fold_lanes(value):
    return value[:, 0:128] + value[:, 128:256] + value[:, 256:384] + value[:, 384:512]


def norm_forward(stream, gain, shift):
    center = stream - jnp.sum(stream, axis=0, keepdims=True) * (1.0 / D)
    inverse = lax.rsqrt(jnp.sum(center * center, axis=0, keepdims=True) * (1.0 / D) + EPS)
    unit = center * inverse
    return (unit * gain + shift, unit, inverse)


def norm_backward(grad, unit, inverse, gain):
    scaled = grad * gain
    mean = jnp.sum(scaled, axis=0, keepdims=True) * (1.0 / D)
    slope = jnp.sum(scaled * unit, axis=0, keepdims=True) * (1.0 / D)
    return inverse * (scaled - mean - unit * slope)


def tree_sum(parts):
    while len(parts) > 1:
        parts = [parts[i] + parts[i + 1] for i in range(0, len(parts), 2)]
    return parts[0]


def ds(start, size, step):
    return pl.ds(pl.multiple_of(start, step), size)


def take(refs, count):
    taken = refs[:count]
    del refs[:count]
    return taken


def unit(size):
    row = lax.broadcasted_iota(jnp.int32, (size, size), 0)
    column = lax.broadcasted_iota(jnp.int32, (size, size), 1)
    return (row == column).astype(f32).astype(bf16)


def head_selector(padded_axis):
    shape = (WIDE, D) if padded_axis == 0 else (D, WIDE)
    padded = lax.broadcasted_iota(jnp.int32, shape, padded_axis)
    plain = lax.broadcasted_iota(jnp.int32, shape, 1 - padded_axis)
    inside = padded & (SLOT - 1)
    same = jnp.logical_and(plain == HEAD * (padded >> 5) + inside, inside < HEAD)
    return same.astype(f32).astype(bf16)


def head_rows(h):
    return slice(SLOT * h, SLOT * (h + 1))


def sample_window(step, rows_total, align):
    base = step * PAIRS
    start = jnp.minimum(base // align * align, rows_total - HALF)
    return ds(start, HALF, align), base - start


def load_sample(ref, step, fill_first):
    window, shift = sample_window(step, ref.shape[0], 16)
    rows = pltpu.roll(ref[window, :].astype(f32), lax.rem(HALF - shift, HALF), 0)
    pair_row = lax.broadcasted_iota(jnp.int32, (HALF, 2 * D), 0)
    cols = jnp.where(pair_row < PAIRS, rows, rows[0:1] if fill_first else 0.0).T
    return jnp.concatenate([cols[:D], cols[D:]], axis=1)


def store_sample(ref, step, value):
    window, shift = sample_window(step, ref.shape[0], 16 if ref.dtype == bf16 else 8)
    cols = jnp.concatenate([value[:, :HALF], value[:, HALF:]], axis=0)
    rows = pltpu.roll(cols.T, shift, 0)
    pair_row = lax.broadcasted_iota(jnp.int32, (HALF, 2 * D), 0)
    here = jnp.logical_and(pair_row >= shift, pair_row < shift + PAIRS)
    ref[window, :] = jnp.where(here, rows, ref[window, :].astype(f32)).astype(ref.dtype)


def attention_forward(normed_b, wqkv_t, wo_t, state, kh_ref, v_ref):
    e_ref, vh_ref, q_ref, k_ref, ctx_ref, rinv_ref = state
    lane = lax.broadcasted_iota(jnp.int32, (WIDE, LANES), 1)
    slot_row = lax.broadcasted_iota(jnp.int32, (WIDE, LANES), 0) & (SLOT - 1)
    real = (lane & (HALF - 1)) < PAIRS
    ones_rows = jnp.logical_or(slot_row == HEAD, slot_row == HEAD + 1).astype(f32)
    qkv = mm(wqkv_t, normed_b)
    queries = (qkv[:WIDE] * (SCALE * LOG2E)).astype(bf16)
    q_ref[...] = queries
    keys = qkv[WIDE : 2 * WIDE].astype(bf16)
    k_ref[...] = keys
    values = jnp.where(real, qkv[2 * WIDE :] + ones_rows, 0.0).astype(bf16)
    v_ref[...] = values
    for tall, ref in ((keys.T, kh_ref), (values.T, vh_ref)):
        for h in range(HEADS):
            ref[h, 0:KEYS] = tall[0:KEYS, head_rows(h)]
            ref[h, KEYS:] = tall[HALF : HALF + KEYS, head_rows(h)]

    def scores_of(h):
        return mm(kh_ref[h], q_ref[head_rows(h), :])

    scores = scores_of(0)
    for h in range(HEADS):
        rows = head_rows(h)
        ahead = scores_of(h + 1) if h + 1 < HEADS else None
        top = jnp.max(scores, axis=0, keepdims=True)
        weights = jnp.exp2(scores - top).astype(bf16)
        e_ref[:, LANES * h : LANES * (h + 1)] = weights
        out = mm(v_ref[rows, 0:KEYS], weights[0:KEYS]) + mm(
            v_ref[rows, HALF : HALF + KEYS], weights[KEYS:]
        )
        inverse = 1.0 / out[HEAD : HEAD + 1]
        rinv_ref[h : h + 1, :] = inverse
        ctx_ref[rows, :] = out * inverse
        scores = ahead
    return mm(wo_t, ctx_ref[...].astype(bf16))


def attention_backward(grad_b, normed_b, wo, wqkv, state, work, sums):
    e_ref, vh_ref, q_ref, k_ref, ctx_ref, rinv_ref = state
    ds_ref, do_ref, do_all, q_all, dq_ref, dkv_ref = work
    d_wq, d_wkv, d_wo = sums
    head_row = lax.broadcasted_iota(jnp.int32, (SLOT, LANES), 0)
    key_row = lax.broadcasted_iota(jnp.int32, (2 * KEYS, WIDE), 0)
    real_key = jnp.where(key_row < KEYS, key_row, key_row - KEYS) < PAIRS

    def spread_heads(ref, tall):
        for h in range(HEADS):
            ref[LANES * h : LANES * (h + 1), head_rows(h)] = tall[:, head_rows(h)]

    d_wo[...] += mm_nt(ctx_ref[...].astype(bf16), grad_b)
    d_context = mm(wo, grad_b)
    for h in range(HEADS):
        rows = head_rows(h)
        grad = (d_context[rows] * rinv_ref[h : h + 1, :]).astype(bf16).astype(f32)
        dot = -jnp.sum(grad[:HEAD] * ctx_ref[rows, :][:HEAD], axis=0, keepdims=True)
        dot_high = dot.astype(bf16).astype(f32)
        grad = jnp.where(head_row == HEAD, dot_high, grad)
        grad = jnp.where(head_row == HEAD + 1, dot - dot_high, grad)
        do_ref[rows, :] = grad.astype(bf16)
    spread_heads(do_all, do_ref[...].T)
    spread_heads(q_all, q_ref[...].T)

    for h in range(HEADS + 1):
        if h < HEADS:
            lanes = slice(LANES * h, LANES * (h + 1))
            grad_probs = mm(vh_ref[h], do_ref[head_rows(h), :])
            ds_ref[:, lanes] = e_ref[:, lanes] * grad_probs.astype(bf16)
        if h > 0:
            rows = head_rows(h - 1)
            lanes = slice(LANES * (h - 1), LANES * h)
            dq = mm(k_ref[rows, 0:KEYS], ds_ref[0:KEYS, lanes]) + mm(
                k_ref[rows, HALF : HALF + KEYS], ds_ref[KEYS:, lanes]
            )
            dq_ref[rows, :] = (dq * SCALE).astype(bf16)
    dk = (mm(ds_ref[...], q_all[...]) * (1.0 / LOG2E)).astype(bf16)
    dv = jnp.where(real_key, mm(e_ref[...], do_all[...]), 0.0).astype(bf16)
    for half in range(2):
        here = slice(half * KEYS, (half + 1) * KEYS)
        there = slice(half * HALF, half * HALF + KEYS)
        dkv_ref[there, 0:WIDE] = dk[here]
        dkv_ref[there, WIDE:] = dv[here]
    d_wq[...] += mm_nt(normed_b, dq_ref[...])
    d_wkv[...] += mm(normed_b, dkv_ref[...])
    return mm(wqkv[:, 0:WIDE], dq_ref[...]) + mm_nt(wqkv[:, WIDE:], dkv_ref[...])


def resplit(sums):
    high = sums.astype(bf16).astype(f32)
    return jnp.concatenate([high, sums - high], axis=0).astype(bf16)


def finish_attention(d_attn, sums):
    tall, wide = head_selector(0), head_selector(1)
    for layer in range(LAYERS):
        d_wq, d_wkv, d_wo = sums[layer]
        sources = (d_wq[...], d_wkv[:, :WIDE], d_wkv[:, WIDE:], d_wo[...])
        for j, source in enumerate(sources):
            source = source.astype(bf16)
            base = (4 * layer + j) * D
            d_attn[base : base + D, :] = mm(source, tall) if j < 3 else mm(wide, source)


def finish_norms(d_norm):
    sums = [jnp.sum(d_norm[j].T, axis=0, keepdims=True) for j in range(2 * NORMS)]
    return jnp.concatenate(sums + [jnp.zeros((8 - 2 * NORMS, D), f32)], axis=0)


def pack_gradients(outs, me, parts, d_attn, d_win, d_wout, norms):
    each, upper = ATTN_ROWS // parts, parts // GROUP
    norms = resplit(norms)
    for t, out in enumerate(outs):
        for j, k in enumerate(NEAR):
            kind = out.dtype
            low = (me % GROUP) ^ k ^ (TWIN * t)
            quarter = low // 2
            half = k % 2
            for u in range(upper):
                rows = d_attn[ds((u * GROUP + low) * each, each, each), :]
                out[j, u * each : (u + 1) * each, 0:D] = rows.astype(kind)
            first = (quarter // 2) * FF + half * FFH + (quarter % 2) * WOUT_PART
            out[j, OFF_WOUT:OFF_NORM, 0:D] = d_wout[ds(first, WOUT_PART, WOUT_PART), :].astype(kind)
            out[j, OFF_NORM:OFF_WIN, 0:D] = norms.astype(kind)
            rows = d_win[ds(quarter * WIN_PART, WIN_PART, WIN_PART), half * FF : (half + 1) * FF]
            out[j, OFF_WIN:PAY_ROWS, :] = rows.astype(kind)


STATE = [
    ((2 * KEYS, HEADS * LANES), bf16),
    ((HEADS, 2 * KEYS, SLOT), bf16),
    ((WIDE, LANES), bf16),
    ((WIDE, LANES), bf16),
    ((WIDE, LANES), f32),
    ((HEADS, LANES), f32),
]
WORK = [
    ((2 * KEYS, HEADS * LANES), bf16),
    ((WIDE, LANES), bf16),
    ((HEADS * LANES, WIDE), bf16),
    ((HEADS * LANES, WIDE), bf16),
    ((WIDE, LANES), bf16),
    ((LANES, 2 * WIDE), bf16),
]
SUMS = [((D, WIDE), f32), ((D, 2 * WIDE), f32), ((WIDE, D), f32)]
GRADS = [
    *SUMS,
    *SUMS,
    ((LAYERS * D, 2 * FF), f32),
    ((LAYERS * FF, D), f32),
    ((2 * NORMS, D, 128), f32),
    ((ATTN_ROWS, D), f32),
]
SCRATCH = [
    ((LAYERS, 3 * WIDE, D), bf16),
    ((LAYERS, D, 3 * WIDE), bf16),
    ((LAYERS, D, WIDE), bf16),
    ((LAYERS, WIDE, D), bf16),
    ((LAYERS, 2 * FF, D), bf16),
    ((LAYERS, D, 2 * FF), bf16),
    ((LAYERS, D, FF), bf16),
    ((LAYERS, FF, D), bf16),
    ((2 * NORMS, D, 128), f32),
    ((ATTN_ROWS, D), bf16),
    *GRADS,
    *STATE,
    *STATE,
    *WORK,
    ((HEADS, 2 * KEYS, SLOT), bf16),
    ((WIDE, LANES), bf16),
    ((LAYERS, 2 * FF, LANES), f32),
    ((2 * LAYERS * D, FFH), f32),
]


def main_kernel(parts, attn_diffs, *refs):
    refs = list(refs)
    me_ref, x_ref, g_ref, norm_ref, win_own, win_other, wout_own, wout_other = take(refs, 8)
    attn_refs = take(refs, len(attn_diffs) if attn_diffs else 1)
    res_ref, ig_ref = take(refs, 2)
    outs = take(refs, 2 if attn_diffs else 4)
    wqkv_t, wqkv, wo_t, wo, win_t, win, wout_t, wout, norm_t, attn_ref = take(refs, 10)
    sums = (take(refs, 3), take(refs, 3))
    d_win, d_wout, d_norm, d_attn = take(refs, 4)
    states = (take(refs, len(STATE)), take(refs, len(STATE)))
    work = take(refs, len(WORK))
    kh_ref, v_ref, mixed_ref, win_rows = refs
    _, _, do_all, q_all, _, dkv_ref = work
    step = pl.program_id(0)

    @pl.when(step == 0)
    def _():
        for ref in (*sums[0], *sums[1], d_win, d_wout, d_norm, do_all, q_all, dkv_ref):
            ref[...] = jnp.zeros_like(ref)
        if attn_diffs:
            me = me_ref[0]
            for ref, diffs in zip(attn_refs, attn_diffs, strict=True):
                each = ref.shape[1]
                for i, diff in enumerate(diffs):
                    attn_ref[ds((me ^ diff) * each, each, each), :] = ref[i]
        else:
            attn_ref[...] = attn_refs[0][...]
        norms = [norm_ref[i] for i in range(NORMS)]
        turned = jnp.concatenate(norms + [jnp.zeros((8 - 2 * NORMS, D), f32)], axis=0).T
        for i in range(2 * NORMS):
            norm_t[i] = jnp.broadcast_to(turned[:, i : i + 1], (D, 128))
        tall, wide = head_selector(0), head_selector(1)
        for layer in range(LAYERS):
            for j in range(4):
                base = (4 * layer + j) * D
                matrix = attn_ref[base : base + D, :]
                if j < 3:
                    wqkv_t[layer, j * WIDE : (j + 1) * WIDE, :] = mm_nt(tall, matrix).astype(bf16)
                    wqkv[layer, :, j * WIDE : (j + 1) * WIDE] = mm(matrix, wide).astype(bf16)
                else:
                    padded = mm(tall, matrix).astype(bf16)
                    wo[layer] = padded
                    wo_t[layer] = mm_nt(unit(D), padded).astype(bf16)
        for p, (w1, w2) in enumerate(((win_own, wout_own), (win_other, wout_other))):
            win_rows[...] = w1[...].astype(f32)
            for layer in range(LAYERS):
                for g in range(2):
                    part = win_rows[pl.ds(2 * layer * D + g, D, stride=2), :].astype(bf16)
                    here = slice(p * FF + g * FFH, p * FF + (g + 1) * FFH)
                    win[layer, :, here] = part
                    win_t[layer, here, :] = mm_nt(unit(FFH), part).astype(bf16)
                wout_t[layer, :, p * FFH : (p + 1) * FFH] = w2[layer]
                wout[layer, p * FFH : (p + 1) * FFH, :] = mm_nt(unit(FFH), w2[layer]).astype(bf16)

    def add_norm(index, grad, unit):
        d_norm[2 * index] += fold_lanes(grad * unit)
        d_norm[2 * index + 1] += fold_lanes(grad)

    def gain_of(index):
        return jnp.concatenate([norm_t[2 * index]] * (LANES // 128), axis=1)

    def shift_of(index):
        return jnp.concatenate([norm_t[2 * index + 1]] * (LANES // 128), axis=1)

    kept = []
    normed_b = x_ref[0]
    stream = normed_b.astype(f32)
    unit_a = inv_a = None
    for layer in range(LAYERS):
        if layer > 0:
            normed, unit_a, inv_a = norm_forward(stream, gain_of(2 * layer - 1), shift_of(2 * layer - 1))
            normed_b = normed.astype(bf16)
        stream = stream + attention_forward(
            normed_b, wqkv_t[layer], wo_t[layer], states[layer], kh_ref, v_ref
        )
        normed, unit_f, inv_f = norm_forward(stream, gain_of(2 * layer), shift_of(2 * layer))
        ffn_b = normed.astype(bf16)
        mixed = mm(win_t[layer], ffn_b)
        mixed_ref[layer] = mixed
        hidden = []
        for p in range(2):
            value = mixed[FF * p : FF * p + FFH]
            gate = mixed[FF * p + FFH : FF * (p + 1)]
            hidden.append((value * (gate * sigmoid(gate))).astype(bf16))
        hidden = jnp.concatenate(hidden, axis=0)
        stream = stream + mm(wout_t[layer], hidden)
        kept.append((normed_b, unit_a, inv_a, ffn_b, unit_f, inv_f, hidden))
    res_ref[0] = stream.astype(bf16)

    grad = g_ref[0].astype(f32)
    for layer in reversed(range(LAYERS)):
        normed_b, unit_a, inv_a, ffn_b, unit_f, inv_f, hidden = kept[layer]
        grad_b = grad.astype(bf16)
        d_wout[FF * layer : FF * (layer + 1), :] += mm_nt(hidden, grad_b)
        d_hidden = mm(wout[layer], grad_b)
        d_mixed = []
        for p in range(2):
            value = mixed_ref[layer, FF * p : FF * p + FFH]
            gate = mixed_ref[layer, FF * p + FFH : FF * (p + 1)]
            part = d_hidden[FFH * p : FFH * (p + 1)]
            sig = sigmoid(gate)
            d_mixed.append((part * (gate * sig)).astype(bf16))
            d_mixed.append((part * value * sig * (1.0 + gate * (1.0 - sig))).astype(bf16))
        d_mixed = jnp.concatenate(d_mixed, axis=0)
        d_win[D * layer : D * (layer + 1), :] += mm_nt(ffn_b, d_mixed)
        d_normed = mm(win[layer], d_mixed)
        add_norm(2 * layer, d_normed, unit_f)
        grad = grad + norm_backward(d_normed, unit_f, inv_f, gain_of(2 * layer))
        d_att = attention_backward(
            grad.astype(bf16), normed_b, wo[layer], wqkv[layer], states[layer], work, sums[layer]
        )
        if layer > 0:
            add_norm(2 * layer - 1, d_att, unit_a)
            grad = grad + norm_backward(d_att, unit_a, inv_a, gain_of(2 * layer - 1))
        else:
            grad = grad + d_att
    ig_ref[0] = grad

    @pl.when(step == pl.num_programs(0) - 1)
    def _():
        finish_attention(d_attn, sums)
        norms = finish_norms(d_norm)
        if attn_diffs:
            pack_gradients(outs, me_ref[0], parts, d_attn, d_win, d_wout, norms)
        else:
            for out, value in zip(outs, (d_attn[...], d_win[...], d_wout[...], norms), strict=True):
                out[...] = value


VMEM = pl.BlockSpec(memory_space=pltpu.VMEM)
SMEM = pl.BlockSpec(memory_space=pltpu.SMEM)


def shapes_of(pairs):
    return [jax.ShapeDtypeStruct(*pair) for pair in pairs]


def vmem_of(pairs):
    return [pltpu.VMEM(*pair) for pair in pairs]


def per_sample():
    return pl.BlockSpec((1, D, LANES), lambda i: (i, 0, 0))


def to_columns(rows, fill_first):
    samples = rows.shape[0] // PAIRS

    def body(rows_ref, out_ref):
        out_ref[0] = load_sample(rows_ref, pl.program_id(0), fill_first).astype(bf16)

    return pl.pallas_call(
        body,
        grid=(samples,),
        in_specs=[VMEM],
        out_specs=per_sample(),
        out_shape=jax.ShapeDtypeStruct((samples, D, LANES), bf16),
        compiler_params=pltpu.CompilerParams(vmem_limit_bytes=32 * 1024 * 1024),
    )(rows)


def to_rows(columns):
    samples = columns.shape[0]

    def body(columns_ref, out_ref):
        store_sample(out_ref, pl.program_id(0), columns_ref[0].astype(f32))

    return pl.pallas_call(
        body,
        grid=(samples,),
        in_specs=[per_sample()],
        out_specs=VMEM,
        out_shape=jax.ShapeDtypeStruct((samples * PAIRS, 2 * D), columns.dtype),
        compiler_params=pltpu.CompilerParams(vmem_limit_bytes=32 * 1024 * 1024),
    )(columns)


def run_main(me, tokens, cotangent, norm_params, ffn, attn_parts, parts, attn_diffs):
    samples = tokens.shape[0]
    inputs = (norm_params, *ffn, *attn_parts)
    if attn_diffs:
        grads = [((len(NEAR), PAY_ROWS, 2 * FFH), bf16)] * 2
    else:
        grads = [((ATTN_ROWS, D), f32), GRADS[6], GRADS[7], ((8, D), f32)]

    def body(*refs):
        main_kernel(parts, attn_diffs, *refs)

    out_shape = [((samples, D, LANES), bf16), ((samples, D, LANES), f32), *grads]
    res, ig, *grads = pl.pallas_call(
        body,
        grid=(samples,),
        in_specs=[SMEM, per_sample(), per_sample()] + [VMEM] * len(inputs),
        out_specs=[per_sample(), per_sample()] + [VMEM] * len(grads),
        out_shape=shapes_of(out_shape),
        scratch_shapes=vmem_of(SCRATCH),
        compiler_params=pltpu.CompilerParams(
            dimension_semantics=("arbitrary",), vmem_limit_bytes=VMEM_BYTES
        ),
        cost_estimate=pl.CostEstimate(
            flops=samples * 5_000_000_000, bytes_accessed=20_000_000, transcendentals=0
        ),
    )(me, tokens, cotangent, *inputs)
    return res, ig, grads


def small_kernel(body, out_shape, *inputs, scratch=()):
    return pl.pallas_call(
        body,
        in_specs=[SMEM] + [VMEM] * (len(inputs) - 1),
        out_specs=[VMEM] * len(out_shape),
        out_shape=shapes_of(out_shape),
        scratch_shapes=vmem_of(scratch),
        compiler_params=pltpu.CompilerParams(vmem_limit_bytes=32 * 1024 * 1024),
    )(*inputs)


class Exchange:
    def __init__(self, me, parts):
        self.me = me
        self.parts = parts
        self.upper = parts // GROUP
        self.each = ATTN_ROWS // parts
        self.bits = [1 << i for i in range(self.upper.bit_length() - 1)]

    def swap(self, value, k):
        return lax.ppermute(value, AXES, [(i, i ^ k) for i in range(self.parts)])

    def stack(self, blocks):
        size, kind = blocks[0].shape, blocks[0].dtype
        count = math.prod(size[:-2])

        def body(me_ref, *refs):
            ins, out = refs[:-1], refs[-1]
            for i, ref in enumerate(ins):
                if len(size) == 2:
                    out[i] = ref[...]
                else:
                    out[i * count : (i + 1) * count] = ref[...]

        shape = (len(blocks) * count, *size[-2:])
        return small_kernel(body, [(shape, kind)], self.me, *blocks)[0]

    def gather(self, rows, beside_rest, beside_plane):
        far = [GROUP * u for u in range(self.upper)]
        landed = [rows] + [self.swap(rows, k) for k in far[1:]]
        landed, beside_rest = lax.optimization_barrier((landed, beside_rest))
        column = self.stack(landed)
        landed = [column] + [self.swap(column, k) for k in NEAR[1:]]
        landed, beside_plane = lax.optimization_barrier((landed, beside_plane))
        plane = self.stack(landed)
        diffs = [k ^ u for k in NEAR for u in far]
        parts, diffs = [plane, self.swap(plane, TWIN)], [diffs, [d ^ TWIN for d in diffs]]
        return parts, diffs, beside_rest, beside_plane

    def twins(self, mine, theirs):
        def body(me_ref, mine, theirs, *outs):
            for j, out in enumerate(outs):
                total = mine[j].astype(f32) + theirs[j].astype(f32)
                out[0:OFF_NORM] = total[0:OFF_NORM].astype(out.dtype)
                sums = total[OFF_NORM : OFF_NORM + 8] + total[OFF_NORM + 8 : OFF_WIN]
                out[OFF_NORM:OFF_WIN] = resplit(sums).astype(out.dtype)
                out[OFF_WIN:] = total[OFF_WIN:].astype(out.dtype)

        shape = (PAY_ROWS, 2 * FFH)
        shapes = [(shape, f32)] + [(shape, bf16)] * (len(NEAR) - 1)
        return small_kernel(body, shapes, self.me, mine, theirs)

    def across_plane(self, pieces):
        return [pieces[0]] + [self.swap(piece, k) for piece, k in zip(pieces[1:], NEAR[1:], strict=True)]

    def emit(self, total, blocks, at, keep, send):
        half = len(blocks) // 2
        each = self.each
        for out, rows in ((keep, blocks[:half]), (send, blocks[half:])):
            for i, row in enumerate(rows):
                out[i * each : (i + 1) * each, :] = total[ds(row, each, 8), :].astype(out.dtype)
        first = half * each
        last = at + OFF_NORM - OFF_WOUT
        norm = resplit(total[last : last + 8, :] + total[last + 8 : last + 16, :])
        rest = [
            total[at:last, :].astype(bf16),
            norm,
            total[last + 16 : at + PAY_ROWS - OFF_WOUT, :].astype(bf16),
        ]
        for out in (keep, send):
            row = first
            for part in rest:
                out[row : row + part.shape[0], :] = part.astype(out.dtype)
                row += part.shape[0]

    def stage_shapes(self, blocks):
        shape = (blocks * self.each + PAY_ROWS - OFF_WOUT, 2 * FFH)
        return [(shape, f32), (shape, bf16)]

    def after_plane(self, landed):
        def body(me_ref, *refs):
            ins, (keep, send, total) = refs[: len(NEAR)], refs[len(NEAR) :]
            total[...] = tree_sum([r[...].astype(f32) for r in ins])
            mine = me_ref[0] // GROUP
            order = [r for r in range(self.upper) if not r & 1] + [r for r in range(self.upper) if r & 1]
            self.emit(total, [(mine ^ r) * self.each for r in order], OFF_WOUT, keep, send)

        scratch = [((PAY_ROWS, 2 * FFH), f32)]
        return small_kernel(body, self.stage_shapes(self.upper // 2), self.me, *landed, scratch=scratch)

    def after_bit(self, mine, theirs, blocks):
        def body(me_ref, mine, theirs, keep, send, total):
            total[...] = mine[...] + theirs[...].astype(f32)
            self.emit(total, [i * self.each for i in range(blocks)], blocks * self.each, keep, send)

        (shape, _), _ = self.stage_shapes(blocks)
        return small_kernel(
            body, self.stage_shapes(blocks // 2), self.me, mine, theirs, scratch=[(shape, f32)]
        )

    def after_rest(self, mine, theirs):
        each = self.each
        at_norm = each + WOUT_PART
        ffn_rows = WOUT_PART + WIN_PART

        def body(me_ref, mine, theirs, attn, norm, ffn):
            total = mine[...] + theirs[...].astype(f32)
            attn[...] = total[0:each, 0:D]
            norm[...] = total[at_norm : at_norm + 8, 0:D] + total[at_norm + 8 : at_norm + 16, 0:D]
            ffn[0, 0:WOUT_PART, :] = total[each:at_norm, :].astype(bf16)
            ffn[0, WOUT_PART:, :] = total[at_norm + 16 :, :].astype(bf16)

        shapes = [((each, D), f32), ((8, D), f32), ((1, ffn_rows, 2 * FFH), bf16)]
        return small_kernel(body, shapes, self.me, mine, theirs)

    def spread(self, ffn):
        block = self.stack([ffn, self.swap(ffn, 4)])
        theirs = self.swap(block, TWIN)

        def body(me_ref, mine, theirs, win, wout, rows):
            for t, ref in enumerate((mine, theirs)):
                for i in range(2):
                    quarter = ((me_ref[0] % GROUP) ^ (4 * i) ^ (TWIN * t)) // 2
                    part = ref[i].astype(f32)
                    rows[ds(quarter * WOUT_PART, WOUT_PART, WOUT_PART), :] = part[:WOUT_PART, 0:D]
                    for g in range(2):
                        there = pl.ds(2 * WIN_PART * quarter + g, WIN_PART, stride=2)
                        win[there, :] = part[WOUT_PART:, FFH * g : FFH * (g + 1)]
            for layer in range(LAYERS):
                wout[layer] = rows[FFH * layer : FFH * (layer + 1), :].T

        shapes = [((2 * LAYERS * D, FFH), f32), ((LAYERS, D, FFH), f32)]
        scratch = [((LAYERS * FFH, D), f32)]
        return small_kernel(body, shapes, self.me, block, theirs, scratch=scratch)

    def sum_all(self, keep, send, res, ig):
        landed = self.across_plane(self.twins(keep, self.swap(send, TWIN)))
        landed, res = lax.optimization_barrier((landed, to_rows(res)))
        keep, send = self.after_plane(landed)
        blocks = self.upper // 2
        for bit in self.bits[:-1]:
            keep, send = self.after_bit(keep, self.swap(send, GROUP * bit), blocks)
            blocks //= 2
        theirs = self.swap(send, GROUP * self.bits[-1])
        theirs, ig = lax.optimization_barrier((theirs, to_rows(ig)))
        attn, norm, ffn = self.after_rest(keep, theirs)
        return res, ig, attn, norm, *self.spread(ffn)


def on_device(devices, tokens, attn_weights, norm_params, w_in, w_out, cotangent):
    each = attn_weights.shape[0]
    me = (lax.axis_index("dp") * 2 + lax.axis_index("narrow")).astype(jnp.int32).reshape(1)
    staged = devices % (2 * GROUP) == 0 and each % 16 == 0
    x_t = to_columns(tokens, True)
    g_t = to_columns(cotangent, False)
    swap_halves = [(0, 1), (1, 0)]
    w_in = w_in.reshape(2 * LAYERS * D, FFH)
    w_out = w_out.transpose(0, 2, 1)
    w_in_other = lax.ppermute(w_in, "narrow", swap_halves)
    w_out_other = lax.ppermute(w_out, "narrow", swap_halves)
    ffn = (w_in, w_in_other, w_out, w_out_other)
    if not staged:
        attn_all = lax.all_gather(attn_weights, AXES, axis=0, tiled=True)
        res, ig, grads = run_main(me, x_t, g_t, norm_params, ffn, (attn_all,), devices, None)
        res, ig = to_rows(res), to_rows(ig)
        d_attn, d_win, d_wout, sums = grads
        attn = lax.psum_scatter(d_attn, AXES, scatter_dimension=0, tiled=True)
        norm = lax.psum(sums, AXES)
        d_wout = d_wout.reshape(LAYERS, FF, D)
        own_in, other_in = d_win[:, :FF], d_win[:, FF:]
        own_out, other_out = d_wout[:, :FFH], d_wout[:, FFH:]
        win = lax.psum(own_in + lax.ppermute(other_in, "narrow", swap_halves), "dp")
        wout = lax.psum(own_out + lax.ppermute(other_out, "narrow", swap_halves), "dp")
        wout = wout.transpose(0, 2, 1)
    else:
        ex = Exchange(me, devices)
        attn_parts, attn_diffs, (x_t, *others), g_t = ex.gather(
            attn_weights, (x_t, w_in_other, w_out_other), g_t
        )
        ffn = (w_in, others[0], w_out, others[1])
        res, ig, grads = run_main(me, x_t, g_t, norm_params, ffn, attn_parts, devices, attn_diffs)
        res, ig, attn, norm, win, wout = ex.sum_all(*grads, res, ig)
    return (
        res,
        ig,
        attn,
        norm[: 2 * NORMS].reshape(norm_params.shape),
        win.reshape(LAYERS, D, 2, FFH),
        wout.transpose(0, 2, 1),
    )


def solution(mesh):
    rows = P(("dp", "narrow"), None)
    hidden_in = P(None, None, None, "narrow")
    hidden_out = P(None, "narrow", None)
    devices = mesh.shape["dp"] * mesh.shape["narrow"]

    def per_device(*args):
        return on_device(devices, *args)

    return jax.shard_map(
        per_device,
        mesh=mesh,
        in_specs=(rows, rows, P(), hidden_in, hidden_out, rows),
        out_specs=(rows, rows, rows, P(), hidden_in, hidden_out),
        check_vma=False,
    )
```

```python
import math

import jax
import jax.numpy as jnp
from jax import lax
from jax.experimental import pallas as pl
from jax.experimental.pallas import tpu as pltpu
from jax.sharding import PartitionSpec as P

HEADS = 8
HEAD = 24
SLOT = 32
WIDE = HEADS * SLOT
D = HEADS * HEAD
FF = 256
FFH = FF // 2
LAYERS = 2
NORMS = 2 * LAYERS - 1
SEQ = 476
PAIRS = SEQ // 2
KEYS = 240
HALF = 256
LANES = 2 * HALF
EPS = 1e-05
SCALE = HEAD ** (-0.5)
LOG2E = math.log2(math.e)
ATTN_ROWS = LAYERS * 4 * D

GROUP = 8
NEAR = (0, 1, 4, 5)
TWIN = 2
WIN_PART = LAYERS * D // 4
WOUT_PART = LAYERS * FFH // 4
ATTN_PART = ATTN_ROWS // GROUP
OFF_WOUT = ATTN_PART
OFF_NORM = OFF_WOUT + WOUT_PART
OFF_WIN = OFF_NORM + 16
PAY_ROWS = OFF_WIN + WIN_PART

bf16 = jnp.bfloat16
f32 = jnp.float32
AXES = ("dp", "narrow")

VMEM_BYTES = 60 * 1024 * 1024


def mm(left, right):
    return jnp.dot(left, right, preferred_element_type=f32)


def mm_nt(left, right):
    return lax.dot_general(left, right, (((1,), (1,)), ((), ())), preferred_element_type=f32)


def sigmoid(value):
    return 0.5 + 0.5 * jnp.tanh(0.5 * value)


def fold_lanes(value):
    return value[:, 0:128] + value[:, 128:256] + value[:, 256:384] + value[:, 384:512]


def norm_forward(stream, gain, shift):
    center = stream - jnp.sum(stream, axis=0, keepdims=True) * (1.0 / D)
    inverse = lax.rsqrt(jnp.sum(center * center, axis=0, keepdims=True) * (1.0 / D) + EPS)
    unit = center * inverse
    return (unit * gain + shift, unit, inverse)


def norm_backward(grad, unit, inverse, gain):
    scaled = grad * gain
    mean = jnp.sum(scaled, axis=0, keepdims=True) * (1.0 / D)
    slope = jnp.sum(scaled * unit, axis=0, keepdims=True) * (1.0 / D)
    return inverse * (scaled - mean - unit * slope)


def tree_sum(parts):
    while len(parts) > 1:
        parts = [parts[i] + parts[i + 1] for i in range(0, len(parts), 2)]
    return parts[0]


def ds(start, size, step):
    return pl.ds(pl.multiple_of(start, step), size)


def take(refs, count):
    taken = refs[:count]
    del refs[:count]
    return taken


def unit(size):
    row = lax.broadcasted_iota(jnp.int32, (size, size), 0)
    column = lax.broadcasted_iota(jnp.int32, (size, size), 1)
    return (row == column).astype(f32).astype(bf16)


def head_selector(padded_axis):
    shape = (WIDE, D) if padded_axis == 0 else (D, WIDE)
    padded = lax.broadcasted_iota(jnp.int32, shape, padded_axis)
    plain = lax.broadcasted_iota(jnp.int32, shape, 1 - padded_axis)
    inside = padded & (SLOT - 1)
    same = jnp.logical_and(plain == HEAD * (padded >> 5) + inside, inside < HEAD)
    return same.astype(f32).astype(bf16)


def head_rows(h):
    return slice(SLOT * h, SLOT * (h + 1))


def sample_window(step, rows_total, align):
    base = step * PAIRS
    start = jnp.minimum(base // align * align, rows_total - HALF)
    return ds(start, HALF, align), base - start


def load_sample(ref, step, fill_first):
    window, shift = sample_window(step, ref.shape[0], 16)
    rows = pltpu.roll(ref[window, :].astype(f32), lax.rem(HALF - shift, HALF), 0)
    pair_row = lax.broadcasted_iota(jnp.int32, (HALF, 2 * D), 0)
    cols = jnp.where(pair_row < PAIRS, rows, rows[0:1] if fill_first else 0.0).T
    return jnp.concatenate([cols[:D], cols[D:]], axis=1)


def store_sample(ref, step, value):
    window, shift = sample_window(step, ref.shape[0], 16 if ref.dtype == bf16 else 8)
    cols = jnp.concatenate([value[:, :HALF], value[:, HALF:]], axis=0)
    rows = pltpu.roll(cols.T, shift, 0)
    pair_row = lax.broadcasted_iota(jnp.int32, (HALF, 2 * D), 0)
    here = jnp.logical_and(pair_row >= shift, pair_row < shift + PAIRS)
    ref[window, :] = jnp.where(here, rows, ref[window, :].astype(f32)).astype(ref.dtype)


def attention_forward(normed_b, wqkv_t, wo_t, state, kh_ref, v_ref):
    e_ref, vh_ref, q_ref, k_ref, ctx_ref, rinv_ref = state
    lane = lax.broadcasted_iota(jnp.int32, (WIDE, LANES), 1)
    slot_row = lax.broadcasted_iota(jnp.int32, (WIDE, LANES), 0) & (SLOT - 1)
    real = (lane & (HALF - 1)) < PAIRS
    ones_rows = jnp.logical_or(slot_row == HEAD, slot_row == HEAD + 1).astype(f32)
    qkv = mm(wqkv_t, normed_b)
    queries = (qkv[:WIDE] * (SCALE * LOG2E)).astype(bf16)
    q_ref[...] = queries
    keys = qkv[WIDE : 2 * WIDE].astype(bf16)
    k_ref[...] = keys
    values = jnp.where(real, qkv[2 * WIDE :] + ones_rows, 0.0).astype(bf16)
    v_ref[...] = values
    for tall, ref in ((keys.T, kh_ref), (values.T, vh_ref)):
        for h in range(HEADS):
            ref[h, 0:KEYS] = tall[0:KEYS, head_rows(h)]
            ref[h, KEYS:] = tall[HALF : HALF + KEYS, head_rows(h)]

    def scores_of(h):
        return mm(kh_ref[h], q_ref[head_rows(h), :])

    scores = scores_of(0)
    for h in range(HEADS):
        rows = head_rows(h)
        ahead = scores_of(h + 1) if h + 1 < HEADS else None
        top = jnp.max(scores, axis=0, keepdims=True)
        weights = jnp.exp2(scores - top).astype(bf16)
        e_ref[:, LANES * h : LANES * (h + 1)] = weights
        out = mm(v_ref[rows, 0:KEYS], weights[0:KEYS]) + mm(
            v_ref[rows, HALF : HALF + KEYS], weights[KEYS:]
        )
        inverse = 1.0 / out[HEAD : HEAD + 1]
        rinv_ref[h : h + 1, :] = inverse
        ctx_ref[rows, :] = out * inverse
        scores = ahead
    return mm(wo_t, ctx_ref[...].astype(bf16))


def attention_backward(grad_b, normed_b, wo, wqkv, state, work, sums):
    e_ref, vh_ref, q_ref, k_ref, ctx_ref, rinv_ref = state
    do_ref, dp_ref = work
    d_wqkv, d_wo = sums
    head_row = lax.broadcasted_iota(jnp.int32, (SLOT, LANES), 0)
    real_key = lax.broadcasted_iota(jnp.int32, (SLOT, KEYS), 1) < PAIRS

    d_wo[...] += mm_nt(ctx_ref[...].astype(bf16), grad_b)
    d_context = mm(wo, grad_b)
    for h in range(HEADS):
        rows = head_rows(h)
        grad = (d_context[rows] * rinv_ref[h : h + 1, :]).astype(bf16).astype(f32)
        dot = -jnp.sum(grad[:HEAD] * ctx_ref[rows, :][:HEAD], axis=0, keepdims=True)
        dot_high = dot.astype(bf16).astype(f32)
        grad = jnp.where(head_row == HEAD, dot_high, grad)
        grad = jnp.where(head_row == HEAD + 1, dot - dot_high, grad)
        do_ref[rows, :] = grad.astype(bf16)
    halves = [(slice(KEYS * i, KEYS * (i + 1)), slice(HALF * i, HALF * i + KEYS)) for i in range(2)]
    for h in range(HEADS):
        rows = head_rows(h)
        lanes = slice(LANES * h, LANES * (h + 1))
        weights = e_ref[:, lanes]
        d_scores = weights * mm(vh_ref[h], do_ref[rows, :]).astype(bf16)
        dq = 0.0
        for keys, there in halves:
            dq += mm(k_ref[rows, there], d_scores[keys])
            dk = mm_nt(q_ref[rows, :], d_scores[keys]) * (1.0 / LOG2E)
            dv = jnp.where(real_key, mm_nt(do_ref[rows, :], weights[keys]), 0.0)
            dp_ref[WIDE + SLOT * h : WIDE + SLOT * (h + 1), there] = dk.astype(bf16)
            dp_ref[2 * WIDE + SLOT * h : 2 * WIDE + SLOT * (h + 1), there] = dv.astype(bf16)
        dp_ref[rows, :] = (dq * SCALE).astype(bf16)
    d_wqkv[...] += mm_nt(normed_b, dp_ref[...])
    return mm(wqkv, dp_ref[...])


def resplit(sums):
    high = sums.astype(bf16).astype(f32)
    return jnp.concatenate([high, sums - high], axis=0).astype(bf16)


def finish_attention(d_attn, sums):
    tall, wide = head_selector(0), head_selector(1)
    for layer in range(LAYERS):
        d_wqkv, d_wo = sums[layer]
        sources = [d_wqkv[:, WIDE * j : WIDE * (j + 1)] for j in range(3)] + [d_wo[...]]
        for j, source in enumerate(sources):
            source = source.astype(bf16)
            base = (4 * layer + j) * D
            d_attn[base : base + D, :] = mm(source, tall) if j < 3 else mm(wide, source)


def finish_norms(d_norm):
    sums = [jnp.sum(d_norm[j].T, axis=0, keepdims=True) for j in range(2 * NORMS)]
    return jnp.concatenate(sums + [jnp.zeros((8 - 2 * NORMS, D), f32)], axis=0)


def pack_gradients(outs, me, parts, d_attn, d_win, d_wout, norms):
    each, upper = ATTN_ROWS // parts, parts // GROUP
    norms = resplit(norms)
    for t, out in enumerate(outs):
        for j, k in enumerate(NEAR):
            kind = out.dtype
            low = (me % GROUP) ^ k ^ (TWIN * t)
            quarter = low // 2
            half = k % 2
            for u in range(upper):
                rows = d_attn[ds((u * GROUP + low) * each, each, each), :]
                out[j, u * each : (u + 1) * each, 0:D] = rows.astype(kind)
            first = (quarter // 2) * FF + half * FFH + (quarter % 2) * WOUT_PART
            out[j, OFF_WOUT:OFF_NORM, 0:D] = d_wout[ds(first, WOUT_PART, WOUT_PART), :].astype(kind)
            out[j, OFF_NORM:OFF_WIN, 0:D] = norms.astype(kind)
            rows = d_win[ds(quarter * WIN_PART, WIN_PART, WIN_PART), half * FF : (half + 1) * FF]
            out[j, OFF_WIN:PAY_ROWS, :] = rows.astype(kind)


STATE = [
    ((2 * KEYS, HEADS * LANES), bf16),
    ((HEADS, 2 * KEYS, SLOT), bf16),
    ((WIDE, LANES), bf16),
    ((WIDE, LANES), bf16),
    ((WIDE, LANES), f32),
    ((HEADS, LANES), f32),
]
WORK = [((WIDE, LANES), bf16), ((3 * WIDE, LANES), bf16)]
SUMS = [((D, 3 * WIDE), f32), ((WIDE, D), f32)]
GRADS = [
    *SUMS,
    *SUMS,
    ((LAYERS * D, 2 * FF), f32),
    ((LAYERS * FF, D), f32),
    ((2 * NORMS, D, 128), f32),
    ((ATTN_ROWS, D), f32),
]
SCRATCH = [
    ((LAYERS, 3 * WIDE, D), bf16),
    ((LAYERS, D, 3 * WIDE), bf16),
    ((LAYERS, D, WIDE), bf16),
    ((LAYERS, WIDE, D), bf16),
    ((LAYERS, 2 * FF, D), bf16),
    ((LAYERS, D, 2 * FF), bf16),
    ((LAYERS, D, FF), bf16),
    ((LAYERS, FF, D), bf16),
    ((2 * NORMS, D, 128), f32),
    ((ATTN_ROWS, D), bf16),
    *GRADS,
    *STATE,
    *STATE,
    *WORK,
    ((HEADS, 2 * KEYS, SLOT), bf16),
    ((WIDE, LANES), bf16),
    ((LAYERS, 2 * FF, LANES), f32),
    ((2 * LAYERS * D, FFH), f32),
]


def main_kernel(parts, attn_diffs, *refs):
    refs = list(refs)
    me_ref, x_ref, g_ref, norm_ref, win_own, win_other, wout_own, wout_other = take(refs, 8)
    attn_refs = take(refs, len(attn_diffs) if attn_diffs else 1)
    res_ref, ig_ref = take(refs, 2)
    outs = take(refs, 2 if attn_diffs else 4)
    wqkv_t, wqkv, wo_t, wo, win_t, win, wout_t, wout, norm_t, attn_ref = take(refs, 10)
    sums = (take(refs, len(SUMS)), take(refs, len(SUMS)))
    d_win, d_wout, d_norm, d_attn = take(refs, 4)
    states = (take(refs, len(STATE)), take(refs, len(STATE)))
    work = take(refs, len(WORK))
    kh_ref, v_ref, mixed_ref, win_rows = refs
    step = pl.program_id(0)

    @pl.when(step == 0)
    def _():
        for ref in (*sums[0], *sums[1], d_win, d_wout, d_norm, work[-1]):
            ref[...] = jnp.zeros_like(ref)
        if attn_diffs:
            me = me_ref[0]
            for ref, diffs in zip(attn_refs, attn_diffs, strict=True):
                each = ref.shape[1]
                for i, diff in enumerate(diffs):
                    attn_ref[ds((me ^ diff) * each, each, each), :] = ref[i]
        else:
            attn_ref[...] = attn_refs[0][...]
        norms = [norm_ref[i] for i in range(NORMS)]
        turned = jnp.concatenate(norms + [jnp.zeros((8 - 2 * NORMS, D), f32)], axis=0).T
        for i in range(2 * NORMS):
            norm_t[i] = jnp.broadcast_to(turned[:, i : i + 1], (D, 128))
        tall, wide = head_selector(0), head_selector(1)
        for layer in range(LAYERS):
            for j in range(4):
                base = (4 * layer + j) * D
                matrix = attn_ref[base : base + D, :]
                if j < 3:
                    wqkv_t[layer, j * WIDE : (j + 1) * WIDE, :] = mm_nt(tall, matrix).astype(bf16)
                    wqkv[layer, :, j * WIDE : (j + 1) * WIDE] = mm(matrix, wide).astype(bf16)
                else:
                    padded = mm(tall, matrix).astype(bf16)
                    wo[layer] = padded
                    wo_t[layer] = mm_nt(unit(D), padded).astype(bf16)
        for p, (w1, w2) in enumerate(((win_own, wout_own), (win_other, wout_other))):
            win_rows[...] = w1[...].astype(f32)
            for layer in range(LAYERS):
                for g in range(2):
                    part = win_rows[pl.ds(2 * layer * D + g, D, stride=2), :].astype(bf16)
                    here = slice(p * FF + g * FFH, p * FF + (g + 1) * FFH)
                    win[layer, :, here] = part
                    win_t[layer, here, :] = mm_nt(unit(FFH), part).astype(bf16)
                wout_t[layer, :, p * FFH : (p + 1) * FFH] = w2[layer]
                wout[layer, p * FFH : (p + 1) * FFH, :] = mm_nt(unit(FFH), w2[layer]).astype(bf16)

    def add_norm(index, grad, unit):
        d_norm[2 * index] += fold_lanes(grad * unit)
        d_norm[2 * index + 1] += fold_lanes(grad)

    def gain_of(index):
        return jnp.concatenate([norm_t[2 * index]] * (LANES // 128), axis=1)

    def shift_of(index):
        return jnp.concatenate([norm_t[2 * index + 1]] * (LANES // 128), axis=1)

    kept = []
    normed_b = x_ref[0]
    stream = normed_b.astype(f32)
    unit_a = inv_a = None
    for layer in range(LAYERS):
        if layer > 0:
            normed, unit_a, inv_a = norm_forward(stream, gain_of(2 * layer - 1), shift_of(2 * layer - 1))
            normed_b = normed.astype(bf16)
        stream = stream + attention_forward(
            normed_b, wqkv_t[layer], wo_t[layer], states[layer], kh_ref, v_ref
        )
        normed, unit_f, inv_f = norm_forward(stream, gain_of(2 * layer), shift_of(2 * layer))
        ffn_b = normed.astype(bf16)
        mixed = mm(win_t[layer], ffn_b)
        mixed_ref[layer] = mixed
        hidden = []
        for p in range(2):
            value = mixed[FF * p : FF * p + FFH]
            gate = mixed[FF * p + FFH : FF * (p + 1)]
            hidden.append((value * (gate * sigmoid(gate))).astype(bf16))
        hidden = jnp.concatenate(hidden, axis=0)
        stream = stream + mm(wout_t[layer], hidden)
        kept.append((normed_b, unit_a, inv_a, ffn_b, unit_f, inv_f, hidden))
    res_ref[0] = stream.astype(bf16)

    grad = g_ref[0].astype(f32)
    for layer in reversed(range(LAYERS)):
        normed_b, unit_a, inv_a, ffn_b, unit_f, inv_f, hidden = kept[layer]
        grad_b = grad.astype(bf16)
        d_wout[FF * layer : FF * (layer + 1), :] += mm_nt(hidden, grad_b)
        d_hidden = mm(wout[layer], grad_b)
        d_mixed = []
        for p in range(2):
            value = mixed_ref[layer, FF * p : FF * p + FFH]
            gate = mixed_ref[layer, FF * p + FFH : FF * (p + 1)]
            part = d_hidden[FFH * p : FFH * (p + 1)]
            sig = sigmoid(gate)
            d_mixed.append((part * (gate * sig)).astype(bf16))
            d_mixed.append((part * value * sig * (1.0 + gate * (1.0 - sig))).astype(bf16))
        d_mixed = jnp.concatenate(d_mixed, axis=0)
        d_win[D * layer : D * (layer + 1), :] += mm_nt(ffn_b, d_mixed)
        d_normed = mm(win[layer], d_mixed)
        add_norm(2 * layer, d_normed, unit_f)
        grad = grad + norm_backward(d_normed, unit_f, inv_f, gain_of(2 * layer))
        d_att = attention_backward(
            grad.astype(bf16), normed_b, wo[layer], wqkv[layer], states[layer], work, sums[layer]
        )
        if layer > 0:
            add_norm(2 * layer - 1, d_att, unit_a)
            grad = grad + norm_backward(d_att, unit_a, inv_a, gain_of(2 * layer - 1))
        else:
            grad = grad + d_att
    ig_ref[0] = grad

    @pl.when(step == pl.num_programs(0) - 1)
    def _():
        finish_attention(d_attn, sums)
        norms = finish_norms(d_norm)
        if attn_diffs:
            pack_gradients(outs, me_ref[0], parts, d_attn, d_win, d_wout, norms)
        else:
            for out, value in zip(outs, (d_attn[...], d_win[...], d_wout[...], norms), strict=True):
                out[...] = value


VMEM = pl.BlockSpec(memory_space=pltpu.VMEM)
SMEM = pl.BlockSpec(memory_space=pltpu.SMEM)


def shapes_of(pairs):
    return [jax.ShapeDtypeStruct(*pair) for pair in pairs]


def vmem_of(pairs):
    return [pltpu.VMEM(*pair) for pair in pairs]


def per_sample():
    return pl.BlockSpec((1, D, LANES), lambda i: (i, 0, 0))


def to_columns(rows, fill_first):
    samples = rows.shape[0] // PAIRS

    def body(rows_ref, out_ref):
        out_ref[0] = load_sample(rows_ref, pl.program_id(0), fill_first).astype(bf16)

    return pl.pallas_call(
        body,
        grid=(samples,),
        in_specs=[VMEM],
        out_specs=per_sample(),
        out_shape=jax.ShapeDtypeStruct((samples, D, LANES), bf16),
        compiler_params=pltpu.CompilerParams(vmem_limit_bytes=32 * 1024 * 1024),
    )(rows)


def to_rows(columns):
    samples = columns.shape[0]

    def body(columns_ref, out_ref):
        store_sample(out_ref, pl.program_id(0), columns_ref[0].astype(f32))

    return pl.pallas_call(
        body,
        grid=(samples,),
        in_specs=[per_sample()],
        out_specs=VMEM,
        out_shape=jax.ShapeDtypeStruct((samples * PAIRS, 2 * D), columns.dtype),
        compiler_params=pltpu.CompilerParams(vmem_limit_bytes=32 * 1024 * 1024),
    )(columns)


def run_main(me, tokens, cotangent, norm_params, ffn, attn_parts, parts, attn_diffs):
    samples = tokens.shape[0]
    inputs = (norm_params, *ffn, *attn_parts)
    if attn_diffs:
        grads = [((len(NEAR), PAY_ROWS, 2 * FFH), bf16)] * 2
    else:
        grads = [((ATTN_ROWS, D), f32), GRADS[2 * len(SUMS)], GRADS[2 * len(SUMS) + 1], ((8, D), f32)]

    def body(*refs):
        main_kernel(parts, attn_diffs, *refs)

    out_shape = [((samples, D, LANES), bf16), ((samples, D, LANES), f32), *grads]
    res, ig, *grads = pl.pallas_call(
        body,
        grid=(samples,),
        in_specs=[SMEM, per_sample(), per_sample()] + [VMEM] * len(inputs),
        out_specs=[per_sample(), per_sample()] + [VMEM] * len(grads),
        out_shape=shapes_of(out_shape),
        scratch_shapes=vmem_of(SCRATCH),
        compiler_params=pltpu.CompilerParams(
            dimension_semantics=("arbitrary",), vmem_limit_bytes=VMEM_BYTES
        ),
        cost_estimate=pl.CostEstimate(
            flops=samples * 5_000_000_000, bytes_accessed=20_000_000, transcendentals=0
        ),
    )(me, tokens, cotangent, *inputs)
    return res, ig, grads


def small_kernel(body, out_shape, *inputs, scratch=()):
    return pl.pallas_call(
        body,
        in_specs=[SMEM] + [VMEM] * (len(inputs) - 1),
        out_specs=[VMEM] * len(out_shape),
        out_shape=shapes_of(out_shape),
        scratch_shapes=vmem_of(scratch),
        compiler_params=pltpu.CompilerParams(vmem_limit_bytes=32 * 1024 * 1024),
    )(*inputs)


class Exchange:
    def __init__(self, me, parts):
        self.me = me
        self.parts = parts
        self.upper = parts // GROUP
        self.each = ATTN_ROWS // parts
        self.bits = [1 << i for i in range(self.upper.bit_length() - 1)]

    def swap(self, value, k):
        return lax.ppermute(value, AXES, [(i, i ^ k) for i in range(self.parts)])

    def stack(self, blocks):
        size, kind = blocks[0].shape, blocks[0].dtype
        count = math.prod(size[:-2])

        def body(me_ref, *refs):
            ins, out = refs[:-1], refs[-1]
            for i, ref in enumerate(ins):
                if len(size) == 2:
                    out[i] = ref[...]
                else:
                    out[i * count : (i + 1) * count] = ref[...]

        shape = (len(blocks) * count, *size[-2:])
        return small_kernel(body, [(shape, kind)], self.me, *blocks)[0]

    def gather(self, rows, beside_rest, beside_plane):
        far = [GROUP * u for u in range(self.upper)]
        landed = [rows] + [self.swap(rows, k) for k in far[1:]]
        landed, beside_rest = lax.optimization_barrier((landed, beside_rest))
        column = self.stack(landed)
        landed = [column] + [self.swap(column, k) for k in NEAR[1:]]
        landed, beside_plane = lax.optimization_barrier((landed, beside_plane))
        plane = self.stack(landed)
        diffs = [k ^ u for k in NEAR for u in far]
        parts, diffs = [plane, self.swap(plane, TWIN)], [diffs, [d ^ TWIN for d in diffs]]
        return parts, diffs, beside_rest, beside_plane

    def twins(self, mine, theirs):
        def body(me_ref, mine, theirs, *outs):
            for j, out in enumerate(outs):
                total = mine[j].astype(f32) + theirs[j].astype(f32)
                out[0:OFF_NORM] = total[0:OFF_NORM].astype(out.dtype)
                sums = total[OFF_NORM : OFF_NORM + 8] + total[OFF_NORM + 8 : OFF_WIN]
                out[OFF_NORM:OFF_WIN] = resplit(sums).astype(out.dtype)
                out[OFF_WIN:] = total[OFF_WIN:].astype(out.dtype)

        shape = (PAY_ROWS, 2 * FFH)
        shapes = [(shape, f32)] + [(shape, bf16)] * (len(NEAR) - 1)
        return small_kernel(body, shapes, self.me, mine, theirs)

    def across_plane(self, pieces):
        return [pieces[0]] + [self.swap(piece, k) for piece, k in zip(pieces[1:], NEAR[1:], strict=True)]

    def emit(self, total, blocks, at, keep, send):
        half = len(blocks) // 2
        each = self.each
        for out, rows in ((keep, blocks[:half]), (send, blocks[half:])):
            for i, row in enumerate(rows):
                out[i * each : (i + 1) * each, :] = total[ds(row, each, 8), :].astype(out.dtype)
        first = half * each
        last = at + OFF_NORM - OFF_WOUT
        norm = resplit(total[last : last + 8, :] + total[last + 8 : last + 16, :])
        rest = [
            total[at:last, :].astype(bf16),
            norm,
            total[last + 16 : at + PAY_ROWS - OFF_WOUT, :].astype(bf16),
        ]
        for out in (keep, send):
            row = first
            for part in rest:
                out[row : row + part.shape[0], :] = part.astype(out.dtype)
                row += part.shape[0]

    def stage_shapes(self, blocks):
        shape = (blocks * self.each + PAY_ROWS - OFF_WOUT, 2 * FFH)
        return [(shape, f32), (shape, bf16)]

    def after_plane(self, landed):
        def body(me_ref, *refs):
            ins, (keep, send, total) = refs[: len(NEAR)], refs[len(NEAR) :]
            total[...] = tree_sum([r[...].astype(f32) for r in ins])
            mine = me_ref[0] // GROUP
            order = [r for r in range(self.upper) if not r & 1] + [r for r in range(self.upper) if r & 1]
            self.emit(total, [(mine ^ r) * self.each for r in order], OFF_WOUT, keep, send)

        scratch = [((PAY_ROWS, 2 * FFH), f32)]
        return small_kernel(body, self.stage_shapes(self.upper // 2), self.me, *landed, scratch=scratch)

    def after_bit(self, mine, theirs, blocks):
        def body(me_ref, mine, theirs, keep, send, total):
            total[...] = mine[...] + theirs[...].astype(f32)
            self.emit(total, [i * self.each for i in range(blocks)], blocks * self.each, keep, send)

        (shape, _), _ = self.stage_shapes(blocks)
        return small_kernel(
            body, self.stage_shapes(blocks // 2), self.me, mine, theirs, scratch=[(shape, f32)]
        )

    def after_rest(self, mine, theirs):
        each = self.each
        at_norm = each + WOUT_PART
        ffn_rows = WOUT_PART + WIN_PART

        def body(me_ref, mine, theirs, attn, norm, ffn):
            total = mine[...] + theirs[...].astype(f32)
            attn[...] = total[0:each, 0:D]
            norm[...] = total[at_norm : at_norm + 8, 0:D] + total[at_norm + 8 : at_norm + 16, 0:D]
            ffn[0, 0:WOUT_PART, :] = total[each:at_norm, :].astype(bf16)
            ffn[0, WOUT_PART:, :] = total[at_norm + 16 :, :].astype(bf16)

        shapes = [((each, D), f32), ((8, D), f32), ((1, ffn_rows, 2 * FFH), bf16)]
        return small_kernel(body, shapes, self.me, mine, theirs)

    def spread(self, ffn):
        block = self.stack([ffn, self.swap(ffn, 4)])
        theirs = self.swap(block, TWIN)

        def body(me_ref, mine, theirs, win, wout, rows):
            for t, ref in enumerate((mine, theirs)):
                for i in range(2):
                    quarter = ((me_ref[0] % GROUP) ^ (4 * i) ^ (TWIN * t)) // 2
                    part = ref[i].astype(f32)
                    rows[ds(quarter * WOUT_PART, WOUT_PART, WOUT_PART), :] = part[:WOUT_PART, 0:D]
                    for g in range(2):
                        there = pl.ds(2 * WIN_PART * quarter + g, WIN_PART, stride=2)
                        win[there, :] = part[WOUT_PART:, FFH * g : FFH * (g + 1)]
            for layer in range(LAYERS):
                wout[layer] = rows[FFH * layer : FFH * (layer + 1), :].T

        shapes = [((2 * LAYERS * D, FFH), f32), ((LAYERS, D, FFH), f32)]
        scratch = [((LAYERS * FFH, D), f32)]
        return small_kernel(body, shapes, self.me, block, theirs, scratch=scratch)

    def sum_all(self, keep, send, res, ig):
        landed = self.across_plane(self.twins(keep, self.swap(send, TWIN)))
        landed, res = lax.optimization_barrier((landed, to_rows(res)))
        keep, send = self.after_plane(landed)
        blocks = self.upper // 2
        for bit in self.bits[:-1]:
            keep, send = self.after_bit(keep, self.swap(send, GROUP * bit), blocks)
            blocks //= 2
        theirs = self.swap(send, GROUP * self.bits[-1])
        theirs, ig = lax.optimization_barrier((theirs, to_rows(ig)))
        attn, norm, ffn = self.after_rest(keep, theirs)
        return res, ig, attn, norm, *self.spread(ffn)


def on_device(devices, tokens, attn_weights, norm_params, w_in, w_out, cotangent):
    each = attn_weights.shape[0]
    me = (lax.axis_index("dp") * 2 + lax.axis_index("narrow")).astype(jnp.int32).reshape(1)
    staged = devices % (2 * GROUP) == 0 and each % 16 == 0
    x_t = to_columns(tokens, True)
    g_t = to_columns(cotangent, False)
    swap_halves = [(0, 1), (1, 0)]
    w_in = w_in.reshape(2 * LAYERS * D, FFH)
    w_out = w_out.transpose(0, 2, 1)
    w_in_other = lax.ppermute(w_in, "narrow", swap_halves)
    w_out_other = lax.ppermute(w_out, "narrow", swap_halves)
    ffn = (w_in, w_in_other, w_out, w_out_other)
    if not staged:
        attn_all = lax.all_gather(attn_weights, AXES, axis=0, tiled=True)
        res, ig, grads = run_main(me, x_t, g_t, norm_params, ffn, (attn_all,), devices, None)
        res, ig = to_rows(res), to_rows(ig)
        d_attn, d_win, d_wout, sums = grads
        attn = lax.psum_scatter(d_attn, AXES, scatter_dimension=0, tiled=True)
        norm = lax.psum(sums, AXES)
        d_wout = d_wout.reshape(LAYERS, FF, D)
        own_in, other_in = d_win[:, :FF], d_win[:, FF:]
        own_out, other_out = d_wout[:, :FFH], d_wout[:, FFH:]
        win = lax.psum(own_in + lax.ppermute(other_in, "narrow", swap_halves), "dp")
        wout = lax.psum(own_out + lax.ppermute(other_out, "narrow", swap_halves), "dp")
        wout = wout.transpose(0, 2, 1)
    else:
        ex = Exchange(me, devices)
        attn_parts, attn_diffs, (x_t, *others), g_t = ex.gather(
            attn_weights, (x_t, w_in_other, w_out_other), g_t
        )
        ffn = (w_in, others[0], w_out, others[1])
        res, ig, grads = run_main(me, x_t, g_t, norm_params, ffn, attn_parts, devices, attn_diffs)
        res, ig, attn, norm, win, wout = ex.sum_all(*grads, res, ig)
    return (
        res,
        ig,
        attn,
        norm[: 2 * NORMS].reshape(norm_params.shape),
        win.reshape(LAYERS, D, 2, FFH),
        wout.transpose(0, 2, 1),
    )


def solution(mesh):
    rows = P(("dp", "narrow"), None)
    hidden_in = P(None, None, None, "narrow")
    hidden_out = P(None, "narrow", None)
    devices = mesh.shape["dp"] * mesh.shape["narrow"]

    def per_device(*args):
        return on_device(devices, *args)

    return jax.shard_map(
        per_device,
        mesh=mesh,
        in_specs=(rows, rows, P(), hidden_in, hidden_out, rows),
        out_specs=(rows, rows, rows, P(), hidden_in, hidden_out),
        check_vma=False,
    )
```

```python
import math

import jax
import jax.numpy as jnp
from jax import lax
from jax.experimental import pallas as pl
from jax.experimental.pallas import tpu as pltpu
from jax.sharding import PartitionSpec as P

HEADS = 8
HEAD = 24
SLOT = 32
WIDE = HEADS * SLOT
D = HEADS * HEAD
FF = 256
FFH = FF // 2
LAYERS = 2
NORMS = 2 * LAYERS - 1
SEQ = 476
PAIRS = SEQ // 2
KEYS = 240
HALF = 256
LANES = 2 * HALF
EPS = 1e-05
SCALE = HEAD ** (-0.5)
LOG2E = math.log2(math.e)
ATTN_ROWS = LAYERS * 4 * D

GROUP = 8
NEAR = (0, 1, 4, 5)
TWIN = 2
WIN_PART = LAYERS * D // 4
WOUT_PART = LAYERS * FFH // 4
ATTN_PART = ATTN_ROWS // GROUP
OFF_WOUT = ATTN_PART
OFF_NORM = OFF_WOUT + WOUT_PART
OFF_WIN = OFF_NORM + 16
PAY_ROWS = OFF_WIN + WIN_PART

bf16 = jnp.bfloat16
f32 = jnp.float32
AXES = ("dp", "narrow")

VMEM_BYTES = 60 * 1024 * 1024


def mm(left, right):
    return jnp.dot(left, right, preferred_element_type=f32)


def mm_nt(left, right):
    return lax.dot_general(left, right, (((1,), (1,)), ((), ())), preferred_element_type=f32)


def sigmoid(value):
    return 0.5 + 0.5 * jnp.tanh(0.5 * value)


def fold_lanes(value):
    return value[:, 0:128] + value[:, 128:256] + value[:, 256:384] + value[:, 384:512]


def norm_forward(stream, gain, shift):
    center = stream - jnp.sum(stream, axis=0, keepdims=True) * (1.0 / D)
    inverse = lax.rsqrt(jnp.sum(center * center, axis=0, keepdims=True) * (1.0 / D) + EPS)
    unit = center * inverse
    return (unit * gain + shift, unit, inverse)


def norm_backward(grad, unit, inverse, gain):
    scaled = grad * gain
    mean = jnp.sum(scaled, axis=0, keepdims=True) * (1.0 / D)
    slope = jnp.sum(scaled * unit, axis=0, keepdims=True) * (1.0 / D)
    return inverse * (scaled - mean - unit * slope)


def tree_sum(parts):
    while len(parts) > 1:
        parts = [parts[i] + parts[i + 1] for i in range(0, len(parts), 2)]
    return parts[0]


def ds(start, size, step):
    return pl.ds(pl.multiple_of(start, step), size)


def take(refs, count):
    taken = refs[:count]
    del refs[:count]
    return taken


def unit(size):
    row = lax.broadcasted_iota(jnp.int32, (size, size), 0)
    column = lax.broadcasted_iota(jnp.int32, (size, size), 1)
    return (row == column).astype(f32).astype(bf16)


def head_selector(padded_axis):
    shape = (WIDE, D) if padded_axis == 0 else (D, WIDE)
    padded = lax.broadcasted_iota(jnp.int32, shape, padded_axis)
    plain = lax.broadcasted_iota(jnp.int32, shape, 1 - padded_axis)
    inside = padded & (SLOT - 1)
    same = jnp.logical_and(plain == HEAD * (padded >> 5) + inside, inside < HEAD)
    return same.astype(f32).astype(bf16)


def pair_selector(offset, padded_axis):
    shape = (2 * WIDE, D) if padded_axis == 0 else (D, 2 * WIDE)
    padded = lax.broadcasted_iota(jnp.int32, shape, padded_axis)
    plain = lax.broadcasted_iota(jnp.int32, shape, 1 - padded_axis)
    inside = (padded & (2 * SLOT - 1)) - offset
    same = jnp.logical_and(plain == HEAD * (padded >> 6) + inside, inside >= 0)
    return jnp.logical_and(same, inside < HEAD).astype(f32).astype(bf16)


def head_rows(h):
    return slice(SLOT * h, SLOT * (h + 1))


def sample_window(step, rows_total, align):
    base = step * PAIRS
    start = jnp.minimum(base // align * align, rows_total - HALF)
    return ds(start, HALF, align), base - start


def load_sample(ref, step, fill_first):
    window, shift = sample_window(step, ref.shape[0], 16)
    rows = pltpu.roll(ref[window, :].astype(f32), lax.rem(HALF - shift, HALF), 0)
    pair_row = lax.broadcasted_iota(jnp.int32, (HALF, 2 * D), 0)
    cols = jnp.where(pair_row < PAIRS, rows, rows[0:1] if fill_first else 0.0).T
    return jnp.concatenate([cols[:D], cols[D:]], axis=1)


def store_sample(ref, step, value):
    window, shift = sample_window(step, ref.shape[0], 16 if ref.dtype == bf16 else 8)
    cols = jnp.concatenate([value[:, :HALF], value[:, HALF:]], axis=0)
    rows = pltpu.roll(cols.T, shift, 0)
    pair_row = lax.broadcasted_iota(jnp.int32, (HALF, 2 * D), 0)
    here = jnp.logical_and(pair_row >= shift, pair_row < shift + PAIRS)
    ref[window, :] = jnp.where(here, rows, ref[window, :].astype(f32)).astype(ref.dtype)


def attention_forward(normed_b, wqkv_t, wo_t, state, kh_ref, v_ref):
    e_ref, vh_ref, q_ref, k_ref, ctx_ref, rinv_ref = state
    lane = lax.broadcasted_iota(jnp.int32, (WIDE, LANES), 1)
    slot_row = lax.broadcasted_iota(jnp.int32, (WIDE, LANES), 0) & (SLOT - 1)
    real = (lane & (HALF - 1)) < PAIRS
    ones_rows = jnp.logical_or(slot_row == HEAD, slot_row == HEAD + 1).astype(f32)
    qkv = mm(wqkv_t, normed_b)
    queries = (qkv[:WIDE] * (SCALE * LOG2E)).astype(bf16)
    q_ref[...] = queries
    keys = qkv[WIDE : 2 * WIDE].astype(bf16)
    k_ref[...] = keys
    values = jnp.where(real, qkv[2 * WIDE :] + ones_rows, 0.0).astype(bf16)
    v_ref[...] = values
    for tall, ref in ((keys.T, kh_ref), (values.T, vh_ref)):
        for h in range(HEADS):
            ref[h, 0:KEYS] = tall[0:KEYS, head_rows(h)]
            ref[h, KEYS:] = tall[HALF : HALF + KEYS, head_rows(h)]

    def scores_of(h):
        return mm(kh_ref[h], q_ref[head_rows(h), :])

    scores = scores_of(0)
    for h in range(HEADS):
        rows = head_rows(h)
        ahead = scores_of(h + 1) if h + 1 < HEADS else None
        top = jnp.max(scores, axis=0, keepdims=True)
        weights = jnp.exp2(scores - top).astype(bf16)
        e_ref[0 : 2 * KEYS, LANES * h : LANES * (h + 1)] = weights
        out = mm(v_ref[rows, 0:KEYS], weights[0:KEYS]) + mm(
            v_ref[rows, HALF : HALF + KEYS], weights[KEYS:]
        )
        inverse = 1.0 / out[HEAD : HEAD + 1]
        rinv_ref[h : h + 1, :] = inverse
        ctx_ref[rows, :] = out * inverse
        scores = ahead
    return mm(wo_t, ctx_ref[...].astype(bf16))


def attention_backward(grad_b, normed_b, wo, wq, wvk, state, work, sums):
    e_ref, vh_ref, q_ref, k_ref, ctx_ref, rinv_ref = state
    pair_ref, block_ref, dq_ref, dvk_ref = work
    d_wq, d_wvk, d_wo = sums
    group = HEADS // 2
    head_row = lax.broadcasted_iota(jnp.int32, (SLOT, LANES), 0)
    lane_head = lax.broadcasted_iota(jnp.int32, (LANES, 2 * SLOT * group), 1) // (2 * SLOT)
    key_row = lax.broadcasted_iota(jnp.int32, (2 * KEYS, 2 * SLOT * group), 0)
    real_key = jnp.where(key_row < KEYS, key_row, key_row - KEYS) < PAIRS
    in_pair = lax.broadcasted_iota(jnp.int32, (2 * KEYS, 2 * SLOT * group), 1) & (2 * SLOT - 1)

    d_wo[...] += mm_nt(ctx_ref[...].astype(bf16), grad_b)
    d_context = mm(wo, grad_b)
    for h in range(HEADS):
        rows = head_rows(h)
        grad = (d_context[rows] * rinv_ref[h : h + 1, :]).astype(bf16).astype(f32)
        dot = -jnp.sum(grad[:HEAD] * ctx_ref[rows, :][:HEAD], axis=0, keepdims=True)
        dot_high = dot.astype(bf16).astype(f32)
        grad = jnp.where(head_row == HEAD, dot_high, grad)
        grad = jnp.where(head_row == HEAD + 1, dot - dot_high, grad)
        pair_ref[2 * SLOT * h : 2 * SLOT * h + SLOT, :] = grad.astype(bf16)
        pair_ref[2 * SLOT * h + SLOT : 2 * SLOT * (h + 1), :] = q_ref[rows, :]
    tall = pair_ref[...].T
    for h in range(HEADS):
        part = tall[:, WIDE * (h // group) : WIDE * (h // group + 1)]
        block_ref[LANES * h : LANES * (h + 1), :] = jnp.where(
            lane_head == h % group, part, jnp.zeros_like(part)
        )

    for h in range(HEADS + 1):
        if h < HEADS:
            lanes = slice(LANES * h, LANES * (h + 1))
            grad_probs = mm(vh_ref[h], pair_ref[2 * SLOT * h : 2 * SLOT * h + SLOT, :])
            e_ref[2 * KEYS :, lanes] = e_ref[0 : 2 * KEYS, lanes] * grad_probs.astype(bf16)
        if h > 0:
            rows = head_rows(h - 1)
            lanes = slice(LANES * (h - 1), LANES * h)
            dq = mm(k_ref[rows, 0:KEYS], e_ref[2 * KEYS : 3 * KEYS, lanes]) + mm(
                k_ref[rows, HALF : HALF + KEYS], e_ref[3 * KEYS :, lanes]
            )
            dq_ref[rows, :] = (dq * SCALE).astype(bf16)
    for g in range(2):
        here = slice(group * LANES * g, group * LANES * (g + 1))
        both = mm(e_ref[:, here], block_ref[here, :])
        dv = jnp.where(real_key, both[: 2 * KEYS], 0.0)
        dk = both[2 * KEYS :] * (1.0 / LOG2E)
        dvk = jnp.where(in_pair < SLOT, dv, dk).astype(bf16)
        for half in range(2):
            there = slice(half * HALF, half * HALF + KEYS)
            dvk_ref[there, WIDE * g : WIDE * (g + 1)] = dvk[half * KEYS : (half + 1) * KEYS]
    d_wq[...] += mm_nt(normed_b, dq_ref[...])
    d_wvk[...] += mm(normed_b, dvk_ref[...])
    return mm(wq, dq_ref[...]) + mm_nt(wvk, dvk_ref[...])


def resplit(sums):
    high = sums.astype(bf16).astype(f32)
    return jnp.concatenate([high, sums - high], axis=0).astype(bf16)


def finish_attention(d_attn, sums):
    tall, wide = head_selector(0), head_selector(1)
    for layer in range(LAYERS):
        d_wq, d_wvk, d_wo = sums[layer]
        mixed = d_wvk[...].astype(bf16)
        base = 4 * layer * D
        d_attn[base : base + D, :] = mm(d_wq[...].astype(bf16), tall)
        d_attn[base + D : base + 2 * D, :] = mm(mixed, pair_selector(SLOT, 0))
        d_attn[base + 2 * D : base + 3 * D, :] = mm(mixed, pair_selector(0, 0))
        d_attn[base + 3 * D : base + 4 * D, :] = mm(wide, d_wo[...].astype(bf16))


def finish_norms(d_norm):
    sums = [jnp.sum(d_norm[j].T, axis=0, keepdims=True) for j in range(2 * NORMS)]
    return jnp.concatenate(sums + [jnp.zeros((8 - 2 * NORMS, D), f32)], axis=0)


def pack_gradients(outs, me, parts, d_attn, d_win, d_wout, norms):
    each, upper = ATTN_ROWS // parts, parts // GROUP
    norms = resplit(norms)
    for t, out in enumerate(outs):
        for j, k in enumerate(NEAR):
            kind = out.dtype
            low = (me % GROUP) ^ k ^ (TWIN * t)
            quarter = low // 2
            half = k % 2
            for u in range(upper):
                rows = d_attn[ds((u * GROUP + low) * each, each, each), :]
                out[j, u * each : (u + 1) * each, 0:D] = rows.astype(kind)
            first = (quarter // 2) * FF + half * FFH + (quarter % 2) * WOUT_PART
            out[j, OFF_WOUT:OFF_NORM, 0:D] = d_wout[ds(first, WOUT_PART, WOUT_PART), :].astype(kind)
            out[j, OFF_NORM:OFF_WIN, 0:D] = norms.astype(kind)
            rows = d_win[ds(quarter * WIN_PART, WIN_PART, WIN_PART), half * FF : (half + 1) * FF]
            out[j, OFF_WIN:PAY_ROWS, :] = rows.astype(kind)


STATE = [
    ((4 * KEYS, HEADS * LANES), bf16),
    ((HEADS, 2 * KEYS, SLOT), bf16),
    ((WIDE, LANES), bf16),
    ((WIDE, LANES), bf16),
    ((WIDE, LANES), f32),
    ((HEADS, LANES), f32),
]
WORK = [
    ((2 * WIDE, LANES), bf16),
    ((HEADS * LANES, WIDE), bf16),
    ((WIDE, LANES), bf16),
    ((LANES, 2 * WIDE), bf16),
]
SUMS = [((D, WIDE), f32), ((D, 2 * WIDE), f32), ((WIDE, D), f32)]
GRADS = [
    *SUMS,
    *SUMS,
    ((LAYERS * D, 2 * FF), f32),
    ((LAYERS * FF, D), f32),
    ((2 * NORMS, D, 128), f32),
    ((ATTN_ROWS, D), f32),
]
SCRATCH = [
    ((LAYERS, 3 * WIDE, D), bf16),
    ((LAYERS, D, WIDE), bf16),
    ((LAYERS, D, 2 * WIDE), bf16),
    ((LAYERS, D, WIDE), bf16),
    ((LAYERS, WIDE, D), bf16),
    ((LAYERS, 2 * FF, D), bf16),
    ((LAYERS, D, 2 * FF), bf16),
    ((LAYERS, D, FF), bf16),
    ((LAYERS, FF, D), bf16),
    ((2 * NORMS, D, 128), f32),
    ((ATTN_ROWS, D), bf16),
    *GRADS,
    *STATE,
    *STATE,
    *WORK,
    ((HEADS, 2 * KEYS, SLOT), bf16),
    ((WIDE, LANES), bf16),
    ((LAYERS, 2 * FF, LANES), f32),
    ((2 * LAYERS * D, FFH), f32),
]


def main_kernel(parts, attn_diffs, *refs):
    refs = list(refs)
    me_ref, x_ref, g_ref, norm_ref, win_own, win_other, wout_own, wout_other = take(refs, 8)
    attn_refs = take(refs, len(attn_diffs) if attn_diffs else 1)
    res_ref, ig_ref = take(refs, 2)
    outs = take(refs, 2 if attn_diffs else 4)
    wqkv_t, wq, wvk, wo_t, wo, win_t, win, wout_t, wout, norm_t, attn_ref = take(refs, 11)
    sums = (take(refs, 3), take(refs, 3))
    d_win, d_wout, d_norm, d_attn = take(refs, 4)
    states = (take(refs, len(STATE)), take(refs, len(STATE)))
    work = take(refs, len(WORK))
    kh_ref, v_ref, mixed_ref, win_rows = refs
    dvk_ref = work[-1]
    step = pl.program_id(0)

    @pl.when(step == 0)
    def _():
        for ref in (*sums[0], *sums[1], d_win, d_wout, d_norm, dvk_ref):
            ref[...] = jnp.zeros_like(ref)
        if attn_diffs:
            me = me_ref[0]
            for ref, diffs in zip(attn_refs, attn_diffs, strict=True):
                each = ref.shape[1]
                for i, diff in enumerate(diffs):
                    attn_ref[ds((me ^ diff) * each, each, each), :] = ref[i]
        else:
            attn_ref[...] = attn_refs[0][...]
        norms = [norm_ref[i] for i in range(NORMS)]
        turned = jnp.concatenate(norms + [jnp.zeros((8 - 2 * NORMS, D), f32)], axis=0).T
        for i in range(2 * NORMS):
            norm_t[i] = jnp.broadcast_to(turned[:, i : i + 1], (D, 128))
        tall, wide = head_selector(0), head_selector(1)
        for layer in range(LAYERS):
            for j in range(4):
                base = (4 * layer + j) * D
                matrix = attn_ref[base : base + D, :]
                if j < 3:
                    wqkv_t[layer, j * WIDE : (j + 1) * WIDE, :] = mm_nt(tall, matrix).astype(bf16)
                if j == 0:
                    wq[layer] = mm(matrix, wide).astype(bf16)
                elif j == 1:
                    turned_keys = mm(matrix, pair_selector(SLOT, 1))
                elif j == 2:
                    wvk[layer] = (turned_keys + mm(matrix, pair_selector(0, 1))).astype(bf16)
                else:
                    padded = mm(tall, matrix).astype(bf16)
                    wo[layer] = padded
                    wo_t[layer] = mm_nt(unit(D), padded).astype(bf16)
        for p, (w1, w2) in enumerate(((win_own, wout_own), (win_other, wout_other))):
            win_rows[...] = w1[...].astype(f32)
            for layer in range(LAYERS):
                for g in range(2):
                    part = win_rows[pl.ds(2 * layer * D + g, D, stride=2), :].astype(bf16)
                    here = slice(p * FF + g * FFH, p * FF + (g + 1) * FFH)
                    win[layer, :, here] = part
                    win_t[layer, here, :] = mm_nt(unit(FFH), part).astype(bf16)
                wout_t[layer, :, p * FFH : (p + 1) * FFH] = w2[layer]
                wout[layer, p * FFH : (p + 1) * FFH, :] = mm_nt(unit(FFH), w2[layer]).astype(bf16)

    def add_norm(index, grad, unit):
        d_norm[2 * index] += fold_lanes(grad * unit)
        d_norm[2 * index + 1] += fold_lanes(grad)

    def gain_of(index):
        return jnp.concatenate([norm_t[2 * index]] * (LANES // 128), axis=1)

    def shift_of(index):
        return jnp.concatenate([norm_t[2 * index + 1]] * (LANES // 128), axis=1)

    kept = []
    normed_b = x_ref[0]
    stream = normed_b.astype(f32)
    unit_a = inv_a = None
    for layer in range(LAYERS):
        if layer > 0:
            normed, unit_a, inv_a = norm_forward(stream, gain_of(2 * layer - 1), shift_of(2 * layer - 1))
            normed_b = normed.astype(bf16)
        stream = stream + attention_forward(
            normed_b, wqkv_t[layer], wo_t[layer], states[layer], kh_ref, v_ref
        )
        normed, unit_f, inv_f = norm_forward(stream, gain_of(2 * layer), shift_of(2 * layer))
        ffn_b = normed.astype(bf16)
        mixed = mm(win_t[layer], ffn_b)
        mixed_ref[layer] = mixed
        hidden = []
        for p in range(2):
            value = mixed[FF * p : FF * p + FFH]
            gate = mixed[FF * p + FFH : FF * (p + 1)]
            hidden.append((value * (gate * sigmoid(gate))).astype(bf16))
        hidden = jnp.concatenate(hidden, axis=0)
        stream = stream + mm(wout_t[layer], hidden)
        kept.append((normed_b, unit_a, inv_a, ffn_b, unit_f, inv_f, hidden))
    res_ref[0] = stream.astype(bf16)

    grad = g_ref[0].astype(f32)
    for layer in reversed(range(LAYERS)):
        normed_b, unit_a, inv_a, ffn_b, unit_f, inv_f, hidden = kept[layer]
        grad_b = grad.astype(bf16)
        d_wout[FF * layer : FF * (layer + 1), :] += mm_nt(hidden, grad_b)
        d_hidden = mm(wout[layer], grad_b)
        d_mixed = []
        for p in range(2):
            value = mixed_ref[layer, FF * p : FF * p + FFH]
            gate = mixed_ref[layer, FF * p + FFH : FF * (p + 1)]
            part = d_hidden[FFH * p : FFH * (p + 1)]
            sig = sigmoid(gate)
            d_mixed.append((part * (gate * sig)).astype(bf16))
            d_mixed.append((part * value * sig * (1.0 + gate * (1.0 - sig))).astype(bf16))
        d_mixed = jnp.concatenate(d_mixed, axis=0)
        d_win[D * layer : D * (layer + 1), :] += mm_nt(ffn_b, d_mixed)
        d_normed = mm(win[layer], d_mixed)
        add_norm(2 * layer, d_normed, unit_f)
        grad = grad + norm_backward(d_normed, unit_f, inv_f, gain_of(2 * layer))
        d_att = attention_backward(
            grad.astype(bf16), normed_b, wo[layer], wq[layer], wvk[layer], states[layer], work, sums[layer]
        )
        if layer > 0:
            add_norm(2 * layer - 1, d_att, unit_a)
            grad = grad + norm_backward(d_att, unit_a, inv_a, gain_of(2 * layer - 1))
        else:
            grad = grad + d_att
    ig_ref[0] = grad

    @pl.when(step == pl.num_programs(0) - 1)
    def _():
        finish_attention(d_attn, sums)
        norms = finish_norms(d_norm)
        if attn_diffs:
            pack_gradients(outs, me_ref[0], parts, d_attn, d_win, d_wout, norms)
        else:
            for out, value in zip(outs, (d_attn[...], d_win[...], d_wout[...], norms), strict=True):
                out[...] = value


VMEM = pl.BlockSpec(memory_space=pltpu.VMEM)
SMEM = pl.BlockSpec(memory_space=pltpu.SMEM)


def shapes_of(pairs):
    return [jax.ShapeDtypeStruct(*pair) for pair in pairs]


def vmem_of(pairs):
    return [pltpu.VMEM(*pair) for pair in pairs]


def per_sample():
    return pl.BlockSpec((1, D, LANES), lambda i: (i, 0, 0))


def to_columns(rows, fill_first):
    samples = rows.shape[0] // PAIRS

    def body(rows_ref, out_ref):
        out_ref[0] = load_sample(rows_ref, pl.program_id(0), fill_first).astype(bf16)

    return pl.pallas_call(
        body,
        grid=(samples,),
        in_specs=[VMEM],
        out_specs=per_sample(),
        out_shape=jax.ShapeDtypeStruct((samples, D, LANES), bf16),
        compiler_params=pltpu.CompilerParams(vmem_limit_bytes=32 * 1024 * 1024),
    )(rows)


def to_rows(columns):
    samples = columns.shape[0]

    def body(columns_ref, out_ref):
        store_sample(out_ref, pl.program_id(0), columns_ref[0].astype(f32))

    return pl.pallas_call(
        body,
        grid=(samples,),
        in_specs=[per_sample()],
        out_specs=VMEM,
        out_shape=jax.ShapeDtypeStruct((samples * PAIRS, 2 * D), columns.dtype),
        compiler_params=pltpu.CompilerParams(vmem_limit_bytes=32 * 1024 * 1024),
    )(columns)


def run_main(me, tokens, cotangent, norm_params, ffn, attn_parts, parts, attn_diffs):
    samples = tokens.shape[0]
    inputs = (norm_params, *ffn, *attn_parts)
    if attn_diffs:
        grads = [((len(NEAR), PAY_ROWS, 2 * FFH), bf16)] * 2
    else:
        grads = [((ATTN_ROWS, D), f32), GRADS[6], GRADS[7], ((8, D), f32)]

    def body(*refs):
        main_kernel(parts, attn_diffs, *refs)

    out_shape = [((samples, D, LANES), bf16), ((samples, D, LANES), f32), *grads]
    res, ig, *grads = pl.pallas_call(
        body,
        grid=(samples,),
        in_specs=[SMEM, per_sample(), per_sample()] + [VMEM] * len(inputs),
        out_specs=[per_sample(), per_sample()] + [VMEM] * len(grads),
        out_shape=shapes_of(out_shape),
        scratch_shapes=vmem_of(SCRATCH),
        compiler_params=pltpu.CompilerParams(
            dimension_semantics=("arbitrary",), vmem_limit_bytes=VMEM_BYTES
        ),
        cost_estimate=pl.CostEstimate(
            flops=samples * 5_000_000_000, bytes_accessed=20_000_000, transcendentals=0
        ),
    )(me, tokens, cotangent, *inputs)
    return res, ig, grads


def small_kernel(body, out_shape, *inputs, scratch=()):
    return pl.pallas_call(
        body,
        in_specs=[SMEM] + [VMEM] * (len(inputs) - 1),
        out_specs=[VMEM] * len(out_shape),
        out_shape=shapes_of(out_shape),
        scratch_shapes=vmem_of(scratch),
        compiler_params=pltpu.CompilerParams(vmem_limit_bytes=32 * 1024 * 1024),
    )(*inputs)


class Exchange:
    def __init__(self, me, parts):
        self.me = me
        self.parts = parts
        self.upper = parts // GROUP
        self.each = ATTN_ROWS // parts
        self.bits = [1 << i for i in range(self.upper.bit_length() - 1)]

    def swap(self, value, k):
        return lax.ppermute(value, AXES, [(i, i ^ k) for i in range(self.parts)])

    def stack(self, blocks):
        size, kind = blocks[0].shape, blocks[0].dtype
        count = math.prod(size[:-2])

        def body(me_ref, *refs):
            ins, out = refs[:-1], refs[-1]
            for i, ref in enumerate(ins):
                if len(size) == 2:
                    out[i] = ref[...]
                else:
                    out[i * count : (i + 1) * count] = ref[...]

        shape = (len(blocks) * count, *size[-2:])
        return small_kernel(body, [(shape, kind)], self.me, *blocks)[0]

    def gather(self, rows, beside_rest, beside_plane):
        far = [GROUP * u for u in range(self.upper)]
        landed = [rows] + [self.swap(rows, k) for k in far[1:]]
        landed, beside_rest = lax.optimization_barrier((landed, beside_rest))
        column = self.stack(landed)
        landed = [column] + [self.swap(column, k) for k in NEAR[1:]]
        landed, beside_plane = lax.optimization_barrier((landed, beside_plane))
        plane = self.stack(landed)
        diffs = [k ^ u for k in NEAR for u in far]
        parts, diffs = [plane, self.swap(plane, TWIN)], [diffs, [d ^ TWIN for d in diffs]]
        return parts, diffs, beside_rest, beside_plane

    def twins(self, mine, theirs):
        def body(me_ref, mine, theirs, *outs):
            for j, out in enumerate(outs):
                total = mine[j].astype(f32) + theirs[j].astype(f32)
                out[0:OFF_NORM] = total[0:OFF_NORM].astype(out.dtype)
                sums = total[OFF_NORM : OFF_NORM + 8] + total[OFF_NORM + 8 : OFF_WIN]
                out[OFF_NORM:OFF_WIN] = resplit(sums).astype(out.dtype)
                out[OFF_WIN:] = total[OFF_WIN:].astype(out.dtype)

        shape = (PAY_ROWS, 2 * FFH)
        shapes = [(shape, f32)] + [(shape, bf16)] * (len(NEAR) - 1)
        return small_kernel(body, shapes, self.me, mine, theirs)

    def across_plane(self, pieces):
        return [pieces[0]] + [self.swap(piece, k) for piece, k in zip(pieces[1:], NEAR[1:], strict=True)]

    def emit(self, total, blocks, at, keep, send):
        half = len(blocks) // 2
        each = self.each
        for out, rows in ((keep, blocks[:half]), (send, blocks[half:])):
            for i, row in enumerate(rows):
                out[i * each : (i + 1) * each, :] = total[ds(row, each, 8), :].astype(out.dtype)
        first = half * each
        last = at + OFF_NORM - OFF_WOUT
        norm = resplit(total[last : last + 8, :] + total[last + 8 : last + 16, :])
        rest = [
            total[at:last, :].astype(bf16),
            norm,
            total[last + 16 : at + PAY_ROWS - OFF_WOUT, :].astype(bf16),
        ]
        for out in (keep, send):
            row = first
            for part in rest:
                out[row : row + part.shape[0], :] = part.astype(out.dtype)
                row += part.shape[0]

    def stage_shapes(self, blocks):
        shape = (blocks * self.each + PAY_ROWS - OFF_WOUT, 2 * FFH)
        return [(shape, f32), (shape, bf16)]

    def after_plane(self, landed):
        def body(me_ref, *refs):
            ins, (keep, send, total) = refs[: len(NEAR)], refs[len(NEAR) :]
            total[...] = tree_sum([r[...].astype(f32) for r in ins])
            mine = me_ref[0] // GROUP
            order = [r for r in range(self.upper) if not r & 1] + [r for r in range(self.upper) if r & 1]
            self.emit(total, [(mine ^ r) * self.each for r in order], OFF_WOUT, keep, send)

        scratch = [((PAY_ROWS, 2 * FFH), f32)]
        return small_kernel(body, self.stage_shapes(self.upper // 2), self.me, *landed, scratch=scratch)

    def after_bit(self, mine, theirs, blocks):
        def body(me_ref, mine, theirs, keep, send, total):
            total[...] = mine[...] + theirs[...].astype(f32)
            self.emit(total, [i * self.each for i in range(blocks)], blocks * self.each, keep, send)

        (shape, _), _ = self.stage_shapes(blocks)
        return small_kernel(
            body, self.stage_shapes(blocks // 2), self.me, mine, theirs, scratch=[(shape, f32)]
        )

    def after_rest(self, mine, theirs):
        each = self.each
        at_norm = each + WOUT_PART
        ffn_rows = WOUT_PART + WIN_PART

        def body(me_ref, mine, theirs, attn, norm, ffn):
            total = mine[...] + theirs[...].astype(f32)
            attn[...] = total[0:each, 0:D]
            norm[...] = total[at_norm : at_norm + 8, 0:D] + total[at_norm + 8 : at_norm + 16, 0:D]
            ffn[0, 0:WOUT_PART, :] = total[each:at_norm, :].astype(bf16)
            ffn[0, WOUT_PART:, :] = total[at_norm + 16 :, :].astype(bf16)

        shapes = [((each, D), f32), ((8, D), f32), ((1, ffn_rows, 2 * FFH), bf16)]
        return small_kernel(body, shapes, self.me, mine, theirs)

    def spread(self, ffn):
        block = self.stack([ffn, self.swap(ffn, 4)])
        theirs = self.swap(block, TWIN)

        def body(me_ref, mine, theirs, win, wout, rows):
            for t, ref in enumerate((mine, theirs)):
                for i in range(2):
                    quarter = ((me_ref[0] % GROUP) ^ (4 * i) ^ (TWIN * t)) // 2
                    part = ref[i].astype(f32)
                    rows[ds(quarter * WOUT_PART, WOUT_PART, WOUT_PART), :] = part[:WOUT_PART, 0:D]
                    for g in range(2):
                        there = pl.ds(2 * WIN_PART * quarter + g, WIN_PART, stride=2)
                        win[there, :] = part[WOUT_PART:, FFH * g : FFH * (g + 1)]
            for layer in range(LAYERS):
                wout[layer] = rows[FFH * layer : FFH * (layer + 1), :].T

        shapes = [((2 * LAYERS * D, FFH), f32), ((LAYERS, D, FFH), f32)]
        scratch = [((LAYERS * FFH, D), f32)]
        return small_kernel(body, shapes, self.me, block, theirs, scratch=scratch)

    def sum_all(self, keep, send, res, ig):
        landed = self.across_plane(self.twins(keep, self.swap(send, TWIN)))
        landed, res = lax.optimization_barrier((landed, to_rows(res)))
        keep, send = self.after_plane(landed)
        blocks = self.upper // 2
        for bit in self.bits[:-1]:
            keep, send = self.after_bit(keep, self.swap(send, GROUP * bit), blocks)
            blocks //= 2
        theirs = self.swap(send, GROUP * self.bits[-1])
        theirs, ig = lax.optimization_barrier((theirs, to_rows(ig)))
        attn, norm, ffn = self.after_rest(keep, theirs)
        return res, ig, attn, norm, *self.spread(ffn)


def on_device(devices, tokens, attn_weights, norm_params, w_in, w_out, cotangent):
    each = attn_weights.shape[0]
    me = (lax.axis_index("dp") * 2 + lax.axis_index("narrow")).astype(jnp.int32).reshape(1)
    staged = devices % (2 * GROUP) == 0 and each % 16 == 0
    x_t = to_columns(tokens, True)
    g_t = to_columns(cotangent, False)
    swap_halves = [(0, 1), (1, 0)]
    w_in = w_in.reshape(2 * LAYERS * D, FFH)
    w_out = w_out.transpose(0, 2, 1)
    w_in_other = lax.ppermute(w_in, "narrow", swap_halves)
    w_out_other = lax.ppermute(w_out, "narrow", swap_halves)
    ffn = (w_in, w_in_other, w_out, w_out_other)
    if not staged:
        attn_all = lax.all_gather(attn_weights, AXES, axis=0, tiled=True)
        res, ig, grads = run_main(me, x_t, g_t, norm_params, ffn, (attn_all,), devices, None)
        res, ig = to_rows(res), to_rows(ig)
        d_attn, d_win, d_wout, sums = grads
        attn = lax.psum_scatter(d_attn, AXES, scatter_dimension=0, tiled=True)
        norm = lax.psum(sums, AXES)
        d_wout = d_wout.reshape(LAYERS, FF, D)
        own_in, other_in = d_win[:, :FF], d_win[:, FF:]
        own_out, other_out = d_wout[:, :FFH], d_wout[:, FFH:]
        win = lax.psum(own_in + lax.ppermute(other_in, "narrow", swap_halves), "dp")
        wout = lax.psum(own_out + lax.ppermute(other_out, "narrow", swap_halves), "dp")
        wout = wout.transpose(0, 2, 1)
    else:
        ex = Exchange(me, devices)
        attn_parts, attn_diffs, (x_t, *others), g_t = ex.gather(
            attn_weights, (x_t, w_in_other, w_out_other), g_t
        )
        ffn = (w_in, others[0], w_out, others[1])
        res, ig, grads = run_main(me, x_t, g_t, norm_params, ffn, attn_parts, devices, attn_diffs)
        res, ig, attn, norm, win, wout = ex.sum_all(*grads, res, ig)
    return (
        res,
        ig,
        attn,
        norm[: 2 * NORMS].reshape(norm_params.shape),
        win.reshape(LAYERS, D, 2, FFH),
        wout.transpose(0, 2, 1),
    )


def solution(mesh):
    rows = P(("dp", "narrow"), None)
    hidden_in = P(None, None, None, "narrow")
    hidden_out = P(None, "narrow", None)
    devices = mesh.shape["dp"] * mesh.shape["narrow"]

    def per_device(*args):
        return on_device(devices, *args)

    return jax.shard_map(
        per_device,
        mesh=mesh,
        in_specs=(rows, rows, P(), hidden_in, hidden_out, rows),
        out_specs=(rows, rows, rows, P(), hidden_in, hidden_out),
        check_vma=False,
    )
```

```python
import math

import jax
import jax.numpy as jnp
from jax import lax
from jax.experimental import pallas as pl
from jax.experimental.pallas import tpu as pltpu
from jax.sharding import PartitionSpec as P

HEADS = 8
HEAD = 24
SLOT = 32
WIDE = HEADS * SLOT
D = HEADS * HEAD
FF = 256
FFH = FF // 2
LAYERS = 2
NORMS = 2 * LAYERS - 1
SEQ = 476
PAIRS = SEQ // 2
KEYS = 240
HALF = 256
LANES = 2 * HALF
EPS = 1e-05
SCALE = HEAD ** (-0.5)
LOG2E = math.log2(math.e)
ATTN_ROWS = LAYERS * 4 * D

GROUP = 8
NEAR = (0, 1, 4, 5)
TWIN = 2
WIN_PART = LAYERS * D // 4
WOUT_PART = LAYERS * FFH // 4
ATTN_PART = ATTN_ROWS // GROUP
OFF_WOUT = ATTN_PART
OFF_NORM = OFF_WOUT + WOUT_PART
OFF_WIN = OFF_NORM + 16
PAY_ROWS = OFF_WIN + WIN_PART

bf16 = jnp.bfloat16
f32 = jnp.float32
AXES = ("dp", "narrow")

VMEM_BYTES = 60 * 1024 * 1024


def mm(left, right):
    return jnp.dot(left, right, preferred_element_type=f32)


def mm_nt(left, right):
    return lax.dot_general(left, right, (((1,), (1,)), ((), ())), preferred_element_type=f32)


def sigmoid(value):
    return 0.5 + 0.5 * jnp.tanh(0.5 * value)


def fold_lanes(value):
    return value[:, 0:128] + value[:, 128:256] + value[:, 256:384] + value[:, 384:512]


def norm_forward(stream, gain, shift):
    center = stream - jnp.sum(stream, axis=0, keepdims=True) * (1.0 / D)
    inverse = lax.rsqrt(jnp.sum(center * center, axis=0, keepdims=True) * (1.0 / D) + EPS)
    unit = center * inverse
    return (unit * gain + shift, unit, inverse)


def norm_backward(grad, unit, inverse, gain):
    scaled = grad * gain
    mean = jnp.sum(scaled, axis=0, keepdims=True) * (1.0 / D)
    slope = jnp.sum(scaled * unit, axis=0, keepdims=True) * (1.0 / D)
    return inverse * (scaled - mean - unit * slope)


def tree_sum(parts):
    while len(parts) > 1:
        parts = [parts[i] + parts[i + 1] for i in range(0, len(parts), 2)]
    return parts[0]


def ds(start, size, step):
    return pl.ds(pl.multiple_of(start, step), size)


def take(refs, count):
    taken = refs[:count]
    del refs[:count]
    return taken


def unit(size):
    row = lax.broadcasted_iota(jnp.int32, (size, size), 0)
    column = lax.broadcasted_iota(jnp.int32, (size, size), 1)
    return (row == column).astype(f32).astype(bf16)


def head_selector(padded_axis):
    shape = (WIDE, D) if padded_axis == 0 else (D, WIDE)
    padded = lax.broadcasted_iota(jnp.int32, shape, padded_axis)
    plain = lax.broadcasted_iota(jnp.int32, shape, 1 - padded_axis)
    inside = padded & (SLOT - 1)
    same = jnp.logical_and(plain == HEAD * (padded >> 5) + inside, inside < HEAD)
    return same.astype(f32).astype(bf16)


def pair_selector(offset, padded_axis):
    shape = (2 * WIDE, D) if padded_axis == 0 else (D, 2 * WIDE)
    padded = lax.broadcasted_iota(jnp.int32, shape, padded_axis)
    plain = lax.broadcasted_iota(jnp.int32, shape, 1 - padded_axis)
    inside = (padded & (2 * SLOT - 1)) - offset
    same = jnp.logical_and(plain == HEAD * (padded >> 6) + inside, inside >= 0)
    return jnp.logical_and(same, inside < HEAD).astype(f32).astype(bf16)


def head_rows(h):
    return slice(SLOT * h, SLOT * (h + 1))


def sample_window(step, rows_total, align):
    base = step * PAIRS
    start = jnp.minimum(base // align * align, rows_total - HALF)
    return ds(start, HALF, align), base - start


def load_sample(ref, step, fill_first):
    window, shift = sample_window(step, ref.shape[0], 16)
    rows = pltpu.roll(ref[window, :].astype(f32), lax.rem(HALF - shift, HALF), 0)
    pair_row = lax.broadcasted_iota(jnp.int32, (HALF, 2 * D), 0)
    cols = jnp.where(pair_row < PAIRS, rows, rows[0:1] if fill_first else 0.0).T
    return jnp.concatenate([cols[:D], cols[D:]], axis=1)


def store_sample(ref, step, value):
    window, shift = sample_window(step, ref.shape[0], 16 if ref.dtype == bf16 else 8)
    cols = jnp.concatenate([value[:, :HALF], value[:, HALF:]], axis=0)
    rows = pltpu.roll(cols.T, shift, 0)
    pair_row = lax.broadcasted_iota(jnp.int32, (HALF, 2 * D), 0)
    here = jnp.logical_and(pair_row >= shift, pair_row < shift + PAIRS)
    ref[window, :] = jnp.where(here, rows, ref[window, :].astype(f32)).astype(ref.dtype)


def attention_forward(normed_b, wqkv_t, wo_t, state, kh_ref, v_ref):
    e_ref, vh_ref, q_ref, k_ref, ctx_ref, rinv_ref = state
    lane = lax.broadcasted_iota(jnp.int32, (WIDE, LANES), 1)
    slot_row = lax.broadcasted_iota(jnp.int32, (WIDE, LANES), 0) & (SLOT - 1)
    real = (lane & (HALF - 1)) < PAIRS
    ones_rows = jnp.logical_or(slot_row == HEAD, slot_row == HEAD + 1).astype(f32)
    qkv = mm(wqkv_t, normed_b)
    queries = (qkv[:WIDE] * (SCALE * LOG2E)).astype(bf16)
    q_ref[...] = queries
    keys = qkv[WIDE : 2 * WIDE].astype(bf16)
    k_ref[...] = keys
    values = jnp.where(real, qkv[2 * WIDE :] + ones_rows, 0.0).astype(bf16)
    v_ref[...] = values
    for tall, ref in ((keys.T, kh_ref), (values.T, vh_ref)):
        for h in range(HEADS):
            ref[h, 0:KEYS] = tall[0:KEYS, head_rows(h)]
            ref[h, KEYS:] = tall[HALF : HALF + KEYS, head_rows(h)]

    def scores_of(h):
        return mm(kh_ref[h], q_ref[head_rows(h), :])

    scores = scores_of(0)
    for h in range(HEADS):
        rows = head_rows(h)
        ahead = scores_of(h + 1) if h + 1 < HEADS else None
        top = jnp.max(scores, axis=0, keepdims=True)
        weights = jnp.exp2((scores - top).astype(bf16))
        e_ref[0 : 2 * KEYS, LANES * h : LANES * (h + 1)] = weights
        out = mm(v_ref[rows, 0:KEYS], weights[0:KEYS]) + mm(
            v_ref[rows, HALF : HALF + KEYS], weights[KEYS:]
        )
        inverse = 1.0 / out[HEAD : HEAD + 1]
        rinv_ref[h : h + 1, :] = inverse
        ctx_ref[rows, :] = out * inverse
        scores = ahead
    return mm(wo_t, ctx_ref[...].astype(bf16))


def attention_backward(grad_b, normed_b, wo, wq, wvk, state, work, sums):
    e_ref, vh_ref, q_ref, k_ref, ctx_ref, rinv_ref = state
    pair_ref, block_ref, dq_ref, dvk_ref = work
    d_wq, d_wvk, d_wo = sums
    group = HEADS // 2
    head_row = lax.broadcasted_iota(jnp.int32, (SLOT, LANES), 0)
    lane_head = lax.broadcasted_iota(jnp.int32, (LANES, 2 * SLOT * group), 1) // (2 * SLOT)
    key_row = lax.broadcasted_iota(jnp.int32, (2 * KEYS, 2 * SLOT * group), 0)
    real_key = jnp.where(key_row < KEYS, key_row, key_row - KEYS) < PAIRS
    in_pair = lax.broadcasted_iota(jnp.int32, (2 * KEYS, 2 * SLOT * group), 1) & (2 * SLOT - 1)

    d_wo[...] += mm_nt(ctx_ref[...].astype(bf16), grad_b)
    d_context = mm(wo, grad_b)
    for h in range(HEADS):
        rows = head_rows(h)
        grad = (d_context[rows] * rinv_ref[h : h + 1, :]).astype(bf16).astype(f32)
        dot = -jnp.sum(grad[:HEAD] * ctx_ref[rows, :][:HEAD], axis=0, keepdims=True)
        dot_high = dot.astype(bf16).astype(f32)
        grad = jnp.where(head_row == HEAD, dot_high, grad)
        grad = jnp.where(head_row == HEAD + 1, dot - dot_high, grad)
        pair_ref[2 * SLOT * h : 2 * SLOT * h + SLOT, :] = grad.astype(bf16)
        pair_ref[2 * SLOT * h + SLOT : 2 * SLOT * (h + 1), :] = q_ref[rows, :]
    tall = pair_ref[...].T
    for h in range(HEADS):
        part = tall[:, WIDE * (h // group) : WIDE * (h // group + 1)]
        block_ref[LANES * h : LANES * (h + 1), :] = jnp.where(
            lane_head == h % group, part, jnp.zeros_like(part)
        )

    for h in range(HEADS + 1):
        if h < HEADS:
            lanes = slice(LANES * h, LANES * (h + 1))
            grad_probs = mm(vh_ref[h], pair_ref[2 * SLOT * h : 2 * SLOT * h + SLOT, :])
            e_ref[2 * KEYS :, lanes] = e_ref[0 : 2 * KEYS, lanes] * grad_probs.astype(bf16)
        if h > 0:
            rows = head_rows(h - 1)
            lanes = slice(LANES * (h - 1), LANES * h)
            dq = mm(k_ref[rows, 0:KEYS], e_ref[2 * KEYS : 3 * KEYS, lanes]) + mm(
                k_ref[rows, HALF : HALF + KEYS], e_ref[3 * KEYS :, lanes]
            )
            dq_ref[rows, :] = (dq * SCALE).astype(bf16)
    for g in range(2):
        here = slice(group * LANES * g, group * LANES * (g + 1))
        both = mm(e_ref[:, here], block_ref[here, :])
        dv = jnp.where(real_key, both[: 2 * KEYS], 0.0)
        dk = both[2 * KEYS :] * (1.0 / LOG2E)
        dvk = jnp.where(in_pair < SLOT, dv, dk).astype(bf16)
        for half in range(2):
            there = slice(half * HALF, half * HALF + KEYS)
            dvk_ref[there, WIDE * g : WIDE * (g + 1)] = dvk[half * KEYS : (half + 1) * KEYS]
    d_wq[...] += mm_nt(normed_b, dq_ref[...])
    d_wvk[...] += mm(normed_b, dvk_ref[...])
    return mm(wq, dq_ref[...]) + mm_nt(wvk, dvk_ref[...])


def resplit(sums):
    high = sums.astype(bf16).astype(f32)
    return jnp.concatenate([high, sums - high], axis=0).astype(bf16)


def finish_attention(d_attn, sums):
    tall, wide = head_selector(0), head_selector(1)
    for layer in range(LAYERS):
        d_wq, d_wvk, d_wo = sums[layer]
        mixed = d_wvk[...].astype(bf16)
        base = 4 * layer * D
        d_attn[base : base + D, :] = mm(d_wq[...].astype(bf16), tall)
        d_attn[base + D : base + 2 * D, :] = mm(mixed, pair_selector(SLOT, 0))
        d_attn[base + 2 * D : base + 3 * D, :] = mm(mixed, pair_selector(0, 0))
        d_attn[base + 3 * D : base + 4 * D, :] = mm(wide, d_wo[...].astype(bf16))


def finish_norms(d_norm):
    sums = [jnp.sum(d_norm[j].T, axis=0, keepdims=True) for j in range(2 * NORMS)]
    return jnp.concatenate(sums + [jnp.zeros((8 - 2 * NORMS, D), f32)], axis=0)


def pack_gradients(outs, me, parts, d_attn, d_win, d_wout, norms):
    each, upper = ATTN_ROWS // parts, parts // GROUP
    norms = resplit(norms)
    for t, out in enumerate(outs):
        for j, k in enumerate(NEAR):
            kind = out.dtype
            low = (me % GROUP) ^ k ^ (TWIN * t)
            quarter = low // 2
            half = k % 2
            for u in range(upper):
                rows = d_attn[ds((u * GROUP + low) * each, each, each), :]
                out[j, u * each : (u + 1) * each, 0:D] = rows.astype(kind)
            first = (quarter // 2) * FF + half * FFH + (quarter % 2) * WOUT_PART
            out[j, OFF_WOUT:OFF_NORM, 0:D] = d_wout[ds(first, WOUT_PART, WOUT_PART), :].astype(kind)
            out[j, OFF_NORM:OFF_WIN, 0:D] = norms.astype(kind)
            rows = d_win[ds(quarter * WIN_PART, WIN_PART, WIN_PART), half * FF : (half + 1) * FF]
            out[j, OFF_WIN:PAY_ROWS, :] = rows.astype(kind)


STATE = [
    ((4 * KEYS, HEADS * LANES), bf16),
    ((HEADS, 2 * KEYS, SLOT), bf16),
    ((WIDE, LANES), bf16),
    ((WIDE, LANES), bf16),
    ((WIDE, LANES), f32),
    ((HEADS, LANES), f32),
]
WORK = [
    ((2 * WIDE, LANES), bf16),
    ((HEADS * LANES, WIDE), bf16),
    ((WIDE, LANES), bf16),
    ((LANES, 2 * WIDE), bf16),
]
SUMS = [((D, WIDE), f32), ((D, 2 * WIDE), f32), ((WIDE, D), f32)]
GRADS = [
    *SUMS,
    *SUMS,
    ((LAYERS * D, 2 * FF), f32),
    ((LAYERS * FF, D), f32),
    ((2 * NORMS, D, 128), f32),
    ((ATTN_ROWS, D), f32),
]
SCRATCH = [
    ((LAYERS, 3 * WIDE, D), bf16),
    ((LAYERS, D, WIDE), bf16),
    ((LAYERS, D, 2 * WIDE), bf16),
    ((LAYERS, D, WIDE), bf16),
    ((LAYERS, WIDE, D), bf16),
    ((LAYERS, 2 * FF, D), bf16),
    ((LAYERS, D, 2 * FF), bf16),
    ((LAYERS, D, FF), bf16),
    ((LAYERS, FF, D), bf16),
    ((2 * NORMS, D, 128), f32),
    ((ATTN_ROWS, D), bf16),
    *GRADS,
    *STATE,
    *STATE,
    *WORK,
    ((HEADS, 2 * KEYS, SLOT), bf16),
    ((WIDE, LANES), bf16),
    ((LAYERS, 2 * FF, LANES), f32),
    ((2 * LAYERS * D, FFH), f32),
]


def main_kernel(parts, attn_diffs, *refs):
    refs = list(refs)
    me_ref, x_ref, g_ref, norm_ref, win_own, win_other, wout_own, wout_other = take(refs, 8)
    attn_refs = take(refs, len(attn_diffs) if attn_diffs else 1)
    res_ref, ig_ref = take(refs, 2)
    outs = take(refs, 2 if attn_diffs else 4)
    wqkv_t, wq, wvk, wo_t, wo, win_t, win, wout_t, wout, norm_t, attn_ref = take(refs, 11)
    sums = (take(refs, 3), take(refs, 3))
    d_win, d_wout, d_norm, d_attn = take(refs, 4)
    states = (take(refs, len(STATE)), take(refs, len(STATE)))
    work = take(refs, len(WORK))
    kh_ref, v_ref, mixed_ref, win_rows = refs
    dvk_ref = work[-1]
    step = pl.program_id(0)

    @pl.when(step == 0)
    def _():
        for ref in (*sums[0], *sums[1], d_win, d_wout, d_norm, dvk_ref):
            ref[...] = jnp.zeros_like(ref)
        if attn_diffs:
            me = me_ref[0]
            for ref, diffs in zip(attn_refs, attn_diffs, strict=True):
                each = ref.shape[1]
                for i, diff in enumerate(diffs):
                    attn_ref[ds((me ^ diff) * each, each, each), :] = ref[i]
        else:
            attn_ref[...] = attn_refs[0][...]
        norms = [norm_ref[i] for i in range(NORMS)]
        turned = jnp.concatenate(norms + [jnp.zeros((8 - 2 * NORMS, D), f32)], axis=0).T
        for i in range(2 * NORMS):
            norm_t[i] = jnp.broadcast_to(turned[:, i : i + 1], (D, 128))
        tall, wide = head_selector(0), head_selector(1)
        for layer in range(LAYERS):
            for j in range(4):
                base = (4 * layer + j) * D
                matrix = attn_ref[base : base + D, :]
                if j < 3:
                    wqkv_t[layer, j * WIDE : (j + 1) * WIDE, :] = mm_nt(tall, matrix).astype(bf16)
                if j == 0:
                    wq[layer] = mm(matrix, wide).astype(bf16)
                elif j == 1:
                    turned_keys = mm(matrix, pair_selector(SLOT, 1))
                elif j == 2:
                    wvk[layer] = (turned_keys + mm(matrix, pair_selector(0, 1))).astype(bf16)
                else:
                    padded = mm(tall, matrix).astype(bf16)
                    wo[layer] = padded
                    wo_t[layer] = mm_nt(unit(D), padded).astype(bf16)
        for p, (w1, w2) in enumerate(((win_own, wout_own), (win_other, wout_other))):
            win_rows[...] = w1[...].astype(f32)
            for layer in range(LAYERS):
                for g in range(2):
                    part = win_rows[pl.ds(2 * layer * D + g, D, stride=2), :].astype(bf16)
                    here = slice(p * FF + g * FFH, p * FF + (g + 1) * FFH)
                    win[layer, :, here] = part
                    win_t[layer, here, :] = mm_nt(unit(FFH), part).astype(bf16)
                wout_t[layer, :, p * FFH : (p + 1) * FFH] = w2[layer]
                wout[layer, p * FFH : (p + 1) * FFH, :] = mm_nt(unit(FFH), w2[layer]).astype(bf16)

    def add_norm(index, grad, unit):
        d_norm[2 * index] += fold_lanes(grad * unit)
        d_norm[2 * index + 1] += fold_lanes(grad)

    def gain_of(index):
        return jnp.concatenate([norm_t[2 * index]] * (LANES // 128), axis=1)

    def shift_of(index):
        return jnp.concatenate([norm_t[2 * index + 1]] * (LANES // 128), axis=1)

    kept = []
    normed_b = x_ref[0]
    stream = normed_b.astype(f32)
    unit_a = inv_a = None
    for layer in range(LAYERS):
        if layer > 0:
            normed, unit_a, inv_a = norm_forward(stream, gain_of(2 * layer - 1), shift_of(2 * layer - 1))
            normed_b = normed.astype(bf16)
        stream = stream + attention_forward(
            normed_b, wqkv_t[layer], wo_t[layer], states[layer], kh_ref, v_ref
        )
        normed, unit_f, inv_f = norm_forward(stream, gain_of(2 * layer), shift_of(2 * layer))
        ffn_b = normed.astype(bf16)
        mixed = mm(win_t[layer], ffn_b)
        mixed_ref[layer] = mixed
        hidden = []
        for p in range(2):
            value = mixed[FF * p : FF * p + FFH]
            gate = mixed[FF * p + FFH : FF * (p + 1)]
            hidden.append((value * (gate * sigmoid(gate))).astype(bf16))
        hidden = jnp.concatenate(hidden, axis=0)
        stream = stream + mm(wout_t[layer], hidden)
        kept.append((normed_b, unit_a, inv_a, ffn_b, unit_f, inv_f, hidden))
    res_ref[0] = stream.astype(bf16)

    grad = g_ref[0].astype(f32)
    for layer in reversed(range(LAYERS)):
        normed_b, unit_a, inv_a, ffn_b, unit_f, inv_f, hidden = kept[layer]
        grad_b = grad.astype(bf16)
        d_wout[FF * layer : FF * (layer + 1), :] += mm_nt(hidden, grad_b)
        d_hidden = mm(wout[layer], grad_b)
        d_mixed = []
        for p in range(2):
            value = mixed_ref[layer, FF * p : FF * p + FFH]
            gate = mixed_ref[layer, FF * p + FFH : FF * (p + 1)]
            part = d_hidden[FFH * p : FFH * (p + 1)]
            sig = sigmoid(gate)
            d_mixed.append((part * (gate * sig)).astype(bf16))
            d_mixed.append((part * value * sig * (1.0 + gate * (1.0 - sig))).astype(bf16))
        d_mixed = jnp.concatenate(d_mixed, axis=0)
        d_win[D * layer : D * (layer + 1), :] += mm_nt(ffn_b, d_mixed)
        d_normed = mm(win[layer], d_mixed)
        add_norm(2 * layer, d_normed, unit_f)
        grad = grad + norm_backward(d_normed, unit_f, inv_f, gain_of(2 * layer))
        d_att = attention_backward(
            grad.astype(bf16), normed_b, wo[layer], wq[layer], wvk[layer], states[layer], work, sums[layer]
        )
        if layer > 0:
            add_norm(2 * layer - 1, d_att, unit_a)
            grad = grad + norm_backward(d_att, unit_a, inv_a, gain_of(2 * layer - 1))
        else:
            grad = grad + d_att
    ig_ref[0] = grad

    @pl.when(step == pl.num_programs(0) - 1)
    def _():
        finish_attention(d_attn, sums)
        norms = finish_norms(d_norm)
        if attn_diffs:
            pack_gradients(outs, me_ref[0], parts, d_attn, d_win, d_wout, norms)
        else:
            for out, value in zip(outs, (d_attn[...], d_win[...], d_wout[...], norms), strict=True):
                out[...] = value


VMEM = pl.BlockSpec(memory_space=pltpu.VMEM)
SMEM = pl.BlockSpec(memory_space=pltpu.SMEM)


def shapes_of(pairs):
    return [jax.ShapeDtypeStruct(*pair) for pair in pairs]


def vmem_of(pairs):
    return [pltpu.VMEM(*pair) for pair in pairs]


def per_sample():
    return pl.BlockSpec((1, D, LANES), lambda i: (i, 0, 0))


def to_columns(rows, fill_first):
    samples = rows.shape[0] // PAIRS

    def body(rows_ref, out_ref):
        out_ref[0] = load_sample(rows_ref, pl.program_id(0), fill_first).astype(bf16)

    return pl.pallas_call(
        body,
        grid=(samples,),
        in_specs=[VMEM],
        out_specs=per_sample(),
        out_shape=jax.ShapeDtypeStruct((samples, D, LANES), bf16),
        compiler_params=pltpu.CompilerParams(vmem_limit_bytes=32 * 1024 * 1024),
    )(rows)


def to_rows(columns):
    samples = columns.shape[0]

    def body(columns_ref, out_ref):
        store_sample(out_ref, pl.program_id(0), columns_ref[0].astype(f32))

    return pl.pallas_call(
        body,
        grid=(samples,),
        in_specs=[per_sample()],
        out_specs=VMEM,
        out_shape=jax.ShapeDtypeStruct((samples * PAIRS, 2 * D), columns.dtype),
        compiler_params=pltpu.CompilerParams(vmem_limit_bytes=32 * 1024 * 1024),
    )(columns)


def run_main(me, tokens, cotangent, norm_params, ffn, attn_parts, parts, attn_diffs):
    samples = tokens.shape[0]
    inputs = (norm_params, *ffn, *attn_parts)
    if attn_diffs:
        grads = [((len(NEAR), PAY_ROWS, 2 * FFH), bf16)] * 2
    else:
        grads = [((ATTN_ROWS, D), f32), GRADS[6], GRADS[7], ((8, D), f32)]

    def body(*refs):
        main_kernel(parts, attn_diffs, *refs)

    out_shape = [((samples, D, LANES), bf16), ((samples, D, LANES), f32), *grads]
    res, ig, *grads = pl.pallas_call(
        body,
        grid=(samples,),
        in_specs=[SMEM, per_sample(), per_sample()] + [VMEM] * len(inputs),
        out_specs=[per_sample(), per_sample()] + [VMEM] * len(grads),
        out_shape=shapes_of(out_shape),
        scratch_shapes=vmem_of(SCRATCH),
        compiler_params=pltpu.CompilerParams(
            dimension_semantics=("arbitrary",), vmem_limit_bytes=VMEM_BYTES
        ),
        cost_estimate=pl.CostEstimate(
            flops=samples * 5_000_000_000, bytes_accessed=20_000_000, transcendentals=0
        ),
    )(me, tokens, cotangent, *inputs)
    return res, ig, grads


def small_kernel(body, out_shape, *inputs, scratch=()):
    return pl.pallas_call(
        body,
        in_specs=[SMEM] + [VMEM] * (len(inputs) - 1),
        out_specs=[VMEM] * len(out_shape),
        out_shape=shapes_of(out_shape),
        scratch_shapes=vmem_of(scratch),
        compiler_params=pltpu.CompilerParams(vmem_limit_bytes=32 * 1024 * 1024),
    )(*inputs)


class Exchange:
    def __init__(self, me, parts):
        self.me = me
        self.parts = parts
        self.upper = parts // GROUP
        self.each = ATTN_ROWS // parts
        self.bits = [1 << i for i in range(self.upper.bit_length() - 1)]

    def swap(self, value, k):
        return lax.ppermute(value, AXES, [(i, i ^ k) for i in range(self.parts)])

    def stack(self, blocks):
        size, kind = blocks[0].shape, blocks[0].dtype
        count = math.prod(size[:-2])

        def body(me_ref, *refs):
            ins, out = refs[:-1], refs[-1]
            for i, ref in enumerate(ins):
                if len(size) == 2:
                    out[i] = ref[...]
                else:
                    out[i * count : (i + 1) * count] = ref[...]

        shape = (len(blocks) * count, *size[-2:])
        return small_kernel(body, [(shape, kind)], self.me, *blocks)[0]

    def gather(self, rows, beside_rest, beside_plane):
        far = [GROUP * u for u in range(self.upper)]
        landed = [rows] + [self.swap(rows, k) for k in far[1:]]
        landed, beside_rest = lax.optimization_barrier((landed, beside_rest))
        column = self.stack(landed)
        landed = [column] + [self.swap(column, k) for k in NEAR[1:]]
        landed, beside_plane = lax.optimization_barrier((landed, beside_plane))
        plane = self.stack(landed)
        diffs = [k ^ u for k in NEAR for u in far]
        parts, diffs = [plane, self.swap(plane, TWIN)], [diffs, [d ^ TWIN for d in diffs]]
        return parts, diffs, beside_rest, beside_plane

    def twins(self, mine, theirs):
        def body(me_ref, mine, theirs, *outs):
            for j, out in enumerate(outs):
                total = mine[j].astype(f32) + theirs[j].astype(f32)
                out[0:OFF_NORM] = total[0:OFF_NORM].astype(out.dtype)
                sums = total[OFF_NORM : OFF_NORM + 8] + total[OFF_NORM + 8 : OFF_WIN]
                out[OFF_NORM:OFF_WIN] = resplit(sums).astype(out.dtype)
                out[OFF_WIN:] = total[OFF_WIN:].astype(out.dtype)

        shape = (PAY_ROWS, 2 * FFH)
        shapes = [(shape, f32)] + [(shape, bf16)] * (len(NEAR) - 1)
        return small_kernel(body, shapes, self.me, mine, theirs)

    def across_plane(self, pieces):
        return [pieces[0]] + [self.swap(piece, k) for piece, k in zip(pieces[1:], NEAR[1:], strict=True)]

    def emit(self, total, blocks, at, keep, send):
        half = len(blocks) // 2
        each = self.each
        for out, rows in ((keep, blocks[:half]), (send, blocks[half:])):
            for i, row in enumerate(rows):
                out[i * each : (i + 1) * each, :] = total[ds(row, each, 8), :].astype(out.dtype)
        first = half * each
        last = at + OFF_NORM - OFF_WOUT
        norm = resplit(total[last : last + 8, :] + total[last + 8 : last + 16, :])
        rest = [
            total[at:last, :].astype(bf16),
            norm,
            total[last + 16 : at + PAY_ROWS - OFF_WOUT, :].astype(bf16),
        ]
        for out in (keep, send):
            row = first
            for part in rest:
                out[row : row + part.shape[0], :] = part.astype(out.dtype)
                row += part.shape[0]

    def stage_shapes(self, blocks):
        shape = (blocks * self.each + PAY_ROWS - OFF_WOUT, 2 * FFH)
        return [(shape, f32), (shape, bf16)]

    def after_plane(self, landed):
        def body(me_ref, *refs):
            ins, (keep, send, total) = refs[: len(NEAR)], refs[len(NEAR) :]
            total[...] = tree_sum([r[...].astype(f32) for r in ins])
            mine = me_ref[0] // GROUP
            order = [r for r in range(self.upper) if not r & 1] + [r for r in range(self.upper) if r & 1]
            self.emit(total, [(mine ^ r) * self.each for r in order], OFF_WOUT, keep, send)

        scratch = [((PAY_ROWS, 2 * FFH), f32)]
        return small_kernel(body, self.stage_shapes(self.upper // 2), self.me, *landed, scratch=scratch)

    def after_bit(self, mine, theirs, blocks):
        def body(me_ref, mine, theirs, keep, send, total):
            total[...] = mine[...] + theirs[...].astype(f32)
            self.emit(total, [i * self.each for i in range(blocks)], blocks * self.each, keep, send)

        (shape, _), _ = self.stage_shapes(blocks)
        return small_kernel(
            body, self.stage_shapes(blocks // 2), self.me, mine, theirs, scratch=[(shape, f32)]
        )

    def after_rest(self, mine, theirs):
        each = self.each
        at_norm = each + WOUT_PART
        ffn_rows = WOUT_PART + WIN_PART

        def body(me_ref, mine, theirs, attn, norm, ffn):
            total = mine[...] + theirs[...].astype(f32)
            attn[...] = total[0:each, 0:D]
            norm[...] = total[at_norm : at_norm + 8, 0:D] + total[at_norm + 8 : at_norm + 16, 0:D]
            ffn[0, 0:WOUT_PART, :] = total[each:at_norm, :].astype(bf16)
            ffn[0, WOUT_PART:, :] = total[at_norm + 16 :, :].astype(bf16)

        shapes = [((each, D), f32), ((8, D), f32), ((1, ffn_rows, 2 * FFH), bf16)]
        return small_kernel(body, shapes, self.me, mine, theirs)

    def spread(self, ffn):
        block = self.stack([ffn, self.swap(ffn, 4)])
        theirs = self.swap(block, TWIN)

        def body(me_ref, mine, theirs, win, wout, rows):
            for t, ref in enumerate((mine, theirs)):
                for i in range(2):
                    quarter = ((me_ref[0] % GROUP) ^ (4 * i) ^ (TWIN * t)) // 2
                    part = ref[i].astype(f32)
                    rows[ds(quarter * WOUT_PART, WOUT_PART, WOUT_PART), :] = part[:WOUT_PART, 0:D]
                    for g in range(2):
                        there = pl.ds(2 * WIN_PART * quarter + g, WIN_PART, stride=2)
                        win[there, :] = part[WOUT_PART:, FFH * g : FFH * (g + 1)]
            for layer in range(LAYERS):
                wout[layer] = rows[FFH * layer : FFH * (layer + 1), :].T

        shapes = [((2 * LAYERS * D, FFH), f32), ((LAYERS, D, FFH), f32)]
        scratch = [((LAYERS * FFH, D), f32)]
        return small_kernel(body, shapes, self.me, block, theirs, scratch=scratch)

    def sum_all(self, keep, send, res, ig):
        landed = self.across_plane(self.twins(keep, self.swap(send, TWIN)))
        landed, res = lax.optimization_barrier((landed, to_rows(res)))
        keep, send = self.after_plane(landed)
        blocks = self.upper // 2
        for bit in self.bits[:-1]:
            keep, send = self.after_bit(keep, self.swap(send, GROUP * bit), blocks)
            blocks //= 2
        theirs = self.swap(send, GROUP * self.bits[-1])
        theirs, ig = lax.optimization_barrier((theirs, to_rows(ig)))
        attn, norm, ffn = self.after_rest(keep, theirs)
        return res, ig, attn, norm, *self.spread(ffn)


def on_device(devices, tokens, attn_weights, norm_params, w_in, w_out, cotangent):
    each = attn_weights.shape[0]
    me = (lax.axis_index("dp") * 2 + lax.axis_index("narrow")).astype(jnp.int32).reshape(1)
    staged = devices % (2 * GROUP) == 0 and each % 16 == 0
    x_t = to_columns(tokens, True)
    g_t = to_columns(cotangent, False)
    swap_halves = [(0, 1), (1, 0)]
    w_in = w_in.reshape(2 * LAYERS * D, FFH)
    w_out = w_out.transpose(0, 2, 1)
    w_in_other = lax.ppermute(w_in, "narrow", swap_halves)
    w_out_other = lax.ppermute(w_out, "narrow", swap_halves)
    ffn = (w_in, w_in_other, w_out, w_out_other)
    if not staged:
        attn_all = lax.all_gather(attn_weights, AXES, axis=0, tiled=True)
        res, ig, grads = run_main(me, x_t, g_t, norm_params, ffn, (attn_all,), devices, None)
        res, ig = to_rows(res), to_rows(ig)
        d_attn, d_win, d_wout, sums = grads
        attn = lax.psum_scatter(d_attn, AXES, scatter_dimension=0, tiled=True)
        norm = lax.psum(sums, AXES)
        d_wout = d_wout.reshape(LAYERS, FF, D)
        own_in, other_in = d_win[:, :FF], d_win[:, FF:]
        own_out, other_out = d_wout[:, :FFH], d_wout[:, FFH:]
        win = lax.psum(own_in + lax.ppermute(other_in, "narrow", swap_halves), "dp")
        wout = lax.psum(own_out + lax.ppermute(other_out, "narrow", swap_halves), "dp")
        wout = wout.transpose(0, 2, 1)
    else:
        ex = Exchange(me, devices)
        attn_parts, attn_diffs, (x_t, *others), g_t = ex.gather(
            attn_weights, (x_t, w_in_other, w_out_other), g_t
        )
        ffn = (w_in, others[0], w_out, others[1])
        res, ig, grads = run_main(me, x_t, g_t, norm_params, ffn, attn_parts, devices, attn_diffs)
        res, ig, attn, norm, win, wout = ex.sum_all(*grads, res, ig)
    return (
        res,
        ig,
        attn,
        norm[: 2 * NORMS].reshape(norm_params.shape),
        win.reshape(LAYERS, D, 2, FFH),
        wout.transpose(0, 2, 1),
    )


def solution(mesh):
    rows = P(("dp", "narrow"), None)
    hidden_in = P(None, None, None, "narrow")
    hidden_out = P(None, "narrow", None)
    devices = mesh.shape["dp"] * mesh.shape["narrow"]

    def per_device(*args):
        return on_device(devices, *args)

    return jax.shard_map(
        per_device,
        mesh=mesh,
        in_specs=(rows, rows, P(), hidden_in, hidden_out, rows),
        out_specs=(rows, rows, rows, P(), hidden_in, hidden_out),
        check_vma=False,
    )
```

```python
import math

import jax
import jax.numpy as jnp
from jax import lax
from jax.experimental import pallas as pl
from jax.experimental.pallas import tpu as pltpu
from jax.sharding import PartitionSpec as P

HEADS = 8
HEAD = 24
SLOT = 32
WIDE = HEADS * SLOT
QUAD = 128 // SLOT
D = HEADS * HEAD
FF = 256
FFH = FF // 2
LAYERS = 2
NORMS = 2 * LAYERS - 1
SEQ = 476
PAIRS = SEQ // 2
KEYS = 240
HALF = 256
LANES = 2 * HALF
EPS = 1e-05
SCALE = HEAD ** (-0.5)
LOG2E = math.log2(math.e)
ATTN_ROWS = LAYERS * 4 * D

GROUP = 8
NEAR = (0, 1, 4, 5)
TWIN = 2
WIN_PART = LAYERS * D // 4
WOUT_PART = LAYERS * FFH // 4
ATTN_PART = ATTN_ROWS // GROUP
OFF_WOUT = ATTN_PART
OFF_NORM = OFF_WOUT + WOUT_PART
OFF_WIN = OFF_NORM + 16
PAY_ROWS = OFF_WIN + WIN_PART

bf16 = jnp.bfloat16
f32 = jnp.float32
AXES = ("dp", "narrow")

VMEM_BYTES = 60 * 1024 * 1024


def mm(left, right):
    return jnp.dot(left, right, preferred_element_type=f32)


def mm_nt(left, right):
    return lax.dot_general(left, right, (((1,), (1,)), ((), ())), preferred_element_type=f32)


def sigmoid(value):
    return 0.5 + 0.5 * jnp.tanh(0.5 * value)


def fold_lanes(value):
    return value[:, 0:128] + value[:, 128:256] + value[:, 256:384] + value[:, 384:512]


def norm_forward(stream, gain, shift):
    center = stream - jnp.sum(stream, axis=0, keepdims=True) * (1.0 / D)
    inverse = lax.rsqrt(jnp.sum(center * center, axis=0, keepdims=True) * (1.0 / D) + EPS)
    unit = center * inverse
    return (unit * gain + shift, unit, inverse)


def norm_backward(grad, unit, inverse, gain):
    scaled = grad * gain
    mean = jnp.sum(scaled, axis=0, keepdims=True) * (1.0 / D)
    slope = jnp.sum(scaled * unit, axis=0, keepdims=True) * (1.0 / D)
    return inverse * (scaled - mean - unit * slope)


def tree_sum(parts):
    while len(parts) > 1:
        parts = [parts[i] + parts[i + 1] for i in range(0, len(parts), 2)]
    return parts[0]


def ds(start, size, step):
    return pl.ds(pl.multiple_of(start, step), size)


def take(refs, count):
    taken = refs[:count]
    del refs[:count]
    return taken


def unit(size):
    row = lax.broadcasted_iota(jnp.int32, (size, size), 0)
    column = lax.broadcasted_iota(jnp.int32, (size, size), 1)
    return (row == column).astype(f32).astype(bf16)


def head_selector(padded_axis):
    shape = (WIDE, D) if padded_axis == 0 else (D, WIDE)
    padded = lax.broadcasted_iota(jnp.int32, shape, padded_axis)
    plain = lax.broadcasted_iota(jnp.int32, shape, 1 - padded_axis)
    inside = padded & (SLOT - 1)
    same = jnp.logical_and(plain == HEAD * (padded >> 5) + inside, inside < HEAD)
    return same.astype(f32).astype(bf16)


def pair_selector(offset, padded_axis):
    shape = (2 * WIDE, D) if padded_axis == 0 else (D, 2 * WIDE)
    padded = lax.broadcasted_iota(jnp.int32, shape, padded_axis)
    plain = lax.broadcasted_iota(jnp.int32, shape, 1 - padded_axis)
    inside = (padded & (2 * SLOT - 1)) - offset
    same = jnp.logical_and(plain == HEAD * (padded >> 6) + inside, inside >= 0)
    return jnp.logical_and(same, inside < HEAD).astype(f32).astype(bf16)


def head_rows(h):
    return slice(SLOT * h, SLOT * (h + 1))


def quad_lanes(h):
    return slice(128 * (h // QUAD), 128 * (h // QUAD + 1))


def sample_window(step, rows_total, align):
    base = step * PAIRS
    start = jnp.minimum(base // align * align, rows_total - HALF)
    return ds(start, HALF, align), base - start


def load_sample(ref, step, fill_first):
    window, shift = sample_window(step, ref.shape[0], 16)
    rows = pltpu.roll(ref[window, :].astype(f32), lax.rem(HALF - shift, HALF), 0)
    pair_row = lax.broadcasted_iota(jnp.int32, (HALF, 2 * D), 0)
    cols = jnp.where(pair_row < PAIRS, rows, rows[0:1] if fill_first else 0.0).T
    return jnp.concatenate([cols[:D], cols[D:]], axis=1)


def store_sample(ref, step, value):
    window, shift = sample_window(step, ref.shape[0], 16 if ref.dtype == bf16 else 8)
    cols = jnp.concatenate([value[:, :HALF], value[:, HALF:]], axis=0)
    rows = pltpu.roll(cols.T, shift, 0)
    pair_row = lax.broadcasted_iota(jnp.int32, (HALF, 2 * D), 0)
    here = jnp.logical_and(pair_row >= shift, pair_row < shift + PAIRS)
    ref[window, :] = jnp.where(here, rows, ref[window, :].astype(f32)).astype(ref.dtype)


def attention_forward(normed_b, wqkv_t, wo_t, state, kt_ref, v_ref, alone_ref):
    e_ref, vt_ref, q_ref, k_ref, ctx_ref, rinv_ref = state
    lane = lax.broadcasted_iota(jnp.int32, (WIDE, LANES), 1)
    slot_row = lax.broadcasted_iota(jnp.int32, (WIDE, LANES), 0) & (SLOT - 1)
    real = (lane & (HALF - 1)) < PAIRS
    ones_rows = jnp.logical_or(slot_row == HEAD, slot_row == HEAD + 1).astype(f32)
    qkv = mm(wqkv_t, normed_b)
    queries = (qkv[:WIDE] * (SCALE * LOG2E)).astype(bf16)
    q_ref[...] = queries
    keys = qkv[WIDE : 2 * WIDE].astype(bf16)
    k_ref[...] = keys
    values = jnp.where(real, qkv[2 * WIDE :] + ones_rows, 0.0).astype(bf16)
    v_ref[...] = values
    for tall, ref in ((keys.T, kt_ref), (values.T, vt_ref)):
        ref[0:KEYS] = tall[0:KEYS]
        ref[KEYS:] = tall[HALF : HALF + KEYS]
    for h in range(HEADS):
        alone_ref[h, head_rows(h % QUAD), :] = queries[head_rows(h)]

    def scores_of(h):
        return mm(kt_ref[:, quad_lanes(h)], alone_ref[h])

    scores = scores_of(0)
    for h in range(HEADS):
        rows = head_rows(h)
        ahead = scores_of(h + 1) if h + 1 < HEADS else None
        top = jnp.max(scores, axis=0, keepdims=True)
        weights = jnp.exp2(scores - top).astype(bf16)
        e_ref[0 : 2 * KEYS, LANES * h : LANES * (h + 1)] = weights
        out = mm(v_ref[rows, 0:KEYS], weights[0:KEYS]) + mm(
            v_ref[rows, HALF : HALF + KEYS], weights[KEYS:]
        )
        inverse = 1.0 / out[HEAD : HEAD + 1]
        rinv_ref[h : h + 1, :] = inverse
        ctx_ref[rows, :] = out * inverse
        scores = ahead
    return mm(wo_t, ctx_ref[...].astype(bf16))


def attention_backward(grad_b, normed_b, wo, wq, wvk, state, work, sums):
    e_ref, vt_ref, q_ref, k_ref, ctx_ref, rinv_ref = state
    pair_ref, alone_ref, block_ref, dq_ref, dvk_ref = work
    d_wq, d_wvk, d_wo = sums
    group = HEADS // 2
    head_row = lax.broadcasted_iota(jnp.int32, (SLOT, LANES), 0)
    lane_head = lax.broadcasted_iota(jnp.int32, (LANES, 2 * SLOT * group), 1) // (2 * SLOT)
    key_row = lax.broadcasted_iota(jnp.int32, (2 * KEYS, 2 * SLOT * group), 0)
    real_key = jnp.where(key_row < KEYS, key_row, key_row - KEYS) < PAIRS
    in_pair = lax.broadcasted_iota(jnp.int32, (2 * KEYS, 2 * SLOT * group), 1) & (2 * SLOT - 1)

    d_wo[...] += mm_nt(ctx_ref[...].astype(bf16), grad_b)
    d_context = mm(wo, grad_b)
    for h in range(HEADS):
        rows = head_rows(h)
        grad = (d_context[rows] * rinv_ref[h : h + 1, :]).astype(bf16).astype(f32)
        dot = -jnp.sum(grad[:HEAD] * ctx_ref[rows, :][:HEAD], axis=0, keepdims=True)
        dot_high = dot.astype(bf16).astype(f32)
        grad = jnp.where(head_row == HEAD, dot_high, grad)
        grad = jnp.where(head_row == HEAD + 1, dot - dot_high, grad)
        pair_ref[2 * SLOT * h : 2 * SLOT * h + SLOT, :] = grad.astype(bf16)
        alone_ref[h, head_rows(h % QUAD), :] = grad.astype(bf16)
        pair_ref[2 * SLOT * h + SLOT : 2 * SLOT * (h + 1), :] = q_ref[rows, :]
    tall = pair_ref[...].T
    for h in range(HEADS):
        part = tall[:, WIDE * (h // group) : WIDE * (h // group + 1)]
        block_ref[LANES * h : LANES * (h + 1), :] = jnp.where(
            lane_head == h % group, part, jnp.zeros_like(part)
        )

    for h in range(HEADS + 1):
        if h < HEADS:
            lanes = slice(LANES * h, LANES * (h + 1))
            grad_probs = mm(vt_ref[:, quad_lanes(h)], alone_ref[h])
            e_ref[2 * KEYS :, lanes] = e_ref[0 : 2 * KEYS, lanes] * grad_probs.astype(bf16)
        if h > 0:
            rows = head_rows(h - 1)
            lanes = slice(LANES * (h - 1), LANES * h)
            dq = mm(k_ref[rows, 0:KEYS], e_ref[2 * KEYS : 3 * KEYS, lanes]) + mm(
                k_ref[rows, HALF : HALF + KEYS], e_ref[3 * KEYS :, lanes]
            )
            dq_ref[rows, :] = (dq * SCALE).astype(bf16)
    for g in range(2):
        here = slice(group * LANES * g, group * LANES * (g + 1))
        both = mm(e_ref[:, here], block_ref[here, :])
        dv = jnp.where(real_key, both[: 2 * KEYS], 0.0)
        dk = both[2 * KEYS :] * (1.0 / LOG2E)
        dvk = jnp.where(in_pair < SLOT, dv, dk).astype(bf16)
        for half in range(2):
            there = slice(half * HALF, half * HALF + KEYS)
            dvk_ref[there, WIDE * g : WIDE * (g + 1)] = dvk[half * KEYS : (half + 1) * KEYS]
    d_wq[...] += mm_nt(normed_b, dq_ref[...])
    d_wvk[...] += mm(normed_b, dvk_ref[...])
    return mm(wq, dq_ref[...]) + mm_nt(wvk, dvk_ref[...])


def resplit(sums):
    high = sums.astype(bf16).astype(f32)
    return jnp.concatenate([high, sums - high], axis=0).astype(bf16)


def finish_attention(d_attn, sums):
    tall, wide = head_selector(0), head_selector(1)
    for layer in range(LAYERS):
        d_wq, d_wvk, d_wo = sums[layer]
        mixed = d_wvk[...].astype(bf16)
        base = 4 * layer * D
        d_attn[base : base + D, :] = mm(d_wq[...].astype(bf16), tall)
        d_attn[base + D : base + 2 * D, :] = mm(mixed, pair_selector(SLOT, 0))
        d_attn[base + 2 * D : base + 3 * D, :] = mm(mixed, pair_selector(0, 0))
        d_attn[base + 3 * D : base + 4 * D, :] = mm(wide, d_wo[...].astype(bf16))


def finish_norms(d_norm):
    sums = [jnp.sum(d_norm[j].T, axis=0, keepdims=True) for j in range(2 * NORMS)]
    return jnp.concatenate(sums + [jnp.zeros((8 - 2 * NORMS, D), f32)], axis=0)


def pack_gradients(outs, me, parts, d_attn, d_win, d_wout, norms):
    each, upper = ATTN_ROWS // parts, parts // GROUP
    norms = resplit(norms)
    for t, out in enumerate(outs):
        for j, k in enumerate(NEAR):
            kind = out.dtype
            low = (me % GROUP) ^ k ^ (TWIN * t)
            quarter = low // 2
            half = k % 2
            for u in range(upper):
                rows = d_attn[ds((u * GROUP + low) * each, each, each), :]
                out[j, u * each : (u + 1) * each, 0:D] = rows.astype(kind)
            first = (quarter // 2) * FF + half * FFH + (quarter % 2) * WOUT_PART
            out[j, OFF_WOUT:OFF_NORM, 0:D] = d_wout[ds(first, WOUT_PART, WOUT_PART), :].astype(kind)
            out[j, OFF_NORM:OFF_WIN, 0:D] = norms.astype(kind)
            rows = d_win[ds(quarter * WIN_PART, WIN_PART, WIN_PART), half * FF : (half + 1) * FF]
            out[j, OFF_WIN:PAY_ROWS, :] = rows.astype(kind)


STATE = [
    ((4 * KEYS, HEADS * LANES), bf16),
    ((2 * KEYS, WIDE), bf16),
    ((WIDE, LANES), bf16),
    ((WIDE, LANES), bf16),
    ((WIDE, LANES), f32),
    ((HEADS, LANES), f32),
]
WORK = [
    ((2 * WIDE, LANES), bf16),
    ((HEADS, 128, LANES), bf16),
    ((HEADS * LANES, WIDE), bf16),
    ((WIDE, LANES), bf16),
    ((LANES, 2 * WIDE), bf16),
]
SUMS = [((D, WIDE), f32), ((D, 2 * WIDE), f32), ((WIDE, D), f32)]
GRADS = [
    *SUMS,
    *SUMS,
    ((LAYERS * D, 2 * FF), f32),
    ((LAYERS * FF, D), f32),
    ((2 * NORMS, D, 128), f32),
    ((ATTN_ROWS, D), f32),
]
SCRATCH = [
    ((LAYERS, 3 * WIDE, D), bf16),
    ((LAYERS, D, WIDE), bf16),
    ((LAYERS, D, 2 * WIDE), bf16),
    ((LAYERS, D, WIDE), bf16),
    ((LAYERS, WIDE, D), bf16),
    ((LAYERS, 2 * FF, D), bf16),
    ((LAYERS, D, 2 * FF), bf16),
    ((LAYERS, D, FF), bf16),
    ((LAYERS, FF, D), bf16),
    ((2 * NORMS, D, 128), f32),
    ((ATTN_ROWS, D), bf16),
    *GRADS,
    *STATE,
    *STATE,
    *WORK,
    ((2 * KEYS, WIDE), bf16),
    ((WIDE, LANES), bf16),
    ((HEADS, 128, LANES), bf16),
    ((LAYERS, 2 * FF, LANES), f32),
    ((2 * LAYERS * D, FFH), f32),
]


def main_kernel(parts, attn_diffs, *refs):
    refs = list(refs)
    me_ref, x_ref, g_ref, norm_ref, win_own, win_other, wout_own, wout_other = take(refs, 8)
    attn_refs = take(refs, len(attn_diffs) if attn_diffs else 1)
    res_ref, ig_ref = take(refs, 2)
    outs = take(refs, 2 if attn_diffs else 4)
    wqkv_t, wq, wvk, wo_t, wo, win_t, win, wout_t, wout, norm_t, attn_ref = take(refs, 11)
    sums = (take(refs, 3), take(refs, 3))
    d_win, d_wout, d_norm, d_attn = take(refs, 4)
    states = (take(refs, len(STATE)), take(refs, len(STATE)))
    work = take(refs, len(WORK))
    kt_ref, v_ref, alone_ref, mixed_ref, win_rows = refs
    dvk_ref, grad_alone_ref = work[-1], work[1]
    step = pl.program_id(0)

    @pl.when(step == 0)
    def _():
        for ref in (*sums[0], *sums[1], d_win, d_wout, d_norm, dvk_ref, alone_ref, grad_alone_ref):
            ref[...] = jnp.zeros_like(ref)
        if attn_diffs:
            me = me_ref[0]
            for ref, diffs in zip(attn_refs, attn_diffs, strict=True):
                each = ref.shape[1]
                for i, diff in enumerate(diffs):
                    attn_ref[ds((me ^ diff) * each, each, each), :] = ref[i]
        else:
            attn_ref[...] = attn_refs[0][...]
        norms = [norm_ref[i] for i in range(NORMS)]
        turned = jnp.concatenate(norms + [jnp.zeros((8 - 2 * NORMS, D), f32)], axis=0).T
        for i in range(2 * NORMS):
            norm_t[i] = jnp.broadcast_to(turned[:, i : i + 1], (D, 128))
        tall, wide = head_selector(0), head_selector(1)
        for layer in range(LAYERS):
            for j in range(4):
                base = (4 * layer + j) * D
                matrix = attn_ref[base : base + D, :]
                if j < 3:
                    wqkv_t[layer, j * WIDE : (j + 1) * WIDE, :] = mm_nt(tall, matrix).astype(bf16)
                if j == 0:
                    wq[layer] = mm(matrix, wide).astype(bf16)
                elif j == 1:
                    turned_keys = mm(matrix, pair_selector(SLOT, 1))
                elif j == 2:
                    wvk[layer] = (turned_keys + mm(matrix, pair_selector(0, 1))).astype(bf16)
                else:
                    padded = mm(tall, matrix).astype(bf16)
                    wo[layer] = padded
                    wo_t[layer] = mm_nt(unit(D), padded).astype(bf16)
        for p, (w1, w2) in enumerate(((win_own, wout_own), (win_other, wout_other))):
            win_rows[...] = w1[...].astype(f32)
            for layer in range(LAYERS):
                for g in range(2):
                    part = win_rows[pl.ds(2 * layer * D + g, D, stride=2), :].astype(bf16)
                    here = slice(p * FF + g * FFH, p * FF + (g + 1) * FFH)
                    win[layer, :, here] = part
                    win_t[layer, here, :] = mm_nt(unit(FFH), part).astype(bf16)
                wout_t[layer, :, p * FFH : (p + 1) * FFH] = w2[layer]
                wout[layer, p * FFH : (p + 1) * FFH, :] = mm_nt(unit(FFH), w2[layer]).astype(bf16)

    def add_norm(index, grad, unit):
        d_norm[2 * index] += fold_lanes(grad * unit)
        d_norm[2 * index + 1] += fold_lanes(grad)

    def gain_of(index):
        return jnp.concatenate([norm_t[2 * index]] * (LANES // 128), axis=1)

    def shift_of(index):
        return jnp.concatenate([norm_t[2 * index + 1]] * (LANES // 128), axis=1)

    kept = []
    normed_b = x_ref[0]
    stream = normed_b.astype(f32)
    unit_a = inv_a = None
    for layer in range(LAYERS):
        if layer > 0:
            normed, unit_a, inv_a = norm_forward(stream, gain_of(2 * layer - 1), shift_of(2 * layer - 1))
            normed_b = normed.astype(bf16)
        stream = stream + attention_forward(
            normed_b, wqkv_t[layer], wo_t[layer], states[layer], kt_ref, v_ref, alone_ref
        )
        normed, unit_f, inv_f = norm_forward(stream, gain_of(2 * layer), shift_of(2 * layer))
        ffn_b = normed.astype(bf16)
        mixed = mm(win_t[layer], ffn_b)
        mixed_ref[layer] = mixed
        hidden = []
        for p in range(2):
            value = mixed[FF * p : FF * p + FFH]
            gate = mixed[FF * p + FFH : FF * (p + 1)]
            hidden.append((value * (gate * sigmoid(gate))).astype(bf16))
        hidden = jnp.concatenate(hidden, axis=0)
        stream = stream + mm(wout_t[layer], hidden)
        kept.append((normed_b, unit_a, inv_a, ffn_b, unit_f, inv_f, hidden))
    res_ref[0] = stream.astype(bf16)

    grad = g_ref[0].astype(f32)
    for layer in reversed(range(LAYERS)):
        normed_b, unit_a, inv_a, ffn_b, unit_f, inv_f, hidden = kept[layer]
        grad_b = grad.astype(bf16)
        d_wout[FF * layer : FF * (layer + 1), :] += mm_nt(hidden, grad_b)
        d_hidden = mm(wout[layer], grad_b)
        d_mixed = []
        for p in range(2):
            value = mixed_ref[layer, FF * p : FF * p + FFH]
            gate = mixed_ref[layer, FF * p + FFH : FF * (p + 1)]
            part = d_hidden[FFH * p : FFH * (p + 1)]
            sig = sigmoid(gate)
            d_mixed.append((part * (gate * sig)).astype(bf16))
            d_mixed.append((part * value * sig * (1.0 + gate * (1.0 - sig))).astype(bf16))
        d_mixed = jnp.concatenate(d_mixed, axis=0)
        d_win[D * layer : D * (layer + 1), :] += mm_nt(ffn_b, d_mixed)
        d_normed = mm(win[layer], d_mixed)
        add_norm(2 * layer, d_normed, unit_f)
        grad = grad + norm_backward(d_normed, unit_f, inv_f, gain_of(2 * layer))
        d_att = attention_backward(
            grad.astype(bf16), normed_b, wo[layer], wq[layer], wvk[layer], states[layer], work, sums[layer]
        )
        if layer > 0:
            add_norm(2 * layer - 1, d_att, unit_a)
            grad = grad + norm_backward(d_att, unit_a, inv_a, gain_of(2 * layer - 1))
        else:
            grad = grad + d_att
    ig_ref[0] = grad

    @pl.when(step == pl.num_programs(0) - 1)
    def _():
        finish_attention(d_attn, sums)
        norms = finish_norms(d_norm)
        if attn_diffs:
            pack_gradients(outs, me_ref[0], parts, d_attn, d_win, d_wout, norms)
        else:
            for out, value in zip(outs, (d_attn[...], d_win[...], d_wout[...], norms), strict=True):
                out[...] = value


VMEM = pl.BlockSpec(memory_space=pltpu.VMEM)
SMEM = pl.BlockSpec(memory_space=pltpu.SMEM)


def shapes_of(pairs):
    return [jax.ShapeDtypeStruct(*pair) for pair in pairs]


def vmem_of(pairs):
    return [pltpu.VMEM(*pair) for pair in pairs]


def per_sample():
    return pl.BlockSpec((1, D, LANES), lambda i: (i, 0, 0))


def to_columns(rows, fill_first):
    samples = rows.shape[0] // PAIRS

    def body(rows_ref, out_ref):
        out_ref[0] = load_sample(rows_ref, pl.program_id(0), fill_first).astype(bf16)

    return pl.pallas_call(
        body,
        grid=(samples,),
        in_specs=[VMEM],
        out_specs=per_sample(),
        out_shape=jax.ShapeDtypeStruct((samples, D, LANES), bf16),
        compiler_params=pltpu.CompilerParams(vmem_limit_bytes=32 * 1024 * 1024),
    )(rows)


def to_rows(columns):
    samples = columns.shape[0]

    def body(columns_ref, out_ref):
        store_sample(out_ref, pl.program_id(0), columns_ref[0].astype(f32))

    return pl.pallas_call(
        body,
        grid=(samples,),
        in_specs=[per_sample()],
        out_specs=VMEM,
        out_shape=jax.ShapeDtypeStruct((samples * PAIRS, 2 * D), columns.dtype),
        compiler_params=pltpu.CompilerParams(vmem_limit_bytes=32 * 1024 * 1024),
    )(columns)


def run_main(me, tokens, cotangent, norm_params, ffn, attn_parts, parts, attn_diffs):
    samples = tokens.shape[0]
    inputs = (norm_params, *ffn, *attn_parts)
    if attn_diffs:
        grads = [((len(NEAR), PAY_ROWS, 2 * FFH), bf16)] * 2
    else:
        grads = [((ATTN_ROWS, D), f32), GRADS[6], GRADS[7], ((8, D), f32)]

    def body(*refs):
        main_kernel(parts, attn_diffs, *refs)

    out_shape = [((samples, D, LANES), bf16), ((samples, D, LANES), f32), *grads]
    res, ig, *grads = pl.pallas_call(
        body,
        grid=(samples,),
        in_specs=[SMEM, per_sample(), per_sample()] + [VMEM] * len(inputs),
        out_specs=[per_sample(), per_sample()] + [VMEM] * len(grads),
        out_shape=shapes_of(out_shape),
        scratch_shapes=vmem_of(SCRATCH),
        compiler_params=pltpu.CompilerParams(
            dimension_semantics=("arbitrary",), vmem_limit_bytes=VMEM_BYTES
        ),
        cost_estimate=pl.CostEstimate(
            flops=samples * 5_000_000_000, bytes_accessed=20_000_000, transcendentals=0
        ),
    )(me, tokens, cotangent, *inputs)
    return res, ig, grads


def small_kernel(body, out_shape, *inputs, scratch=()):
    return pl.pallas_call(
        body,
        in_specs=[SMEM] + [VMEM] * (len(inputs) - 1),
        out_specs=[VMEM] * len(out_shape),
        out_shape=shapes_of(out_shape),
        scratch_shapes=vmem_of(scratch),
        compiler_params=pltpu.CompilerParams(vmem_limit_bytes=32 * 1024 * 1024),
    )(*inputs)


class Exchange:
    def __init__(self, me, parts):
        self.me = me
        self.parts = parts
        self.upper = parts // GROUP
        self.each = ATTN_ROWS // parts
        self.bits = [1 << i for i in range(self.upper.bit_length() - 1)]

    def swap(self, value, k):
        return lax.ppermute(value, AXES, [(i, i ^ k) for i in range(self.parts)])

    def stack(self, blocks):
        size, kind = blocks[0].shape, blocks[0].dtype
        count = math.prod(size[:-2])

        def body(me_ref, *refs):
            ins, out = refs[:-1], refs[-1]
            for i, ref in enumerate(ins):
                if len(size) == 2:
                    out[i] = ref[...]
                else:
                    out[i * count : (i + 1) * count] = ref[...]

        shape = (len(blocks) * count, *size[-2:])
        return small_kernel(body, [(shape, kind)], self.me, *blocks)[0]

    def gather(self, rows, beside_rest, beside_plane):
        far = [GROUP * u for u in range(self.upper)]
        landed = [rows] + [self.swap(rows, k) for k in far[1:]]
        landed, beside_rest = lax.optimization_barrier((landed, beside_rest))
        column = self.stack(landed)
        landed = [column] + [self.swap(column, k) for k in NEAR[1:]]
        landed, beside_plane = lax.optimization_barrier((landed, beside_plane))
        plane = self.stack(landed)
        diffs = [k ^ u for k in NEAR for u in far]
        parts, diffs = [plane, self.swap(plane, TWIN)], [diffs, [d ^ TWIN for d in diffs]]
        return parts, diffs, beside_rest, beside_plane

    def twins(self, mine, theirs):
        def body(me_ref, mine, theirs, *outs):
            for j, out in enumerate(outs):
                total = mine[j].astype(f32) + theirs[j].astype(f32)
                out[0:OFF_NORM] = total[0:OFF_NORM].astype(out.dtype)
                sums = total[OFF_NORM : OFF_NORM + 8] + total[OFF_NORM + 8 : OFF_WIN]
                out[OFF_NORM:OFF_WIN] = resplit(sums).astype(out.dtype)
                out[OFF_WIN:] = total[OFF_WIN:].astype(out.dtype)

        shape = (PAY_ROWS, 2 * FFH)
        shapes = [(shape, f32)] + [(shape, bf16)] * (len(NEAR) - 1)
        return small_kernel(body, shapes, self.me, mine, theirs)

    def across_plane(self, pieces):
        return [pieces[0]] + [self.swap(piece, k) for piece, k in zip(pieces[1:], NEAR[1:], strict=True)]

    def emit(self, total, blocks, at, keep, send):
        half = len(blocks) // 2
        each = self.each
        for out, rows in ((keep, blocks[:half]), (send, blocks[half:])):
            for i, row in enumerate(rows):
                out[i * each : (i + 1) * each, :] = total[ds(row, each, 8), :].astype(out.dtype)
        first = half * each
        last = at + OFF_NORM - OFF_WOUT
        norm = resplit(total[last : last + 8, :] + total[last + 8 : last + 16, :])
        rest = [
            total[at:last, :].astype(bf16),
            norm,
            total[last + 16 : at + PAY_ROWS - OFF_WOUT, :].astype(bf16),
        ]
        for out in (keep, send):
            row = first
            for part in rest:
                out[row : row + part.shape[0], :] = part.astype(out.dtype)
                row += part.shape[0]

    def stage_shapes(self, blocks):
        shape = (blocks * self.each + PAY_ROWS - OFF_WOUT, 2 * FFH)
        return [(shape, f32), (shape, bf16)]

    def after_plane(self, landed):
        def body(me_ref, *refs):
            ins, (keep, send, total) = refs[: len(NEAR)], refs[len(NEAR) :]
            total[...] = tree_sum([r[...].astype(f32) for r in ins])
            mine = me_ref[0] // GROUP
            order = [r for r in range(self.upper) if not r & 1] + [r for r in range(self.upper) if r & 1]
            self.emit(total, [(mine ^ r) * self.each for r in order], OFF_WOUT, keep, send)

        scratch = [((PAY_ROWS, 2 * FFH), f32)]
        return small_kernel(body, self.stage_shapes(self.upper // 2), self.me, *landed, scratch=scratch)

    def after_bit(self, mine, theirs, blocks):
        def body(me_ref, mine, theirs, keep, send, total):
            total[...] = mine[...] + theirs[...].astype(f32)
            self.emit(total, [i * self.each for i in range(blocks)], blocks * self.each, keep, send)

        (shape, _), _ = self.stage_shapes(blocks)
        return small_kernel(
            body, self.stage_shapes(blocks // 2), self.me, mine, theirs, scratch=[(shape, f32)]
        )

    def after_rest(self, mine, theirs):
        each = self.each
        at_norm = each + WOUT_PART
        ffn_rows = WOUT_PART + WIN_PART

        def body(me_ref, mine, theirs, attn, norm, ffn):
            total = mine[...] + theirs[...].astype(f32)
            attn[...] = total[0:each, 0:D]
            norm[...] = total[at_norm : at_norm + 8, 0:D] + total[at_norm + 8 : at_norm + 16, 0:D]
            ffn[0, 0:WOUT_PART, :] = total[each:at_norm, :].astype(bf16)
            ffn[0, WOUT_PART:, :] = total[at_norm + 16 :, :].astype(bf16)

        shapes = [((each, D), f32), ((8, D), f32), ((1, ffn_rows, 2 * FFH), bf16)]
        return small_kernel(body, shapes, self.me, mine, theirs)

    def spread(self, ffn):
        block = self.stack([ffn, self.swap(ffn, 4)])
        theirs = self.swap(block, TWIN)

        def body(me_ref, mine, theirs, win, wout, rows):
            for t, ref in enumerate((mine, theirs)):
                for i in range(2):
                    quarter = ((me_ref[0] % GROUP) ^ (4 * i) ^ (TWIN * t)) // 2
                    part = ref[i].astype(f32)
                    rows[ds(quarter * WOUT_PART, WOUT_PART, WOUT_PART), :] = part[:WOUT_PART, 0:D]
                    for g in range(2):
                        there = pl.ds(2 * WIN_PART * quarter + g, WIN_PART, stride=2)
                        win[there, :] = part[WOUT_PART:, FFH * g : FFH * (g + 1)]
            for layer in range(LAYERS):
                wout[layer] = rows[FFH * layer : FFH * (layer + 1), :].T

        shapes = [((2 * LAYERS * D, FFH), f32), ((LAYERS, D, FFH), f32)]
        scratch = [((LAYERS * FFH, D), f32)]
        return small_kernel(body, shapes, self.me, block, theirs, scratch=scratch)

    def sum_all(self, keep, send, res, ig):
        landed = self.across_plane(self.twins(keep, self.swap(send, TWIN)))
        landed, res = lax.optimization_barrier((landed, to_rows(res)))
        keep, send = self.after_plane(landed)
        blocks = self.upper // 2
        for bit in self.bits[:-1]:
            keep, send = self.after_bit(keep, self.swap(send, GROUP * bit), blocks)
            blocks //= 2
        theirs = self.swap(send, GROUP * self.bits[-1])
        theirs, ig = lax.optimization_barrier((theirs, to_rows(ig)))
        attn, norm, ffn = self.after_rest(keep, theirs)
        return res, ig, attn, norm, *self.spread(ffn)


def on_device(devices, tokens, attn_weights, norm_params, w_in, w_out, cotangent):
    each = attn_weights.shape[0]
    me = (lax.axis_index("dp") * 2 + lax.axis_index("narrow")).astype(jnp.int32).reshape(1)
    staged = devices % (2 * GROUP) == 0 and each % 16 == 0
    x_t = to_columns(tokens, True)
    g_t = to_columns(cotangent, False)
    swap_halves = [(0, 1), (1, 0)]
    w_in = w_in.reshape(2 * LAYERS * D, FFH)
    w_out = w_out.transpose(0, 2, 1)
    w_in_other = lax.ppermute(w_in, "narrow", swap_halves)
    w_out_other = lax.ppermute(w_out, "narrow", swap_halves)
    ffn = (w_in, w_in_other, w_out, w_out_other)
    if not staged:
        attn_all = lax.all_gather(attn_weights, AXES, axis=0, tiled=True)
        res, ig, grads = run_main(me, x_t, g_t, norm_params, ffn, (attn_all,), devices, None)
        res, ig = to_rows(res), to_rows(ig)
        d_attn, d_win, d_wout, sums = grads
        attn = lax.psum_scatter(d_attn, AXES, scatter_dimension=0, tiled=True)
        norm = lax.psum(sums, AXES)
        d_wout = d_wout.reshape(LAYERS, FF, D)
        own_in, other_in = d_win[:, :FF], d_win[:, FF:]
        own_out, other_out = d_wout[:, :FFH], d_wout[:, FFH:]
        win = lax.psum(own_in + lax.ppermute(other_in, "narrow", swap_halves), "dp")
        wout = lax.psum(own_out + lax.ppermute(other_out, "narrow", swap_halves), "dp")
        wout = wout.transpose(0, 2, 1)
    else:
        ex = Exchange(me, devices)
        attn_parts, attn_diffs, (x_t, *others), g_t = ex.gather(
            attn_weights, (x_t, w_in_other, w_out_other), g_t
        )
        ffn = (w_in, others[0], w_out, others[1])
        res, ig, grads = run_main(me, x_t, g_t, norm_params, ffn, attn_parts, devices, attn_diffs)
        res, ig, attn, norm, win, wout = ex.sum_all(*grads, res, ig)
    return (
        res,
        ig,
        attn,
        norm[: 2 * NORMS].reshape(norm_params.shape),
        win.reshape(LAYERS, D, 2, FFH),
        wout.transpose(0, 2, 1),
    )


def solution(mesh):
    rows = P(("dp", "narrow"), None)
    hidden_in = P(None, None, None, "narrow")
    hidden_out = P(None, "narrow", None)
    devices = mesh.shape["dp"] * mesh.shape["narrow"]

    def per_device(*args):
        return on_device(devices, *args)

    return jax.shard_map(
        per_device,
        mesh=mesh,
        in_specs=(rows, rows, P(), hidden_in, hidden_out, rows),
        out_specs=(rows, rows, rows, P(), hidden_in, hidden_out),
        check_vma=False,
    )
```

```python
import math

import jax
import jax.numpy as jnp
from jax import lax
from jax.experimental import pallas as pl
from jax.experimental.pallas import tpu as pltpu
from jax.sharding import PartitionSpec as P

HEADS = 8
HEAD = 24
SLOT = 32
WIDE = HEADS * SLOT
D = HEADS * HEAD
FF = 256
FFH = FF // 2
LAYERS = 2
NORMS = 2 * LAYERS - 1
SEQ = 476
PAIRS = SEQ // 2
KEYS = 240
HALF = 256
LANES = 2 * HALF
EPS = 1e-05
SCALE = HEAD ** (-0.5)
LOG2E = math.log2(math.e)
ATTN_ROWS = LAYERS * 4 * D

GROUP = 8
NEAR = (0, 1, 4, 5)
TWIN = 2
WIN_PART = LAYERS * D // 4
SIDE = 2 * FFH - D
WOUT_PART = LAYERS * FFH // 4
ATTN_PART = ATTN_ROWS // GROUP
OFF_WOUT = ATTN_PART
OFF_NORM = OFF_WOUT + WOUT_PART
OFF_WIN = OFF_NORM + 16
PAY_ROWS = OFF_WIN + WIN_PART
PACK_WOUT = 3 * ATTN_PART // 4
PACK_NORM = PACK_WOUT + 3 * WOUT_PART // 4
PACK_WIN = PACK_NORM + 16
PACK_ROWS = PACK_WIN + WIN_PART

bf16 = jnp.bfloat16
f32 = jnp.float32
AXES = ("dp", "narrow")

VMEM_BYTES = 52 * 1024 * 1024


def mm(left, right):
    return jnp.dot(left, right, preferred_element_type=f32)


def mm_nt(left, right):
    return lax.dot_general(left, right, (((1,), (1,)), ((), ())), preferred_element_type=f32)


def sigmoid(value):
    return 0.5 + 0.5 * jnp.tanh(0.5 * value)


def fold_lanes(value):
    return value[:, 0:128] + value[:, 128:256] + value[:, 256:384] + value[:, 384:512]


def norm_forward(stream, gain, shift):
    center = stream - jnp.sum(stream, axis=0, keepdims=True) * (1.0 / D)
    inverse = lax.rsqrt(jnp.sum(center * center, axis=0, keepdims=True) * (1.0 / D) + EPS)
    unit = center * inverse
    return (unit * gain + shift, unit, inverse)


def norm_backward(grad, unit, inverse, gain):
    scaled = grad * gain
    mean = jnp.sum(scaled, axis=0, keepdims=True) * (1.0 / D)
    slope = jnp.sum(scaled * unit, axis=0, keepdims=True) * (1.0 / D)
    return inverse * (scaled - mean - unit * slope)


def tree_sum(parts):
    while len(parts) > 1:
        parts = [parts[i] + parts[i + 1] for i in range(0, len(parts), 2)]
    return parts[0]


def ds(start, size, step):
    return pl.ds(pl.multiple_of(start, step), size)


def take(refs, count):
    taken = refs[:count]
    del refs[:count]
    return taken


def unit(size):
    row = lax.broadcasted_iota(jnp.int32, (size, size), 0)
    column = lax.broadcasted_iota(jnp.int32, (size, size), 1)
    return (row == column).astype(f32).astype(bf16)


def head_selector(padded_axis):
    shape = (WIDE, D) if padded_axis == 0 else (D, WIDE)
    padded = lax.broadcasted_iota(jnp.int32, shape, padded_axis)
    plain = lax.broadcasted_iota(jnp.int32, shape, 1 - padded_axis)
    inside = padded & (SLOT - 1)
    same = jnp.logical_and(plain == HEAD * (padded >> 5) + inside, inside < HEAD)
    return same.astype(f32).astype(bf16)


def pair_selector(offset, padded_axis):
    shape = (2 * WIDE, D) if padded_axis == 0 else (D, 2 * WIDE)
    padded = lax.broadcasted_iota(jnp.int32, shape, padded_axis)
    plain = lax.broadcasted_iota(jnp.int32, shape, 1 - padded_axis)
    inside = (padded & (2 * SLOT - 1)) - offset
    same = jnp.logical_and(plain == HEAD * (padded >> 6) + inside, inside >= 0)
    return jnp.logical_and(same, inside < HEAD).astype(f32).astype(bf16)


def head_rows(h):
    return slice(SLOT * h, SLOT * (h + 1))


def sample_window(step, rows_total, align):
    base = step * PAIRS
    start = jnp.minimum(base // align * align, rows_total - HALF)
    return ds(start, HALF, align), base - start


def load_sample(ref, step, fill_first):
    window, shift = sample_window(step, ref.shape[0], 16)
    rows = pltpu.roll(ref[window, :].astype(f32), lax.rem(HALF - shift, HALF), 0)
    pair_row = lax.broadcasted_iota(jnp.int32, (HALF, 2 * D), 0)
    cols = jnp.where(pair_row < PAIRS, rows, rows[0:1] if fill_first else 0.0).T
    return jnp.concatenate([cols[:D], cols[D:]], axis=1)


def store_sample(ref, step, value):
    window, shift = sample_window(step, ref.shape[0], 16 if ref.dtype == bf16 else 8)
    cols = jnp.concatenate([value[:, :HALF], value[:, HALF:]], axis=0)
    rows = pltpu.roll(cols.T, shift, 0)
    pair_row = lax.broadcasted_iota(jnp.int32, (HALF, 2 * D), 0)
    here = jnp.logical_and(pair_row >= shift, pair_row < shift + PAIRS)
    ref[window, :] = jnp.where(here, rows, ref[window, :].astype(f32)).astype(ref.dtype)


def attention_forward(normed_b, wqkv_t, wo_t, state, kh_ref, v_ref):
    e_ref, vh_ref, q_ref, k_ref, ctx_ref, rinv_ref = state
    lane = lax.broadcasted_iota(jnp.int32, (WIDE, LANES), 1)
    slot_row = lax.broadcasted_iota(jnp.int32, (WIDE, LANES), 0) & (SLOT - 1)
    real = (lane & (HALF - 1)) < PAIRS
    ones_rows = jnp.logical_or(slot_row == HEAD, slot_row == HEAD + 1).astype(f32)
    qkv = mm(wqkv_t, normed_b)
    queries = (qkv[:WIDE] * (SCALE * LOG2E)).astype(bf16)
    q_ref[...] = queries
    keys = qkv[WIDE : 2 * WIDE].astype(bf16)
    k_ref[...] = keys
    values = jnp.where(real, qkv[2 * WIDE :] + ones_rows, 0.0).astype(bf16)
    v_ref[...] = values
    for tall, ref in ((keys.T, kh_ref), (values.T, vh_ref)):
        for h in range(HEADS):
            ref[h, 0:KEYS] = tall[0:KEYS, head_rows(h)]
            ref[h, KEYS:] = tall[HALF : HALF + KEYS, head_rows(h)]

    def scores_of(h):
        return mm(kh_ref[h], q_ref[head_rows(h), :])

    scores = scores_of(0)
    for h in range(HEADS):
        rows = head_rows(h)
        ahead = scores_of(h + 1) if h + 1 < HEADS else None
        top = jnp.max(scores, axis=0, keepdims=True)
        weights = jnp.exp2(scores - top).astype(bf16)
        e_ref[0 : 2 * KEYS, LANES * h : LANES * (h + 1)] = weights
        out = mm(v_ref[rows, 0:KEYS], weights[0:KEYS]) + mm(
            v_ref[rows, HALF : HALF + KEYS], weights[KEYS:]
        )
        inverse = 1.0 / out[HEAD : HEAD + 1]
        rinv_ref[h : h + 1, :] = inverse
        ctx_ref[rows, :] = out * inverse
        scores = ahead
    return mm(wo_t, ctx_ref[...].astype(bf16))


def attention_backward(grad_b, normed_b, wo, wq, wvk, state, work, sums):
    e_ref, vh_ref, q_ref, k_ref, ctx_ref, rinv_ref = state
    pair_ref, block_ref, dq_ref, dvk_ref = work
    d_wq, d_wvk, d_wo = sums
    group = HEADS // 2
    head_row = lax.broadcasted_iota(jnp.int32, (SLOT, LANES), 0)
    lane_head = lax.broadcasted_iota(jnp.int32, (LANES, 2 * SLOT * group), 1) // (2 * SLOT)
    key_row = lax.broadcasted_iota(jnp.int32, (2 * KEYS, 2 * SLOT * group), 0)
    real_key = jnp.where(key_row < KEYS, key_row, key_row - KEYS) < PAIRS
    in_pair = lax.broadcasted_iota(jnp.int32, (2 * KEYS, 2 * SLOT * group), 1) & (2 * SLOT - 1)

    d_wo[...] += mm_nt(ctx_ref[...].astype(bf16), grad_b)
    d_context = mm(wo, grad_b)
    for h in range(HEADS):
        rows = head_rows(h)
        grad = (d_context[rows] * rinv_ref[h : h + 1, :]).astype(bf16).astype(f32)
        dot = -jnp.sum(grad[:HEAD] * ctx_ref[rows, :][:HEAD], axis=0, keepdims=True)
        dot_high = dot.astype(bf16).astype(f32)
        grad = jnp.where(head_row == HEAD, dot_high, grad)
        grad = jnp.where(head_row == HEAD + 1, dot - dot_high, grad)
        pair_ref[2 * SLOT * h : 2 * SLOT * h + SLOT, :] = grad.astype(bf16)
        pair_ref[2 * SLOT * h + SLOT : 2 * SLOT * (h + 1), :] = q_ref[rows, :]
    tall = pair_ref[...].T
    for h in range(HEADS):
        part = tall[:, WIDE * (h // group) : WIDE * (h // group + 1)]
        block_ref[LANES * h : LANES * (h + 1), :] = jnp.where(
            lane_head == h % group, part, jnp.zeros_like(part)
        )

    for h in range(HEADS + 1):
        if h < HEADS:
            lanes = slice(LANES * h, LANES * (h + 1))
            grad_probs = mm(vh_ref[h], pair_ref[2 * SLOT * h : 2 * SLOT * h + SLOT, :])
            e_ref[2 * KEYS :, lanes] = e_ref[0 : 2 * KEYS, lanes] * grad_probs.astype(bf16)
        if h > 0:
            rows = head_rows(h - 1)
            lanes = slice(LANES * (h - 1), LANES * h)
            dq = mm(k_ref[rows, 0:KEYS], e_ref[2 * KEYS : 3 * KEYS, lanes]) + mm(
                k_ref[rows, HALF : HALF + KEYS], e_ref[3 * KEYS :, lanes]
            )
            dq_ref[rows, :] = (dq * SCALE).astype(bf16)
    for g in range(2):
        here = slice(group * LANES * g, group * LANES * (g + 1))
        both = mm(e_ref[:, here], block_ref[here, :])
        dv = jnp.where(real_key, both[: 2 * KEYS], 0.0)
        dk = both[2 * KEYS :] * (1.0 / LOG2E)
        dvk = jnp.where(in_pair < SLOT, dv, dk).astype(bf16)
        for half in range(2):
            there = slice(half * HALF, half * HALF + KEYS)
            dvk_ref[there, WIDE * g : WIDE * (g + 1)] = dvk[half * KEYS : (half + 1) * KEYS]
    d_wq[...] += mm_nt(normed_b, dq_ref[...])
    d_wvk[...] += mm(normed_b, dvk_ref[...])
    return mm(wq, dq_ref[...]) + mm_nt(wvk, dvk_ref[...])


def resplit(sums):
    high = sums.astype(bf16).astype(f32)
    return jnp.concatenate([high, sums - high], axis=0).astype(bf16)


def finish_attention(d_attn, sums):
    tall, wide = head_selector(0), head_selector(1)
    for layer in range(LAYERS):
        d_wq, d_wvk, d_wo = sums[layer]
        mixed = d_wvk[...].astype(bf16)
        base = 4 * layer * D
        d_attn[base : base + D, :] = mm(d_wq[...].astype(bf16), tall)
        d_attn[base + D : base + 2 * D, :] = mm(mixed, pair_selector(SLOT, 0))
        d_attn[base + 2 * D : base + 3 * D, :] = mm(mixed, pair_selector(0, 0))
        d_attn[base + 3 * D : base + 4 * D, :] = mm(wide, d_wo[...].astype(bf16))


def finish_norms(d_norm):
    sums = [jnp.sum(d_norm[j].T, axis=0, keepdims=True) for j in range(2 * NORMS)]
    return jnp.concatenate(sums + [jnp.zeros((8 - 2 * NORMS, D), f32)], axis=0)


def pack_gradients(outs, me, parts, d_attn, d_win, d_wout, norms):
    each, upper = ATTN_ROWS // parts, parts // GROUP
    norms = resplit(norms)
    for t, out in enumerate(outs):
        for j, k in enumerate(NEAR):
            low = (me % GROUP) ^ k ^ (TWIN * t)
            quarter = low // 2
            half = k % 2
            attn = [d_attn[ds((u * GROUP + low) * each, each, each), :] for u in range(upper)]
            first = (quarter // 2) * FF + half * FFH + (quarter % 2) * WOUT_PART
            wout = d_wout[ds(first, WOUT_PART, WOUT_PART), :]
            win = d_win[ds(quarter * WIN_PART, WIN_PART, WIN_PART), half * FF : (half + 1) * FF]
            for at, value in ((0, jnp.concatenate(attn, axis=0)), (PACK_WOUT, wout)):
                value = value.astype(bf16)
                rows = value.shape[0] // 4
                out[j, at : at + 3 * rows, 0:D] = value[: 3 * rows]
                for c in range(3):
                    part = value[3 * rows :, SIDE * c : SIDE * (c + 1)]
                    out[j, at + rows * c : at + rows * (c + 1), D:] = part
            out[j, PACK_NORM:PACK_WIN, 0:D] = norms
            out[j, PACK_WIN:PACK_ROWS, :] = win.astype(bf16)


STATE = [
    ((4 * KEYS, HEADS * LANES), bf16),
    ((HEADS, 2 * KEYS, SLOT), bf16),
    ((WIDE, LANES), bf16),
    ((WIDE, LANES), bf16),
    ((WIDE, LANES), f32),
    ((HEADS, LANES), f32),
]
WORK = [
    ((2 * WIDE, LANES), bf16),
    ((HEADS * LANES, WIDE), bf16),
    ((WIDE, LANES), bf16),
    ((LANES, 2 * WIDE), bf16),
]
SUMS = [((D, WIDE), f32), ((D, 2 * WIDE), f32), ((WIDE, D), f32)]
GRADS = [
    *SUMS,
    *SUMS,
    ((LAYERS * D, 2 * FF), f32),
    ((LAYERS * FF, D), f32),
    ((2 * NORMS, D, 128), f32),
    ((ATTN_ROWS, D), f32),
]
SCRATCH = [
    ((LAYERS, 3 * WIDE, D), bf16),
    ((LAYERS, D, WIDE), bf16),
    ((LAYERS, D, 2 * WIDE), bf16),
    ((LAYERS, D, WIDE), bf16),
    ((LAYERS, WIDE, D), bf16),
    ((LAYERS, 2 * FF, D), bf16),
    ((LAYERS, D, 2 * FF), bf16),
    ((LAYERS, D, FF), bf16),
    ((LAYERS, FF, D), bf16),
    ((2 * NORMS, D, 128), f32),
    ((ATTN_ROWS, D), bf16),
    *GRADS,
    *STATE,
    *STATE,
    *WORK,
    ((HEADS, 2 * KEYS, SLOT), bf16),
    ((WIDE, LANES), bf16),
    ((LAYERS, 2 * FF, LANES), f32),
    ((2 * LAYERS * D, FFH), f32),
]


def main_kernel(parts, attn_diffs, *refs):
    refs = list(refs)
    me_ref, x_ref, g_ref, norm_ref, win_own, win_other, wout_own, wout_other = take(refs, 8)
    attn_refs = take(refs, len(attn_diffs) if attn_diffs else 1)
    res_ref, ig_ref = take(refs, 2)
    outs = take(refs, 2 if attn_diffs else 4)
    wqkv_t, wq, wvk, wo_t, wo, win_t, win, wout_t, wout, norm_t, attn_ref = take(refs, 11)
    sums = (take(refs, 3), take(refs, 3))
    d_win, d_wout, d_norm, d_attn = take(refs, 4)
    states = (take(refs, len(STATE)), take(refs, len(STATE)))
    work = take(refs, len(WORK))
    kh_ref, v_ref, mixed_ref, win_rows = refs
    dvk_ref = work[-1]
    step = pl.program_id(0)

    @pl.when(step == 0)
    def _():
        for ref in (*sums[0], *sums[1], d_win, d_wout, d_norm, dvk_ref):
            ref[...] = jnp.zeros_like(ref)
        if attn_diffs:
            me = me_ref[0]
            for ref, diffs in zip(attn_refs, attn_diffs, strict=True):
                each = ref.shape[1]
                for i, diff in enumerate(diffs):
                    attn_ref[ds((me ^ diff) * each, each, each), :] = ref[i]
        else:
            attn_ref[...] = attn_refs[0][...]
        norms = [norm_ref[i] for i in range(NORMS)]
        turned = jnp.concatenate(norms + [jnp.zeros((8 - 2 * NORMS, D), f32)], axis=0).T
        for i in range(2 * NORMS):
            norm_t[i] = jnp.broadcast_to(turned[:, i : i + 1], (D, 128))
        tall, wide = head_selector(0), head_selector(1)
        for layer in range(LAYERS):
            for j in range(4):
                base = (4 * layer + j) * D
                matrix = attn_ref[base : base + D, :]
                if j < 3:
                    wqkv_t[layer, j * WIDE : (j + 1) * WIDE, :] = mm_nt(tall, matrix).astype(bf16)
                if j == 0:
                    wq[layer] = mm(matrix, wide).astype(bf16)
                elif j == 1:
                    turned_keys = mm(matrix, pair_selector(SLOT, 1))
                elif j == 2:
                    wvk[layer] = (turned_keys + mm(matrix, pair_selector(0, 1))).astype(bf16)
                else:
                    padded = mm(tall, matrix).astype(bf16)
                    wo[layer] = padded
                    wo_t[layer] = mm_nt(unit(D), padded).astype(bf16)
        for p, (w1, w2) in enumerate(((win_own, wout_own), (win_other, wout_other))):
            win_rows[...] = w1[...].astype(f32)
            for layer in range(LAYERS):
                for g in range(2):
                    part = win_rows[pl.ds(2 * layer * D + g, D, stride=2), :].astype(bf16)
                    here = slice(p * FF + g * FFH, p * FF + (g + 1) * FFH)
                    win[layer, :, here] = part
                    win_t[layer, here, :] = mm_nt(unit(FFH), part).astype(bf16)
                wout_t[layer, :, p * FFH : (p + 1) * FFH] = w2[layer]
                wout[layer, p * FFH : (p + 1) * FFH, :] = mm_nt(unit(FFH), w2[layer]).astype(bf16)

    def add_norm(index, grad, unit):
        d_norm[2 * index] += fold_lanes(grad * unit)
        d_norm[2 * index + 1] += fold_lanes(grad)

    def gain_of(index):
        return jnp.concatenate([norm_t[2 * index]] * (LANES // 128), axis=1)

    def shift_of(index):
        return jnp.concatenate([norm_t[2 * index + 1]] * (LANES // 128), axis=1)

    kept = []
    normed_b = x_ref[0]
    stream = normed_b.astype(f32)
    unit_a = inv_a = None
    for layer in range(LAYERS):
        if layer > 0:
            normed, unit_a, inv_a = norm_forward(stream, gain_of(2 * layer - 1), shift_of(2 * layer - 1))
            normed_b = normed.astype(bf16)
        stream = stream + attention_forward(
            normed_b, wqkv_t[layer], wo_t[layer], states[layer], kh_ref, v_ref
        )
        normed, unit_f, inv_f = norm_forward(stream, gain_of(2 * layer), shift_of(2 * layer))
        ffn_b = normed.astype(bf16)
        mixed = mm(win_t[layer], ffn_b)
        mixed_ref[layer] = mixed
        hidden = []
        for p in range(2):
            value = mixed[FF * p : FF * p + FFH]
            gate = mixed[FF * p + FFH : FF * (p + 1)]
            hidden.append((value * (gate * sigmoid(gate))).astype(bf16))
        hidden = jnp.concatenate(hidden, axis=0)
        stream = stream + mm(wout_t[layer], hidden)
        kept.append((normed_b, unit_a, inv_a, ffn_b, unit_f, inv_f, hidden))
    res_ref[0] = stream.astype(bf16)

    grad = g_ref[0].astype(f32)
    for layer in reversed(range(LAYERS)):
        normed_b, unit_a, inv_a, ffn_b, unit_f, inv_f, hidden = kept[layer]
        grad_b = grad.astype(bf16)
        d_wout[FF * layer : FF * (layer + 1), :] += mm_nt(hidden, grad_b)
        d_hidden = mm(wout[layer], grad_b)
        d_mixed = []
        for p in range(2):
            value = mixed_ref[layer, FF * p : FF * p + FFH]
            gate = mixed_ref[layer, FF * p + FFH : FF * (p + 1)]
            part = d_hidden[FFH * p : FFH * (p + 1)]
            sig = sigmoid(gate)
            d_mixed.append((part * (gate * sig)).astype(bf16))
            d_mixed.append((part * value * sig * (1.0 + gate * (1.0 - sig))).astype(bf16))
        d_mixed = jnp.concatenate(d_mixed, axis=0)
        d_win[D * layer : D * (layer + 1), :] += mm_nt(ffn_b, d_mixed)
        d_normed = mm(win[layer], d_mixed)
        add_norm(2 * layer, d_normed, unit_f)
        grad = grad + norm_backward(d_normed, unit_f, inv_f, gain_of(2 * layer))
        d_att = attention_backward(
            grad.astype(bf16), normed_b, wo[layer], wq[layer], wvk[layer], states[layer], work, sums[layer]
        )
        if layer > 0:
            add_norm(2 * layer - 1, d_att, unit_a)
            grad = grad + norm_backward(d_att, unit_a, inv_a, gain_of(2 * layer - 1))
        else:
            grad = grad + d_att
    ig_ref[0] = grad

    @pl.when(step == pl.num_programs(0) - 1)
    def _():
        finish_attention(d_attn, sums)
        norms = finish_norms(d_norm)
        if attn_diffs:
            pack_gradients(outs, me_ref[0], parts, d_attn, d_win, d_wout, norms)
        else:
            for out, value in zip(outs, (d_attn[...], d_win[...], d_wout[...], norms), strict=True):
                out[...] = value


VMEM = pl.BlockSpec(memory_space=pltpu.VMEM)
SMEM = pl.BlockSpec(memory_space=pltpu.SMEM)


def shapes_of(pairs):
    return [jax.ShapeDtypeStruct(*pair) for pair in pairs]


def vmem_of(pairs):
    return [pltpu.VMEM(*pair) for pair in pairs]


def per_sample():
    return pl.BlockSpec((1, D, LANES), lambda i: (i, 0, 0))


def to_columns(rows, fill_first):
    samples = rows.shape[0] // PAIRS

    def body(rows_ref, out_ref):
        out_ref[0] = load_sample(rows_ref, pl.program_id(0), fill_first).astype(bf16)

    return pl.pallas_call(
        body,
        grid=(samples,),
        in_specs=[VMEM],
        out_specs=per_sample(),
        out_shape=jax.ShapeDtypeStruct((samples, D, LANES), bf16),
        compiler_params=pltpu.CompilerParams(vmem_limit_bytes=32 * 1024 * 1024),
    )(rows)


def to_rows(columns):
    samples = columns.shape[0]

    def body(columns_ref, out_ref):
        store_sample(out_ref, pl.program_id(0), columns_ref[0].astype(f32))

    return pl.pallas_call(
        body,
        grid=(samples,),
        in_specs=[per_sample()],
        out_specs=VMEM,
        out_shape=jax.ShapeDtypeStruct((samples * PAIRS, 2 * D), columns.dtype),
        compiler_params=pltpu.CompilerParams(vmem_limit_bytes=32 * 1024 * 1024),
    )(columns)


def run_main(me, tokens, cotangent, norm_params, ffn, attn_parts, parts, attn_diffs):
    samples = tokens.shape[0]
    inputs = (norm_params, *ffn, *attn_parts)
    if attn_diffs:
        grads = [((len(NEAR), PACK_ROWS, 2 * FFH), bf16)] * 2
    else:
        grads = [((ATTN_ROWS, D), f32), GRADS[6], GRADS[7], ((8, D), f32)]

    def body(*refs):
        main_kernel(parts, attn_diffs, *refs)

    out_shape = [((samples, D, LANES), bf16), ((samples, D, LANES), f32), *grads]
    res, ig, *grads = pl.pallas_call(
        body,
        grid=(samples,),
        in_specs=[SMEM, per_sample(), per_sample()] + [VMEM] * len(inputs),
        out_specs=[per_sample(), per_sample()] + [VMEM] * len(grads),
        out_shape=shapes_of(out_shape),
        scratch_shapes=vmem_of(SCRATCH),
        compiler_params=pltpu.CompilerParams(
            dimension_semantics=("arbitrary",), vmem_limit_bytes=VMEM_BYTES
        ),
        cost_estimate=pl.CostEstimate(
            flops=samples * 5_000_000_000, bytes_accessed=20_000_000, transcendentals=0
        ),
    )(me, tokens, cotangent, *inputs)
    return res, ig, grads


def small_kernel(body, out_shape, *inputs, scratch=()):
    return pl.pallas_call(
        body,
        in_specs=[SMEM] + [VMEM] * (len(inputs) - 1),
        out_specs=[VMEM] * len(out_shape),
        out_shape=shapes_of(out_shape),
        scratch_shapes=vmem_of(scratch),
        compiler_params=pltpu.CompilerParams(vmem_limit_bytes=32 * 1024 * 1024),
    )(*inputs)


class Exchange:
    def __init__(self, me, parts):
        self.me = me
        self.parts = parts
        self.upper = parts // GROUP
        self.each = ATTN_ROWS // parts
        self.bits = [1 << i for i in range(self.upper.bit_length() - 1)]

    def swap(self, value, k):
        return lax.ppermute(value, AXES, [(i, i ^ k) for i in range(self.parts)])

    def stack(self, blocks):
        size, kind = blocks[0].shape, blocks[0].dtype
        count = math.prod(size[:-2])

        def body(me_ref, *refs):
            ins, out = refs[:-1], refs[-1]
            for i, ref in enumerate(ins):
                if len(size) == 2:
                    out[i] = ref[...]
                else:
                    out[i * count : (i + 1) * count] = ref[...]

        shape = (len(blocks) * count, *size[-2:])
        return small_kernel(body, [(shape, kind)], self.me, *blocks)[0]

    def gather(self, rows, beside_rest, beside_plane):
        far = [GROUP * u for u in range(self.upper)]
        landed = [rows] + [self.swap(rows, k) for k in far[1:]]
        landed, beside_rest = lax.optimization_barrier((landed, beside_rest))
        column = self.stack(landed)
        landed = [column] + [self.swap(column, k) for k in NEAR[1:]]
        landed, beside_plane = lax.optimization_barrier((landed, beside_plane))
        plane = self.stack(landed)
        diffs = [k ^ u for k in NEAR for u in far]
        parts, diffs = [plane, self.swap(plane, TWIN)], [diffs, [d ^ TWIN for d in diffs]]
        return parts, diffs, beside_rest, beside_plane

    def twins(self, mine, theirs):
        def body(me_ref, mine, theirs, *outs):
            for j, out in enumerate(outs):
                total = mine[j].astype(f32) + theirs[j].astype(f32)
                out[0:PACK_NORM] = total[0:PACK_NORM].astype(out.dtype)
                sums = total[PACK_NORM : PACK_NORM + 8] + total[PACK_NORM + 8 : PACK_WIN]
                out[PACK_NORM:PACK_WIN] = resplit(sums).astype(out.dtype)
                out[PACK_WIN:] = total[PACK_WIN:].astype(out.dtype)

        shape = (PACK_ROWS, 2 * FFH)
        shapes = [(shape, f32)] + [(shape, bf16)] * (len(NEAR) - 1)
        return small_kernel(body, shapes, self.me, mine, theirs)

    def across_plane(self, pieces):
        return [pieces[0]] + [self.swap(piece, k) for piece, k in zip(pieces[1:], NEAR[1:], strict=True)]

    def emit(self, total, blocks, at, keep, send):
        half = len(blocks) // 2
        each = self.each
        for out, rows in ((keep, blocks[:half]), (send, blocks[half:])):
            for i, row in enumerate(rows):
                out[i * each : (i + 1) * each, :] = total[ds(row, each, 8), :].astype(out.dtype)
        first = half * each
        last = at + OFF_NORM - OFF_WOUT
        norm = resplit(total[last : last + 8, :] + total[last + 8 : last + 16, :])
        rest = [
            total[at:last, :].astype(bf16),
            norm,
            total[last + 16 : at + PAY_ROWS - OFF_WOUT, :].astype(bf16),
        ]
        for out in (keep, send):
            row = first
            for part in rest:
                out[row : row + part.shape[0], :] = part.astype(out.dtype)
                row += part.shape[0]

    def stage_shapes(self, blocks):
        shape = (blocks * self.each + PAY_ROWS - OFF_WOUT, 2 * FFH)
        return [(shape, f32), (shape, bf16)]

    def after_plane(self, landed):
        def body(me_ref, *refs):
            ins, (keep, send, packed, total) = refs[: len(NEAR)], refs[len(NEAR) :]
            packed[...] = tree_sum([r[...].astype(f32) for r in ins])
            for at, to, size in ((0, 0, ATTN_PART), (PACK_WOUT, OFF_WOUT, WOUT_PART)):
                rows = size // 4
                total[to : to + 3 * rows, 0:D] = packed[at : at + 3 * rows, 0:D]
                for c in range(3):
                    part = packed[at + rows * c : at + rows * (c + 1), D:]
                    total[to + 3 * rows : to + size, SIDE * c : SIDE * (c + 1)] = part
            total[OFF_NORM:OFF_WIN, :] = packed[PACK_NORM:PACK_WIN, :]
            total[OFF_WIN:, :] = packed[PACK_WIN:, :]
            mine = me_ref[0] // GROUP
            order = [r for r in range(self.upper) if not r & 1] + [r for r in range(self.upper) if r & 1]
            self.emit(total, [(mine ^ r) * self.each for r in order], OFF_WOUT, keep, send)

        scratch = [((PACK_ROWS, 2 * FFH), f32), ((PAY_ROWS, 2 * FFH), f32)]
        return small_kernel(body, self.stage_shapes(self.upper // 2), self.me, *landed, scratch=scratch)

    def after_bit(self, mine, theirs, blocks):
        def body(me_ref, mine, theirs, keep, send, total):
            total[...] = mine[...] + theirs[...].astype(f32)
            self.emit(total, [i * self.each for i in range(blocks)], blocks * self.each, keep, send)

        (shape, _), _ = self.stage_shapes(blocks)
        return small_kernel(
            body, self.stage_shapes(blocks // 2), self.me, mine, theirs, scratch=[(shape, f32)]
        )

    def after_rest(self, mine, theirs):
        each = self.each
        at_norm = each + WOUT_PART
        ffn_rows = WOUT_PART + WIN_PART

        def body(me_ref, mine, theirs, attn, norm, ffn):
            total = mine[...] + theirs[...].astype(f32)
            attn[...] = total[0:each, 0:D]
            norm[...] = total[at_norm : at_norm + 8, 0:D] + total[at_norm + 8 : at_norm + 16, 0:D]
            ffn[0, 0:WOUT_PART, :] = total[each:at_norm, :].astype(bf16)
            ffn[0, WOUT_PART:, :] = total[at_norm + 16 :, :].astype(bf16)

        shapes = [((each, D), f32), ((8, D), f32), ((1, ffn_rows, 2 * FFH), bf16)]
        return small_kernel(body, shapes, self.me, mine, theirs)

    def spread(self, ffn):
        block = self.stack([ffn, self.swap(ffn, 4)])
        theirs = self.swap(block, TWIN)

        def body(me_ref, mine, theirs, win, wout, rows):
            for t, ref in enumerate((mine, theirs)):
                for i in range(2):
                    quarter = ((me_ref[0] % GROUP) ^ (4 * i) ^ (TWIN * t)) // 2
                    part = ref[i].astype(f32)
                    rows[ds(quarter * WOUT_PART, WOUT_PART, WOUT_PART), :] = part[:WOUT_PART, 0:D]
                    for g in range(2):
                        there = pl.ds(2 * WIN_PART * quarter + g, WIN_PART, stride=2)
                        win[there, :] = part[WOUT_PART:, FFH * g : FFH * (g + 1)]
            for layer in range(LAYERS):
                wout[layer] = rows[FFH * layer : FFH * (layer + 1), :].T

        shapes = [((2 * LAYERS * D, FFH), f32), ((LAYERS, D, FFH), f32)]
        scratch = [((LAYERS * FFH, D), f32)]
        return small_kernel(body, shapes, self.me, block, theirs, scratch=scratch)

    def sum_all(self, keep, send, res, ig):
        landed = self.across_plane(self.twins(keep, self.swap(send, TWIN)))
        landed, res = lax.optimization_barrier((landed, to_rows(res)))
        keep, send = self.after_plane(landed)
        blocks = self.upper // 2
        for bit in self.bits[:-1]:
            keep, send = self.after_bit(keep, self.swap(send, GROUP * bit), blocks)
            blocks //= 2
        theirs = self.swap(send, GROUP * self.bits[-1])
        theirs, ig = lax.optimization_barrier((theirs, to_rows(ig)))
        attn, norm, ffn = self.after_rest(keep, theirs)
        return res, ig, attn, norm, *self.spread(ffn)


def on_device(devices, tokens, attn_weights, norm_params, w_in, w_out, cotangent):
    each = attn_weights.shape[0]
    me = (lax.axis_index("dp") * 2 + lax.axis_index("narrow")).astype(jnp.int32).reshape(1)
    staged = devices % (2 * GROUP) == 0 and each % 16 == 0
    x_t = to_columns(tokens, True)
    g_t = to_columns(cotangent, False)
    swap_halves = [(0, 1), (1, 0)]
    w_in = w_in.reshape(2 * LAYERS * D, FFH)
    w_out = w_out.transpose(0, 2, 1)
    w_in_other = lax.ppermute(w_in, "narrow", swap_halves)
    w_out_other = lax.ppermute(w_out, "narrow", swap_halves)
    ffn = (w_in, w_in_other, w_out, w_out_other)
    if not staged:
        attn_all = lax.all_gather(attn_weights, AXES, axis=0, tiled=True)
        res, ig, grads = run_main(me, x_t, g_t, norm_params, ffn, (attn_all,), devices, None)
        res, ig = to_rows(res), to_rows(ig)
        d_attn, d_win, d_wout, sums = grads
        attn = lax.psum_scatter(d_attn, AXES, scatter_dimension=0, tiled=True)
        norm = lax.psum(sums, AXES)
        d_wout = d_wout.reshape(LAYERS, FF, D)
        own_in, other_in = d_win[:, :FF], d_win[:, FF:]
        own_out, other_out = d_wout[:, :FFH], d_wout[:, FFH:]
        win = lax.psum(own_in + lax.ppermute(other_in, "narrow", swap_halves), "dp")
        wout = lax.psum(own_out + lax.ppermute(other_out, "narrow", swap_halves), "dp")
        wout = wout.transpose(0, 2, 1)
    else:
        ex = Exchange(me, devices)
        attn_parts, attn_diffs, (x_t, *others), g_t = ex.gather(
            attn_weights, (x_t, w_in_other, w_out_other), g_t
        )
        ffn = (w_in, others[0], w_out, others[1])
        res, ig, grads = run_main(me, x_t, g_t, norm_params, ffn, attn_parts, devices, attn_diffs)
        res, ig, attn, norm, win, wout = ex.sum_all(*grads, res, ig)
    return (
        res,
        ig,
        attn,
        norm[: 2 * NORMS].reshape(norm_params.shape),
        win.reshape(LAYERS, D, 2, FFH),
        wout.transpose(0, 2, 1),
    )


def solution(mesh):
    rows = P(("dp", "narrow"), None)
    hidden_in = P(None, None, None, "narrow")
    hidden_out = P(None, "narrow", None)
    devices = mesh.shape["dp"] * mesh.shape["narrow"]

    def per_device(*args):
        return on_device(devices, *args)

    return jax.shard_map(
        per_device,
        mesh=mesh,
        in_specs=(rows, rows, P(), hidden_in, hidden_out, rows),
        out_specs=(rows, rows, rows, P(), hidden_in, hidden_out),
        check_vma=False,
    )
```

```python
import math

import jax
import jax.numpy as jnp
from jax import lax
from jax.experimental import pallas as pl
from jax.experimental.pallas import tpu as pltpu
from jax.sharding import PartitionSpec as P

HEADS = 8
HEAD = 24
SLOT = 32
WIDE = HEADS * SLOT
D = HEADS * HEAD
FF = 256
FFH = FF // 2
LAYERS = 2
NORMS = 2 * LAYERS - 1
SEQ = 476
PAIRS = SEQ // 2
KEYS = 240
HALF = 256
LANES = 2 * HALF
EPS = 1e-05
SCALE = HEAD ** (-0.5)
LOG2E = math.log2(math.e)
ATTN_ROWS = LAYERS * 4 * D

GROUP = 8
NEAR = (0, 1, 4, 5)
TWIN = 2
WIN_PART = LAYERS * D // 4
SIDE = 2 * FFH - D
WOUT_PART = LAYERS * FFH // 4
ATTN_PART = ATTN_ROWS // GROUP
OFF_WOUT = ATTN_PART
OFF_NORM = OFF_WOUT + WOUT_PART
OFF_WIN = OFF_NORM + 16
PAY_ROWS = OFF_WIN + WIN_PART
PACK_WOUT = 3 * ATTN_PART // 4
PACK_NORM = PACK_WOUT + 3 * WOUT_PART // 4
PACK_WIN = PACK_NORM + 16
PACK_ROWS = PACK_WIN + WIN_PART

bf16 = jnp.bfloat16
f32 = jnp.float32
AXES = ("dp", "narrow")

TOGETHER = 2
VMEM_BYTES = 56 * 1024 * 1024


def mm(left, right):
    return jnp.dot(left, right, preferred_element_type=f32)


def mm_nt(left, right):
    return lax.dot_general(left, right, (((1,), (1,)), ((), ())), preferred_element_type=f32)


def sigmoid(value):
    return 0.5 + 0.5 * jnp.tanh(0.5 * value)


def fold_lanes(value):
    return value[:, 0:128] + value[:, 128:256] + value[:, 256:384] + value[:, 384:512]


def norm_forward(stream, gain, shift):
    center = stream - jnp.sum(stream, axis=0, keepdims=True) * (1.0 / D)
    inverse = lax.rsqrt(jnp.sum(center * center, axis=0, keepdims=True) * (1.0 / D) + EPS)
    unit = center * inverse
    return (unit * gain + shift, unit, inverse)


def norm_backward(grad, unit, inverse, gain):
    scaled = grad * gain
    mean = jnp.sum(scaled, axis=0, keepdims=True) * (1.0 / D)
    slope = jnp.sum(scaled * unit, axis=0, keepdims=True) * (1.0 / D)
    return inverse * (scaled - mean - unit * slope)


def tree_sum(parts):
    while len(parts) > 1:
        parts = [parts[i] + parts[i + 1] for i in range(0, len(parts), 2)]
    return parts[0]


def ds(start, size, step):
    return pl.ds(pl.multiple_of(start, step), size)


def take(refs, count):
    taken = refs[:count]
    del refs[:count]
    return taken


def unit(size):
    row = lax.broadcasted_iota(jnp.int32, (size, size), 0)
    column = lax.broadcasted_iota(jnp.int32, (size, size), 1)
    return (row == column).astype(f32).astype(bf16)


def head_selector(padded_axis):
    shape = (WIDE, D) if padded_axis == 0 else (D, WIDE)
    padded = lax.broadcasted_iota(jnp.int32, shape, padded_axis)
    plain = lax.broadcasted_iota(jnp.int32, shape, 1 - padded_axis)
    inside = padded & (SLOT - 1)
    same = jnp.logical_and(plain == HEAD * (padded >> 5) + inside, inside < HEAD)
    return same.astype(f32).astype(bf16)


def pair_selector(offset, padded_axis):
    shape = (2 * WIDE, D) if padded_axis == 0 else (D, 2 * WIDE)
    padded = lax.broadcasted_iota(jnp.int32, shape, padded_axis)
    plain = lax.broadcasted_iota(jnp.int32, shape, 1 - padded_axis)
    inside = (padded & (2 * SLOT - 1)) - offset
    same = jnp.logical_and(plain == HEAD * (padded >> 6) + inside, inside >= 0)
    return jnp.logical_and(same, inside < HEAD).astype(f32).astype(bf16)


def head_rows(h):
    return slice(SLOT * h, SLOT * (h + 1))


def sample_window(step, rows_total, align):
    base = step * PAIRS
    start = jnp.minimum(base // align * align, rows_total - HALF)
    return ds(start, HALF, align), base - start


def load_sample(ref, step, fill_first):
    window, shift = sample_window(step, ref.shape[0], 16)
    rows = pltpu.roll(ref[window, :].astype(f32), lax.rem(HALF - shift, HALF), 0)
    pair_row = lax.broadcasted_iota(jnp.int32, (HALF, 2 * D), 0)
    cols = jnp.where(pair_row < PAIRS, rows, rows[0:1] if fill_first else 0.0).T
    return jnp.concatenate([cols[:D], cols[D:]], axis=1)


def store_sample(ref, step, value):
    window, shift = sample_window(step, ref.shape[0], 16 if ref.dtype == bf16 else 8)
    cols = jnp.concatenate([value[:, :HALF], value[:, HALF:]], axis=0)
    rows = pltpu.roll(cols.T, shift, 0)
    pair_row = lax.broadcasted_iota(jnp.int32, (HALF, 2 * D), 0)
    here = jnp.logical_and(pair_row >= shift, pair_row < shift + PAIRS)
    ref[window, :] = jnp.where(here, rows, ref[window, :].astype(f32)).astype(ref.dtype)


def attention_forward(normed_b, wqkv_t, wo_t, state, kh_ref, v_ref):
    e_ref, vh_ref, q_ref, k_ref, ctx_ref, rinv_ref = state
    lane = lax.broadcasted_iota(jnp.int32, (WIDE, LANES), 1)
    slot_row = lax.broadcasted_iota(jnp.int32, (WIDE, LANES), 0) & (SLOT - 1)
    real = (lane & (HALF - 1)) < PAIRS
    ones_rows = jnp.logical_or(slot_row == HEAD, slot_row == HEAD + 1).astype(f32)
    qkv = mm(wqkv_t, normed_b)
    queries = (qkv[:WIDE] * (SCALE * LOG2E)).astype(bf16)
    q_ref[...] = queries
    keys = qkv[WIDE : 2 * WIDE].astype(bf16)
    k_ref[...] = keys
    values = jnp.where(real, qkv[2 * WIDE :] + ones_rows, 0.0).astype(bf16)
    v_ref[...] = values
    for tall, ref in ((keys.T, kh_ref), (values.T, vh_ref)):
        for h in range(HEADS):
            ref[h, 0:KEYS] = tall[0:KEYS, head_rows(h)]
            ref[h, KEYS:] = tall[HALF : HALF + KEYS, head_rows(h)]

    def scores_of(h):
        return mm(kh_ref[h], q_ref[head_rows(h), :])

    scores = scores_of(0)
    for h in range(HEADS):
        rows = head_rows(h)
        ahead = scores_of(h + 1) if h + 1 < HEADS else None
        top = jnp.max(scores, axis=0, keepdims=True)
        weights = jnp.exp2(scores - top).astype(bf16)
        e_ref[0 : 2 * KEYS, LANES * h : LANES * (h + 1)] = weights
        out = mm(v_ref[rows, 0:KEYS], weights[0:KEYS]) + mm(
            v_ref[rows, HALF : HALF + KEYS], weights[KEYS:]
        )
        inverse = 1.0 / out[HEAD : HEAD + 1]
        rinv_ref[h : h + 1, :] = inverse
        ctx_ref[rows, :] = out * inverse
        scores = ahead
    return mm(wo_t, ctx_ref[...].astype(bf16))


def attention_backward(grad_b, normed_b, wo, wq, wvk, state, work, sums):
    e_ref, vh_ref, q_ref, k_ref, ctx_ref, rinv_ref = state
    pair_ref, block_ref, dq_ref, dvk_ref = work
    d_wq, d_wvk, d_wo = sums
    group = HEADS // 2
    head_row = lax.broadcasted_iota(jnp.int32, (SLOT, LANES), 0)
    lane_head = lax.broadcasted_iota(jnp.int32, (LANES, 2 * SLOT * group), 1) // (2 * SLOT)
    key_row = lax.broadcasted_iota(jnp.int32, (2 * KEYS, 2 * SLOT * group), 0)
    real_key = jnp.where(key_row < KEYS, key_row, key_row - KEYS) < PAIRS
    in_pair = lax.broadcasted_iota(jnp.int32, (2 * KEYS, 2 * SLOT * group), 1) & (2 * SLOT - 1)

    d_wo[...] += mm_nt(ctx_ref[...].astype(bf16), grad_b)
    d_context = mm(wo, grad_b)
    for h in range(HEADS):
        rows = head_rows(h)
        grad = (d_context[rows] * rinv_ref[h : h + 1, :]).astype(bf16).astype(f32)
        dot = -jnp.sum(grad[:HEAD] * ctx_ref[rows, :][:HEAD], axis=0, keepdims=True)
        dot_high = dot.astype(bf16).astype(f32)
        grad = jnp.where(head_row == HEAD, dot_high, grad)
        grad = jnp.where(head_row == HEAD + 1, dot - dot_high, grad)
        pair_ref[2 * SLOT * h : 2 * SLOT * h + SLOT, :] = grad.astype(bf16)
        pair_ref[2 * SLOT * h + SLOT : 2 * SLOT * (h + 1), :] = q_ref[rows, :]
    tall = pair_ref[...].T
    for h in range(HEADS):
        part = tall[:, WIDE * (h // group) : WIDE * (h // group + 1)]
        block_ref[LANES * h : LANES * (h + 1), :] = jnp.where(
            lane_head == h % group, part, jnp.zeros_like(part)
        )

    for h in range(HEADS + 1):
        if h < HEADS:
            lanes = slice(LANES * h, LANES * (h + 1))
            grad_probs = mm(vh_ref[h], pair_ref[2 * SLOT * h : 2 * SLOT * h + SLOT, :])
            e_ref[2 * KEYS :, lanes] = e_ref[0 : 2 * KEYS, lanes] * grad_probs.astype(bf16)
        if h > 0:
            rows = head_rows(h - 1)
            lanes = slice(LANES * (h - 1), LANES * h)
            dq = mm(k_ref[rows, 0:KEYS], e_ref[2 * KEYS : 3 * KEYS, lanes]) + mm(
                k_ref[rows, HALF : HALF + KEYS], e_ref[3 * KEYS :, lanes]
            )
            dq_ref[rows, :] = (dq * SCALE).astype(bf16)
    for g in range(2):
        here = slice(group * LANES * g, group * LANES * (g + 1))
        both = mm(e_ref[:, here], block_ref[here, :])
        dv = jnp.where(real_key, both[: 2 * KEYS], 0.0)
        dk = both[2 * KEYS :] * (1.0 / LOG2E)
        dvk = jnp.where(in_pair < SLOT, dv, dk).astype(bf16)
        for half in range(2):
            there = slice(half * HALF, half * HALF + KEYS)
            dvk_ref[there, WIDE * g : WIDE * (g + 1)] = dvk[half * KEYS : (half + 1) * KEYS]
    d_wq[...] += mm_nt(normed_b, dq_ref[...])
    d_wvk[...] += mm(normed_b, dvk_ref[...])
    return mm(wq, dq_ref[...]) + mm_nt(wvk, dvk_ref[...])


def resplit(sums):
    high = sums.astype(bf16).astype(f32)
    return jnp.concatenate([high, sums - high], axis=0).astype(bf16)


def finish_attention(d_attn, sums):
    tall, wide = head_selector(0), head_selector(1)
    for layer in range(LAYERS):
        d_wq, d_wvk, d_wo = sums[layer]
        mixed = d_wvk[...].astype(bf16)
        base = 4 * layer * D
        d_attn[base : base + D, :] = mm(d_wq[...].astype(bf16), tall)
        d_attn[base + D : base + 2 * D, :] = mm(mixed, pair_selector(SLOT, 0))
        d_attn[base + 2 * D : base + 3 * D, :] = mm(mixed, pair_selector(0, 0))
        d_attn[base + 3 * D : base + 4 * D, :] = mm(wide, d_wo[...].astype(bf16))


def finish_norms(d_norm):
    sums = [jnp.sum(d_norm[j].T, axis=0, keepdims=True) for j in range(2 * NORMS)]
    return jnp.concatenate(sums + [jnp.zeros((8 - 2 * NORMS, D), f32)], axis=0)


def pack_gradients(outs, me, parts, d_attn, d_win, d_wout, norms):
    each, upper = ATTN_ROWS // parts, parts // GROUP
    norms = resplit(norms)
    for t, out in enumerate(outs):
        for j, k in enumerate(NEAR):
            low = (me % GROUP) ^ k ^ (TWIN * t)
            quarter = low // 2
            half = k % 2
            attn = [d_attn[ds((u * GROUP + low) * each, each, each), :] for u in range(upper)]
            first = (quarter // 2) * FF + half * FFH + (quarter % 2) * WOUT_PART
            wout = d_wout[ds(first, WOUT_PART, WOUT_PART), :]
            win = d_win[ds(quarter * WIN_PART, WIN_PART, WIN_PART), half * FF : (half + 1) * FF]
            for at, value in ((0, jnp.concatenate(attn, axis=0)), (PACK_WOUT, wout)):
                value = value.astype(bf16)
                rows = value.shape[0] // 4
                out[j, at : at + 3 * rows, 0:D] = value[: 3 * rows]
                for c in range(3):
                    part = value[3 * rows :, SIDE * c : SIDE * (c + 1)]
                    out[j, at + rows * c : at + rows * (c + 1), D:] = part
            out[j, PACK_NORM:PACK_WIN, 0:D] = norms
            out[j, PACK_WIN:PACK_ROWS, :] = win.astype(bf16)


STATE = [
    ((4 * KEYS, HEADS * LANES), bf16),
    ((HEADS, 2 * KEYS, SLOT), bf16),
    ((WIDE, LANES), bf16),
    ((WIDE, LANES), bf16),
    ((WIDE, LANES), f32),
    ((HEADS, LANES), f32),
]
WORK = [
    ((2 * WIDE, LANES), bf16),
    ((HEADS * LANES, WIDE), bf16),
    ((WIDE, LANES), bf16),
    ((LANES, 2 * WIDE), bf16),
]
SUMS = [((D, WIDE), f32), ((D, 2 * WIDE), f32), ((WIDE, D), f32)]
GRADS = [
    *SUMS,
    *SUMS,
    ((LAYERS * D, 2 * FF), f32),
    ((LAYERS * FF, D), f32),
    ((2 * NORMS, D, 128), f32),
    ((ATTN_ROWS, D), f32),
]
SCRATCH = [
    ((LAYERS, 3 * WIDE, D), bf16),
    ((LAYERS, D, WIDE), bf16),
    ((LAYERS, D, 2 * WIDE), bf16),
    ((LAYERS, D, WIDE), bf16),
    ((LAYERS, WIDE, D), bf16),
    ((LAYERS, 2 * FF, D), bf16),
    ((LAYERS, D, 2 * FF), bf16),
    ((LAYERS, D, FF), bf16),
    ((LAYERS, FF, D), bf16),
    ((2 * NORMS, D, 128), f32),
    ((ATTN_ROWS, D), bf16),
    *GRADS,
    *STATE,
    *STATE,
    *WORK,
    ((HEADS, 2 * KEYS, SLOT), bf16),
    ((WIDE, LANES), bf16),
    ((LAYERS, 2 * FF, LANES), f32),
    ((2 * LAYERS * D, FFH), f32),
]


def main_kernel(parts, attn_diffs, *refs):
    refs = list(refs)
    me_ref, x_ref, g_ref, norm_ref, win_own, win_other, wout_own, wout_other = take(refs, 8)
    attn_refs = take(refs, len(attn_diffs) if attn_diffs else 1)
    res_ref, ig_ref = take(refs, 2)
    outs = take(refs, 2 if attn_diffs else 4)
    wqkv_t, wq, wvk, wo_t, wo, win_t, win, wout_t, wout, norm_t, attn_ref = take(refs, 11)
    sums = (take(refs, 3), take(refs, 3))
    d_win, d_wout, d_norm, d_attn = take(refs, 4)
    states = (take(refs, len(STATE)), take(refs, len(STATE)))
    work = take(refs, len(WORK))
    kh_ref, v_ref, mixed_ref, win_rows = refs
    dvk_ref = work[-1]
    step = pl.program_id(0)

    @pl.when(step == 0)
    def _():
        for ref in (*sums[0], *sums[1], d_win, d_wout, d_norm, dvk_ref):
            ref[...] = jnp.zeros_like(ref)
        if attn_diffs:
            me = me_ref[0]
            for ref, diffs in zip(attn_refs, attn_diffs, strict=True):
                each = ref.shape[1]
                for i, diff in enumerate(diffs):
                    attn_ref[ds((me ^ diff) * each, each, each), :] = ref[i]
        else:
            attn_ref[...] = attn_refs[0][...]
        norms = [norm_ref[i] for i in range(NORMS)]
        turned = jnp.concatenate(norms + [jnp.zeros((8 - 2 * NORMS, D), f32)], axis=0).T
        for i in range(2 * NORMS):
            norm_t[i] = jnp.broadcast_to(turned[:, i : i + 1], (D, 128))
        tall, wide = head_selector(0), head_selector(1)
        for layer in range(LAYERS):
            for j in range(4):
                base = (4 * layer + j) * D
                matrix = attn_ref[base : base + D, :]
                if j < 3:
                    wqkv_t[layer, j * WIDE : (j + 1) * WIDE, :] = mm_nt(tall, matrix).astype(bf16)
                if j == 0:
                    wq[layer] = mm(matrix, wide).astype(bf16)
                elif j == 1:
                    turned_keys = mm(matrix, pair_selector(SLOT, 1))
                elif j == 2:
                    wvk[layer] = (turned_keys + mm(matrix, pair_selector(0, 1))).astype(bf16)
                else:
                    padded = mm(tall, matrix).astype(bf16)
                    wo[layer] = padded
                    wo_t[layer] = mm_nt(unit(D), padded).astype(bf16)
        for p, (w1, w2) in enumerate(((win_own, wout_own), (win_other, wout_other))):
            win_rows[...] = w1[...].astype(f32)
            for layer in range(LAYERS):
                for g in range(2):
                    part = win_rows[pl.ds(2 * layer * D + g, D, stride=2), :].astype(bf16)
                    here = slice(p * FF + g * FFH, p * FF + (g + 1) * FFH)
                    win[layer, :, here] = part
                    win_t[layer, here, :] = mm_nt(unit(FFH), part).astype(bf16)
                wout_t[layer, :, p * FFH : (p + 1) * FFH] = w2[layer]
                wout[layer, p * FFH : (p + 1) * FFH, :] = mm_nt(unit(FFH), w2[layer]).astype(bf16)

    def add_norm(index, grad, unit):
        d_norm[2 * index] += fold_lanes(grad * unit)
        d_norm[2 * index + 1] += fold_lanes(grad)

    def gain_of(index):
        return jnp.concatenate([norm_t[2 * index]] * (LANES // 128), axis=1)

    def shift_of(index):
        return jnp.concatenate([norm_t[2 * index + 1]] * (LANES // 128), axis=1)

    def one_sample(sample):
        kept = []
        normed_b = x_ref[sample]
        stream = normed_b.astype(f32)
        unit_a = inv_a = None
        for layer in range(LAYERS):
            if layer > 0:
                normed, unit_a, inv_a = norm_forward(stream, gain_of(2 * layer - 1), shift_of(2 * layer - 1))
                normed_b = normed.astype(bf16)
            stream = stream + attention_forward(
                normed_b, wqkv_t[layer], wo_t[layer], states[layer], kh_ref, v_ref
            )
            normed, unit_f, inv_f = norm_forward(stream, gain_of(2 * layer), shift_of(2 * layer))
            ffn_b = normed.astype(bf16)
            mixed = mm(win_t[layer], ffn_b)
            mixed_ref[layer] = mixed
            hidden = []
            for p in range(2):
                value = mixed[FF * p : FF * p + FFH]
                gate = mixed[FF * p + FFH : FF * (p + 1)]
                hidden.append((value * (gate * sigmoid(gate))).astype(bf16))
            hidden = jnp.concatenate(hidden, axis=0)
            stream = stream + mm(wout_t[layer], hidden)
            kept.append((normed_b, unit_a, inv_a, ffn_b, unit_f, inv_f, hidden))
        res_ref[sample] = stream.astype(bf16)

        grad = g_ref[sample].astype(f32)
        for layer in reversed(range(LAYERS)):
            normed_b, unit_a, inv_a, ffn_b, unit_f, inv_f, hidden = kept[layer]
            grad_b = grad.astype(bf16)
            d_wout[FF * layer : FF * (layer + 1), :] += mm_nt(hidden, grad_b)
            d_hidden = mm(wout[layer], grad_b)
            d_mixed = []
            for p in range(2):
                value = mixed_ref[layer, FF * p : FF * p + FFH]
                gate = mixed_ref[layer, FF * p + FFH : FF * (p + 1)]
                part = d_hidden[FFH * p : FFH * (p + 1)]
                sig = sigmoid(gate)
                d_mixed.append((part * (gate * sig)).astype(bf16))
                d_mixed.append((part * value * sig * (1.0 + gate * (1.0 - sig))).astype(bf16))
            d_mixed = jnp.concatenate(d_mixed, axis=0)
            d_win[D * layer : D * (layer + 1), :] += mm_nt(ffn_b, d_mixed)
            d_normed = mm(win[layer], d_mixed)
            add_norm(2 * layer, d_normed, unit_f)
            grad = grad + norm_backward(d_normed, unit_f, inv_f, gain_of(2 * layer))
            d_att = attention_backward(
                grad.astype(bf16), normed_b, wo[layer], wq[layer], wvk[layer], states[layer], work, sums[layer]
            )
            if layer > 0:
                add_norm(2 * layer - 1, d_att, unit_a)
                grad = grad + norm_backward(d_att, unit_a, inv_a, gain_of(2 * layer - 1))
            else:
                grad = grad + d_att
        ig_ref[sample] = grad

    for sample in range(x_ref.shape[0]):
        one_sample(sample)

    @pl.when(step == pl.num_programs(0) - 1)
    def _():
        finish_attention(d_attn, sums)
        norms = finish_norms(d_norm)
        if attn_diffs:
            pack_gradients(outs, me_ref[0], parts, d_attn, d_win, d_wout, norms)
        else:
            for out, value in zip(outs, (d_attn[...], d_win[...], d_wout[...], norms), strict=True):
                out[...] = value


VMEM = pl.BlockSpec(memory_space=pltpu.VMEM)
SMEM = pl.BlockSpec(memory_space=pltpu.SMEM)


def shapes_of(pairs):
    return [jax.ShapeDtypeStruct(*pair) for pair in pairs]


def vmem_of(pairs):
    return [pltpu.VMEM(*pair) for pair in pairs]


def per_sample(count=1):
    return pl.BlockSpec((count, D, LANES), lambda i: (i, 0, 0))


def to_columns(rows, fill_first):
    samples = rows.shape[0] // PAIRS

    def body(rows_ref, out_ref):
        out_ref[0] = load_sample(rows_ref, pl.program_id(0), fill_first).astype(bf16)

    return pl.pallas_call(
        body,
        grid=(samples,),
        in_specs=[VMEM],
        out_specs=per_sample(),
        out_shape=jax.ShapeDtypeStruct((samples, D, LANES), bf16),
        compiler_params=pltpu.CompilerParams(vmem_limit_bytes=32 * 1024 * 1024),
    )(rows)


def to_rows(columns):
    samples = columns.shape[0]

    def body(columns_ref, out_ref):
        store_sample(out_ref, pl.program_id(0), columns_ref[0].astype(f32))

    return pl.pallas_call(
        body,
        grid=(samples,),
        in_specs=[per_sample()],
        out_specs=VMEM,
        out_shape=jax.ShapeDtypeStruct((samples * PAIRS, 2 * D), columns.dtype),
        compiler_params=pltpu.CompilerParams(vmem_limit_bytes=32 * 1024 * 1024),
    )(columns)


def run_main(me, tokens, cotangent, norm_params, ffn, attn_parts, parts, attn_diffs):
    samples = tokens.shape[0]
    inputs = (norm_params, *ffn, *attn_parts)
    if attn_diffs:
        grads = [((len(NEAR), PACK_ROWS, 2 * FFH), bf16)] * 2
    else:
        grads = [((ATTN_ROWS, D), f32), GRADS[6], GRADS[7], ((8, D), f32)]

    def body(*refs):
        main_kernel(parts, attn_diffs, *refs)

    out_shape = [((samples, D, LANES), bf16), ((samples, D, LANES), f32), *grads]
    res, ig, *grads = pl.pallas_call(
        body,
        grid=(samples // TOGETHER,),
        in_specs=[SMEM, per_sample(TOGETHER), per_sample(TOGETHER)] + [VMEM] * len(inputs),
        out_specs=[per_sample(TOGETHER), per_sample(TOGETHER)] + [VMEM] * len(grads),
        out_shape=shapes_of(out_shape),
        scratch_shapes=vmem_of(SCRATCH),
        compiler_params=pltpu.CompilerParams(
            dimension_semantics=("arbitrary",), vmem_limit_bytes=VMEM_BYTES
        ),
        cost_estimate=pl.CostEstimate(
            flops=samples * 5_000_000_000, bytes_accessed=20_000_000, transcendentals=0
        ),
    )(me, tokens, cotangent, *inputs)
    return res, ig, grads


def small_kernel(body, out_shape, *inputs, scratch=()):
    return pl.pallas_call(
        body,
        in_specs=[SMEM] + [VMEM] * (len(inputs) - 1),
        out_specs=[VMEM] * len(out_shape),
        out_shape=shapes_of(out_shape),
        scratch_shapes=vmem_of(scratch),
        compiler_params=pltpu.CompilerParams(vmem_limit_bytes=32 * 1024 * 1024),
    )(*inputs)


class Exchange:
    def __init__(self, me, parts):
        self.me = me
        self.parts = parts
        self.upper = parts // GROUP
        self.each = ATTN_ROWS // parts
        self.bits = [1 << i for i in range(self.upper.bit_length() - 1)]

    def swap(self, value, k):
        return lax.ppermute(value, AXES, [(i, i ^ k) for i in range(self.parts)])

    def stack(self, blocks):
        size, kind = blocks[0].shape, blocks[0].dtype
        count = math.prod(size[:-2])

        def body(me_ref, *refs):
            ins, out = refs[:-1], refs[-1]
            for i, ref in enumerate(ins):
                if len(size) == 2:
                    out[i] = ref[...]
                else:
                    out[i * count : (i + 1) * count] = ref[...]

        shape = (len(blocks) * count, *size[-2:])
        return small_kernel(body, [(shape, kind)], self.me, *blocks)[0]

    def gather(self, rows, beside_rest, beside_plane):
        far = [GROUP * u for u in range(self.upper)]
        landed = [rows] + [self.swap(rows, k) for k in far[1:]]
        landed, beside_rest = lax.optimization_barrier((landed, beside_rest))
        column = self.stack(landed)
        landed = [column] + [self.swap(column, k) for k in NEAR[1:]]
        landed, beside_plane = lax.optimization_barrier((landed, beside_plane))
        plane = self.stack(landed)
        diffs = [k ^ u for k in NEAR for u in far]
        parts, diffs = [plane, self.swap(plane, TWIN)], [diffs, [d ^ TWIN for d in diffs]]
        return parts, diffs, beside_rest, beside_plane

    def twins(self, mine, theirs):
        def body(me_ref, mine, theirs, *outs):
            for j, out in enumerate(outs):
                total = mine[j].astype(f32) + theirs[j].astype(f32)
                out[0:PACK_NORM] = total[0:PACK_NORM].astype(out.dtype)
                sums = total[PACK_NORM : PACK_NORM + 8] + total[PACK_NORM + 8 : PACK_WIN]
                out[PACK_NORM:PACK_WIN] = resplit(sums).astype(out.dtype)
                out[PACK_WIN:] = total[PACK_WIN:].astype(out.dtype)

        shape = (PACK_ROWS, 2 * FFH)
        shapes = [(shape, f32)] + [(shape, bf16)] * (len(NEAR) - 1)
        return small_kernel(body, shapes, self.me, mine, theirs)

    def across_plane(self, pieces):
        return [pieces[0]] + [self.swap(piece, k) for piece, k in zip(pieces[1:], NEAR[1:], strict=True)]

    def emit(self, total, blocks, at, keep, send):
        half = len(blocks) // 2
        each = self.each
        for out, rows in ((keep, blocks[:half]), (send, blocks[half:])):
            for i, row in enumerate(rows):
                out[i * each : (i + 1) * each, :] = total[ds(row, each, 8), :].astype(out.dtype)
        first = half * each
        last = at + OFF_NORM - OFF_WOUT
        norm = resplit(total[last : last + 8, :] + total[last + 8 : last + 16, :])
        rest = [
            total[at:last, :].astype(bf16),
            norm,
            total[last + 16 : at + PAY_ROWS - OFF_WOUT, :].astype(bf16),
        ]
        for out in (keep, send):
            row = first
            for part in rest:
                out[row : row + part.shape[0], :] = part.astype(out.dtype)
                row += part.shape[0]

    def stage_shapes(self, blocks):
        shape = (blocks * self.each + PAY_ROWS - OFF_WOUT, 2 * FFH)
        return [(shape, f32), (shape, bf16)]

    def after_plane(self, landed):
        def body(me_ref, *refs):
            ins, (keep, send, packed, total) = refs[: len(NEAR)], refs[len(NEAR) :]
            packed[...] = tree_sum([r[...].astype(f32) for r in ins])
            for at, to, size in ((0, 0, ATTN_PART), (PACK_WOUT, OFF_WOUT, WOUT_PART)):
                rows = size // 4
                total[to : to + 3 * rows, 0:D] = packed[at : at + 3 * rows, 0:D]
                for c in range(3):
                    part = packed[at + rows * c : at + rows * (c + 1), D:]
                    total[to + 3 * rows : to + size, SIDE * c : SIDE * (c + 1)] = part
            total[OFF_NORM:OFF_WIN, :] = packed[PACK_NORM:PACK_WIN, :]
            total[OFF_WIN:, :] = packed[PACK_WIN:, :]
            mine = me_ref[0] // GROUP
            order = [r for r in range(self.upper) if not r & 1] + [r for r in range(self.upper) if r & 1]
            self.emit(total, [(mine ^ r) * self.each for r in order], OFF_WOUT, keep, send)

        scratch = [((PACK_ROWS, 2 * FFH), f32), ((PAY_ROWS, 2 * FFH), f32)]
        return small_kernel(body, self.stage_shapes(self.upper // 2), self.me, *landed, scratch=scratch)

    def after_bit(self, mine, theirs, blocks):
        def body(me_ref, mine, theirs, keep, send, total):
            total[...] = mine[...] + theirs[...].astype(f32)
            self.emit(total, [i * self.each for i in range(blocks)], blocks * self.each, keep, send)

        (shape, _), _ = self.stage_shapes(blocks)
        return small_kernel(
            body, self.stage_shapes(blocks // 2), self.me, mine, theirs, scratch=[(shape, f32)]
        )

    def after_rest(self, mine, theirs):
        each = self.each
        at_norm = each + WOUT_PART
        ffn_rows = WOUT_PART + WIN_PART

        def body(me_ref, mine, theirs, attn, norm, ffn):
            total = mine[...] + theirs[...].astype(f32)
            attn[...] = total[0:each, 0:D]
            norm[...] = total[at_norm : at_norm + 8, 0:D] + total[at_norm + 8 : at_norm + 16, 0:D]
            ffn[0, 0:WOUT_PART, :] = total[each:at_norm, :].astype(bf16)
            ffn[0, WOUT_PART:, :] = total[at_norm + 16 :, :].astype(bf16)

        shapes = [((each, D), f32), ((8, D), f32), ((1, ffn_rows, 2 * FFH), bf16)]
        return small_kernel(body, shapes, self.me, mine, theirs)

    def spread(self, ffn):
        block = self.stack([ffn, self.swap(ffn, 4)])
        theirs = self.swap(block, TWIN)

        def body(me_ref, mine, theirs, win, wout, rows):
            for t, ref in enumerate((mine, theirs)):
                for i in range(2):
                    quarter = ((me_ref[0] % GROUP) ^ (4 * i) ^ (TWIN * t)) // 2
                    part = ref[i].astype(f32)
                    rows[ds(quarter * WOUT_PART, WOUT_PART, WOUT_PART), :] = part[:WOUT_PART, 0:D]
                    for g in range(2):
                        there = pl.ds(2 * WIN_PART * quarter + g, WIN_PART, stride=2)
                        win[there, :] = part[WOUT_PART:, FFH * g : FFH * (g + 1)]
            for layer in range(LAYERS):
                wout[layer] = rows[FFH * layer : FFH * (layer + 1), :].T

        shapes = [((2 * LAYERS * D, FFH), f32), ((LAYERS, D, FFH), f32)]
        scratch = [((LAYERS * FFH, D), f32)]
        return small_kernel(body, shapes, self.me, block, theirs, scratch=scratch)

    def sum_all(self, keep, send, res, ig):
        landed = self.across_plane(self.twins(keep, self.swap(send, TWIN)))
        landed, res = lax.optimization_barrier((landed, to_rows(res)))
        keep, send = self.after_plane(landed)
        blocks = self.upper // 2
        for bit in self.bits[:-1]:
            keep, send = self.after_bit(keep, self.swap(send, GROUP * bit), blocks)
            blocks //= 2
        theirs = self.swap(send, GROUP * self.bits[-1])
        theirs, ig = lax.optimization_barrier((theirs, to_rows(ig)))
        attn, norm, ffn = self.after_rest(keep, theirs)
        return res, ig, attn, norm, *self.spread(ffn)


def on_device(devices, tokens, attn_weights, norm_params, w_in, w_out, cotangent):
    each = attn_weights.shape[0]
    me = (lax.axis_index("dp") * 2 + lax.axis_index("narrow")).astype(jnp.int32).reshape(1)
    staged = devices % (2 * GROUP) == 0 and each % 16 == 0
    x_t = to_columns(tokens, True)
    g_t = to_columns(cotangent, False)
    swap_halves = [(0, 1), (1, 0)]
    w_in = w_in.reshape(2 * LAYERS * D, FFH)
    w_out = w_out.transpose(0, 2, 1)
    w_in_other = lax.ppermute(w_in, "narrow", swap_halves)
    w_out_other = lax.ppermute(w_out, "narrow", swap_halves)
    ffn = (w_in, w_in_other, w_out, w_out_other)
    if not staged:
        attn_all = lax.all_gather(attn_weights, AXES, axis=0, tiled=True)
        res, ig, grads = run_main(me, x_t, g_t, norm_params, ffn, (attn_all,), devices, None)
        res, ig = to_rows(res), to_rows(ig)
        d_attn, d_win, d_wout, sums = grads
        attn = lax.psum_scatter(d_attn, AXES, scatter_dimension=0, tiled=True)
        norm = lax.psum(sums, AXES)
        d_wout = d_wout.reshape(LAYERS, FF, D)
        own_in, other_in = d_win[:, :FF], d_win[:, FF:]
        own_out, other_out = d_wout[:, :FFH], d_wout[:, FFH:]
        win = lax.psum(own_in + lax.ppermute(other_in, "narrow", swap_halves), "dp")
        wout = lax.psum(own_out + lax.ppermute(other_out, "narrow", swap_halves), "dp")
        wout = wout.transpose(0, 2, 1)
    else:
        ex = Exchange(me, devices)
        attn_parts, attn_diffs, (x_t, *others), g_t = ex.gather(
            attn_weights, (x_t, w_in_other, w_out_other), g_t
        )
        ffn = (w_in, others[0], w_out, others[1])
        res, ig, grads = run_main(me, x_t, g_t, norm_params, ffn, attn_parts, devices, attn_diffs)
        res, ig, attn, norm, win, wout = ex.sum_all(*grads, res, ig)
    return (
        res,
        ig,
        attn,
        norm[: 2 * NORMS].reshape(norm_params.shape),
        win.reshape(LAYERS, D, 2, FFH),
        wout.transpose(0, 2, 1),
    )


def solution(mesh):
    rows = P(("dp", "narrow"), None)
    hidden_in = P(None, None, None, "narrow")
    hidden_out = P(None, "narrow", None)
    devices = mesh.shape["dp"] * mesh.shape["narrow"]

    def per_device(*args):
        return on_device(devices, *args)

    return jax.shard_map(
        per_device,
        mesh=mesh,
        in_specs=(rows, rows, P(), hidden_in, hidden_out, rows),
        out_specs=(rows, rows, rows, P(), hidden_in, hidden_out),
        check_vma=False,
    )
```

```python
import math

import jax
import jax.numpy as jnp
from jax import lax
from jax.experimental import pallas as pl
from jax.experimental.pallas import tpu as pltpu
from jax.sharding import PartitionSpec as P

HEADS = 8
HEAD = 24
SLOT = 32
WIDE = HEADS * SLOT
D = HEADS * HEAD
FF = 256
FFH = FF // 2
LAYERS = 2
NORMS = 2 * LAYERS - 1
SEQ = 476
PAIRS = SEQ // 2
KEYS = 240
HALF = 256
LANES = 2 * HALF
EPS = 1e-05
SCALE = HEAD ** (-0.5)
LOG2E = math.log2(math.e)
ATTN_ROWS = LAYERS * 4 * D

GROUP = 8
NEAR = (0, 1, 4, 5)
TWIN = 2
WIN_PART = LAYERS * D // 4
SIDE = 2 * FFH - D
WOUT_PART = LAYERS * FFH // 4
ATTN_PART = ATTN_ROWS // GROUP
OFF_WOUT = ATTN_PART
OFF_NORM = OFF_WOUT + WOUT_PART
OFF_WIN = OFF_NORM + 16
PAY_ROWS = OFF_WIN + WIN_PART
PACK_WOUT = 3 * ATTN_PART // 4
PACK_NORM = PACK_WOUT + 3 * WOUT_PART // 4
PACK_WIN = PACK_NORM + 16
PACK_ROWS = PACK_WIN + WIN_PART

bf16 = jnp.bfloat16
f32 = jnp.float32
AXES = ("dp", "narrow")

VMEM_BYTES = 52 * 1024 * 1024


def mm(left, right):
    return jnp.dot(left, right, preferred_element_type=f32)


def mm_nt(left, right):
    return lax.dot_general(left, right, (((1,), (1,)), ((), ())), preferred_element_type=f32)


def sigmoid(value):
    return 0.5 + 0.5 * jnp.tanh(0.5 * value)


def fold_lanes(value):
    return value[:, 0:128] + value[:, 128:256] + value[:, 256:384] + value[:, 384:512]


def norm_forward(stream, gain, shift):
    center = stream - jnp.sum(stream, axis=0, keepdims=True) * (1.0 / D)
    inverse = lax.rsqrt(jnp.sum(center * center, axis=0, keepdims=True) * (1.0 / D) + EPS)
    unit = center * inverse
    return (unit * gain + shift, unit, inverse)


def norm_backward(grad, unit, inverse, gain):
    scaled = grad * gain
    mean = jnp.sum(scaled, axis=0, keepdims=True) * (1.0 / D)
    slope = jnp.sum(scaled * unit, axis=0, keepdims=True) * (1.0 / D)
    return inverse * (scaled - mean - unit * slope)


def tree_sum(parts):
    while len(parts) > 1:
        parts = [parts[i] + parts[i + 1] for i in range(0, len(parts), 2)]
    return parts[0]


def ds(start, size, step):
    return pl.ds(pl.multiple_of(start, step), size)


def take(refs, count):
    taken = refs[:count]
    del refs[:count]
    return taken


def unit(size):
    row = lax.broadcasted_iota(jnp.int32, (size, size), 0)
    column = lax.broadcasted_iota(jnp.int32, (size, size), 1)
    return (row == column).astype(f32).astype(bf16)


def head_selector(padded_axis):
    shape = (WIDE, D) if padded_axis == 0 else (D, WIDE)
    padded = lax.broadcasted_iota(jnp.int32, shape, padded_axis)
    plain = lax.broadcasted_iota(jnp.int32, shape, 1 - padded_axis)
    inside = padded & (SLOT - 1)
    same = jnp.logical_and(plain == HEAD * (padded >> 5) + inside, inside < HEAD)
    return same.astype(f32).astype(bf16)


def pair_selector(offset, padded_axis):
    shape = (2 * WIDE, D) if padded_axis == 0 else (D, 2 * WIDE)
    padded = lax.broadcasted_iota(jnp.int32, shape, padded_axis)
    plain = lax.broadcasted_iota(jnp.int32, shape, 1 - padded_axis)
    inside = (padded & (2 * SLOT - 1)) - offset
    same = jnp.logical_and(plain == HEAD * (padded >> 6) + inside, inside >= 0)
    return jnp.logical_and(same, inside < HEAD).astype(f32).astype(bf16)


def head_rows(h):
    return slice(SLOT * h, SLOT * (h + 1))


def sample_window(step, rows_total, align):
    base = step * PAIRS
    start = jnp.minimum(base // align * align, rows_total - HALF)
    return ds(start, HALF, align), base - start


def load_sample(ref, step, fill_first):
    window, shift = sample_window(step, ref.shape[0], 16)
    rows = pltpu.roll(ref[window, :].astype(f32), lax.rem(HALF - shift, HALF), 0)
    pair_row = lax.broadcasted_iota(jnp.int32, (HALF, 2 * D), 0)
    cols = jnp.where(pair_row < PAIRS, rows, rows[0:1] if fill_first else 0.0).T
    return jnp.concatenate([cols[:D], cols[D:]], axis=1)


def store_sample(ref, step, value):
    window, shift = sample_window(step, ref.shape[0], 16 if ref.dtype == bf16 else 8)
    cols = jnp.concatenate([value[:, :HALF], value[:, HALF:]], axis=0)
    rows = pltpu.roll(cols.T, shift, 0)
    pair_row = lax.broadcasted_iota(jnp.int32, (HALF, 2 * D), 0)
    here = jnp.logical_and(pair_row >= shift, pair_row < shift + PAIRS)
    ref[window, :] = jnp.where(here, rows, ref[window, :].astype(f32)).astype(ref.dtype)


def attention_forward(normed_b, wqkv_t, wo_t, state, kh_ref, v_ref):
    e_ref, vh_ref, q_ref, k_ref, ctx_ref, rinv_ref = state
    lane = lax.broadcasted_iota(jnp.int32, (WIDE, LANES), 1)
    slot_row = lax.broadcasted_iota(jnp.int32, (WIDE, LANES), 0) & (SLOT - 1)
    real = (lane & (HALF - 1)) < PAIRS
    ones_rows = jnp.logical_or(slot_row == HEAD, slot_row == HEAD + 1).astype(f32)
    qkv = mm(wqkv_t, normed_b)
    queries = (qkv[:WIDE] * (SCALE * LOG2E)).astype(bf16)
    q_ref[...] = queries
    keys = qkv[WIDE : 2 * WIDE].astype(bf16)
    k_ref[...] = keys
    values = jnp.where(real, qkv[2 * WIDE :] + ones_rows, 0.0).astype(bf16)
    v_ref[...] = values
    for tall, ref in ((keys.T, kh_ref), (values.T, vh_ref)):
        for h in range(HEADS):
            ref[h, 0:KEYS] = tall[0:KEYS, head_rows(h)]
            ref[h, KEYS:] = tall[HALF : HALF + KEYS, head_rows(h)]

    def scores_of(h):
        return mm(kh_ref[h], q_ref[head_rows(h), :])

    scores = scores_of(0)
    for h in range(HEADS):
        rows = head_rows(h)
        ahead = scores_of(h + 1) if h + 1 < HEADS else None
        top = jnp.max(scores, axis=0, keepdims=True)
        weights = jnp.exp2(scores - top).astype(bf16)
        e_ref[0 : 2 * KEYS, LANES * h : LANES * (h + 1)] = weights
        out = mm(v_ref[rows, 0:KEYS], weights[0:KEYS]) + mm(
            v_ref[rows, HALF : HALF + KEYS], weights[KEYS:]
        )
        inverse = 1.0 / out[HEAD : HEAD + 1]
        rinv_ref[h : h + 1, :] = inverse
        ctx_ref[rows, :] = out * inverse
        scores = ahead
    return mm(wo_t, ctx_ref[...].astype(bf16))


def attention_backward(grad_b, normed_b, wo, wq, wvk, state, work, sums):
    e_ref, vh_ref, q_ref, k_ref, ctx_ref, rinv_ref = state
    pair_ref, block_ref, dq_ref, dvk_ref = work
    d_wq, d_wvk, d_wo = sums
    group = HEADS // 2
    head_row = lax.broadcasted_iota(jnp.int32, (SLOT, LANES), 0)
    lane_head = lax.broadcasted_iota(jnp.int32, (LANES, 2 * SLOT * group), 1) // (2 * SLOT)
    key_row = lax.broadcasted_iota(jnp.int32, (2 * KEYS, 2 * SLOT * group), 0)
    real_key = jnp.where(key_row < KEYS, key_row, key_row - KEYS) < PAIRS
    in_pair = lax.broadcasted_iota(jnp.int32, (2 * KEYS, 2 * SLOT * group), 1) & (2 * SLOT - 1)

    d_wo[...] += mm_nt(ctx_ref[...].astype(bf16), grad_b)
    d_context = mm(wo, grad_b)
    for h in range(HEADS):
        rows = head_rows(h)
        grad = (d_context[rows] * rinv_ref[h : h + 1, :]).astype(bf16).astype(f32)
        dot = -jnp.sum(grad[:HEAD] * ctx_ref[rows, :][:HEAD], axis=0, keepdims=True)
        dot_high = dot.astype(bf16).astype(f32)
        grad = jnp.where(head_row == HEAD, dot_high, grad)
        grad = jnp.where(head_row == HEAD + 1, dot - dot_high, grad)
        pair_ref[2 * SLOT * h : 2 * SLOT * h + SLOT, :] = grad.astype(bf16)
        pair_ref[2 * SLOT * h + SLOT : 2 * SLOT * (h + 1), :] = q_ref[rows, :]
    tall = pair_ref[...].T
    for h in range(HEADS):
        part = tall[:, WIDE * (h // group) : WIDE * (h // group + 1)]
        block_ref[LANES * h : LANES * (h + 1), :] = jnp.where(
            lane_head == h % group, part, jnp.zeros_like(part)
        )

    for h in range(HEADS + 1):
        if h < HEADS:
            lanes = slice(LANES * h, LANES * (h + 1))
            grad_probs = mm(vh_ref[h], pair_ref[2 * SLOT * h : 2 * SLOT * h + SLOT, :])
            e_ref[2 * KEYS :, lanes] = e_ref[0 : 2 * KEYS, lanes] * grad_probs.astype(bf16)
        if h > 0:
            rows = head_rows(h - 1)
            lanes = slice(LANES * (h - 1), LANES * h)
            dq = mm(k_ref[rows, 0:KEYS], e_ref[2 * KEYS : 3 * KEYS, lanes]) + mm(
                k_ref[rows, HALF : HALF + KEYS], e_ref[3 * KEYS :, lanes]
            )
            dq_ref[rows, :] = (dq * SCALE).astype(bf16)
    for g in range(2):
        here = slice(group * LANES * g, group * LANES * (g + 1))
        both = mm(e_ref[:, here], block_ref[here, :])
        dv = jnp.where(real_key, both[: 2 * KEYS], 0.0)
        dk = both[2 * KEYS :] * (1.0 / LOG2E)
        dvk = jnp.where(in_pair < SLOT, dv, dk).astype(bf16)
        for half in range(2):
            there = slice(half * HALF, half * HALF + KEYS)
            dvk_ref[there, WIDE * g : WIDE * (g + 1)] = dvk[half * KEYS : (half + 1) * KEYS]
    d_wq[...] += mm_nt(normed_b, dq_ref[...])
    d_wvk[...] += mm(normed_b, dvk_ref[...])
    return mm(wq, dq_ref[...]) + mm_nt(wvk, dvk_ref[...])


def resplit(sums):
    high = sums.astype(bf16).astype(f32)
    return jnp.concatenate([high, sums - high], axis=0).astype(bf16)


def finish_attention(d_attn, sums):
    tall, wide = head_selector(0), head_selector(1)
    for layer in range(LAYERS):
        d_wq, d_wvk, d_wo = sums[layer]
        mixed = d_wvk[...].astype(bf16)
        base = 4 * layer * D
        d_attn[base : base + D, :] = mm(d_wq[...].astype(bf16), tall)
        d_attn[base + D : base + 2 * D, :] = mm(mixed, pair_selector(SLOT, 0))
        d_attn[base + 2 * D : base + 3 * D, :] = mm(mixed, pair_selector(0, 0))
        d_attn[base + 3 * D : base + 4 * D, :] = mm(wide, d_wo[...].astype(bf16))


def finish_norms(d_norm):
    sums = [jnp.sum(d_norm[j].T, axis=0, keepdims=True) for j in range(2 * NORMS)]
    return jnp.concatenate(sums + [jnp.zeros((8 - 2 * NORMS, D), f32)], axis=0)


def pack_gradients(outs, me, parts, d_attn, d_win, d_wout, norms):
    each, upper = ATTN_ROWS // parts, parts // GROUP
    norms = resplit(norms)
    for t, out in enumerate(outs):
        for j, k in enumerate(NEAR):
            low = (me % GROUP) ^ k ^ (TWIN * t)
            quarter = low // 2
            half = k % 2
            attn = [d_attn[ds((u * GROUP + low) * each, each, each), :] for u in range(upper)]
            first = (quarter // 2) * FF + half * FFH + (quarter % 2) * WOUT_PART
            wout = d_wout[ds(first, WOUT_PART, WOUT_PART), :]
            win = d_win[ds(quarter * WIN_PART, WIN_PART, WIN_PART), half * FF : (half + 1) * FF]
            for at, value in ((0, jnp.concatenate(attn, axis=0)), (PACK_WOUT, wout)):
                value = value.astype(bf16)
                rows = value.shape[0] // 4
                out[j, at : at + 3 * rows, 0:D] = value[: 3 * rows]
                for c in range(3):
                    part = value[3 * rows :, SIDE * c : SIDE * (c + 1)]
                    out[j, at + rows * c : at + rows * (c + 1), D:] = part
            out[j, PACK_NORM:PACK_WIN, 0:D] = norms
            out[j, PACK_WIN:PACK_ROWS, :] = win.astype(bf16)


STATE = [
    ((4 * KEYS, HEADS * LANES), bf16),
    ((HEADS, 2 * KEYS, SLOT), bf16),
    ((WIDE, LANES), bf16),
    ((WIDE, LANES), bf16),
    ((WIDE, LANES), f32),
    ((HEADS, LANES), f32),
]
WORK = [
    ((2 * WIDE, LANES), bf16),
    ((HEADS * LANES, WIDE), bf16),
    ((WIDE, LANES), bf16),
    ((LANES, 2 * WIDE), bf16),
]
SUMS = [((D, WIDE), f32), ((D, 2 * WIDE), f32), ((WIDE, D), f32)]
GRADS = [
    *SUMS,
    *SUMS,
    ((LAYERS * D, 2 * FF), f32),
    ((LAYERS * FF, D), f32),
    ((2 * NORMS, D, 128), f32),
    ((ATTN_ROWS, D), f32),
]
SCRATCH = [
    ((LAYERS, 3 * WIDE, D), bf16),
    ((LAYERS, D, WIDE), bf16),
    ((LAYERS, D, 2 * WIDE), bf16),
    ((LAYERS, D, WIDE), bf16),
    ((LAYERS, WIDE, D), bf16),
    ((LAYERS, 2 * FF, D), bf16),
    ((LAYERS, D, 2 * FF), bf16),
    ((LAYERS, D, FF), bf16),
    ((LAYERS, FF, D), bf16),
    ((2 * NORMS, D, 128), f32),
    ((ATTN_ROWS, D), bf16),
    *GRADS,
    *STATE,
    *STATE,
    *WORK,
    ((HEADS, 2 * KEYS, SLOT), bf16),
    ((WIDE, LANES), bf16),
    ((LAYERS, 2 * FF, LANES), bf16),
    ((2 * LAYERS * D, FFH), f32),
]


def main_kernel(parts, attn_diffs, *refs):
    refs = list(refs)
    me_ref, x_ref, g_ref, norm_ref, win_own, win_other, wout_own, wout_other = take(refs, 8)
    attn_refs = take(refs, len(attn_diffs) if attn_diffs else 1)
    res_ref, ig_ref = take(refs, 2)
    outs = take(refs, 2 if attn_diffs else 4)
    wqkv_t, wq, wvk, wo_t, wo, win_t, win, wout_t, wout, norm_t, attn_ref = take(refs, 11)
    sums = (take(refs, 3), take(refs, 3))
    d_win, d_wout, d_norm, d_attn = take(refs, 4)
    states = (take(refs, len(STATE)), take(refs, len(STATE)))
    work = take(refs, len(WORK))
    kh_ref, v_ref, mixed_ref, win_rows = refs
    dvk_ref = work[-1]
    step = pl.program_id(0)

    @pl.when(step == 0)
    def _():
        for ref in (*sums[0], *sums[1], d_win, d_wout, d_norm, dvk_ref):
            ref[...] = jnp.zeros_like(ref)
        if attn_diffs:
            me = me_ref[0]
            for ref, diffs in zip(attn_refs, attn_diffs, strict=True):
                each = ref.shape[1]
                for i, diff in enumerate(diffs):
                    attn_ref[ds((me ^ diff) * each, each, each), :] = ref[i]
        else:
            attn_ref[...] = attn_refs[0][...]
        norms = [norm_ref[i] for i in range(NORMS)]
        turned = jnp.concatenate(norms + [jnp.zeros((8 - 2 * NORMS, D), f32)], axis=0).T
        for i in range(2 * NORMS):
            norm_t[i] = jnp.broadcast_to(turned[:, i : i + 1], (D, 128))
        tall, wide = head_selector(0), head_selector(1)
        for layer in range(LAYERS):
            for j in range(4):
                base = (4 * layer + j) * D
                matrix = attn_ref[base : base + D, :]
                if j < 3:
                    wqkv_t[layer, j * WIDE : (j + 1) * WIDE, :] = mm_nt(tall, matrix).astype(bf16)
                if j == 0:
                    wq[layer] = mm(matrix, wide).astype(bf16)
                elif j == 1:
                    turned_keys = mm(matrix, pair_selector(SLOT, 1))
                elif j == 2:
                    wvk[layer] = (turned_keys + mm(matrix, pair_selector(0, 1))).astype(bf16)
                else:
                    padded = mm(tall, matrix).astype(bf16)
                    wo[layer] = padded
                    wo_t[layer] = mm_nt(unit(D), padded).astype(bf16)
        for p, (w1, w2) in enumerate(((win_own, wout_own), (win_other, wout_other))):
            win_rows[...] = w1[...].astype(f32)
            for layer in range(LAYERS):
                for g in range(2):
                    part = win_rows[pl.ds(2 * layer * D + g, D, stride=2), :].astype(bf16)
                    here = slice(p * FF + g * FFH, p * FF + (g + 1) * FFH)
                    win[layer, :, here] = part
                    win_t[layer, here, :] = mm_nt(unit(FFH), part).astype(bf16)
                wout_t[layer, :, p * FFH : (p + 1) * FFH] = w2[layer]
                wout[layer, p * FFH : (p + 1) * FFH, :] = mm_nt(unit(FFH), w2[layer]).astype(bf16)

    def add_norm(index, grad, unit):
        d_norm[2 * index] += fold_lanes(grad * unit)
        d_norm[2 * index + 1] += fold_lanes(grad)

    def gain_of(index):
        return jnp.concatenate([norm_t[2 * index]] * (LANES // 128), axis=1)

    def shift_of(index):
        return jnp.concatenate([norm_t[2 * index + 1]] * (LANES // 128), axis=1)

    kept = []
    normed_b = x_ref[0]
    stream = normed_b.astype(f32)
    unit_a = inv_a = None
    for layer in range(LAYERS):
        if layer > 0:
            normed, unit_a, inv_a = norm_forward(stream, gain_of(2 * layer - 1), shift_of(2 * layer - 1))
            normed_b = normed.astype(bf16)
        stream = stream + attention_forward(
            normed_b, wqkv_t[layer], wo_t[layer], states[layer], kh_ref, v_ref
        )
        normed, unit_f, inv_f = norm_forward(stream, gain_of(2 * layer), shift_of(2 * layer))
        ffn_b = normed.astype(bf16)
        mixed = mm(win_t[layer], ffn_b)
        mixed_ref[layer] = mixed.astype(bf16)
        hidden = []
        for p in range(2):
            value = mixed[FF * p : FF * p + FFH]
            gate = mixed[FF * p + FFH : FF * (p + 1)]
            hidden.append((value * (gate * sigmoid(gate))).astype(bf16))
        hidden = jnp.concatenate(hidden, axis=0)
        stream = stream + mm(wout_t[layer], hidden)
        kept.append((normed_b, unit_a, inv_a, ffn_b, unit_f, inv_f, hidden))
    res_ref[0] = stream.astype(bf16)

    grad = g_ref[0].astype(f32)
    for layer in reversed(range(LAYERS)):
        normed_b, unit_a, inv_a, ffn_b, unit_f, inv_f, hidden = kept[layer]
        grad_b = grad.astype(bf16)
        d_wout[FF * layer : FF * (layer + 1), :] += mm_nt(hidden, grad_b)
        d_hidden = mm(wout[layer], grad_b)
        d_mixed = []
        for p in range(2):
            value = mixed_ref[layer, FF * p : FF * p + FFH].astype(f32)
            gate = mixed_ref[layer, FF * p + FFH : FF * (p + 1)].astype(f32)
            part = d_hidden[FFH * p : FFH * (p + 1)]
            sig = sigmoid(gate)
            d_mixed.append((part * (gate * sig)).astype(bf16))
            d_mixed.append((part * value * sig * (1.0 + gate * (1.0 - sig))).astype(bf16))
        d_mixed = jnp.concatenate(d_mixed, axis=0)
        d_win[D * layer : D * (layer + 1), :] += mm_nt(ffn_b, d_mixed)
        d_normed = mm(win[layer], d_mixed)
        add_norm(2 * layer, d_normed, unit_f)
        grad = grad + norm_backward(d_normed, unit_f, inv_f, gain_of(2 * layer))
        d_att = attention_backward(
            grad.astype(bf16), normed_b, wo[layer], wq[layer], wvk[layer], states[layer], work, sums[layer]
        )
        if layer > 0:
            add_norm(2 * layer - 1, d_att, unit_a)
            grad = grad + norm_backward(d_att, unit_a, inv_a, gain_of(2 * layer - 1))
        else:
            grad = grad + d_att
    ig_ref[0] = grad

    @pl.when(step == pl.num_programs(0) - 1)
    def _():
        finish_attention(d_attn, sums)
        norms = finish_norms(d_norm)
        if attn_diffs:
            pack_gradients(outs, me_ref[0], parts, d_attn, d_win, d_wout, norms)
        else:
            for out, value in zip(outs, (d_attn[...], d_win[...], d_wout[...], norms), strict=True):
                out[...] = value


VMEM = pl.BlockSpec(memory_space=pltpu.VMEM)
SMEM = pl.BlockSpec(memory_space=pltpu.SMEM)


def shapes_of(pairs):
    return [jax.ShapeDtypeStruct(*pair) for pair in pairs]


def vmem_of(pairs):
    return [pltpu.VMEM(*pair) for pair in pairs]


def per_sample():
    return pl.BlockSpec((1, D, LANES), lambda i: (i, 0, 0))


def to_columns(rows, fill_first):
    samples = rows.shape[0] // PAIRS

    def body(rows_ref, out_ref):
        out_ref[0] = load_sample(rows_ref, pl.program_id(0), fill_first).astype(bf16)

    return pl.pallas_call(
        body,
        grid=(samples,),
        in_specs=[VMEM],
        out_specs=per_sample(),
        out_shape=jax.ShapeDtypeStruct((samples, D, LANES), bf16),
        compiler_params=pltpu.CompilerParams(vmem_limit_bytes=32 * 1024 * 1024),
    )(rows)


def to_rows(columns):
    samples = columns.shape[0]

    def body(columns_ref, out_ref):
        store_sample(out_ref, pl.program_id(0), columns_ref[0].astype(f32))

    return pl.pallas_call(
        body,
        grid=(samples,),
        in_specs=[per_sample()],
        out_specs=VMEM,
        out_shape=jax.ShapeDtypeStruct((samples * PAIRS, 2 * D), columns.dtype),
        compiler_params=pltpu.CompilerParams(vmem_limit_bytes=32 * 1024 * 1024),
    )(columns)


def run_main(me, tokens, cotangent, norm_params, ffn, attn_parts, parts, attn_diffs):
    samples = tokens.shape[0]
    inputs = (norm_params, *ffn, *attn_parts)
    if attn_diffs:
        grads = [((len(NEAR), PACK_ROWS, 2 * FFH), bf16)] * 2
    else:
        grads = [((ATTN_ROWS, D), f32), GRADS[6], GRADS[7], ((8, D), f32)]

    def body(*refs):
        main_kernel(parts, attn_diffs, *refs)

    out_shape = [((samples, D, LANES), bf16), ((samples, D, LANES), f32), *grads]
    res, ig, *grads = pl.pallas_call(
        body,
        grid=(samples,),
        in_specs=[SMEM, per_sample(), per_sample()] + [VMEM] * len(inputs),
        out_specs=[per_sample(), per_sample()] + [VMEM] * len(grads),
        out_shape=shapes_of(out_shape),
        scratch_shapes=vmem_of(SCRATCH),
        compiler_params=pltpu.CompilerParams(
            dimension_semantics=("arbitrary",), vmem_limit_bytes=VMEM_BYTES
        ),
        cost_estimate=pl.CostEstimate(
            flops=samples * 5_000_000_000, bytes_accessed=20_000_000, transcendentals=0
        ),
    )(me, tokens, cotangent, *inputs)
    return res, ig, grads


def small_kernel(body, out_shape, *inputs, scratch=()):
    return pl.pallas_call(
        body,
        in_specs=[SMEM] + [VMEM] * (len(inputs) - 1),
        out_specs=[VMEM] * len(out_shape),
        out_shape=shapes_of(out_shape),
        scratch_shapes=vmem_of(scratch),
        compiler_params=pltpu.CompilerParams(vmem_limit_bytes=32 * 1024 * 1024),
    )(*inputs)


class Exchange:
    def __init__(self, me, parts):
        self.me = me
        self.parts = parts
        self.upper = parts // GROUP
        self.each = ATTN_ROWS // parts
        self.bits = [1 << i for i in range(self.upper.bit_length() - 1)]

    def swap(self, value, k):
        return lax.ppermute(value, AXES, [(i, i ^ k) for i in range(self.parts)])

    def stack(self, blocks):
        size, kind = blocks[0].shape, blocks[0].dtype
        count = math.prod(size[:-2])

        def body(me_ref, *refs):
            ins, out = refs[:-1], refs[-1]
            for i, ref in enumerate(ins):
                if len(size) == 2:
                    out[i] = ref[...]
                else:
                    out[i * count : (i + 1) * count] = ref[...]

        shape = (len(blocks) * count, *size[-2:])
        return small_kernel(body, [(shape, kind)], self.me, *blocks)[0]

    def gather(self, rows, beside_rest, beside_plane):
        far = [GROUP * u for u in range(self.upper)]
        landed = [rows] + [self.swap(rows, k) for k in far[1:]]
        landed, beside_rest = lax.optimization_barrier((landed, beside_rest))
        column = self.stack(landed)
        landed = [column] + [self.swap(column, k) for k in NEAR[1:]]
        landed, beside_plane = lax.optimization_barrier((landed, beside_plane))
        plane = self.stack(landed)
        diffs = [k ^ u for k in NEAR for u in far]
        parts, diffs = [plane, self.swap(plane, TWIN)], [diffs, [d ^ TWIN for d in diffs]]
        return parts, diffs, beside_rest, beside_plane

    def twins(self, mine, theirs):
        def body(me_ref, mine, theirs, *outs):
            for j, out in enumerate(outs):
                total = mine[j].astype(f32) + theirs[j].astype(f32)
                out[0:PACK_NORM] = total[0:PACK_NORM].astype(out.dtype)
                sums = total[PACK_NORM : PACK_NORM + 8] + total[PACK_NORM + 8 : PACK_WIN]
                out[PACK_NORM:PACK_WIN] = resplit(sums).astype(out.dtype)
                out[PACK_WIN:] = total[PACK_WIN:].astype(out.dtype)

        shape = (PACK_ROWS, 2 * FFH)
        shapes = [(shape, f32)] + [(shape, bf16)] * (len(NEAR) - 1)
        return small_kernel(body, shapes, self.me, mine, theirs)

    def across_plane(self, pieces):
        return [pieces[0]] + [self.swap(piece, k) for piece, k in zip(pieces[1:], NEAR[1:], strict=True)]

    def emit(self, total, blocks, at, keep, send):
        half = len(blocks) // 2
        each = self.each
        for out, rows in ((keep, blocks[:half]), (send, blocks[half:])):
            for i, row in enumerate(rows):
                out[i * each : (i + 1) * each, :] = total[ds(row, each, 8), :].astype(out.dtype)
        first = half * each
        last = at + OFF_NORM - OFF_WOUT
        norm = resplit(total[last : last + 8, :] + total[last + 8 : last + 16, :])
        rest = [
            total[at:last, :].astype(bf16),
            norm,
            total[last + 16 : at + PAY_ROWS - OFF_WOUT, :].astype(bf16),
        ]
        for out in (keep, send):
            row = first
            for part in rest:
                out[row : row + part.shape[0], :] = part.astype(out.dtype)
                row += part.shape[0]

    def stage_shapes(self, blocks):
        shape = (blocks * self.each + PAY_ROWS - OFF_WOUT, 2 * FFH)
        return [(shape, f32), (shape, bf16)]

    def after_plane(self, landed):
        def body(me_ref, *refs):
            ins, (keep, send, packed, total) = refs[: len(NEAR)], refs[len(NEAR) :]
            packed[...] = tree_sum([r[...].astype(f32) for r in ins])
            for at, to, size in ((0, 0, ATTN_PART), (PACK_WOUT, OFF_WOUT, WOUT_PART)):
                rows = size // 4
                total[to : to + 3 * rows, 0:D] = packed[at : at + 3 * rows, 0:D]
                for c in range(3):
                    part = packed[at + rows * c : at + rows * (c + 1), D:]
                    total[to + 3 * rows : to + size, SIDE * c : SIDE * (c + 1)] = part
            total[OFF_NORM:OFF_WIN, :] = packed[PACK_NORM:PACK_WIN, :]
            total[OFF_WIN:, :] = packed[PACK_WIN:, :]
            mine = me_ref[0] // GROUP
            order = [r for r in range(self.upper) if not r & 1] + [r for r in range(self.upper) if r & 1]
            self.emit(total, [(mine ^ r) * self.each for r in order], OFF_WOUT, keep, send)

        scratch = [((PACK_ROWS, 2 * FFH), f32), ((PAY_ROWS, 2 * FFH), f32)]
        return small_kernel(body, self.stage_shapes(self.upper // 2), self.me, *landed, scratch=scratch)

    def after_bit(self, mine, theirs, blocks):
        def body(me_ref, mine, theirs, keep, send, total):
            total[...] = mine[...] + theirs[...].astype(f32)
            self.emit(total, [i * self.each for i in range(blocks)], blocks * self.each, keep, send)

        (shape, _), _ = self.stage_shapes(blocks)
        return small_kernel(
            body, self.stage_shapes(blocks // 2), self.me, mine, theirs, scratch=[(shape, f32)]
        )

    def after_rest(self, mine, theirs):
        each = self.each
        at_norm = each + WOUT_PART
        ffn_rows = WOUT_PART + WIN_PART

        def body(me_ref, mine, theirs, attn, norm, ffn):
            total = mine[...] + theirs[...].astype(f32)
            attn[...] = total[0:each, 0:D]
            norm[...] = total[at_norm : at_norm + 8, 0:D] + total[at_norm + 8 : at_norm + 16, 0:D]
            ffn[0, 0:WOUT_PART, :] = total[each:at_norm, :].astype(bf16)
            ffn[0, WOUT_PART:, :] = total[at_norm + 16 :, :].astype(bf16)

        shapes = [((each, D), f32), ((8, D), f32), ((1, ffn_rows, 2 * FFH), bf16)]
        return small_kernel(body, shapes, self.me, mine, theirs)

    def spread(self, ffn):
        block = self.stack([ffn, self.swap(ffn, 4)])
        theirs = self.swap(block, TWIN)

        def body(me_ref, mine, theirs, win, wout, rows):
            for t, ref in enumerate((mine, theirs)):
                for i in range(2):
                    quarter = ((me_ref[0] % GROUP) ^ (4 * i) ^ (TWIN * t)) // 2
                    part = ref[i].astype(f32)
                    rows[ds(quarter * WOUT_PART, WOUT_PART, WOUT_PART), :] = part[:WOUT_PART, 0:D]
                    for g in range(2):
                        there = pl.ds(2 * WIN_PART * quarter + g, WIN_PART, stride=2)
                        win[there, :] = part[WOUT_PART:, FFH * g : FFH * (g + 1)]
            for layer in range(LAYERS):
                wout[layer] = rows[FFH * layer : FFH * (layer + 1), :].T

        shapes = [((2 * LAYERS * D, FFH), f32), ((LAYERS, D, FFH), f32)]
        scratch = [((LAYERS * FFH, D), f32)]
        return small_kernel(body, shapes, self.me, block, theirs, scratch=scratch)

    def sum_all(self, keep, send, res, ig):
        landed = self.across_plane(self.twins(keep, self.swap(send, TWIN)))
        landed, res = lax.optimization_barrier((landed, to_rows(res)))
        keep, send = self.after_plane(landed)
        blocks = self.upper // 2
        for bit in self.bits[:-1]:
            keep, send = self.after_bit(keep, self.swap(send, GROUP * bit), blocks)
            blocks //= 2
        theirs = self.swap(send, GROUP * self.bits[-1])
        theirs, ig = lax.optimization_barrier((theirs, to_rows(ig)))
        attn, norm, ffn = self.after_rest(keep, theirs)
        return res, ig, attn, norm, *self.spread(ffn)


def on_device(devices, tokens, attn_weights, norm_params, w_in, w_out, cotangent):
    each = attn_weights.shape[0]
    me = (lax.axis_index("dp") * 2 + lax.axis_index("narrow")).astype(jnp.int32).reshape(1)
    staged = devices % (2 * GROUP) == 0 and each % 16 == 0
    x_t = to_columns(tokens, True)
    g_t = to_columns(cotangent, False)
    swap_halves = [(0, 1), (1, 0)]
    w_in = w_in.reshape(2 * LAYERS * D, FFH)
    w_out = w_out.transpose(0, 2, 1)
    w_in_other = lax.ppermute(w_in, "narrow", swap_halves)
    w_out_other = lax.ppermute(w_out, "narrow", swap_halves)
    ffn = (w_in, w_in_other, w_out, w_out_other)
    if not staged:
        attn_all = lax.all_gather(attn_weights, AXES, axis=0, tiled=True)
        res, ig, grads = run_main(me, x_t, g_t, norm_params, ffn, (attn_all,), devices, None)
        res, ig = to_rows(res), to_rows(ig)
        d_attn, d_win, d_wout, sums = grads
        attn = lax.psum_scatter(d_attn, AXES, scatter_dimension=0, tiled=True)
        norm = lax.psum(sums, AXES)
        d_wout = d_wout.reshape(LAYERS, FF, D)
        own_in, other_in = d_win[:, :FF], d_win[:, FF:]
        own_out, other_out = d_wout[:, :FFH], d_wout[:, FFH:]
        win = lax.psum(own_in + lax.ppermute(other_in, "narrow", swap_halves), "dp")
        wout = lax.psum(own_out + lax.ppermute(other_out, "narrow", swap_halves), "dp")
        wout = wout.transpose(0, 2, 1)
    else:
        ex = Exchange(me, devices)
        attn_parts, attn_diffs, (x_t, *others), g_t = ex.gather(
            attn_weights, (x_t, w_in_other, w_out_other), g_t
        )
        ffn = (w_in, others[0], w_out, others[1])
        res, ig, grads = run_main(me, x_t, g_t, norm_params, ffn, attn_parts, devices, attn_diffs)
        res, ig, attn, norm, win, wout = ex.sum_all(*grads, res, ig)
    return (
        res,
        ig,
        attn,
        norm[: 2 * NORMS].reshape(norm_params.shape),
        win.reshape(LAYERS, D, 2, FFH),
        wout.transpose(0, 2, 1),
    )


def solution(mesh):
    rows = P(("dp", "narrow"), None)
    hidden_in = P(None, None, None, "narrow")
    hidden_out = P(None, "narrow", None)
    devices = mesh.shape["dp"] * mesh.shape["narrow"]

    def per_device(*args):
        return on_device(devices, *args)

    return jax.shard_map(
        per_device,
        mesh=mesh,
        in_specs=(rows, rows, P(), hidden_in, hidden_out, rows),
        out_specs=(rows, rows, rows, P(), hidden_in, hidden_out),
        check_vma=False,
    )
```
